32 devices in a mesh: seq: 4 (over x, core), blk: 8 (over z, y).
Axes of the slice: x: 2, y: 2, z: 4, core: 2. Of those that a mesh axis runs over, the one named last changes fastest.
Arguments:
- tokens: bfloat16 [512, 8, 1024], P('blk', 'seq'), may hold values from -6 to 6
- segment_ids: int32 [512, 8], P('blk', 'seq'), may hold values from 0 to 7, as said below
- ln1_gain: float32 [1024], replicated, may hold values from 0.5 to 1.5
- ln1_bias: float32 [1024], replicated, may hold values from -1.5 to 1.5
- w_qkv: bfloat16 [1024, 3072], replicated, may hold values from -0.1875 to 0.1875
- w_out: bfloat16 [1024, 1024], replicated, may hold values from -0.75 to 0.75
- ln2_gain: float32 [1024], replicated, may hold values from 0.5 to 1.5
- ln2_bias: float32 [1024], replicated, may hold values from -1.5 to 1.5
- w_fc: bfloat16 [1024, 4096], replicated, may hold values from -0.1875 to 0.1875
- w_proj: bfloat16 [4096, 1024], replicated, may hold values from -0.09375 to 0.09375
- prefix_embed: float32 [10, 1024], replicated, may hold values from -5 to 5
- w_mlp1: float32 [1024, 512], replicated, may hold values from -0.1875 to 0.1875
- b_mlp1: float32 [512], replicated, may hold values from -3 to 3
- w_mlp2: float32 [512, 2048], replicated, may hold values from -0.5 to 0.5
- b_mlp2: float32 [2048], replicated, may hold values from -1.5 to 1.5
- cotangent: bfloat16 [512, 8, 1024], P('blk', 'seq'), may hold values from -6 to 6
Outputs:
- block_out: bfloat16 [512, 8, 1024], P('blk', 'seq')
- input_grad: float32 [512, 8, 1024], P('blk', 'seq')
- grad_prefix: float32 [10, 1024], replicated
- grad_mlp1: float32 [1024, 512], replicated
- grad_bias1: float32 [512], replicated
- grad_mlp2: float32 [512, 2048], replicated
- grad_bias2: float32 [2048], replicated
- softmax_lse: float32 [8, 16, 512], P('seq', None, 'blk')
The draws below stay inside these ranges and needn't reach their ends.
Inputs may be any that keep to these rules, and one draw needn't show every extreme that they name: `segment_ids`: along each row the ids never fall. Of the 2 rows that one index of seq holds, one row, drawn, is a single segment; every other row has exactly 8 segments of drawn lengths.
All inputs are finite; a program needn't handle non-finite values.
Results may differ from the reference program's by a relative error of at most 0.012.
Values may be sent and summed in bfloat16 or wider, within the bound.
No kernel may reach another device: no remote copies, remote signals or barrier semaphores. Data moves between devices by JAX's collectives and lax.ppermute only.
A program may use at most 256 MiB of HBM per device.

```python
import math
import jax
import jax.numpy as jnp
from jax import lax

D = 1024
HEADS = 16
HEAD = 64
FF = 4096
MID = 512
PRE = 10
NDOC = 8
ROWS_GRP = 2
ROWS = 8
LENGTH = 512


def draw_segment_ids(key, part):
    key = jax.random.fold_in(key, 7)
    pick_key, bound_key = jax.random.split(key)
    groups = ROWS // ROWS_GRP
    span_row = jax.random.randint(pick_key, (groups,), 0, ROWS_GRP)
    row_keys = jax.random.split(bound_key, ROWS)

    def bounds_of(row_key):
        return jax.random.permutation(row_key, LENGTH - 1)[:NDOC - 1] + 1
    bounds = jax.vmap(bounds_of)(row_keys)
    positions = jnp.arange(LENGTH, dtype=jnp.int32)
    ids = jnp.sum((bounds[:, None, :] <= positions[None, :, None]).astype(jnp.int32), -1)
    rows_idx = jnp.arange(ROWS, dtype=jnp.int32)
    spanning = rows_idx % ROWS_GRP == jnp.repeat(span_row, ROWS_GRP)
    ids = jnp.where(spanning[:, None], 0, ids)
    return ids.T.astype(jnp.int32)


def level_of(rng, extent, cuts, smallest, top_value):
    level = 1.0
    for dim, shards_of in cuts:
        draws = jax.random.uniform(jax.random.fold_in(jax.random.fold_in(rng, 6), dim), (shards_of,), jnp.float32, smallest / len(cuts), top_value / len(cuts))
        level = level * jnp.repeat(jnp.exp(draws), extent[dim] // shards_of).reshape((-1,) + (1,) * (len(extent) - 1 - dim))
    return level


def noise(rng, extent, scale, bound, cuts=(), held_as=jnp.bfloat16):
    values = scale * jax.random.normal(rng, extent, jnp.float32)
    if cuts:
        values = values * level_of(rng, extent, cuts, -0.22, 0.18)
    return jnp.clip(values, -bound, bound).astype(held_as)


def setup_inputs(seed: int = 0) -> dict:
    splits = jax.random.split(jax.random.key(seed), 17)
    return {
        "tokens": noise(splits[0], (LENGTH, ROWS, D), 1.0, 6.0, ((0, 8), (1, 4))),
        "segment_ids": draw_segment_ids(jax.random.fold_in(splits[16], 71), 0),
        "ln1_gain": jnp.clip(1.0 + 0.1 * jax.random.normal(splits[2], (D,), jnp.float32), 0.5, 1.5),
        "ln1_bias": noise(splits[3], (D,), 0.3, 1.5, (), jnp.float32),
        "w_qkv": noise(splits[4], (D, 3 * D), D ** -0.5, 0.1875),
        "w_out": noise(splits[5], (D, D), (D // 16) ** -0.5, 0.75),
        "ln2_gain": jnp.clip(1.0 + 0.1 * jax.random.normal(splits[6], (D,), jnp.float32), 0.5, 1.5),
        "ln2_bias": noise(splits[7], (D,), 0.3, 1.5, (), jnp.float32),
        "w_fc": noise(splits[8], (D, FF), D ** -0.5, 0.1875),
        "w_proj": noise(splits[9], (FF, D), FF ** -0.5, 0.09375),
        "prefix_embed": noise(splits[10], (PRE, D), 1.0, 5.0, (), jnp.float32),
        "w_mlp1": noise(splits[11], (D, MID), D ** -0.5, 0.1875, (), jnp.float32),
        "b_mlp1": noise(splits[12], (MID,), 0.5, 3.0, (), jnp.float32),
        "w_mlp2": noise(splits[13], (MID, 2 * D), (MID // 4) ** -0.5, 0.5, (), jnp.float32),
        "b_mlp2": noise(splits[14], (2 * D,), 0.3, 1.5, (), jnp.float32),
        "cotangent": noise(splits[15], (LENGTH, ROWS, D), 1.0, 6.0, ((0, 8), (1, 4))),
    }


EPS = 1e-05
NEG = -1e+30
HIGH = lax.Precision.HIGHEST

@jax.custom_vjp
def low(v):
    return lax.optimization_barrier(v.astype(jnp.bfloat16)).astype(jnp.float32)

@jax.custom_vjp
def low_back(v):
    return v

def low_keep(v):
    return (low(v), None)

def low_pass(kept, grad):
    return (grad,)

def back_keep(v):
    return (v, None)

def back_low(kept, grad):
    return (low(grad),)
low.defvjp(low_keep, low_pass)
low_back.defvjp(back_keep, back_low)

def layer_norm(value_in, gain, bias):
    average = lax.optimization_barrier(jnp.mean(value_in, axis=-1, keepdims=True))
    centered = value_in - average
    variance = lax.optimization_barrier(jnp.mean(centered * centered, axis=-1, keepdims=True))
    return centered * lax.rsqrt(variance + EPS) * gain + bias

def adapter(prefix_embed, w_mlp1, b_mlp1, w_mlp2, b_mlp2):
    inner_act = jnp.tanh(jnp.dot(prefix_embed, w_mlp1, precision=HIGH) + b_mlp1)
    return jnp.dot(inner_act, w_mlp2, precision=HIGH) + b_mlp2

def reference(tokens, segment_ids, ln1_gain, ln1_bias, w_qkv, w_out, ln2_gain, ln2_bias, w_fc, w_proj, prefix_embed, w_mlp1, b_mlp1, w_mlp2, b_mlp2, cotangent):
    score_scale = HEAD ** (-0.5)
    stride = math.gcd(LENGTH, 1024)
    blocks = LENGTH // stride
    qkv_weight = w_qkv.astype(jnp.float32)
    out_weight = w_out.astype(jnp.float32)
    fc_weight = w_fc.astype(jnp.float32)
    proj_weight = w_proj.astype(jnp.float32)
    seg_rows = segment_ids.T
    positions = jnp.arange(LENGTH, dtype=jnp.int32)

    def block_forward(inputs, embed, first_w, first_b, second_w, second_b):
        normed_one = low(layer_norm(inputs, ln1_gain, ln1_bias))
        projected = jnp.dot(normed_one, qkv_weight, precision=HIGH)
        queries = low(low_back(projected[..., :D]))
        keys = low(low_back(projected[..., D:2 * D]))
        values = low(low_back(projected[..., 2 * D:]))
        prefix_kv = low(adapter(embed, first_w, first_b, second_w, second_b))
        prefix_keys = prefix_kv[:, :D].reshape(PRE, HEADS, HEAD)
        prefix_values = prefix_kv[:, D:].reshape(PRE, HEADS, HEAD)
        query_rows = jnp.transpose(queries.reshape(LENGTH, ROWS, HEADS, HEAD), (1, 0, 2, 3))
        key_rows = jnp.transpose(keys.reshape(LENGTH, ROWS, HEADS, HEAD), (1, 0, 2, 3))
        value_rows = jnp.transpose(values.reshape(LENGTH, ROWS, HEADS, HEAD), (1, 0, 2, 3))

        def attend_block(item_index):
            row_index = item_index // blocks
            first_pos = item_index % blocks * stride
            query_row = lax.dynamic_index_in_dim(query_rows, row_index, 0, keepdims=False)
            query_block = lax.dynamic_slice_in_dim(query_row, first_pos, stride, 0)
            key_row = lax.dynamic_index_in_dim(key_rows, row_index, 0, keepdims=False)
            value_row = lax.dynamic_index_in_dim(value_rows, row_index, 0, keepdims=False)
            seg_row = lax.dynamic_index_in_dim(seg_rows, row_index, 0, keepdims=False)
            seg_query = lax.dynamic_slice_in_dim(seg_row, first_pos, stride, 0)
            query_pos = first_pos + jnp.arange(stride, dtype=jnp.int32)
            token_scores = jnp.einsum('phd,khd->hpk', query_block, key_row, precision=HIGH)
            prefix_scores = jnp.einsum('phd,jhd->hpj', query_block, prefix_keys, precision=HIGH)
            scores = low_back(score_scale * jnp.concatenate([prefix_scores, token_scores], -1))
            visible = jnp.logical_and(seg_query[:, None] == seg_row[None, :], positions[None, :] <= query_pos[:, None])
            visible = jnp.concatenate([jnp.ones((stride, PRE), dtype=bool), visible], -1)
            scores = jnp.where(visible[None], scores, NEG)
            row_top = lax.optimization_barrier(jnp.max(scores, -1, keepdims=True))
            log_total = row_top + jnp.log(lax.optimization_barrier(jnp.sum(jnp.exp(scores - row_top), -1, keepdims=True)))
            weights = low(jnp.exp(scores - log_total))
            all_values = jnp.concatenate([prefix_values, value_row], 0)
            attended = jnp.einsum('hpk,khd->phd', weights, all_values, precision=HIGH)
            return (attended, log_total[..., 0])
        attended, log_totals = lax.map(jax.checkpoint(attend_block), jnp.arange(ROWS * blocks, dtype=jnp.int32))
        attended = attended.reshape(ROWS, LENGTH, HEADS, HEAD)
        attended = jnp.transpose(attended, (1, 0, 2, 3)).reshape(LENGTH, ROWS, D)
        log_totals = jnp.transpose(log_totals.reshape(ROWS, blocks, HEADS, stride), (0, 2, 1, 3)).reshape(ROWS, HEADS, LENGTH)
        attended = low(low_back(attended))
        branch = low_back(jnp.dot(attended, out_weight, precision=HIGH))
        middle = inputs + branch
        normed_two = low(layer_norm(middle, ln2_gain, ln2_bias))
        hidden_pre = low_back(jnp.dot(normed_two, fc_weight, precision=HIGH))
        hidden_act = low(jax.nn.gelu(hidden_pre, approximate=True))
        outputs = middle + jnp.dot(hidden_act, proj_weight, precision=HIGH)
        return (outputs, log_totals)
    outputs, block_back, log_totals = jax.vjp(block_forward, tokens.astype(jnp.float32), prefix_embed, w_mlp1, b_mlp1, w_mlp2, b_mlp2, has_aux=True)
    gradients = block_back(cotangent.astype(jnp.float32))
    return (outputs.astype(jnp.bfloat16), gradients[0], gradients[1], gradients[2], gradients[3], gradients[4], gradients[5], log_totals)
```

```python
from functools import partial
import math

import jax
import jax.numpy as jnp
from jax import lax
from jax.experimental import pallas as pl
from jax.experimental.pallas import tpu as pltpu
from jax.sharding import PartitionSpec as P

HEADS = 16
HEAD = 64


EPS = 1e-05
NEG = -1e30
HIGH = lax.Precision.HIGHEST


def layer_norm(value_in, gain, bias):
    average = jnp.mean(value_in, axis=-1, keepdims=True)
    centered = value_in - average
    variance = jnp.mean(centered * centered, axis=-1, keepdims=True)
    return centered * lax.rsqrt(variance + EPS) * gain + bias


def adapter(prefix_embed, w_mlp1, b_mlp1, w_mlp2, b_mlp2):
    inner_act = jnp.tanh(jnp.dot(prefix_embed, w_mlp1, precision=HIGH) + b_mlp1)
    return jnp.dot(inner_act, w_mlp2, precision=HIGH) + b_mlp2


def gelu_tanh(pre_act):
    return jax.nn.gelu(pre_act, approximate=True)


def split_heads(block_in):
    return block_in.reshape(block_in.shape[0], block_in.shape[1], HEADS, HEAD)


def allowed(query_pos, query_seg, key_pos, key_seg):
    same_seg = query_seg.T[:, :, None] == key_seg.T[:, None, :]
    causal = key_pos[None, None, :] <= query_pos[None, :, None]
    return jnp.logical_and(same_seg, causal)[:, None]


def scores_of(query_heads, key_block, score_scale):
    return score_scale * jnp.einsum(
        "prhd,krhd->rhpk", query_heads, split_heads(key_block), preferred_element_type=jnp.float32
    )


def block_grads(
    query_heads,
    grad_heads,
    log_total,
    slope_base,
    query_pos,
    query_seg,
    key_block,
    value_block,
    key_pos,
    key_seg,
    score_scale,
):
    scores = scores_of(query_heads, key_block, score_scale)
    scores = jnp.where(allowed(query_pos, query_seg, key_pos, key_seg), scores, NEG)
    weights = jnp.exp(scores - log_total[..., None])
    grad_weights = jnp.einsum(
        "prhd,krhd->rhpk", grad_heads, split_heads(value_block), preferred_element_type=jnp.float32
    )
    slopes = (weights * (grad_weights - slope_base[..., None])).astype(jnp.bfloat16)
    return (weights.astype(jnp.bfloat16), slopes)


def body_plain(
    tokens,
    segment_ids,
    ln1_gain,
    ln1_bias,
    w_qkv,
    w_out,
    ln2_gain,
    ln2_bias,
    w_fc,
    w_proj,
    prefix_embed,
    w_mlp1,
    b_mlp1,
    w_mlp2,
    b_mlp2,
    cotangent,
):
    pos_dev, row_count, width = tokens.shape
    score_scale = HEAD ** (-0.5)
    flat_rows = pos_dev * row_count
    own_pos = lax.axis_index("blk") * pos_dev + jnp.arange(pos_dev)
    inputs = tokens.astype(jnp.float32).reshape(flat_rows, width)
    normed_one = layer_norm(inputs, ln1_gain, ln1_bias).astype(jnp.bfloat16)
    projected = jnp.dot(normed_one, w_qkv, preferred_element_type=jnp.float32).astype(jnp.bfloat16)
    queries = projected[:, :width].reshape(pos_dev, row_count, width)
    keys = projected[:, width : 2 * width].reshape(pos_dev, row_count, width)
    values = projected[:, 2 * width :].reshape(pos_dev, row_count, width)
    query_heads = split_heads(queries)
    prefix_low = adapter(prefix_embed, w_mlp1, b_mlp1, w_mlp2, b_mlp2).astype(jnp.bfloat16)
    prefix_keys = prefix_low[:, :width].reshape(-1, HEADS, HEAD)
    prefix_values = prefix_low[:, width:].reshape(-1, HEADS, HEAD)
    prefix_scores = score_scale * jnp.einsum(
        "prhd,jhd->rhpj", query_heads, prefix_keys, preferred_element_type=jnp.float32
    )
    start_top = jnp.max(prefix_scores, -1)
    start_weights = jnp.exp(prefix_scores - start_top[..., None])
    start_denom = jnp.sum(start_weights, -1)
    start_numer = jnp.einsum(
        "rhpj,jhd->rhpd",
        start_weights.astype(jnp.bfloat16),
        prefix_values,
        preferred_element_type=jnp.float32,
    )
    start_state = (start_top, start_denom, start_numer)
    running = start_state
    key_shards = lax.all_gather(keys, "blk", axis=0, tiled=True)
    value_shards = lax.all_gather(values, "blk", axis=0, tiled=True)
    seg_shards = lax.all_gather(segment_ids, "blk", axis=0, tiled=True)
    num_rows = key_shards.shape[0]
    forward_stride = math.gcd(num_rows, 512)

    def inner(state, block_index):
        running_top, denominator, numerator = state
        offset = block_index * forward_stride
        key_block = lax.dynamic_slice_in_dim(key_shards, offset, forward_stride, 0)
        value_block = lax.dynamic_slice_in_dim(value_shards, offset, forward_stride, 0)
        seg_block = lax.dynamic_slice_in_dim(seg_shards, offset, forward_stride, 0)
        key_pos = offset + jnp.arange(forward_stride)
        scores = jnp.where(
            allowed(own_pos, segment_ids, key_pos, seg_block),
            scores_of(query_heads, key_block, score_scale),
            NEG,
        )
        new_top = jnp.maximum(running_top, jnp.max(scores, -1))
        fading = jnp.exp(running_top - new_top)
        weights = jnp.exp(scores - new_top[..., None])
        denominator = denominator * fading + jnp.sum(weights, -1)
        numerator = numerator * fading[..., None] + jnp.einsum(
            "rhpk,krhd->rhpd",
            weights.astype(jnp.bfloat16),
            split_heads(value_block),
            preferred_element_type=jnp.float32,
        )
        return ((new_top, denominator, numerator), None)

    running, _ = lax.scan(inner, running, jnp.arange(num_rows // forward_stride))
    final_top, final_denom, final_numer = running
    log_total = final_top + jnp.log(final_denom)
    attended = final_numer / final_denom[..., None]
    attended_rows = jnp.transpose(attended, (2, 0, 1, 3)).reshape(flat_rows, width)
    middle = inputs + jnp.dot(
        attended_rows.astype(jnp.bfloat16), w_out, preferred_element_type=jnp.float32
    )
    normed_two = layer_norm(middle, ln2_gain, ln2_bias).astype(jnp.bfloat16)
    hidden_pre = jnp.dot(normed_two, w_fc, preferred_element_type=jnp.float32)
    hidden_act = gelu_tanh(hidden_pre).astype(jnp.bfloat16)
    outputs = middle + jnp.dot(hidden_act, w_proj, preferred_element_type=jnp.float32)
    block_out = outputs.astype(jnp.bfloat16).reshape(pos_dev, row_count, width)
    grad_out = cotangent.reshape(flat_rows, width)
    grad_act = jnp.dot(grad_out, w_proj.T, preferred_element_type=jnp.float32)
    _, gelu_back = jax.vjp(gelu_tanh, hidden_pre)
    grad_pre = gelu_back(grad_act)[0].astype(jnp.bfloat16)
    grad_norm_two = jnp.dot(grad_pre, w_fc.T, preferred_element_type=jnp.float32)
    _, norm_two_back = jax.vjp(partial(layer_norm, gain=ln2_gain, bias=ln2_bias), middle)
    grad_middle = grad_out.astype(jnp.float32) + norm_two_back(grad_norm_two)[0]
    grad_attended = jnp.dot(
        grad_middle.astype(jnp.bfloat16), w_out.T, preferred_element_type=jnp.float32
    ).astype(jnp.bfloat16)
    grad_flat = grad_attended.reshape(pos_dev, row_count, width)
    grad_heads = split_heads(grad_flat)
    slope_base = jnp.sum(jnp.transpose(grad_heads.astype(jnp.float32), (1, 2, 0, 3)) * attended, -1)
    prefix_weights = jnp.exp(prefix_scores - log_total[..., None])
    prefix_dw = jnp.einsum(
        "prhd,jhd->rhpj", grad_heads, prefix_values, preferred_element_type=jnp.float32
    )
    prefix_slopes = (prefix_weights * (prefix_dw - slope_base[..., None])).astype(jnp.bfloat16)
    grad_query = score_scale * jnp.einsum(
        "rhpj,jhd->prhd", prefix_slopes, prefix_keys, preferred_element_type=jnp.float32
    )
    grad_pkeys = score_scale * jnp.einsum(
        "rhpj,prhd->jhd", prefix_slopes, query_heads, preferred_element_type=jnp.float32
    )
    grad_pvalues = jnp.einsum(
        "rhpj,prhd->jhd",
        prefix_weights.astype(jnp.bfloat16),
        grad_heads,
        preferred_element_type=jnp.float32,
    )
    grad_prefix_kv = jnp.concatenate(
        [grad_pkeys.reshape(-1, width), grad_pvalues.reshape(-1, width)], -1
    )
    keys_all, values_all, segs_all = (
        lax.all_gather(keys, "blk", axis=0, tiled=True),
        lax.all_gather(values, "blk", axis=0, tiled=True),
        lax.all_gather(segment_ids, "blk", axis=0, tiled=True),
    )
    length = keys_all.shape[0]
    stride = math.gcd(length, 512)

    def backward_step(grad_q, block_index):
        offset = block_index * stride
        key_block = lax.dynamic_slice_in_dim(keys_all, offset, stride, 0)
        value_block = lax.dynamic_slice_in_dim(values_all, offset, stride, 0)
        seg_block = lax.dynamic_slice_in_dim(segs_all, offset, stride, 0)
        key_pos = offset + jnp.arange(stride)
        weights_low, slopes = block_grads(
            query_heads,
            grad_heads,
            log_total,
            slope_base,
            own_pos,
            segment_ids,
            key_block,
            value_block,
            key_pos,
            seg_block,
            score_scale,
        )
        grad_q = grad_q + score_scale * jnp.einsum(
            "rhpk,krhd->prhd", slopes, split_heads(key_block), preferred_element_type=jnp.float32
        )
        key_term = score_scale * jnp.einsum(
            "rhpk,prhd->krhd", slopes, query_heads, preferred_element_type=jnp.float32
        )
        value_term = jnp.einsum(
            "rhpk,prhd->krhd", weights_low, grad_heads, preferred_element_type=jnp.float32
        )
        return (
            grad_q,
            (
                key_term.reshape(stride, row_count, width),
                value_term.reshape(stride, row_count, width),
            ),
        )

    grad_query, (key_terms, value_terms) = lax.scan(
        backward_step, grad_query, jnp.arange(length // stride)
    )
    key_terms = key_terms.reshape(length, row_count, width)
    value_terms = value_terms.reshape(length, row_count, width)
    grad_keys, grad_values = (
        lax.psum_scatter(key_terms, "blk", scatter_dimension=0, tiled=True),
        lax.psum_scatter(value_terms, "blk", scatter_dimension=0, tiled=True),
    )
    grad_proj = jnp.concatenate(
        [
            grad_query.reshape(flat_rows, width).astype(jnp.bfloat16),
            grad_keys.reshape(flat_rows, width).astype(jnp.bfloat16),
            grad_values.reshape(flat_rows, width).astype(jnp.bfloat16),
        ],
        -1,
    )
    grad_norm_one = jnp.dot(grad_proj, w_qkv.T, preferred_element_type=jnp.float32)
    _, norm_one_back = jax.vjp(partial(layer_norm, gain=ln1_gain, bias=ln1_bias), inputs)
    input_grad = (grad_middle + norm_one_back(grad_norm_one)[0]).reshape(pos_dev, row_count, width)
    _, adapter_back = jax.vjp(adapter, prefix_embed, w_mlp1, b_mlp1, w_mlp2, b_mlp2)
    local_grads = adapter_back(grad_prefix_kv)
    summed = lax.psum(
        (local_grads[0], local_grads[1], local_grads[2], local_grads[3], local_grads[4]),
        ("seq", "blk"),
    )
    return (block_out, input_grad, summed[0], summed[1], summed[2], summed[3], summed[4], log_total)


F32 = jnp.float32
BF16 = jnp.bfloat16
LANES = 128
PRE_ROWS = 16
MIB = 1 << 20
PRE = 10


def nn(left, right):
    return jnp.dot(left, right, preferred_element_type=F32)


def nt(left, right):
    return lax.dot_general(left, right, (((1,), (1,)), ((), ())), preferred_element_type=F32)


def norm_parts(value_in):
    average = jnp.mean(value_in, axis=-1, keepdims=True)
    centered = value_in - average
    variance = jnp.mean(centered * centered, axis=-1, keepdims=True)
    inverse = lax.rsqrt(variance + EPS)
    return centered * inverse, inverse


def norm_back(unit, inverse, gain, grad):
    scaled = grad * gain
    first = jnp.mean(scaled, axis=-1, keepdims=True)
    second = jnp.mean(scaled * unit, axis=-1, keepdims=True)
    return inverse * (scaled - first - unit * second)


def iota(shape, dim):
    return lax.broadcasted_iota(jnp.int32, shape, dim)


def place():
    blk = lax.axis_index("blk")
    return (blk // 2) % 2, lax.axis_index("seq") % 2, blk % 2


def positions(index, half, row, core, y_at):
    upper = (index >= half).astype(jnp.int32)
    slot = upper + row - 2 * upper * row
    block = (2 * core + slot) * 2 + y_at
    return block * half + index - upper * half


def members(core, y_at):
    return ((core, y_at), (1 - core, y_at), (core, 1 - y_at), (1 - core, 1 - y_at))


def all_positions(shape, dim, half, row, core, y_at):
    part = tuple(2 * half if d == dim else n for d, n in enumerate(shape))
    return jnp.concatenate(
        [positions(iota(part, dim), half, row, c, y) for c, y in members(core, y_at)], dim
    )


def vmem():
    return pl.BlockSpec(memory_space=pltpu.VMEM)


def hbm():
    return pl.BlockSpec(memory_space=pl.ANY)


def project_kernel(count, *refs):
    messages, (gain, bias, weight, out, marks, normed) = refs[:count], refs[count:]
    half, width = messages[0].shape[0], normed.shape[1]

    @pl.when(pl.program_id(0) == 0)
    def _():
        for i, message in enumerate(messages):
            rows = pl.ds(i * half, half)
            unit, _ = norm_parts(message[:, :width].astype(F32))
            normed[rows] = (unit * gain[...] + bias[...]).astype(BF16)
            marks[rows] = message[:, width:]

    out[...] = nn(normed[...], weight[...]).astype(BF16)


def project(messages, gain, bias, weight, step=1024):
    count, (half, wide) = len(messages), messages[0].shape
    width, columns = weight.shape
    rows = count * half
    return pl.pallas_call(
        partial(project_kernel, count),
        grid=(columns // step,),
        in_specs=[pl.BlockSpec((half, wide), lambda i: (0, 0))] * count
        + [pl.BlockSpec((1, width), lambda i: (0, 0))] * 2
        + [pl.BlockSpec((width, step), lambda i: (0, i))],
        out_specs=[
            pl.BlockSpec((rows, step), lambda i: (0, i)),
            pl.BlockSpec((rows, LANES), lambda i: (0, 0)),
        ],
        out_shape=[
            jax.ShapeDtypeStruct((rows, columns), BF16),
            jax.ShapeDtypeStruct((rows, LANES), BF16),
        ],
        scratch_shapes=[pltpu.VMEM((rows, width), BF16)],
        compiler_params=pltpu.CompilerParams(vmem_limit_bytes=30 * MIB),
        cost_estimate=pl.CostEstimate(
            flops=2 * rows * width * columns, bytes_accessed=2 * width * columns, transcendentals=0
        ),
        name="project",
    )(*messages, gain[None], bias[None], weight)


def head_mask(rows):
    return iota((rows, LANES), 1) < HEAD


def two_heads(pair, low):
    zero = jnp.zeros_like(pair)
    return jnp.concatenate([jnp.where(low, pair, zero), jnp.where(low, zero, pair)], 0)


def join_heads(stacked, low):
    rows = stacked.shape[0] // 2
    return jnp.where(low, stacked[:rows], stacked[rows:])


def picks(rows, pair, first, value):
    lane = iota((rows, LANES), 1)
    inside = jnp.logical_and(lane >= first, lane < first + 3 * HEADS)
    parts = [
        jnp.where(jnp.logical_and(inside, lane % HEADS == 2 * pair + i), value, 0.0) for i in range(2)
    ]
    return jnp.concatenate(parts, 0)


def three_parts(value_in, first):
    lane = iota(value_in.shape, 1)
    high = value_in.astype(BF16).astype(F32)
    rest = value_in - high
    middle = rest.astype(BF16).astype(F32)
    low = rest - middle
    part = (lane - first) // HEADS
    chosen = jnp.where(part == 0, high, jnp.where(part == 1, middle, low))
    inside = jnp.logical_and(lane >= first, lane < first + 3 * HEADS)
    return jnp.where(inside, chosen, 0.0)


def key_bias(marks_own, marks_a, marks_b, half):
    row, core, y_at = place()
    rows = 2 * half
    own = positions(iota((rows, 1), 0), half, row, core, y_at)
    other = all_positions((1, 8 * half), 1, half, row, core, y_at)
    same = nt(marks_own, jnp.concatenate([marks_a, marks_b], 0))
    visible = jnp.logical_and(same > 0.5, other <= own)
    token_bias = jnp.where(visible, 0.0, NEG)
    prefix_bias = jnp.where(iota((rows, LANES), 1) < PRE, 0.0, NEG)
    return jnp.concatenate([token_bias, prefix_bias], 1)


def with_prefix(part_a, part_b, prefix):
    pad = jnp.zeros((LANES - prefix.shape[0], prefix.shape[1]), prefix.dtype)
    return jnp.concatenate([part_a, part_b, prefix, pad], 0)


def middle_kernel(
    qkv_a,
    qkv_b,
    marks_a,
    marks_b,
    prefix_kv,
    own_0,
    own_1,
    cot_0,
    cot_1,
    gain,
    bias,
    w_out,
    w_fc,
    w_proj,
    back_0,
    back_1,
    grad_out_heads,
    grad_middle,
    v_out,
    v_fc,
    v_proj,
    sems,
    scores_bias,
    attended,
    stats,
    middle,
    normed,
    total,
    grad_norm,
    cot,
):
    half, rows = own_0.shape[0], 2 * own_0.shape[0]
    width = middle.shape[1]
    steps, step = v_fc.shape[0], v_fc.shape[2]
    copies = [pltpu.make_async_copy(w_out, v_out, sems.at[0])]
    for i in range(steps):
        span = pl.ds(i * step, step)
        copies.append(pltpu.make_async_copy(w_fc.at[:, span], v_fc.at[i], sems.at[1 + 2 * i]))
        copies.append(pltpu.make_async_copy(w_proj.at[span], v_proj.at[i], sems.at[2 + 2 * i]))
    for copy in copies:
        copy.start()

    scores_bias[...] = key_bias(marks_a[:rows], marks_a[...], marks_b[...], half)
    low = head_mask(rows)
    lane = iota((rows, LANES), 1)
    stats[...] = jnp.zeros_like(stats)

    def attend(pair, carry):
        at = pl.ds(pl.multiple_of(pair * LANES, LANES), LANES)
        at_k = pl.ds(pl.multiple_of(width + pair * LANES, LANES), LANES)
        at_v = pl.ds(pl.multiple_of(2 * width + pair * LANES, LANES), LANES)
        query = two_heads(qkv_a[:rows, at] * jnp.asarray(HEAD**-0.5, BF16), low)
        keys = with_prefix(qkv_a[:, at_k], qkv_b[:, at_k], prefix_kv[:, at])
        values = with_prefix(qkv_a[:, at_v], qkv_b[:, at_v], prefix_kv[:, at_k])
        scores = nt(query, keys)
        mask = scores_bias[...]
        scores = scores + jnp.concatenate([mask, mask], 0)
        top = jnp.max(scores, -1, keepdims=True)
        weights = jnp.exp(scores - top)
        denominator = jnp.sum(weights, -1, keepdims=True)
        mixed = nn(weights.astype(BF16), values) / denominator
        attended[:, at] = join_heads(mixed, low)
        log_total = top + jnp.log(denominator)
        inside = lane < 3 * HEADS
        for i in range(2):
            here = jnp.logical_and(inside, lane % HEADS == 2 * pair + i)
            stats[...] = jnp.where(here, log_total[i * rows : (i + 1) * rows], stats[...])
        return carry

    lax.fori_loop(0, HEADS // 2, attend, 0)

    copies[0].wait()
    inputs = jnp.concatenate([own_0[:, :width], own_1[:, :width]], 0).astype(F32)
    middle[...] = inputs + nn(attended[...].astype(BF16), v_out[...])
    unit, _ = norm_parts(middle[...])
    normed[...] = (unit * gain[...] + bias[...]).astype(BF16)
    cot[...] = jnp.concatenate([cot_0[...], cot_1[...]], 0)
    total[...] = middle[...]
    grad_norm[...] = jnp.zeros_like(grad_norm)

    def feed(i, carry):
        for which in (0, 1):
            pltpu.make_async_copy(
                (v_fc, v_proj)[which].at[i], (v_fc, v_proj)[which].at[i], sems.at[1 + 2 * i + which]
            ).wait()
        fc, proj = v_fc[i], v_proj[i]
        pre = nn(normed[...], fc)
        grad_act = nt(cot[...], proj)
        cubic = 0.044715 * pre * pre
        curve = jnp.tanh(math.sqrt(2 / math.pi) * pre * (1.0 + cubic))
        act = 0.5 * pre * (1.0 + curve)
        slope = 0.5 * (1.0 + curve) + 0.5 * math.sqrt(2 / math.pi) * pre * (1.0 - curve * curve) * (
            1.0 + 3.0 * cubic
        )
        grad_pre = (grad_act * slope).astype(BF16)
        total[...] += nn(act.astype(BF16), proj)
        grad_norm[...] += nt(grad_pre, fc)
        return carry

    lax.fori_loop(0, steps, feed, 0)

    out = total[...].astype(BF16)
    back_0[:, :width] = out[:half]
    back_1[:, :width] = out[half:]
    unit, inverse = norm_parts(middle[...])
    grads = cot[...].astype(F32) + norm_back(unit, inverse, gain[...], grad_norm[...])
    grad_middle[...] = grads
    grad_heads = nt(grads.astype(BF16), v_out[...]).astype(BF16)
    grad_out_heads[:, :width] = grad_heads
    product = grad_heads.astype(F32) * attended[...]
    ones = jnp.where(
        jnp.logical_and(
            iota((width, LANES), 0) // HEAD == iota((width, LANES), 1) % HEADS,
            jnp.logical_and(
                iota((width, LANES), 1) >= 3 * HEADS, iota((width, LANES), 1) < 6 * HEADS
            ),
        ),
        1.0,
        0.0,
    ).astype(BF16)
    bases = jnp.zeros((rows, LANES), F32)
    for _ in range(3):
        part = product.astype(BF16)
        bases = bases + nn(part, ones)
        product = product - part.astype(F32)
    marks = three_parts(stats[...], 0) + three_parts(bases, 3 * HEADS)
    marks = marks.astype(BF16)
    grad_out_heads[:, width:] = marks
    back_0[:, width:] = marks[:half]
    back_1[:, width:] = marks[half:]


def middle_part(qkv_a, qkv_b, marks_a, marks_b, prefix_kv, own, cots, gain, bias, w_out, w_fc, w_proj):
    half, width = cots[0].shape
    rows = 2 * half
    hidden = w_fc.shape[1]
    steps = 8
    step = hidden // steps
    wide = width + LANES
    return pl.pallas_call(
        middle_kernel,
        in_specs=[vmem()] * 11 + [hbm()] * 3,
        out_specs=[vmem()] * 4,
        out_shape=[
            jax.ShapeDtypeStruct((half, wide), BF16),
            jax.ShapeDtypeStruct((half, wide), BF16),
            jax.ShapeDtypeStruct((rows, wide), BF16),
            jax.ShapeDtypeStruct((rows, width), F32),
        ],
        scratch_shapes=[
            pltpu.VMEM((width, width), BF16),
            pltpu.VMEM((steps, width, step), BF16),
            pltpu.VMEM((steps, step, width), BF16),
            pltpu.SemaphoreType.DMA((1 + 2 * steps,)),
            pltpu.VMEM((rows, 4 * rows + LANES), F32),
            pltpu.VMEM((rows, width), F32),
            pltpu.VMEM((rows, LANES), F32),
            pltpu.VMEM((rows, width), F32),
            pltpu.VMEM((rows, width), BF16),
            pltpu.VMEM((rows, width), F32),
            pltpu.VMEM((rows, width), F32),
            pltpu.VMEM((rows, width), BF16),
        ],
        compiler_params=pltpu.CompilerParams(vmem_limit_bytes=48 * MIB),
        cost_estimate=pl.CostEstimate(
            flops=2 * rows * width * (4 * hidden + 2 * width),
            bytes_accessed=2 * width * (2 * hidden + width),
            transcendentals=rows * hidden,
        ),
        name="middle",
    )(
        qkv_a, qkv_b, marks_a, marks_b, prefix_kv, *own, *cots, gain[None], bias[None], w_out, w_fc, w_proj
    )


def key_grads(keys, values, queries, grads, marks, pair, low, mask):
    rows = keys.shape[0]
    scale = jnp.asarray(HEAD**-0.5, BF16)
    left = jnp.concatenate(
        [two_heads(keys * scale, low), picks(rows, pair, 0, -1.0).astype(BF16)], 1
    )
    scores = nt(left, jnp.concatenate([queries, marks], 1))
    weights = jnp.exp(scores + jnp.concatenate([mask, mask], 0))
    left = jnp.concatenate(
        [two_heads(values, low), picks(rows, pair, 3 * HEADS, -1.0).astype(BF16)], 1
    )
    slopes = weights * nt(left, jnp.concatenate([grads, marks], 1))
    key_grad = nn(slopes.astype(BF16), queries)
    value_grad = nn(weights.astype(BF16), grads)
    return join_heads(key_grad, low) * HEAD**-0.5, join_heads(value_grad, low)


def prefix_kernel(qkv_a, grads, prefix_kv, out):
    rows, width = grads.shape[0], grads.shape[1] - LANES
    count = prefix_kv.shape[0]
    low = head_mask(count)
    mask = jnp.where(iota((count, rows), 0) < PRE, 0.0, NEG)
    marks = grads[:, width:]

    def step(pair, carry):
        at = pl.ds(pl.multiple_of(pair * LANES, LANES), LANES)
        at_v = pl.ds(pl.multiple_of(width + pair * LANES, LANES), LANES)
        key_grad, value_grad = key_grads(
            prefix_kv[:, at], prefix_kv[:, at_v], qkv_a[:rows, at], grads[:, at], marks, pair, low, mask
        )
        out[:, at] = key_grad[:PRE]
        out[:, at_v] = value_grad[:PRE]
        return carry

    lax.fori_loop(0, HEADS // 2, step, 0)


def prefix_part(qkv_a, grads, prefix_kv):
    return pl.pallas_call(
        prefix_kernel,
        in_specs=[vmem()] * 3,
        out_specs=vmem(),
        out_shape=jax.ShapeDtypeStruct((PRE, prefix_kv.shape[1]), F32),
        compiler_params=pltpu.CompilerParams(vmem_limit_bytes=16 * MIB),
        cost_estimate=pl.CostEstimate(flops=1 << 29, bytes_accessed=1 << 20, transcendentals=1 << 16),
        name="prefix",
    )(qkv_a, grads, prefix_kv)


def query_kernel(qkv_a, qkv_b, marks_a, marks_b, prefix_kv, grads, weight, out, scores_bias, grad_query):
    rows, width = grad_query.shape
    scores_bias[...] = key_bias(marks_a[:rows], marks_a[...], marks_b[...], rows // 2)
    low = head_mask(rows)
    marks = grads[:, width:]
    marks_twice = jnp.concatenate([marks, marks], 0)
    ones = jnp.ones((4 * rows + LANES, LANES), BF16)

    def step(pair, carry):
        at = pl.ds(pl.multiple_of(pair * LANES, LANES), LANES)
        at_k = pl.ds(pl.multiple_of(width + pair * LANES, LANES), LANES)
        at_v = pl.ds(pl.multiple_of(2 * width + pair * LANES, LANES), LANES)
        keys = with_prefix(qkv_a[:, at_k], qkv_b[:, at_k], prefix_kv[:, at])
        values = with_prefix(qkv_a[:, at_v], qkv_b[:, at_v], prefix_kv[:, at_k])
        query = two_heads(qkv_a[:rows, at] * jnp.asarray(HEAD**-0.5, BF16), low)
        tops = marks_twice * picks(rows, pair, 0, -1.0).astype(BF16)
        scores = nt(jnp.concatenate([query, tops], 1), jnp.concatenate([keys, ones], 1))
        mask = scores_bias[...]
        weights = jnp.exp(scores + jnp.concatenate([mask, mask], 0))
        bases = marks_twice * picks(rows, pair, 3 * HEADS, -1.0).astype(BF16)
        left = jnp.concatenate([two_heads(grads[:, at], low), bases], 1)
        slopes = weights * nt(left, jnp.concatenate([values, ones], 1))
        grad = join_heads(nn(slopes.astype(BF16), keys), low)
        grad_query[:, at] = (grad * HEAD**-0.5).astype(BF16)
        return carry

    lax.fori_loop(0, HEADS // 2, step, 0)
    out[...] = nt(grad_query[...], weight[...])


def query_part(qkv_a, qkv_b, marks_a, marks_b, prefix_kv, grads, weight):
    rows, width = grads.shape[0], grads.shape[1] - LANES
    return pl.pallas_call(
        query_kernel,
        grid=(1,),
        in_specs=[pl.BlockSpec(memory_space=pltpu.VMEM)] * 6 + [pl.BlockSpec((width, width), lambda i: (0, 0))],
        out_specs=pl.BlockSpec(memory_space=pltpu.VMEM),
        out_shape=jax.ShapeDtypeStruct((rows, width), F32),
        scratch_shapes=[pltpu.VMEM((rows, 4 * rows + LANES), F32), pltpu.VMEM((rows, width), BF16)],
        compiler_params=pltpu.CompilerParams(vmem_limit_bytes=30 * MIB),
        cost_estimate=pl.CostEstimate(flops=1 << 32, bytes_accessed=1 << 23, transcendentals=1 << 20),
        name="query",
    )(qkv_a, qkv_b, marks_a, marks_b, prefix_kv, grads, weight)


def final_kernel(
    qkv_a,
    qkv_b,
    marks_a,
    marks_b,
    grads_0,
    grads_1,
    grads_2,
    grads_3,
    own_0,
    own_1,
    gain,
    grad_middle,
    grad_partial,
    weight,
    back_0,
    back_1,
    v_weight,
    sem,
    scores_bias,
    grad_keys,
):
    half, rows = own_0.shape[0], 2 * own_0.shape[0]
    width = grad_middle.shape[1]
    load = pltpu.make_async_copy(weight.at[:, pl.ds(width, 2 * width)], v_weight, sem)
    load.start()
    row, core, y_at = place()
    own = positions(iota((rows, 1), 0), half, row, core, y_at)
    other = all_positions((1, 8 * half), 1, half, row, core, y_at)
    same = nt(marks_a[:rows], jnp.concatenate([marks_a[...], marks_b[...]], 0))
    visible = jnp.logical_and(same > 0.5, own <= other)
    scores_bias[...] = jnp.where(visible, 0.0, NEG)
    low = head_mask(rows)
    blocks = (grads_0, grads_1, grads_2, grads_3)
    marks = jnp.concatenate([g[:, width:] for g in blocks], 0)

    def step(pair, carry):
        at = pl.ds(pl.multiple_of(pair * LANES, LANES), LANES)
        at_k = pl.ds(pl.multiple_of(width + pair * LANES, LANES), LANES)
        at_v = pl.ds(pl.multiple_of(2 * width + pair * LANES, LANES), LANES)
        queries = jnp.concatenate([qkv_a[:, at], qkv_b[:, at]], 0)
        grads = jnp.concatenate([g[:, at] for g in blocks], 0)
        key_grad, value_grad = key_grads(
            qkv_a[:rows, at_k], qkv_a[:rows, at_v], queries, grads, marks, pair, low, scores_bias[...]
        )
        grad_keys[:, at] = key_grad.astype(BF16)
        grad_keys[:, at_k] = value_grad.astype(BF16)
        return carry

    lax.fori_loop(0, HEADS // 2, step, 0)
    load.wait()
    grad_norm = grad_partial[...] + nt(grad_keys[...], v_weight[...])
    inputs = jnp.concatenate([own_0[:, :width], own_1[:, :width]], 0).astype(F32)
    unit, inverse = norm_parts(inputs)
    out = (grad_middle[...] + norm_back(unit, inverse, gain[...], grad_norm)).astype(BF16)
    back_0[...] = out[:half]
    back_1[...] = out[half:]


def final_part(qkv_a, qkv_b, marks_a, marks_b, grads, own, gain, grad_middle, grad_partial, weight):
    rows, width = grad_middle.shape
    half = rows // 2
    return pl.pallas_call(
        final_kernel,
        in_specs=[vmem()] * 13 + [hbm()],
        out_specs=[vmem()] * 2,
        out_shape=[jax.ShapeDtypeStruct((half, width), BF16)] * 2,
        scratch_shapes=[
            pltpu.VMEM((width, 2 * width), BF16),
            pltpu.SemaphoreType.DMA,
            pltpu.VMEM((rows, 4 * rows), F32),
            pltpu.VMEM((rows, 2 * width), BF16),
        ],
        compiler_params=pltpu.CompilerParams(vmem_limit_bytes=30 * MIB),
        cost_estimate=pl.CostEstimate(flops=1 << 32, bytes_accessed=1 << 23, transcendentals=1 << 20),
        name="final",
    )(qkv_a, qkv_b, marks_a, marks_b, *grads, *own, gain[None], grad_middle, grad_partial, weight)


def routes(k):
    pairs = []
    for seq in range(4):
        for blk in range(8):
            group, z_at, y_at = seq % 2, blk // 2, blk % 2
            row = (z_at + k) % 2
            pairs.append((seq * 8 + blk, (seq - group + z_at // 2) * 8 + (2 * group + row) * 2 + y_at))
    return pairs


def body_rows(
    tokens,
    segment_ids,
    ln1_gain,
    ln1_bias,
    w_qkv,
    w_out,
    ln2_gain,
    ln2_bias,
    w_fc,
    w_proj,
    prefix_embed,
    w_mlp1,
    b_mlp1,
    w_mlp2,
    b_mlp2,
    cotangent,
):
    half, _, width = tokens.shape
    everyone = ("seq", "blk")
    there = [routes(k) for k in range(2)]
    back = [[(b, a) for a, b in pairs] for pairs in there]
    swap_core = [(i, i ^ 1) for i in range(4)]
    swap_y = [(i, i ^ 1) for i in range(8)]
    odd = (lax.axis_index("blk") // 2) % 2 == 1

    def sorted_rows(first, second):
        return jnp.where(odd, second, first), jnp.where(odd, first, second)

    marks = (segment_ids[:, :, None] == jnp.arange(LANES)[None, None]).astype(BF16)
    marked = jnp.concatenate([tokens, marks], -1)
    out_msgs = sorted_rows(marked[:, 0], marked[:, 1])
    own = [lax.ppermute(m, everyone, there[k]) for k, m in enumerate(out_msgs)]
    across = [lax.ppermute(m, "blk", swap_y) for m in own]
    beside = [lax.ppermute(m, "seq", swap_core) for m in own]
    cot_msgs = sorted_rows(cotangent[:, 0], cotangent[:, 1])
    cots = [lax.ppermute(m, everyone, there[k]) for k, m in enumerate(cot_msgs)]
    beyond = [lax.ppermute(m, "seq", swap_core) for m in across]

    prefix_kv, adapter_back = jax.vjp(adapter, prefix_embed, w_mlp1, b_mlp1, w_mlp2, b_mlp2)
    prefix_kv = jnp.pad(prefix_kv.astype(BF16), ((0, PRE_ROWS - prefix_kv.shape[0]), (0, 0)))

    qkv_a, marks_a = project(own + beside, ln1_gain, ln1_bias, w_qkv)
    qkv_b, marks_b = project(across + beyond, ln1_gain, ln1_bias, w_qkv)
    back_0, back_1, grads, grad_middle = middle_part(
        qkv_a, qkv_b, marks_a, marks_b, prefix_kv, own, cots, ln2_gain, ln2_bias, w_out, w_fc, w_proj
    )
    grads_y = lax.ppermute(grads, "blk", swap_y)
    grads_c = lax.ppermute(grads, "seq", swap_core)
    grads_yc = lax.ppermute(grads_y, "seq", swap_core)
    home = [lax.ppermute(m, everyone, back[k]) for k, m in enumerate((back_0, back_1))]

    grad_prefix_kv = prefix_part(qkv_a, grads, prefix_kv)
    for axis, size, far in (("seq", 4, 2), ("blk", 8, 2), ("blk", 8, 4), ("blk", 8, 1), ("seq", 4, 1)):
        grad_prefix_kv = grad_prefix_kv + lax.ppermute(
            grad_prefix_kv, axis, [(i, i ^ far) for i in range(size)]
        )
    grad_partial = query_part(qkv_a, qkv_b, marks_a, marks_b, prefix_kv, grads, w_qkv)
    final_0, final_1 = final_part(
        qkv_a,
        qkv_b,
        marks_a,
        marks_b,
        (grads, grads_c, grads_y, grads_yc),
        own,
        ln1_gain,
        grad_middle,
        grad_partial,
        w_qkv,
    )
    finals = [lax.ppermute(m, everyone, back[k]) for k, m in enumerate((final_0, final_1))]
    summed = adapter_back(grad_prefix_kv)

    home = sorted_rows(*home)
    block_out = jnp.stack([m[:, :width] for m in home], 1)
    logs = [m[:, width : width + 3 * HEADS].astype(F32).reshape(half, 3, HEADS).sum(1) for m in home]
    log_total = jnp.stack([jnp.transpose(m) for m in logs], 0)
    input_grad = jnp.stack(sorted_rows(*finals), 1).astype(F32)
    return (block_out, input_grad, summed[0], summed[1], summed[2], summed[3], summed[4], log_total)


def solution(mesh):
    four_by_eight = mesh.shape["seq"] == 4 and mesh.shape["blk"] == 8
    placed = (
        P("blk", "seq", None),
        P("blk", "seq"),
        P(),
        P(),
        P(),
        P(),
        P(),
        P(),
        P(),
        P(),
        P(),
        P(),
        P(),
        P(),
        P(),
        P("blk", "seq", None),
    )
    return jax.shard_map(
        body_rows if four_by_eight else body_plain,
        mesh=mesh,
        in_specs=placed,
        out_specs=(
            P("blk", "seq", None),
            P("blk", "seq", None),
            P(),
            P(),
            P(),
            P(),
            P(),
            P("seq", None, "blk"),
        ),
        check_vma=False,
    )
```

```python
from functools import partial
import math

import jax
import jax.numpy as jnp
from jax import lax
from jax.experimental import pallas as pl
from jax.experimental.pallas import tpu as pltpu
from jax.sharding import PartitionSpec as P

HEADS = 16
HEAD = 64


EPS = 1e-05
NEG = -1e30
HIGH = lax.Precision.HIGHEST


def layer_norm(value_in, gain, bias):
    average = jnp.mean(value_in, axis=-1, keepdims=True)
    centered = value_in - average
    variance = jnp.mean(centered * centered, axis=-1, keepdims=True)
    return centered * lax.rsqrt(variance + EPS) * gain + bias


def adapter(prefix_embed, w_mlp1, b_mlp1, w_mlp2, b_mlp2):
    inner_act = jnp.tanh(jnp.dot(prefix_embed, w_mlp1, precision=HIGH) + b_mlp1)
    return jnp.dot(inner_act, w_mlp2, precision=HIGH) + b_mlp2


def gelu_tanh(pre_act):
    return jax.nn.gelu(pre_act, approximate=True)


def split_heads(block_in):
    return block_in.reshape(block_in.shape[0], block_in.shape[1], HEADS, HEAD)


def allowed(query_pos, query_seg, key_pos, key_seg):
    same_seg = query_seg.T[:, :, None] == key_seg.T[:, None, :]
    causal = key_pos[None, None, :] <= query_pos[None, :, None]
    return jnp.logical_and(same_seg, causal)[:, None]


def scores_of(query_heads, key_block, score_scale):
    return score_scale * jnp.einsum(
        "prhd,krhd->rhpk", query_heads, split_heads(key_block), preferred_element_type=jnp.float32
    )


def block_grads(
    query_heads,
    grad_heads,
    log_total,
    slope_base,
    query_pos,
    query_seg,
    key_block,
    value_block,
    key_pos,
    key_seg,
    score_scale,
):
    scores = scores_of(query_heads, key_block, score_scale)
    scores = jnp.where(allowed(query_pos, query_seg, key_pos, key_seg), scores, NEG)
    weights = jnp.exp(scores - log_total[..., None])
    grad_weights = jnp.einsum(
        "prhd,krhd->rhpk", grad_heads, split_heads(value_block), preferred_element_type=jnp.float32
    )
    slopes = (weights * (grad_weights - slope_base[..., None])).astype(jnp.bfloat16)
    return (weights.astype(jnp.bfloat16), slopes)


def body_plain(
    tokens,
    segment_ids,
    ln1_gain,
    ln1_bias,
    w_qkv,
    w_out,
    ln2_gain,
    ln2_bias,
    w_fc,
    w_proj,
    prefix_embed,
    w_mlp1,
    b_mlp1,
    w_mlp2,
    b_mlp2,
    cotangent,
):
    pos_dev, row_count, width = tokens.shape
    score_scale = HEAD ** (-0.5)
    flat_rows = pos_dev * row_count
    own_pos = lax.axis_index("blk") * pos_dev + jnp.arange(pos_dev)
    inputs = tokens.astype(jnp.float32).reshape(flat_rows, width)
    normed_one = layer_norm(inputs, ln1_gain, ln1_bias).astype(jnp.bfloat16)
    projected = jnp.dot(normed_one, w_qkv, preferred_element_type=jnp.float32).astype(jnp.bfloat16)
    queries = projected[:, :width].reshape(pos_dev, row_count, width)
    keys = projected[:, width : 2 * width].reshape(pos_dev, row_count, width)
    values = projected[:, 2 * width :].reshape(pos_dev, row_count, width)
    query_heads = split_heads(queries)
    prefix_low = adapter(prefix_embed, w_mlp1, b_mlp1, w_mlp2, b_mlp2).astype(jnp.bfloat16)
    prefix_keys = prefix_low[:, :width].reshape(-1, HEADS, HEAD)
    prefix_values = prefix_low[:, width:].reshape(-1, HEADS, HEAD)
    prefix_scores = score_scale * jnp.einsum(
        "prhd,jhd->rhpj", query_heads, prefix_keys, preferred_element_type=jnp.float32
    )
    start_top = jnp.max(prefix_scores, -1)
    start_weights = jnp.exp(prefix_scores - start_top[..., None])
    start_denom = jnp.sum(start_weights, -1)
    start_numer = jnp.einsum(
        "rhpj,jhd->rhpd",
        start_weights.astype(jnp.bfloat16),
        prefix_values,
        preferred_element_type=jnp.float32,
    )
    start_state = (start_top, start_denom, start_numer)
    running = start_state
    key_shards = lax.all_gather(keys, "blk", axis=0, tiled=True)
    value_shards = lax.all_gather(values, "blk", axis=0, tiled=True)
    seg_shards = lax.all_gather(segment_ids, "blk", axis=0, tiled=True)
    num_rows = key_shards.shape[0]
    forward_stride = math.gcd(num_rows, 512)

    def inner(state, block_index):
        running_top, denominator, numerator = state
        offset = block_index * forward_stride
        key_block = lax.dynamic_slice_in_dim(key_shards, offset, forward_stride, 0)
        value_block = lax.dynamic_slice_in_dim(value_shards, offset, forward_stride, 0)
        seg_block = lax.dynamic_slice_in_dim(seg_shards, offset, forward_stride, 0)
        key_pos = offset + jnp.arange(forward_stride)
        scores = jnp.where(
            allowed(own_pos, segment_ids, key_pos, seg_block),
            scores_of(query_heads, key_block, score_scale),
            NEG,
        )
        new_top = jnp.maximum(running_top, jnp.max(scores, -1))
        fading = jnp.exp(running_top - new_top)
        weights = jnp.exp(scores - new_top[..., None])
        denominator = denominator * fading + jnp.sum(weights, -1)
        numerator = numerator * fading[..., None] + jnp.einsum(
            "rhpk,krhd->rhpd",
            weights.astype(jnp.bfloat16),
            split_heads(value_block),
            preferred_element_type=jnp.float32,
        )
        return ((new_top, denominator, numerator), None)

    running, _ = lax.scan(inner, running, jnp.arange(num_rows // forward_stride))
    final_top, final_denom, final_numer = running
    log_total = final_top + jnp.log(final_denom)
    attended = final_numer / final_denom[..., None]
    attended_rows = jnp.transpose(attended, (2, 0, 1, 3)).reshape(flat_rows, width)
    middle = inputs + jnp.dot(
        attended_rows.astype(jnp.bfloat16), w_out, preferred_element_type=jnp.float32
    )
    normed_two = layer_norm(middle, ln2_gain, ln2_bias).astype(jnp.bfloat16)
    hidden_pre = jnp.dot(normed_two, w_fc, preferred_element_type=jnp.float32)
    hidden_act = gelu_tanh(hidden_pre).astype(jnp.bfloat16)
    outputs = middle + jnp.dot(hidden_act, w_proj, preferred_element_type=jnp.float32)
    block_out = outputs.astype(jnp.bfloat16).reshape(pos_dev, row_count, width)
    grad_out = cotangent.reshape(flat_rows, width)
    grad_act = jnp.dot(grad_out, w_proj.T, preferred_element_type=jnp.float32)
    _, gelu_back = jax.vjp(gelu_tanh, hidden_pre)
    grad_pre = gelu_back(grad_act)[0].astype(jnp.bfloat16)
    grad_norm_two = jnp.dot(grad_pre, w_fc.T, preferred_element_type=jnp.float32)
    _, norm_two_back = jax.vjp(partial(layer_norm, gain=ln2_gain, bias=ln2_bias), middle)
    grad_middle = grad_out.astype(jnp.float32) + norm_two_back(grad_norm_two)[0]
    grad_attended = jnp.dot(
        grad_middle.astype(jnp.bfloat16), w_out.T, preferred_element_type=jnp.float32
    ).astype(jnp.bfloat16)
    grad_flat = grad_attended.reshape(pos_dev, row_count, width)
    grad_heads = split_heads(grad_flat)
    slope_base = jnp.sum(jnp.transpose(grad_heads.astype(jnp.float32), (1, 2, 0, 3)) * attended, -1)
    prefix_weights = jnp.exp(prefix_scores - log_total[..., None])
    prefix_dw = jnp.einsum(
        "prhd,jhd->rhpj", grad_heads, prefix_values, preferred_element_type=jnp.float32
    )
    prefix_slopes = (prefix_weights * (prefix_dw - slope_base[..., None])).astype(jnp.bfloat16)
    grad_query = score_scale * jnp.einsum(
        "rhpj,jhd->prhd", prefix_slopes, prefix_keys, preferred_element_type=jnp.float32
    )
    grad_pkeys = score_scale * jnp.einsum(
        "rhpj,prhd->jhd", prefix_slopes, query_heads, preferred_element_type=jnp.float32
    )
    grad_pvalues = jnp.einsum(
        "rhpj,prhd->jhd",
        prefix_weights.astype(jnp.bfloat16),
        grad_heads,
        preferred_element_type=jnp.float32,
    )
    grad_prefix_kv = jnp.concatenate(
        [grad_pkeys.reshape(-1, width), grad_pvalues.reshape(-1, width)], -1
    )
    keys_all, values_all, segs_all = (
        lax.all_gather(keys, "blk", axis=0, tiled=True),
        lax.all_gather(values, "blk", axis=0, tiled=True),
        lax.all_gather(segment_ids, "blk", axis=0, tiled=True),
    )
    length = keys_all.shape[0]
    stride = math.gcd(length, 512)

    def backward_step(grad_q, block_index):
        offset = block_index * stride
        key_block = lax.dynamic_slice_in_dim(keys_all, offset, stride, 0)
        value_block = lax.dynamic_slice_in_dim(values_all, offset, stride, 0)
        seg_block = lax.dynamic_slice_in_dim(segs_all, offset, stride, 0)
        key_pos = offset + jnp.arange(stride)
        weights_low, slopes = block_grads(
            query_heads,
            grad_heads,
            log_total,
            slope_base,
            own_pos,
            segment_ids,
            key_block,
            value_block,
            key_pos,
            seg_block,
            score_scale,
        )
        grad_q = grad_q + score_scale * jnp.einsum(
            "rhpk,krhd->prhd", slopes, split_heads(key_block), preferred_element_type=jnp.float32
        )
        key_term = score_scale * jnp.einsum(
            "rhpk,prhd->krhd", slopes, query_heads, preferred_element_type=jnp.float32
        )
        value_term = jnp.einsum(
            "rhpk,prhd->krhd", weights_low, grad_heads, preferred_element_type=jnp.float32
        )
        return (
            grad_q,
            (
                key_term.reshape(stride, row_count, width),
                value_term.reshape(stride, row_count, width),
            ),
        )

    grad_query, (key_terms, value_terms) = lax.scan(
        backward_step, grad_query, jnp.arange(length // stride)
    )
    key_terms = key_terms.reshape(length, row_count, width)
    value_terms = value_terms.reshape(length, row_count, width)
    grad_keys, grad_values = (
        lax.psum_scatter(key_terms, "blk", scatter_dimension=0, tiled=True),
        lax.psum_scatter(value_terms, "blk", scatter_dimension=0, tiled=True),
    )
    grad_proj = jnp.concatenate(
        [
            grad_query.reshape(flat_rows, width).astype(jnp.bfloat16),
            grad_keys.reshape(flat_rows, width).astype(jnp.bfloat16),
            grad_values.reshape(flat_rows, width).astype(jnp.bfloat16),
        ],
        -1,
    )
    grad_norm_one = jnp.dot(grad_proj, w_qkv.T, preferred_element_type=jnp.float32)
    _, norm_one_back = jax.vjp(partial(layer_norm, gain=ln1_gain, bias=ln1_bias), inputs)
    input_grad = (grad_middle + norm_one_back(grad_norm_one)[0]).reshape(pos_dev, row_count, width)
    _, adapter_back = jax.vjp(adapter, prefix_embed, w_mlp1, b_mlp1, w_mlp2, b_mlp2)
    local_grads = adapter_back(grad_prefix_kv)
    summed = lax.psum(
        (local_grads[0], local_grads[1], local_grads[2], local_grads[3], local_grads[4]),
        ("seq", "blk"),
    )
    return (block_out, input_grad, summed[0], summed[1], summed[2], summed[3], summed[4], log_total)


F32 = jnp.float32
BF16 = jnp.bfloat16
LANES = 128
PRE_ROWS = 16
MIB = 1 << 20


def nn(left, right):
    return jnp.dot(left, right, preferred_element_type=F32)


def nt(left, right):
    return lax.dot_general(left, right, (((1,), (1,)), ((), ())), preferred_element_type=F32)


def norm_parts(value_in):
    average = jnp.mean(value_in, axis=-1, keepdims=True)
    centered = value_in - average
    variance = jnp.mean(centered * centered, axis=-1, keepdims=True)
    inverse = lax.rsqrt(variance + EPS)
    return centered * inverse, inverse


def norm_back(unit, inverse, gain, grad):
    scaled = grad * gain
    first = jnp.mean(scaled, axis=-1, keepdims=True)
    second = jnp.mean(scaled * unit, axis=-1, keepdims=True)
    return inverse * (scaled - first - unit * second)


def iota(shape, dim):
    return lax.broadcasted_iota(jnp.int32, shape, dim)


def place():
    blk = lax.axis_index("blk")
    return (blk // 2) % 2, lax.axis_index("seq") % 2, blk % 2


def positions(index, half, row, core, y_at):
    upper = (index >= half).astype(jnp.int32)
    slot = upper + row - 2 * upper * row
    block = (2 * core + slot) * 2 + y_at
    return block * half + index - upper * half


def members(core, y_at):
    return ((core, y_at), (1 - core, y_at), (core, 1 - y_at), (1 - core, 1 - y_at))


def all_positions(shape, dim, half, row, core, y_at):
    part = tuple(2 * half if d == dim else n for d, n in enumerate(shape))
    return jnp.concatenate(
        [positions(iota(part, dim), half, row, c, y) for c, y in members(core, y_at)], dim
    )


def vmem():
    return pl.BlockSpec(memory_space=pltpu.VMEM)


def hbm():
    return pl.BlockSpec(memory_space=pltpu.HBM)


def kept_in_hbm(*arrays):
    return [pltpu.with_memory_space_constraint(a, pltpu.HBM) for a in arrays]


def project_kernel(count, step, *refs):
    messages, (gain, bias, weight, out, marks, normed) = refs[:count], refs[count:]
    half, width = messages[0].shape[0], normed.shape[1]
    for i, message in enumerate(messages):
        rows = pl.ds(i * half, half)
        unit, _ = norm_parts(message[:, :width].astype(F32))
        normed[rows] = (unit * gain[...] + bias[...]).astype(BF16)
        marks[rows] = message[:, width:]

    def columns(i, carry):
        at = pl.ds(pl.multiple_of(i * step, step), step)
        out[:, at] = nn(normed[...], weight[:, at]).astype(BF16)
        return carry

    lax.fori_loop(0, weight.shape[1] // step, columns, 0)


def project(messages, gain, bias, weight, step=512):
    count, half = len(messages), messages[0].shape[0]
    width, columns = weight.shape
    rows = count * half
    return pl.pallas_call(
        partial(project_kernel, count, step),
        in_specs=[vmem()] * (count + 3),
        out_specs=[vmem()] * 2,
        out_shape=[
            jax.ShapeDtypeStruct((rows, columns), BF16),
            jax.ShapeDtypeStruct((rows, LANES), BF16),
        ],
        scratch_shapes=[pltpu.VMEM((rows, width), BF16)],
        compiler_params=pltpu.CompilerParams(vmem_limit_bytes=16 * MIB),
        cost_estimate=pl.CostEstimate(
            flops=2 * rows * width * columns, bytes_accessed=2 * width * columns, transcendentals=0
        ),
        name="project",
    )(*messages, gain[None], bias[None], weight)


def halves(value_in):
    high = value_in.astype(BF16)
    return high, (value_in - high.astype(F32)).astype(BF16)


def pad_rows(value_in, rows):
    return jnp.concatenate(
        [value_in, jnp.zeros((rows - value_in.shape[0], value_in.shape[1]), value_in.dtype)], 0
    )


def three_products(product, left, weight):
    rows = left.shape[0]
    high, low = halves(left)
    w_high, w_low = halves(weight)
    both = product(jnp.concatenate([high, low], 0), w_high)
    return both[:rows] + both[rows:] + product(high, w_low)


def adapter_kernel(
    embed, w_mlp1, b_mlp1, w_mlp2, b_mlp2, w_qkv, out, inner, v_qkv, v_mlp1, v_mlp2, sems
):
    steps, step = v_mlp2.shape[0], v_mlp2.shape[2]
    first = pltpu.make_async_copy(w_mlp1, v_mlp1, sems.at[0])
    first.start()
    rest = []
    for i in range(steps):
        copy = pltpu.make_async_copy(w_mlp2.at[:, pl.ds(i * step, step)], v_mlp2.at[i], sems.at[1 + i])
        copy.start()
        rest.append(copy)
    weights = pltpu.make_async_copy(w_qkv, v_qkv, sems.at[1 + steps])
    weights.start()
    source = pad_rows(embed[...], PRE_ROWS)
    first.wait()
    act = jnp.tanh(three_products(nn, source, v_mlp1[...]) + b_mlp1[...])
    inner[...] = act
    for i, copy in enumerate(rest):
        copy.wait()
        span = pl.ds(i * step, step)
        part = three_products(nn, act, v_mlp2[i]) + b_mlp2[:, span]
        out[:, span] = jnp.where(iota(part.shape, 0) < embed.shape[0], part, 0.0).astype(BF16)
    weights.wait()


def adapter_forward(embed, w_mlp1, b_mlp1, w_mlp2, b_mlp2, w_qkv):
    width, hidden = w_mlp1.shape
    columns = w_mlp2.shape[1]
    steps = 4
    return pl.pallas_call(
        adapter_kernel,
        in_specs=[vmem(), hbm(), vmem(), hbm(), vmem(), hbm()],
        out_specs=[vmem()] * 3,
        out_shape=[
            jax.ShapeDtypeStruct((PRE_ROWS, columns), BF16),
            jax.ShapeDtypeStruct((PRE_ROWS, hidden), F32),
            pltpu.VMEM(w_qkv.shape, w_qkv.dtype),
        ],
        scratch_shapes=[
            pltpu.VMEM((width, hidden), F32),
            pltpu.VMEM((steps, hidden, columns // steps), F32),
            pltpu.SemaphoreType.DMA((2 + steps,)),
        ],
        compiler_params=pltpu.CompilerParams(vmem_limit_bytes=20 * MIB),
        cost_estimate=pl.CostEstimate(flops=1 << 32, bytes_accessed=6 * MIB, transcendentals=1 << 13),
        name="adapter",
    )(embed, *kept_in_hbm(w_mlp1), b_mlp1[None], *kept_in_hbm(w_mlp2), b_mlp2[None], *kept_in_hbm(w_qkv))


def outer(left, right):
    l_high, l_low = halves(left)
    r_high, r_low = halves(right)
    return lax.dot_general(
        jnp.concatenate([l_high, l_high, l_low], 0),
        jnp.concatenate([r_high, r_low, r_high], 0),
        (((0,), (0,)), ((), ())),
        preferred_element_type=F32,
    )


def adapter_back_kernel(
    grads,
    embed,
    inner,
    w_mlp1,
    w_mlp2,
    order,
    grad_prefix,
    grad_mlp1,
    grad_bias1,
    grad_mlp2,
    grad_bias2,
    v_mlp1,
    v_mlp2,
    o_mlp1,
    o_mlp2,
    sems,
):
    del order
    steps, step = v_mlp2.shape[0], v_mlp2.shape[2]
    loads = []
    for i in range(steps):
        span = pl.ds(i * step, step)
        loads.append(pltpu.make_async_copy(w_mlp2.at[:, span], v_mlp2.at[i], sems.at[i]))
    loads.append(pltpu.make_async_copy(w_mlp1, v_mlp1, sems.at[steps]))
    for copy in loads:
        copy.start()
    act = inner[...]
    stores = []
    back = jnp.zeros(act.shape, F32)
    for i in range(steps):
        span = pl.ds(i * step, step)
        part = pad_rows(grads[:, span], PRE_ROWS)
        grad_bias2[:, span] = jnp.sum(part, 0, keepdims=True)
        o_mlp2[i] = outer(act, part)
        copy = pltpu.make_async_copy(o_mlp2.at[i], grad_mlp2.at[:, span], sems.at[steps + 1 + i])
        copy.start()
        stores.append(copy)
        loads[i].wait()
        back = back + three_products(nt, part, v_mlp2[i])
    back = back * (1.0 - act * act)
    grad_bias1[...] = jnp.sum(back, 0, keepdims=True)
    o_mlp1[...] = outer(pad_rows(embed[...], PRE_ROWS), back)
    copy = pltpu.make_async_copy(o_mlp1, grad_mlp1, sems.at[2 * steps + 1])
    copy.start()
    stores.append(copy)
    loads[steps].wait()
    grad_prefix[...] = three_products(nt, back, v_mlp1[...])[: embed.shape[0]]
    for copy in stores:
        copy.wait()


def adapter_backward(grads, embed, inner, w_mlp1, w_mlp2, order):
    width, hidden = w_mlp1.shape
    columns = w_mlp2.shape[1]
    steps = 4
    step = columns // steps
    out = pl.pallas_call(
        adapter_back_kernel,
        in_specs=[vmem()] * 3 + [hbm()] * 2 + [pl.BlockSpec(memory_space=pl.ANY)],
        out_specs=[vmem(), hbm(), vmem(), hbm(), vmem()],
        out_shape=[
            jax.ShapeDtypeStruct(embed.shape, F32),
            jax.ShapeDtypeStruct((width, hidden), F32),
            jax.ShapeDtypeStruct((1, hidden), F32),
            jax.ShapeDtypeStruct((hidden, columns), F32),
            jax.ShapeDtypeStruct((1, columns), F32),
        ],
        scratch_shapes=[
            pltpu.VMEM((width, hidden), F32),
            pltpu.VMEM((steps, hidden, step), F32),
            pltpu.VMEM((width, hidden), F32),
            pltpu.VMEM((steps, hidden, step), F32),
            pltpu.SemaphoreType.DMA((2 * steps + 2,)),
        ],
        compiler_params=pltpu.CompilerParams(vmem_limit_bytes=28 * MIB),
        cost_estimate=pl.CostEstimate(flops=1 << 32, bytes_accessed=12 * MIB, transcendentals=0),
        name="adapter_back",
    )(grads, embed, inner, *kept_in_hbm(w_mlp1, w_mlp2), order)
    return out[0], out[1], out[2][0], out[3], out[4][0]


def head_mask(rows):
    return iota((rows, LANES), 1) < HEAD


def two_heads(pair, low):
    zero = jnp.zeros_like(pair)
    return jnp.concatenate([jnp.where(low, pair, zero), jnp.where(low, zero, pair)], 0)


def join_heads(stacked, low):
    rows = stacked.shape[0] // 2
    return jnp.where(low, stacked[:rows], stacked[rows:])


def picks(rows, pair, first, value):
    lane = iota((rows, LANES), 1)
    inside = jnp.logical_and(lane >= first, lane < first + 3 * HEADS)
    parts = [
        jnp.where(jnp.logical_and(inside, lane % HEADS == 2 * pair + i), value, 0.0) for i in range(2)
    ]
    return jnp.concatenate(parts, 0)


def three_parts(value_in, first):
    lane = iota(value_in.shape, 1)
    high = value_in.astype(BF16).astype(F32)
    rest = value_in - high
    middle = rest.astype(BF16).astype(F32)
    low = rest - middle
    part = (lane - first) // HEADS
    chosen = jnp.where(part == 0, high, jnp.where(part == 1, middle, low))
    inside = jnp.logical_and(lane >= first, lane < first + 3 * HEADS)
    return jnp.where(inside, chosen, 0.0)


def key_bias(marks_own, marks_a, marks_b, half, count):
    row, core, y_at = place()
    rows = 2 * half
    own = positions(iota((rows, 1), 0), half, row, core, y_at)
    other = all_positions((1, 8 * half), 1, half, row, core, y_at)
    same = nt(marks_own, jnp.concatenate([marks_a, marks_b], 0))
    visible = jnp.logical_and(same > 0.5, other <= own)
    token_bias = jnp.where(visible, 0.0, NEG)
    prefix_bias = jnp.where(iota((rows, LANES), 1) < count, 0.0, NEG)
    return jnp.concatenate([token_bias, prefix_bias], 1)


def with_prefix(part_a, part_b, prefix):
    pad = jnp.zeros((LANES - prefix.shape[0], prefix.shape[1]), prefix.dtype)
    return jnp.concatenate([part_a, part_b, prefix, pad], 0)


def middle_kernel(
    count,
    qkv_a,
    qkv_b,
    marks_a,
    marks_b,
    prefix_kv,
    own_0,
    own_1,
    cot_0,
    cot_1,
    gain,
    bias,
    w_out,
    w_fc,
    w_proj,
    back_0,
    back_1,
    grad_out_heads,
    grad_middle,
    v_out,
    v_fc,
    v_proj,
    sems,
    scores_bias,
    attended,
    stats,
    middle,
    normed,
    total,
    grad_norm,
    cot,
):
    half, rows = own_0.shape[0], 2 * own_0.shape[0]
    width = middle.shape[1]
    steps, step = v_fc.shape[0], v_fc.shape[2]
    copies = [pltpu.make_async_copy(w_out, v_out, sems.at[0])]
    for i in range(steps):
        span = pl.ds(i * step, step)
        copies.append(pltpu.make_async_copy(w_fc.at[:, span], v_fc.at[i], sems.at[1 + 2 * i]))
        copies.append(pltpu.make_async_copy(w_proj.at[span], v_proj.at[i], sems.at[2 + 2 * i]))
    for copy in copies:
        copy.start()

    scores_bias[...] = key_bias(marks_a[:rows], marks_a[...], marks_b[...], half, count)
    low = head_mask(rows)
    lane = iota((rows, LANES), 1)
    stats[...] = jnp.zeros_like(stats)

    def attend(pair, carry):
        at = pl.ds(pl.multiple_of(pair * LANES, LANES), LANES)
        at_k = pl.ds(pl.multiple_of(width + pair * LANES, LANES), LANES)
        at_v = pl.ds(pl.multiple_of(2 * width + pair * LANES, LANES), LANES)
        query = two_heads(qkv_a[:rows, at] * jnp.asarray(HEAD**-0.5, BF16), low)
        keys = with_prefix(qkv_a[:, at_k], qkv_b[:, at_k], prefix_kv[:, at])
        values = with_prefix(qkv_a[:, at_v], qkv_b[:, at_v], prefix_kv[:, at_k])
        scores = nt(query, keys)
        mask = scores_bias[...]
        scores = scores + jnp.concatenate([mask, mask], 0)
        top = jnp.max(scores, -1, keepdims=True)
        weights = jnp.exp(scores - top)
        denominator = jnp.sum(weights, -1, keepdims=True)
        mixed = nn(weights.astype(BF16), values) / denominator
        attended[:, at] = join_heads(mixed, low)
        log_total = top + jnp.log(denominator)
        inside = lane < 3 * HEADS
        for i in range(2):
            here = jnp.logical_and(inside, lane % HEADS == 2 * pair + i)
            stats[...] = jnp.where(here, log_total[i * rows : (i + 1) * rows], stats[...])
        return carry

    lax.fori_loop(0, HEADS // 2, attend, 0)

    copies[0].wait()
    inputs = jnp.concatenate([own_0[:, :width], own_1[:, :width]], 0).astype(F32)
    middle[...] = inputs + nn(attended[...].astype(BF16), v_out[...])
    unit, _ = norm_parts(middle[...])
    normed[...] = (unit * gain[...] + bias[...]).astype(BF16)
    cot[...] = jnp.concatenate([cot_0[...], cot_1[...]], 0)
    total[...] = middle[...]
    grad_norm[...] = jnp.zeros_like(grad_norm)

    def feed(i, carry):
        for which in (0, 1):
            pltpu.make_async_copy(
                (v_fc, v_proj)[which].at[i], (v_fc, v_proj)[which].at[i], sems.at[1 + 2 * i + which]
            ).wait()
        fc, proj = v_fc[i], v_proj[i]
        pre = nn(normed[...], fc)
        grad_act = nt(cot[...], proj)
        cubic = 0.044715 * pre * pre
        curve = jnp.tanh(math.sqrt(2 / math.pi) * pre * (1.0 + cubic))
        act = 0.5 * pre * (1.0 + curve)
        slope = 0.5 * (1.0 + curve) + 0.5 * math.sqrt(2 / math.pi) * pre * (1.0 - curve * curve) * (
            1.0 + 3.0 * cubic
        )
        grad_pre = (grad_act * slope).astype(BF16)
        total[...] += nn(act.astype(BF16), proj)
        grad_norm[...] += nt(grad_pre, fc)
        return carry

    lax.fori_loop(0, steps, feed, 0)

    out = total[...].astype(BF16)
    back_0[:, :width] = out[:half]
    back_1[:, :width] = out[half:]
    unit, inverse = norm_parts(middle[...])
    grads = cot[...].astype(F32) + norm_back(unit, inverse, gain[...], grad_norm[...])
    grad_middle[...] = grads
    grad_heads = nt(grads.astype(BF16), v_out[...]).astype(BF16)
    grad_out_heads[:, :width] = grad_heads
    product = grad_heads.astype(F32) * attended[...]
    ones = jnp.where(
        jnp.logical_and(
            iota((width, LANES), 0) // HEAD == iota((width, LANES), 1) % HEADS,
            jnp.logical_and(
                iota((width, LANES), 1) >= 3 * HEADS, iota((width, LANES), 1) < 6 * HEADS
            ),
        ),
        1.0,
        0.0,
    ).astype(BF16)
    bases = jnp.zeros((rows, LANES), F32)
    for _ in range(3):
        part = product.astype(BF16)
        bases = bases + nn(part, ones)
        product = product - part.astype(F32)
    marks = three_parts(stats[...], 0) + three_parts(bases, 3 * HEADS)
    marks = marks.astype(BF16)
    grad_out_heads[:, width:] = marks
    back_0[:, width:] = marks[:half]
    back_1[:, width:] = marks[half:]


def middle_part(count, qkv_a, qkv_b, marks_a, marks_b, prefix_kv, own, cots, gain, bias, w_out, w_fc, w_proj):
    half, width = cots[0].shape
    rows = 2 * half
    hidden = w_fc.shape[1]
    steps = 8
    step = hidden // steps
    wide = width + LANES
    return pl.pallas_call(
        partial(middle_kernel, count),
        in_specs=[vmem()] * 11 + [hbm()] * 3,
        out_specs=[vmem()] * 4,
        out_shape=[
            jax.ShapeDtypeStruct((half, wide), BF16),
            jax.ShapeDtypeStruct((half, wide), BF16),
            jax.ShapeDtypeStruct((rows, wide), BF16),
            jax.ShapeDtypeStruct((rows, width), F32),
        ],
        scratch_shapes=[
            pltpu.VMEM((width, width), BF16),
            pltpu.VMEM((steps, width, step), BF16),
            pltpu.VMEM((steps, step, width), BF16),
            pltpu.SemaphoreType.DMA((1 + 2 * steps,)),
            pltpu.VMEM((rows, 4 * rows + LANES), F32),
            pltpu.VMEM((rows, width), F32),
            pltpu.VMEM((rows, LANES), F32),
            pltpu.VMEM((rows, width), F32),
            pltpu.VMEM((rows, width), BF16),
            pltpu.VMEM((rows, width), F32),
            pltpu.VMEM((rows, width), F32),
            pltpu.VMEM((rows, width), BF16),
        ],
        compiler_params=pltpu.CompilerParams(vmem_limit_bytes=48 * MIB),
        cost_estimate=pl.CostEstimate(
            flops=2 * rows * width * (4 * hidden + 2 * width),
            bytes_accessed=2 * width * (2 * hidden + width),
            transcendentals=rows * hidden,
        ),
        name="middle",
    )(
        qkv_a, qkv_b, marks_a, marks_b, prefix_kv, *own, *cots, gain[None], bias[None], *kept_in_hbm(w_out, w_fc, w_proj)
    )


def key_grads(keys, values, queries, grads, marks, pair, low, mask):
    rows = keys.shape[0]
    scale = jnp.asarray(HEAD**-0.5, BF16)
    left = jnp.concatenate(
        [two_heads(keys * scale, low), picks(rows, pair, 0, -1.0).astype(BF16)], 1
    )
    scores = nt(left, jnp.concatenate([queries, marks], 1))
    weights = jnp.exp(scores + jnp.concatenate([mask, mask], 0))
    left = jnp.concatenate(
        [two_heads(values, low), picks(rows, pair, 3 * HEADS, -1.0).astype(BF16)], 1
    )
    slopes = weights * nt(left, jnp.concatenate([grads, marks], 1))
    key_grad = nn(slopes.astype(BF16), queries)
    value_grad = nn(weights.astype(BF16), grads)
    return join_heads(key_grad, low) * HEAD**-0.5, join_heads(value_grad, low)


def prefix_kernel(qkv_a, grads, prefix_kv, out):
    used = out.shape[0]
    rows, width = grads.shape[0], grads.shape[1] - LANES
    count = prefix_kv.shape[0]
    low = head_mask(count)
    mask = jnp.where(iota((count, rows), 0) < used, 0.0, NEG)
    marks = grads[:, width:]

    def step(pair, carry):
        at = pl.ds(pl.multiple_of(pair * LANES, LANES), LANES)
        at_v = pl.ds(pl.multiple_of(width + pair * LANES, LANES), LANES)
        key_grad, value_grad = key_grads(
            prefix_kv[:, at], prefix_kv[:, at_v], qkv_a[:rows, at], grads[:, at], marks, pair, low, mask
        )
        out[:, at] = key_grad[:used]
        out[:, at_v] = value_grad[:used]
        return carry

    lax.fori_loop(0, HEADS // 2, step, 0)


def prefix_part(count, qkv_a, grads, prefix_kv):
    return pl.pallas_call(
        prefix_kernel,
        in_specs=[vmem()] * 3,
        out_specs=vmem(),
        out_shape=jax.ShapeDtypeStruct((count, prefix_kv.shape[1]), F32),
        compiler_params=pltpu.CompilerParams(vmem_limit_bytes=16 * MIB),
        cost_estimate=pl.CostEstimate(flops=1 << 29, bytes_accessed=1 << 20, transcendentals=1 << 16),
        name="prefix",
    )(qkv_a, grads, prefix_kv)


def query_kernel(count, qkv_a, qkv_b, marks_a, marks_b, prefix_kv, grads, weight, order, out, scores_bias, grad_query):
    del order
    rows, width = grad_query.shape
    scores_bias[...] = key_bias(marks_a[:rows], marks_a[...], marks_b[...], rows // 2, count)
    low = head_mask(rows)
    marks = grads[:, width:]
    marks_twice = jnp.concatenate([marks, marks], 0)
    ones = jnp.ones((4 * rows + LANES, LANES), BF16)

    def step(pair, carry):
        at = pl.ds(pl.multiple_of(pair * LANES, LANES), LANES)
        at_k = pl.ds(pl.multiple_of(width + pair * LANES, LANES), LANES)
        at_v = pl.ds(pl.multiple_of(2 * width + pair * LANES, LANES), LANES)
        keys = with_prefix(qkv_a[:, at_k], qkv_b[:, at_k], prefix_kv[:, at])
        values = with_prefix(qkv_a[:, at_v], qkv_b[:, at_v], prefix_kv[:, at_k])
        query = two_heads(qkv_a[:rows, at] * jnp.asarray(HEAD**-0.5, BF16), low)
        tops = marks_twice * picks(rows, pair, 0, -1.0).astype(BF16)
        scores = nt(jnp.concatenate([query, tops], 1), jnp.concatenate([keys, ones], 1))
        mask = scores_bias[...]
        weights = jnp.exp(scores + jnp.concatenate([mask, mask], 0))
        bases = marks_twice * picks(rows, pair, 3 * HEADS, -1.0).astype(BF16)
        left = jnp.concatenate([two_heads(grads[:, at], low), bases], 1)
        slopes = weights * nt(left, jnp.concatenate([values, ones], 1))
        grad = join_heads(nn(slopes.astype(BF16), keys), low)
        grad_query[:, at] = (grad * HEAD**-0.5).astype(BF16)
        return carry

    lax.fori_loop(0, HEADS // 2, step, 0)
    out[...] = nt(grad_query[...], weight[:, :width])


def query_part(count, qkv_a, qkv_b, marks_a, marks_b, prefix_kv, grads, weight, order):
    rows, width = grads.shape[0], grads.shape[1] - LANES
    return pl.pallas_call(
        partial(query_kernel, count),
        in_specs=[vmem()] * 7 + [pl.BlockSpec(memory_space=pl.ANY)],
        out_specs=vmem(),
        out_shape=jax.ShapeDtypeStruct((rows, width), F32),
        scratch_shapes=[pltpu.VMEM((rows, 4 * rows + LANES), F32), pltpu.VMEM((rows, width), BF16)],
        compiler_params=pltpu.CompilerParams(vmem_limit_bytes=30 * MIB),
        cost_estimate=pl.CostEstimate(flops=1 << 32, bytes_accessed=1 << 23, transcendentals=1 << 20),
        name="query",
    )(qkv_a, qkv_b, marks_a, marks_b, prefix_kv, grads, weight, order)


def final_kernel(
    qkv_a,
    qkv_b,
    marks_a,
    marks_b,
    grads_0,
    grads_1,
    grads_2,
    grads_3,
    own_0,
    own_1,
    gain,
    grad_middle,
    grad_partial,
    weight,
    back_0,
    back_1,
    scores_bias,
    grad_keys,
):
    half, rows = own_0.shape[0], 2 * own_0.shape[0]
    width = grad_middle.shape[1]
    row, core, y_at = place()
    own = positions(iota((rows, 1), 0), half, row, core, y_at)
    other = all_positions((1, 8 * half), 1, half, row, core, y_at)
    same = nt(marks_a[:rows], jnp.concatenate([marks_a[...], marks_b[...]], 0))
    visible = jnp.logical_and(same > 0.5, own <= other)
    scores_bias[...] = jnp.where(visible, 0.0, NEG)
    low = head_mask(rows)
    blocks = (grads_0, grads_1, grads_2, grads_3)
    marks = jnp.concatenate([g[:, width:] for g in blocks], 0)

    def step(pair, carry):
        at = pl.ds(pl.multiple_of(pair * LANES, LANES), LANES)
        at_k = pl.ds(pl.multiple_of(width + pair * LANES, LANES), LANES)
        at_v = pl.ds(pl.multiple_of(2 * width + pair * LANES, LANES), LANES)
        queries = jnp.concatenate([qkv_a[:, at], qkv_b[:, at]], 0)
        grads = jnp.concatenate([g[:, at] for g in blocks], 0)
        key_grad, value_grad = key_grads(
            qkv_a[:rows, at_k], qkv_a[:rows, at_v], queries, grads, marks, pair, low, scores_bias[...]
        )
        grad_keys[:, at] = key_grad.astype(BF16)
        grad_keys[:, at_k] = value_grad.astype(BF16)
        return carry

    lax.fori_loop(0, HEADS // 2, step, 0)
    grad_norm = grad_partial[...] + nt(grad_keys[...], weight[:, width:])
    inputs = jnp.concatenate([own_0[:, :width], own_1[:, :width]], 0).astype(F32)
    unit, inverse = norm_parts(inputs)
    out = (grad_middle[...] + norm_back(unit, inverse, gain[...], grad_norm)).astype(BF16)
    back_0[...] = out[:half]
    back_1[...] = out[half:]


def final_part(qkv_a, qkv_b, marks_a, marks_b, grads, own, gain, grad_middle, grad_partial, weight):
    rows, width = grad_middle.shape
    half = rows // 2
    return pl.pallas_call(
        final_kernel,
        in_specs=[vmem()] * 14,
        out_specs=[vmem()] * 2,
        out_shape=[jax.ShapeDtypeStruct((half, width), BF16)] * 2,
        scratch_shapes=[
            pltpu.VMEM((rows, 4 * rows), F32),
            pltpu.VMEM((rows, 2 * width), BF16),
        ],
        compiler_params=pltpu.CompilerParams(vmem_limit_bytes=30 * MIB),
        cost_estimate=pl.CostEstimate(flops=1 << 32, bytes_accessed=1 << 23, transcendentals=1 << 20),
        name="final",
    )(qkv_a, qkv_b, marks_a, marks_b, *grads, *own, gain[None], grad_middle, grad_partial, weight)


def routes(k):
    pairs = []
    for seq in range(4):
        for blk in range(8):
            group, z_at, y_at = seq % 2, blk // 2, blk % 2
            row = (z_at + k) % 2
            pairs.append((seq * 8 + blk, (seq - group + z_at // 2) * 8 + (2 * group + row) * 2 + y_at))
    return pairs


def body_rows(
    tokens,
    segment_ids,
    ln1_gain,
    ln1_bias,
    w_qkv,
    w_out,
    ln2_gain,
    ln2_bias,
    w_fc,
    w_proj,
    prefix_embed,
    w_mlp1,
    b_mlp1,
    w_mlp2,
    b_mlp2,
    cotangent,
):
    half, _, width = tokens.shape
    everyone = ("seq", "blk")
    there = [routes(k) for k in range(2)]
    back = [[(b, a) for a, b in pairs] for pairs in there]
    swap_core = [(i, i ^ 1) for i in range(4)]
    swap_y = [(i, i ^ 1) for i in range(8)]
    odd = (lax.axis_index("blk") // 2) % 2 == 1

    def sorted_rows(first, second):
        return jnp.where(odd, second, first), jnp.where(odd, first, second)

    def after(value, *done):
        return lax.optimization_barrier((value, done))[0]

    marks = (segment_ids[:, :, None] == jnp.arange(LANES)[None, None]).astype(BF16)
    marked = jnp.concatenate([tokens, marks], -1)
    out_msgs = sorted_rows(marked[:, 0], marked[:, 1])
    cot_msgs = sorted_rows(cotangent[:, 0], cotangent[:, 1])
    own = [lax.ppermute(m, everyone, there[k]) for k, m in enumerate(out_msgs)]
    prefix_kv, inner, w_near = adapter_forward(prefix_embed, w_mlp1, b_mlp1, w_mlp2, b_mlp2, w_qkv)
    count = prefix_embed.shape[0]
    own = after(own, inner)
    across = [lax.ppermute(m, "blk", swap_y) for m in own]
    beside = [lax.ppermute(m, "seq", swap_core) for m in own]
    cots = [lax.ppermute(m, everyone, there[k]) for k, m in enumerate(after(cot_msgs, own))]
    beyond = [lax.ppermute(m, "seq", swap_core) for m in across]

    qkv_a, marks_a = project(own + beside, ln1_gain, ln1_bias, w_near)
    qkv_b, marks_b = project(across + beyond, ln1_gain, ln1_bias, w_near)
    back_0, back_1, grads, grad_middle = middle_part(
        count, qkv_a, qkv_b, marks_a, marks_b, prefix_kv, own, cots, ln2_gain, ln2_bias, w_out, w_fc, w_proj
    )
    grads_y = lax.ppermute(grads, "blk", swap_y)
    grads_c = lax.ppermute(grads, "seq", swap_core)
    grads_yc = lax.ppermute(grads_y, "seq", swap_core)
    home = [lax.ppermute(m, everyone, back[k]) for k, m in enumerate((back_0, back_1))]

    def spread(value, axis, size, partners):
        return [lax.ppermute(value, axis, [(i, i ^ far) for i in range(size)]) for far in partners]

    def add_four(value, others):
        return (value + others[0]) + (others[1] + others[2])

    grad_prefix_kv = prefix_part(count, qkv_a, grads, prefix_kv)
    parts = spread(grad_prefix_kv, "seq", 4, (2, 1, 3))
    grad_partial = query_part(
        count, qkv_a, qkv_b, marks_a, marks_b, prefix_kv, grads, w_near, grad_prefix_kv
    )
    grad_prefix_kv = add_four(grad_prefix_kv, after(parts, grads_y, grad_partial))
    parts = spread(grad_prefix_kv, "blk", 8, (2, 4, 6))
    final_0, final_1 = final_part(
        qkv_a,
        qkv_b,
        marks_a,
        marks_b,
        (grads, grads_c, grads_y, grads_yc),
        own,
        ln1_gain,
        grad_middle,
        grad_partial,
        w_near,
    )
    finals = [lax.ppermute(m, everyone, back[k]) for k, m in enumerate((final_0, final_1))]
    grad_prefix_kv = add_four(grad_prefix_kv, after(parts, final_0))
    parts = spread(grad_prefix_kv, "blk", 8, (1,))
    grad_prefix_kv = grad_prefix_kv + parts[0]
    summed = adapter_backward(grad_prefix_kv, prefix_embed, inner, w_mlp1, w_mlp2, final_0)

    home = sorted_rows(*after(home, final_0))
    block_out = jnp.stack([m[:, :width] for m in home], 1)
    logs = [m[:, width : width + 3 * HEADS].astype(F32).reshape(half, 3, HEADS).sum(1) for m in home]
    log_total = jnp.stack([jnp.transpose(m) for m in logs], 0)
    input_grad = jnp.stack(sorted_rows(*finals), 1).astype(F32)
    return (block_out, input_grad, summed[0], summed[1], summed[2], summed[3], summed[4], log_total)


def solution(mesh):
    four_by_eight = mesh.shape["seq"] == 4 and mesh.shape["blk"] == 8
    placed = (
        P("blk", "seq", None),
        P("blk", "seq"),
        P(),
        P(),
        P(),
        P(),
        P(),
        P(),
        P(),
        P(),
        P(),
        P(),
        P(),
        P(),
        P(),
        P("blk", "seq", None),
    )
    return jax.shard_map(
        body_rows if four_by_eight else body_plain,
        mesh=mesh,
        in_specs=placed,
        out_specs=(
            P("blk", "seq", None),
            P("blk", "seq", None),
            P(),
            P(),
            P(),
            P(),
            P(),
            P("seq", None, "blk"),
        ),
        check_vma=False,
    )
```

```python
from functools import partial
import math

import jax
import jax.numpy as jnp
from jax import lax
from jax.experimental import pallas as pl
from jax.experimental.pallas import tpu as pltpu
from jax.sharding import PartitionSpec as P

HEADS = 16
HEAD = 64


EPS = 1e-05
NEG = -1e30
HIGH = lax.Precision.HIGHEST


def layer_norm(value_in, gain, bias):
    average = jnp.mean(value_in, axis=-1, keepdims=True)
    centered = value_in - average
    variance = jnp.mean(centered * centered, axis=-1, keepdims=True)
    return centered * lax.rsqrt(variance + EPS) * gain + bias


def adapter(prefix_embed, w_mlp1, b_mlp1, w_mlp2, b_mlp2):
    inner_act = jnp.tanh(jnp.dot(prefix_embed, w_mlp1, precision=HIGH) + b_mlp1)
    return jnp.dot(inner_act, w_mlp2, precision=HIGH) + b_mlp2


def gelu_tanh(pre_act):
    return jax.nn.gelu(pre_act, approximate=True)


def split_heads(block_in):
    return block_in.reshape(block_in.shape[0], block_in.shape[1], HEADS, HEAD)


def allowed(query_pos, query_seg, key_pos, key_seg):
    same_seg = query_seg.T[:, :, None] == key_seg.T[:, None, :]
    causal = key_pos[None, None, :] <= query_pos[None, :, None]
    return jnp.logical_and(same_seg, causal)[:, None]


def scores_of(query_heads, key_block, score_scale):
    return score_scale * jnp.einsum(
        "prhd,krhd->rhpk", query_heads, split_heads(key_block), preferred_element_type=jnp.float32
    )


def block_grads(
    query_heads,
    grad_heads,
    log_total,
    slope_base,
    query_pos,
    query_seg,
    key_block,
    value_block,
    key_pos,
    key_seg,
    score_scale,
):
    scores = scores_of(query_heads, key_block, score_scale)
    scores = jnp.where(allowed(query_pos, query_seg, key_pos, key_seg), scores, NEG)
    weights = jnp.exp(scores - log_total[..., None])
    grad_weights = jnp.einsum(
        "prhd,krhd->rhpk", grad_heads, split_heads(value_block), preferred_element_type=jnp.float32
    )
    slopes = (weights * (grad_weights - slope_base[..., None])).astype(jnp.bfloat16)
    return (weights.astype(jnp.bfloat16), slopes)


def body_plain(
    tokens,
    segment_ids,
    ln1_gain,
    ln1_bias,
    w_qkv,
    w_out,
    ln2_gain,
    ln2_bias,
    w_fc,
    w_proj,
    prefix_embed,
    w_mlp1,
    b_mlp1,
    w_mlp2,
    b_mlp2,
    cotangent,
):
    pos_dev, row_count, width = tokens.shape
    score_scale = HEAD ** (-0.5)
    flat_rows = pos_dev * row_count
    own_pos = lax.axis_index("blk") * pos_dev + jnp.arange(pos_dev)
    inputs = tokens.astype(jnp.float32).reshape(flat_rows, width)
    normed_one = layer_norm(inputs, ln1_gain, ln1_bias).astype(jnp.bfloat16)
    projected = jnp.dot(normed_one, w_qkv, preferred_element_type=jnp.float32).astype(jnp.bfloat16)
    queries = projected[:, :width].reshape(pos_dev, row_count, width)
    keys = projected[:, width : 2 * width].reshape(pos_dev, row_count, width)
    values = projected[:, 2 * width :].reshape(pos_dev, row_count, width)
    query_heads = split_heads(queries)
    prefix_low = adapter(prefix_embed, w_mlp1, b_mlp1, w_mlp2, b_mlp2).astype(jnp.bfloat16)
    prefix_keys = prefix_low[:, :width].reshape(-1, HEADS, HEAD)
    prefix_values = prefix_low[:, width:].reshape(-1, HEADS, HEAD)
    prefix_scores = score_scale * jnp.einsum(
        "prhd,jhd->rhpj", query_heads, prefix_keys, preferred_element_type=jnp.float32
    )
    start_top = jnp.max(prefix_scores, -1)
    start_weights = jnp.exp(prefix_scores - start_top[..., None])
    start_denom = jnp.sum(start_weights, -1)
    start_numer = jnp.einsum(
        "rhpj,jhd->rhpd",
        start_weights.astype(jnp.bfloat16),
        prefix_values,
        preferred_element_type=jnp.float32,
    )
    start_state = (start_top, start_denom, start_numer)
    running = start_state
    key_shards = lax.all_gather(keys, "blk", axis=0, tiled=True)
    value_shards = lax.all_gather(values, "blk", axis=0, tiled=True)
    seg_shards = lax.all_gather(segment_ids, "blk", axis=0, tiled=True)
    num_rows = key_shards.shape[0]
    forward_stride = math.gcd(num_rows, 512)

    def inner(state, block_index):
        running_top, denominator, numerator = state
        offset = block_index * forward_stride
        key_block = lax.dynamic_slice_in_dim(key_shards, offset, forward_stride, 0)
        value_block = lax.dynamic_slice_in_dim(value_shards, offset, forward_stride, 0)
        seg_block = lax.dynamic_slice_in_dim(seg_shards, offset, forward_stride, 0)
        key_pos = offset + jnp.arange(forward_stride)
        scores = jnp.where(
            allowed(own_pos, segment_ids, key_pos, seg_block),
            scores_of(query_heads, key_block, score_scale),
            NEG,
        )
        new_top = jnp.maximum(running_top, jnp.max(scores, -1))
        fading = jnp.exp(running_top - new_top)
        weights = jnp.exp(scores - new_top[..., None])
        denominator = denominator * fading + jnp.sum(weights, -1)
        numerator = numerator * fading[..., None] + jnp.einsum(
            "rhpk,krhd->rhpd",
            weights.astype(jnp.bfloat16),
            split_heads(value_block),
            preferred_element_type=jnp.float32,
        )
        return ((new_top, denominator, numerator), None)

    running, _ = lax.scan(inner, running, jnp.arange(num_rows // forward_stride))
    final_top, final_denom, final_numer = running
    log_total = final_top + jnp.log(final_denom)
    attended = final_numer / final_denom[..., None]
    attended_rows = jnp.transpose(attended, (2, 0, 1, 3)).reshape(flat_rows, width)
    middle = inputs + jnp.dot(
        attended_rows.astype(jnp.bfloat16), w_out, preferred_element_type=jnp.float32
    )
    normed_two = layer_norm(middle, ln2_gain, ln2_bias).astype(jnp.bfloat16)
    hidden_pre = jnp.dot(normed_two, w_fc, preferred_element_type=jnp.float32)
    hidden_act = gelu_tanh(hidden_pre).astype(jnp.bfloat16)
    outputs = middle + jnp.dot(hidden_act, w_proj, preferred_element_type=jnp.float32)
    block_out = outputs.astype(jnp.bfloat16).reshape(pos_dev, row_count, width)
    grad_out = cotangent.reshape(flat_rows, width)
    grad_act = jnp.dot(grad_out, w_proj.T, preferred_element_type=jnp.float32)
    _, gelu_back = jax.vjp(gelu_tanh, hidden_pre)
    grad_pre = gelu_back(grad_act)[0].astype(jnp.bfloat16)
    grad_norm_two = jnp.dot(grad_pre, w_fc.T, preferred_element_type=jnp.float32)
    _, norm_two_back = jax.vjp(partial(layer_norm, gain=ln2_gain, bias=ln2_bias), middle)
    grad_middle = grad_out.astype(jnp.float32) + norm_two_back(grad_norm_two)[0]
    grad_attended = jnp.dot(
        grad_middle.astype(jnp.bfloat16), w_out.T, preferred_element_type=jnp.float32
    ).astype(jnp.bfloat16)
    grad_flat = grad_attended.reshape(pos_dev, row_count, width)
    grad_heads = split_heads(grad_flat)
    slope_base = jnp.sum(jnp.transpose(grad_heads.astype(jnp.float32), (1, 2, 0, 3)) * attended, -1)
    prefix_weights = jnp.exp(prefix_scores - log_total[..., None])
    prefix_dw = jnp.einsum(
        "prhd,jhd->rhpj", grad_heads, prefix_values, preferred_element_type=jnp.float32
    )
    prefix_slopes = (prefix_weights * (prefix_dw - slope_base[..., None])).astype(jnp.bfloat16)
    grad_query = score_scale * jnp.einsum(
        "rhpj,jhd->prhd", prefix_slopes, prefix_keys, preferred_element_type=jnp.float32
    )
    grad_pkeys = score_scale * jnp.einsum(
        "rhpj,prhd->jhd", prefix_slopes, query_heads, preferred_element_type=jnp.float32
    )
    grad_pvalues = jnp.einsum(
        "rhpj,prhd->jhd",
        prefix_weights.astype(jnp.bfloat16),
        grad_heads,
        preferred_element_type=jnp.float32,
    )
    grad_prefix_kv = jnp.concatenate(
        [grad_pkeys.reshape(-1, width), grad_pvalues.reshape(-1, width)], -1
    )
    keys_all, values_all, segs_all = (
        lax.all_gather(keys, "blk", axis=0, tiled=True),
        lax.all_gather(values, "blk", axis=0, tiled=True),
        lax.all_gather(segment_ids, "blk", axis=0, tiled=True),
    )
    length = keys_all.shape[0]
    stride = math.gcd(length, 512)

    def backward_step(grad_q, block_index):
        offset = block_index * stride
        key_block = lax.dynamic_slice_in_dim(keys_all, offset, stride, 0)
        value_block = lax.dynamic_slice_in_dim(values_all, offset, stride, 0)
        seg_block = lax.dynamic_slice_in_dim(segs_all, offset, stride, 0)
        key_pos = offset + jnp.arange(stride)
        weights_low, slopes = block_grads(
            query_heads,
            grad_heads,
            log_total,
            slope_base,
            own_pos,
            segment_ids,
            key_block,
            value_block,
            key_pos,
            seg_block,
            score_scale,
        )
        grad_q = grad_q + score_scale * jnp.einsum(
            "rhpk,krhd->prhd", slopes, split_heads(key_block), preferred_element_type=jnp.float32
        )
        key_term = score_scale * jnp.einsum(
            "rhpk,prhd->krhd", slopes, query_heads, preferred_element_type=jnp.float32
        )
        value_term = jnp.einsum(
            "rhpk,prhd->krhd", weights_low, grad_heads, preferred_element_type=jnp.float32
        )
        return (
            grad_q,
            (
                key_term.reshape(stride, row_count, width),
                value_term.reshape(stride, row_count, width),
            ),
        )

    grad_query, (key_terms, value_terms) = lax.scan(
        backward_step, grad_query, jnp.arange(length // stride)
    )
    key_terms = key_terms.reshape(length, row_count, width)
    value_terms = value_terms.reshape(length, row_count, width)
    grad_keys, grad_values = (
        lax.psum_scatter(key_terms, "blk", scatter_dimension=0, tiled=True),
        lax.psum_scatter(value_terms, "blk", scatter_dimension=0, tiled=True),
    )
    grad_proj = jnp.concatenate(
        [
            grad_query.reshape(flat_rows, width).astype(jnp.bfloat16),
            grad_keys.reshape(flat_rows, width).astype(jnp.bfloat16),
            grad_values.reshape(flat_rows, width).astype(jnp.bfloat16),
        ],
        -1,
    )
    grad_norm_one = jnp.dot(grad_proj, w_qkv.T, preferred_element_type=jnp.float32)
    _, norm_one_back = jax.vjp(partial(layer_norm, gain=ln1_gain, bias=ln1_bias), inputs)
    input_grad = (grad_middle + norm_one_back(grad_norm_one)[0]).reshape(pos_dev, row_count, width)
    _, adapter_back = jax.vjp(adapter, prefix_embed, w_mlp1, b_mlp1, w_mlp2, b_mlp2)
    local_grads = adapter_back(grad_prefix_kv)
    summed = lax.psum(
        (local_grads[0], local_grads[1], local_grads[2], local_grads[3], local_grads[4]),
        ("seq", "blk"),
    )
    return (block_out, input_grad, summed[0], summed[1], summed[2], summed[3], summed[4], log_total)


F32 = jnp.float32
BF16 = jnp.bfloat16
LANES = 128
PRE_ROWS = 16
MIB = 1 << 20


def nn(left, right):
    return jnp.dot(left, right, preferred_element_type=F32)


def nt(left, right):
    return lax.dot_general(left, right, (((1,), (1,)), ((), ())), preferred_element_type=F32)


def norm_parts(value_in):
    average = jnp.mean(value_in, axis=-1, keepdims=True)
    centered = value_in - average
    variance = jnp.mean(centered * centered, axis=-1, keepdims=True)
    inverse = lax.rsqrt(variance + EPS)
    return centered * inverse, inverse


def norm_back(unit, inverse, gain, grad):
    scaled = grad * gain
    first = jnp.mean(scaled, axis=-1, keepdims=True)
    second = jnp.mean(scaled * unit, axis=-1, keepdims=True)
    return inverse * (scaled - first - unit * second)


def iota(shape, dim):
    return lax.broadcasted_iota(jnp.int32, shape, dim)


def place():
    blk = lax.axis_index("blk")
    return (blk // 2) % 2, lax.axis_index("seq") % 2, blk % 2


def positions(index, half, row, core, y_at):
    upper = (index >= half).astype(jnp.int32)
    slot = upper + row - 2 * upper * row
    block = (2 * core + slot) * 2 + y_at
    return block * half + index - upper * half


def members(core, y_at):
    return ((core, y_at), (1 - core, y_at), (core, 1 - y_at), (1 - core, 1 - y_at))


def all_positions(shape, dim, half, row, core, y_at):
    part = tuple(2 * half if d == dim else n for d, n in enumerate(shape))
    return jnp.concatenate(
        [positions(iota(part, dim), half, row, c, y) for c, y in members(core, y_at)], dim
    )


def vmem():
    return pl.BlockSpec(memory_space=pltpu.VMEM)


def hbm():
    return pl.BlockSpec(memory_space=pltpu.HBM)


def kept_in_hbm(*arrays):
    return [pltpu.with_memory_space_constraint(a, pltpu.HBM) for a in arrays]


def project_kernel(count, *refs):
    messages, (gain, bias, weight, out, marks, normed) = refs[:count], refs[count:]
    half, width = messages[0].shape[0], normed.shape[1]
    for i, message in enumerate(messages):
        rows = pl.ds(i * half, half)
        unit, _ = norm_parts(message[:, :width].astype(F32))
        normed[rows] = (unit * gain[...] + bias[...]).astype(BF16)
        marks[rows] = message[:, width:]
    for i in range(3):
        at = pl.ds(i * width, width)
        out[:, at] = nn(normed[...], weight[:, at]).astype(BF16)


def project(messages, gain, bias, weight):
    count, half = len(messages), messages[0].shape[0]
    width, columns = weight.shape
    rows = count * half
    return pl.pallas_call(
        partial(project_kernel, count),
        in_specs=[vmem()] * (count + 3),
        out_specs=[vmem()] * 2,
        out_shape=[
            jax.ShapeDtypeStruct((rows, columns), BF16),
            jax.ShapeDtypeStruct((rows, LANES), BF16),
        ],
        scratch_shapes=[pltpu.VMEM((rows, width), BF16)],
        compiler_params=pltpu.CompilerParams(vmem_limit_bytes=16 * MIB),
        cost_estimate=pl.CostEstimate(
            flops=2 * rows * width * columns, bytes_accessed=2 * width * columns, transcendentals=0
        ),
        name="project",
    )(*messages, gain[None], bias[None], weight)


def halves(value_in):
    high = value_in.astype(BF16)
    return high, (value_in - high.astype(F32)).astype(BF16)


def pad_rows(value_in, rows):
    return jnp.concatenate(
        [value_in, jnp.zeros((rows - value_in.shape[0], value_in.shape[1]), value_in.dtype)], 0
    )


def three_products(product, left, weight):
    rows = left.shape[0]
    high, low = halves(left)
    w_high, w_low = halves(weight)
    both = product(jnp.concatenate([high, low], 0), w_high)
    return both[:rows] + both[rows:] + product(high, w_low)


def adapter_kernel(
    h_embed,
    w_mlp1,
    h_mlp1,
    w_mlp2,
    h_mlp2,
    w_qkv,
    out,
    inner,
    v_qkv,
    embed,
    v_mlp1,
    v_mlp2,
    b_mlp1,
    b_mlp2,
    sems,
):
    steps, step = v_mlp2.shape[0], v_mlp2.shape[2]
    small = []
    for i, (source, target) in enumerate(
        ((h_embed, embed), (h_mlp1, b_mlp1), (h_mlp2, b_mlp2), (w_mlp1, v_mlp1))
    ):
        small.append(pltpu.make_async_copy(source, target, sems.at[steps + i]))
        small[-1].start()
    rest = []
    for i in range(steps):
        copy = pltpu.make_async_copy(w_mlp2.at[:, pl.ds(i * step, step)], v_mlp2.at[i], sems.at[i])
        copy.start()
        rest.append(copy)
    weights = pltpu.make_async_copy(w_qkv, v_qkv, sems.at[steps + len(small)])
    weights.start()
    for copy in small:
        copy.wait()
    source = pad_rows(embed[...], PRE_ROWS)
    act = jnp.tanh(three_products(nn, source, v_mlp1[...]) + b_mlp1[...])
    inner[...] = act
    for i, copy in enumerate(rest):
        copy.wait()
        span = pl.ds(i * step, step)
        part = three_products(nn, act, v_mlp2[i]) + b_mlp2[:, span]
        out[:, span] = jnp.where(iota(part.shape, 0) < embed.shape[0], part, 0.0).astype(BF16)
    weights.wait()


def adapter_forward(embed, w_mlp1, b_mlp1, w_mlp2, b_mlp2, w_qkv):
    width, hidden = w_mlp1.shape
    columns = w_mlp2.shape[1]
    steps = 4
    return pl.pallas_call(
        adapter_kernel,
        in_specs=[hbm()] * 6,
        out_specs=[vmem()] * 6,
        out_shape=[
            jax.ShapeDtypeStruct((PRE_ROWS, columns), BF16),
            jax.ShapeDtypeStruct((PRE_ROWS, hidden), F32),
            pltpu.VMEM(w_qkv.shape, w_qkv.dtype),
            pltpu.VMEM(embed.shape, F32),
            pltpu.VMEM((width, hidden), F32),
            pltpu.VMEM((steps, hidden, columns // steps), F32),
        ],
        scratch_shapes=[
            pltpu.VMEM((1, hidden), F32),
            pltpu.VMEM((1, columns), F32),
            pltpu.SemaphoreType.DMA((5 + steps,)),
        ],
        compiler_params=pltpu.CompilerParams(vmem_limit_bytes=20 * MIB),
        cost_estimate=pl.CostEstimate(flops=1 << 32, bytes_accessed=6 * MIB, transcendentals=1 << 13),
        name="adapter",
    )(*kept_in_hbm(embed, w_mlp1, b_mlp1[None], w_mlp2, b_mlp2[None], w_qkv))


def outer(left, right):
    l_high, l_low = halves(left)
    r_high, r_low = halves(right)
    return lax.dot_general(
        jnp.concatenate([l_high, l_high, l_low], 0),
        jnp.concatenate([r_high, r_low, r_high], 0),
        (((0,), (0,)), ((), ())),
        preferred_element_type=F32,
    )


def adapter_back_kernel(
    mine,
    mine_y,
    other,
    other_y,
    embed,
    inner,
    v_mlp1,
    v_mlp2,
    order,
    grad_prefix,
    grad_mlp1,
    grad_bias1,
    grad_mlp2,
    grad_bias2,
    o_mlp1,
    o_mlp2,
    sems,
):
    del order
    steps, step = v_mlp2.shape[0], v_mlp2.shape[2]
    first = lax.axis_index("seq") % 2 == 0
    own, beside = mine[...] + mine_y[...], other[...] + other_y[...]
    grads = jnp.concatenate([jnp.where(first, own, beside), jnp.where(first, beside, own)], 1)
    grads = pad_rows(grads, PRE_ROWS)
    act = inner[...]
    stores = []
    back = jnp.zeros(act.shape, F32)
    grad_bias2[...] = jnp.sum(grads, 0, keepdims=True)
    for i in range(steps):
        part = grads[:, i * step : (i + 1) * step]
        o_mlp2[i] = outer(act, part)
        stores.append(
            pltpu.make_async_copy(o_mlp2.at[i], grad_mlp2.at[:, pl.ds(i * step, step)], sems.at[i])
        )
        stores[-1].start()
    for i in range(steps):
        back = back + three_products(nt, grads[:, i * step : (i + 1) * step], v_mlp2[i])
    back = back * (1.0 - act * act)
    grad_bias1[...] = jnp.sum(back, 0, keepdims=True)
    o_mlp1[...] = outer(pad_rows(embed[...], PRE_ROWS), back)
    stores.append(pltpu.make_async_copy(o_mlp1, grad_mlp1, sems.at[steps]))
    stores[-1].start()
    grad_prefix[...] = three_products(nt, back, v_mlp1[...])[: embed.shape[0]]
    for copy in stores:
        copy.wait()


def adapter_backward(parts, embed, inner, v_mlp1, v_mlp2, order):
    width, hidden = v_mlp1.shape
    steps, _, step = v_mlp2.shape
    columns = steps * step
    out = pl.pallas_call(
        adapter_back_kernel,
        in_specs=[vmem()] * 8 + [pl.BlockSpec(memory_space=pl.ANY)],
        out_specs=[vmem(), hbm(), vmem(), hbm(), vmem()],
        out_shape=[
            jax.ShapeDtypeStruct(embed.shape, F32),
            jax.ShapeDtypeStruct((width, hidden), F32),
            jax.ShapeDtypeStruct((1, hidden), F32),
            jax.ShapeDtypeStruct((hidden, columns), F32),
            jax.ShapeDtypeStruct((1, columns), F32),
        ],
        scratch_shapes=[
            pltpu.VMEM((width, hidden), F32),
            pltpu.VMEM((steps, hidden, step), F32),
            pltpu.SemaphoreType.DMA((steps + 1,)),
        ],
        compiler_params=pltpu.CompilerParams(vmem_limit_bytes=28 * MIB),
        cost_estimate=pl.CostEstimate(flops=1 << 32, bytes_accessed=6 * MIB, transcendentals=0),
        name="adapter_back",
    )(*parts, embed, inner, v_mlp1, v_mlp2, order)
    return out[0], out[1], out[2][0], out[3], out[4][0]


def head_mask(rows):
    return iota((rows, LANES), 1) < HEAD


def two_heads(pair, low):
    zero = jnp.zeros_like(pair)
    return jnp.concatenate([jnp.where(low, pair, zero), jnp.where(low, zero, pair)], 0)


def join_heads(stacked, low):
    rows = stacked.shape[0] // 2
    return jnp.where(low, stacked[:rows], stacked[rows:])


def picks(rows, pair, first, value):
    lane = iota((rows, LANES), 1)
    inside = jnp.logical_and(lane >= first, lane < first + 3 * HEADS)
    parts = [
        jnp.where(jnp.logical_and(inside, lane % HEADS == 2 * pair + i), value, 0.0) for i in range(2)
    ]
    return jnp.concatenate(parts, 0)


def three_parts(value_in, first):
    lane = iota(value_in.shape, 1)
    high = value_in.astype(BF16).astype(F32)
    rest = value_in - high
    middle = rest.astype(BF16).astype(F32)
    low = rest - middle
    part = (lane - first) // HEADS
    chosen = jnp.where(part == 0, high, jnp.where(part == 1, middle, low))
    inside = jnp.logical_and(lane >= first, lane < first + 3 * HEADS)
    return jnp.where(inside, chosen, 0.0)


def key_bias(marks_own, marks_a, marks_b, half, count):
    row, core, y_at = place()
    rows = 2 * half
    own = positions(iota((rows, 1), 0), half, row, core, y_at)
    other = all_positions((1, 8 * half), 1, half, row, core, y_at)
    same = nt(marks_own, jnp.concatenate([marks_a, marks_b], 0))
    visible = jnp.logical_and(same > 0.5, other <= own)
    token_bias = jnp.where(visible, 0.0, NEG)
    prefix_bias = jnp.where(iota((rows, LANES), 1) < count, 0.0, NEG)
    return jnp.concatenate([token_bias, prefix_bias], 1)


def with_prefix(part_a, part_b, prefix):
    pad = jnp.zeros((LANES - prefix.shape[0], prefix.shape[1]), prefix.dtype)
    return jnp.concatenate([part_a, part_b, prefix, pad], 0)


def middle_kernel(
    count,
    qkv_a,
    qkv_b,
    marks_a,
    marks_b,
    prefix_kv,
    own_0,
    own_1,
    cot_0,
    cot_1,
    gain,
    bias,
    w_out,
    w_fc,
    w_proj,
    back_0,
    back_1,
    grad_out_heads,
    grad_middle,
    v_out,
    v_fc,
    v_proj,
    sems,
    scores_bias,
    attended,
    stats,
    middle,
    normed,
    total,
    grad_norm,
    cot,
):
    half, rows = own_0.shape[0], 2 * own_0.shape[0]
    width = middle.shape[1]
    steps, step = v_fc.shape[0], v_fc.shape[2]
    copies = [pltpu.make_async_copy(w_out, v_out, sems.at[0])]
    for i in range(steps):
        span = pl.ds(i * step, step)
        copies.append(pltpu.make_async_copy(w_fc.at[:, span], v_fc.at[i], sems.at[1 + 2 * i]))
        copies.append(pltpu.make_async_copy(w_proj.at[span], v_proj.at[i], sems.at[2 + 2 * i]))
    for copy in copies:
        copy.start()

    scores_bias[...] = key_bias(marks_a[:rows], marks_a[...], marks_b[...], half, count)
    low = head_mask(rows)
    lane = iota((rows, LANES), 1)
    stats[...] = jnp.zeros_like(stats)

    def attend(pair, carry):
        at = pl.ds(pl.multiple_of(pair * LANES, LANES), LANES)
        at_k = pl.ds(pl.multiple_of(width + pair * LANES, LANES), LANES)
        at_v = pl.ds(pl.multiple_of(2 * width + pair * LANES, LANES), LANES)
        query = two_heads(qkv_a[:rows, at] * jnp.asarray(HEAD**-0.5, BF16), low)
        keys = with_prefix(qkv_a[:, at_k], qkv_b[:, at_k], prefix_kv[:, at])
        values = with_prefix(qkv_a[:, at_v], qkv_b[:, at_v], prefix_kv[:, at_k])
        scores = nt(query, keys)
        mask = scores_bias[...]
        scores = scores + jnp.concatenate([mask, mask], 0)
        top = jnp.max(scores, -1, keepdims=True)
        weights = jnp.exp(scores - top)
        denominator = jnp.sum(weights, -1, keepdims=True)
        mixed = nn(weights.astype(BF16), values) / denominator
        attended[:, at] = join_heads(mixed, low)
        log_total = top + jnp.log(denominator)
        inside = lane < 3 * HEADS
        for i in range(2):
            here = jnp.logical_and(inside, lane % HEADS == 2 * pair + i)
            stats[...] = jnp.where(here, log_total[i * rows : (i + 1) * rows], stats[...])
        return carry

    lax.fori_loop(0, HEADS // 2, attend, 0, unroll=4)

    copies[0].wait()
    inputs = jnp.concatenate([own_0[:, :width], own_1[:, :width]], 0).astype(F32)
    middle[...] = inputs + nn(attended[...].astype(BF16), v_out[...])
    unit, _ = norm_parts(middle[...])
    normed[...] = (unit * gain[...] + bias[...]).astype(BF16)
    cot[...] = jnp.concatenate([cot_0[...], cot_1[...]], 0)
    total[...] = middle[...]
    grad_norm[...] = jnp.zeros_like(grad_norm)

    def feed(i, carry):
        for which in (0, 1):
            pltpu.make_async_copy(
                (v_fc, v_proj)[which].at[i], (v_fc, v_proj)[which].at[i], sems.at[1 + 2 * i + which]
            ).wait()
        fc, proj = v_fc[i], v_proj[i]
        pre = nn(normed[...], fc)
        grad_act = nt(cot[...], proj)
        cubic = 0.044715 * pre * pre
        curve = jnp.tanh(math.sqrt(2 / math.pi) * pre * (1.0 + cubic))
        act = 0.5 * pre * (1.0 + curve)
        slope = 0.5 * (1.0 + curve) + 0.5 * math.sqrt(2 / math.pi) * pre * (1.0 - curve * curve) * (
            1.0 + 3.0 * cubic
        )
        grad_pre = (grad_act * slope).astype(BF16)
        total[...] += nn(act.astype(BF16), proj)
        grad_norm[...] += nt(grad_pre, fc)
        return carry

    lax.fori_loop(0, steps, feed, 0, unroll=True)

    out = total[...].astype(BF16)
    back_0[:, :width] = out[:half]
    back_1[:, :width] = out[half:]
    unit, inverse = norm_parts(middle[...])
    grads = cot[...].astype(F32) + norm_back(unit, inverse, gain[...], grad_norm[...])
    grad_middle[...] = grads
    grad_heads = nt(grads.astype(BF16), v_out[...]).astype(BF16)
    grad_out_heads[:, :width] = grad_heads
    product = grad_heads.astype(F32) * attended[...]
    ones = jnp.where(
        jnp.logical_and(
            iota((width, LANES), 0) // HEAD == iota((width, LANES), 1) % HEADS,
            jnp.logical_and(
                iota((width, LANES), 1) >= 3 * HEADS, iota((width, LANES), 1) < 6 * HEADS
            ),
        ),
        1.0,
        0.0,
    ).astype(BF16)
    bases = jnp.zeros((rows, LANES), F32)
    for _ in range(3):
        part = product.astype(BF16)
        bases = bases + nn(part, ones)
        product = product - part.astype(F32)
    marks = three_parts(stats[...], 0) + three_parts(bases, 3 * HEADS)
    marks = marks.astype(BF16)
    grad_out_heads[:, width:] = marks
    back_0[:, width:] = marks[:half]
    back_1[:, width:] = marks[half:]


def middle_part(count, qkv_a, qkv_b, marks_a, marks_b, prefix_kv, own, cots, gain, bias, w_out, w_fc, w_proj):
    half, width = cots[0].shape
    rows = 2 * half
    hidden = w_fc.shape[1]
    steps = 2
    step = hidden // steps
    wide = width + LANES
    return pl.pallas_call(
        partial(middle_kernel, count),
        in_specs=[vmem()] * 11 + [hbm()] * 3,
        out_specs=[vmem()] * 4,
        out_shape=[
            jax.ShapeDtypeStruct((half, wide), BF16),
            jax.ShapeDtypeStruct((half, wide), BF16),
            jax.ShapeDtypeStruct((rows, wide), BF16),
            jax.ShapeDtypeStruct((rows, width), F32),
        ],
        scratch_shapes=[
            pltpu.VMEM((width, width), BF16),
            pltpu.VMEM((steps, width, step), BF16),
            pltpu.VMEM((steps, step, width), BF16),
            pltpu.SemaphoreType.DMA((1 + 2 * steps,)),
            pltpu.VMEM((rows, 4 * rows + LANES), F32),
            pltpu.VMEM((rows, width), F32),
            pltpu.VMEM((rows, LANES), F32),
            pltpu.VMEM((rows, width), F32),
            pltpu.VMEM((rows, width), BF16),
            pltpu.VMEM((rows, width), F32),
            pltpu.VMEM((rows, width), F32),
            pltpu.VMEM((rows, width), BF16),
        ],
        compiler_params=pltpu.CompilerParams(vmem_limit_bytes=48 * MIB),
        cost_estimate=pl.CostEstimate(
            flops=2 * rows * width * (4 * hidden + 2 * width),
            bytes_accessed=2 * width * (2 * hidden + width),
            transcendentals=rows * hidden,
        ),
        name="middle",
    )(
        qkv_a, qkv_b, marks_a, marks_b, prefix_kv, *own, *cots, gain[None], bias[None], *kept_in_hbm(w_out, w_fc, w_proj)
    )


def key_grads(keys, values, queries, grads, marks, pair, low, mask):
    rows = keys.shape[0]
    scale = jnp.asarray(HEAD**-0.5, BF16)
    left = jnp.concatenate(
        [two_heads(keys * scale, low), picks(rows, pair, 0, -1.0).astype(BF16)], 1
    )
    scores = nt(left, jnp.concatenate([queries, marks], 1))
    weights = jnp.exp(scores + jnp.concatenate([mask, mask], 0))
    left = jnp.concatenate(
        [two_heads(values, low), picks(rows, pair, 3 * HEADS, -1.0).astype(BF16)], 1
    )
    slopes = weights * nt(left, jnp.concatenate([grads, marks], 1))
    key_grad = nn(slopes.astype(BF16), queries)
    value_grad = nn(weights.astype(BF16), grads)
    return join_heads(key_grad, low) * HEAD**-0.5, join_heads(value_grad, low)


def prefix_kernel(qkv_a, grads, prefix_kv, mine, theirs):
    used = mine.shape[0]
    first = lax.axis_index("seq") % 2 == 0
    rows, width = grads.shape[0], grads.shape[1] - LANES
    count = prefix_kv.shape[0]
    low = head_mask(count)
    mask = jnp.where(iota((count, rows), 0) < used, 0.0, NEG)
    marks = grads[:, width:]

    def step(pair, carry):
        at = pl.ds(pl.multiple_of(pair * LANES, LANES), LANES)
        at_v = pl.ds(pl.multiple_of(width + pair * LANES, LANES), LANES)
        key_grad, value_grad = key_grads(
            prefix_kv[:, at], prefix_kv[:, at_v], qkv_a[:rows, at], grads[:, at], marks, pair, low, mask
        )
        mine[:, at] = jnp.where(first, key_grad, value_grad)[:used]
        theirs[:, at] = jnp.where(first, value_grad, key_grad)[:used]
        return carry

    lax.fori_loop(0, HEADS // 2, step, 0, unroll=True)


def prefix_part(count, qkv_a, grads, prefix_kv):
    half = prefix_kv.shape[1] // 2
    return pl.pallas_call(
        prefix_kernel,
        in_specs=[vmem()] * 3,
        out_specs=[vmem()] * 2,
        out_shape=[jax.ShapeDtypeStruct((count, half), F32)] * 2,
        compiler_params=pltpu.CompilerParams(vmem_limit_bytes=16 * MIB),
        cost_estimate=pl.CostEstimate(flops=1 << 29, bytes_accessed=1 << 20, transcendentals=1 << 16),
        name="prefix",
    )(qkv_a, grads, prefix_kv)


def query_kernel(count, qkv_a, qkv_b, marks_a, marks_b, prefix_kv, grads, weight, order, out, scores_bias, grad_query):
    del order
    rows, width = grad_query.shape
    scores_bias[...] = key_bias(marks_a[:rows], marks_a[...], marks_b[...], rows // 2, count)
    low = head_mask(rows)
    marks = grads[:, width:]
    marks_twice = jnp.concatenate([marks, marks], 0)
    ones = jnp.ones((4 * rows + LANES, LANES), BF16)

    def step(pair, carry):
        at = pl.ds(pl.multiple_of(pair * LANES, LANES), LANES)
        at_k = pl.ds(pl.multiple_of(width + pair * LANES, LANES), LANES)
        at_v = pl.ds(pl.multiple_of(2 * width + pair * LANES, LANES), LANES)
        keys = with_prefix(qkv_a[:, at_k], qkv_b[:, at_k], prefix_kv[:, at])
        values = with_prefix(qkv_a[:, at_v], qkv_b[:, at_v], prefix_kv[:, at_k])
        query = two_heads(qkv_a[:rows, at] * jnp.asarray(HEAD**-0.5, BF16), low)
        tops = marks_twice * picks(rows, pair, 0, -1.0).astype(BF16)
        scores = nt(jnp.concatenate([query, tops], 1), jnp.concatenate([keys, ones], 1))
        mask = scores_bias[...]
        weights = jnp.exp(scores + jnp.concatenate([mask, mask], 0))
        bases = marks_twice * picks(rows, pair, 3 * HEADS, -1.0).astype(BF16)
        left = jnp.concatenate([two_heads(grads[:, at], low), bases], 1)
        slopes = weights * nt(left, jnp.concatenate([values, ones], 1))
        grad = join_heads(nn(slopes.astype(BF16), keys), low)
        grad_query[:, at] = (grad * HEAD**-0.5).astype(BF16)
        return carry

    lax.fori_loop(0, HEADS // 2, step, 0, unroll=True)
    out[...] = nt(grad_query[...], weight[:, :width])


def query_part(count, qkv_a, qkv_b, marks_a, marks_b, prefix_kv, grads, weight, order):
    rows, width = grads.shape[0], grads.shape[1] - LANES
    return pl.pallas_call(
        partial(query_kernel, count),
        in_specs=[vmem()] * 7 + [pl.BlockSpec(memory_space=pl.ANY)],
        out_specs=vmem(),
        out_shape=jax.ShapeDtypeStruct((rows, width), F32),
        scratch_shapes=[pltpu.VMEM((rows, 4 * rows + LANES), F32), pltpu.VMEM((rows, width), BF16)],
        compiler_params=pltpu.CompilerParams(vmem_limit_bytes=30 * MIB),
        cost_estimate=pl.CostEstimate(flops=1 << 32, bytes_accessed=1 << 23, transcendentals=1 << 20),
        name="query",
    )(qkv_a, qkv_b, marks_a, marks_b, prefix_kv, grads, weight, order)


def final_kernel(
    qkv_a,
    qkv_b,
    marks_a,
    marks_b,
    grads_0,
    grads_1,
    grads_2,
    grads_3,
    own_0,
    own_1,
    gain,
    grad_middle,
    grad_partial,
    weight,
    back_0,
    back_1,
    scores_bias,
    grad_keys,
):
    half, rows = own_0.shape[0], 2 * own_0.shape[0]
    width = grad_middle.shape[1]
    row, core, y_at = place()
    own = positions(iota((rows, 1), 0), half, row, core, y_at)
    other = all_positions((1, 8 * half), 1, half, row, core, y_at)
    same = nt(marks_a[:rows], jnp.concatenate([marks_a[...], marks_b[...]], 0))
    visible = jnp.logical_and(same > 0.5, own <= other)
    scores_bias[...] = jnp.where(visible, 0.0, NEG)
    low = head_mask(rows)
    blocks = (grads_0, grads_1, grads_2, grads_3)
    marks = jnp.concatenate([g[:, width:] for g in blocks], 0)

    def step(pair, carry):
        at = pl.ds(pl.multiple_of(pair * LANES, LANES), LANES)
        at_k = pl.ds(pl.multiple_of(width + pair * LANES, LANES), LANES)
        at_v = pl.ds(pl.multiple_of(2 * width + pair * LANES, LANES), LANES)
        queries = jnp.concatenate([qkv_a[:, at], qkv_b[:, at]], 0)
        grads = jnp.concatenate([g[:, at] for g in blocks], 0)
        key_grad, value_grad = key_grads(
            qkv_a[:rows, at_k], qkv_a[:rows, at_v], queries, grads, marks, pair, low, scores_bias[...]
        )
        grad_keys[:, at] = key_grad.astype(BF16)
        grad_keys[:, at_k] = value_grad.astype(BF16)
        return carry

    lax.fori_loop(0, HEADS // 2, step, 0, unroll=True)
    grad_norm = grad_partial[...] + nt(grad_keys[...], weight[:, width:])
    inputs = jnp.concatenate([own_0[:, :width], own_1[:, :width]], 0).astype(F32)
    unit, inverse = norm_parts(inputs)
    out = (grad_middle[...] + norm_back(unit, inverse, gain[...], grad_norm)).astype(BF16)
    back_0[...] = out[:half]
    back_1[...] = out[half:]


def final_part(qkv_a, qkv_b, marks_a, marks_b, grads, own, gain, grad_middle, grad_partial, weight):
    rows, width = grad_middle.shape
    half = rows // 2
    return pl.pallas_call(
        final_kernel,
        in_specs=[vmem()] * 14,
        out_specs=[vmem()] * 2,
        out_shape=[jax.ShapeDtypeStruct((half, width), BF16)] * 2,
        scratch_shapes=[
            pltpu.VMEM((rows, 4 * rows), F32),
            pltpu.VMEM((rows, 2 * width), BF16),
        ],
        compiler_params=pltpu.CompilerParams(vmem_limit_bytes=30 * MIB),
        cost_estimate=pl.CostEstimate(flops=1 << 32, bytes_accessed=1 << 23, transcendentals=1 << 20),
        name="final",
    )(qkv_a, qkv_b, marks_a, marks_b, *grads, *own, gain[None], grad_middle, grad_partial, weight)


def routes(k):
    pairs = []
    for seq in range(4):
        for blk in range(8):
            group, z_at, y_at = seq % 2, blk // 2, blk % 2
            row = (z_at + k) % 2
            pairs.append((seq * 8 + blk, (seq - group + z_at // 2) * 8 + (2 * group + row) * 2 + y_at))
    return pairs


def body_rows(
    tokens,
    segment_ids,
    ln1_gain,
    ln1_bias,
    w_qkv,
    w_out,
    ln2_gain,
    ln2_bias,
    w_fc,
    w_proj,
    prefix_embed,
    w_mlp1,
    b_mlp1,
    w_mlp2,
    b_mlp2,
    cotangent,
):
    half, _, width = tokens.shape
    everyone = ("seq", "blk")
    there = [routes(k) for k in range(2)]
    back = [[(b, a) for a, b in pairs] for pairs in there]
    swap_core = [(i, i ^ 1) for i in range(4)]
    swap_y = [(i, i ^ 1) for i in range(8)]
    swap_both = [(i, i ^ 9) for i in range(32)]
    odd = (lax.axis_index("blk") // 2) % 2 == 1

    def sorted_rows(first, second):
        return jnp.where(odd, second, first), jnp.where(odd, first, second)

    def after(value, *done):
        return lax.optimization_barrier((value, done))[0]

    marks = (segment_ids[:, :, None] == jnp.arange(LANES)[None, None]).astype(BF16)
    marked = jnp.concatenate([tokens, marks], -1)
    out_msgs = sorted_rows(marked[:, 0], marked[:, 1])
    cot_msgs = sorted_rows(cotangent[:, 0], cotangent[:, 1])
    own = [lax.ppermute(m, everyone, there[k]) for k, m in enumerate(out_msgs)]
    prefix_kv, inner, w_near, near_embed, near_mlp1, near_mlp2 = adapter_forward(
        prefix_embed, w_mlp1, b_mlp1, w_mlp2, b_mlp2, w_qkv
    )
    count = prefix_embed.shape[0]
    own = after(own, inner)
    across = [lax.ppermute(m, "blk", swap_y) for m in own]
    beside = [lax.ppermute(m, "seq", swap_core) for m in own]
    cots = [lax.ppermute(m, everyone, there[k]) for k, m in enumerate(after(cot_msgs, beside))]
    beyond = [lax.ppermute(m, "seq", swap_core) for m in across]

    qkv_a, marks_a = project(own + beside, ln1_gain, ln1_bias, w_near)
    qkv_b, marks_b = project(across + beyond, ln1_gain, ln1_bias, w_near)
    back_0, back_1, grads, grad_middle = middle_part(
        count, qkv_a, qkv_b, marks_a, marks_b, prefix_kv, own, cots, ln2_gain, ln2_bias, w_out, w_fc, w_proj
    )
    grads_y = lax.ppermute(grads, "blk", swap_y)
    grads_c = lax.ppermute(grads, "seq", swap_core)
    grads_yc = lax.ppermute(grads_y, "seq", swap_core)
    home = [lax.ppermute(m, everyone, back[k]) for k, m in enumerate((back_0, back_1))]

    def spread(value, axis, size, partners):
        return [lax.ppermute(value, axis, [(i, i ^ far) for i in range(size)]) for far in partners]

    def add_four(value, others):
        return (value + others[0]) + (others[1] + others[2])

    mine, theirs = prefix_part(count, qkv_a, grads, prefix_kv)
    parts = spread(mine, "seq", 4, (2,)) + spread(theirs, "seq", 4, (1, 3))
    grad_partial = query_part(count, qkv_a, qkv_b, marks_a, marks_b, prefix_kv, grads, w_near, mine)
    final_0, final_1 = final_part(
        qkv_a,
        qkv_b,
        marks_a,
        marks_b,
        (grads, grads_c, grads_y, grads_yc),
        own,
        ln1_gain,
        grad_middle,
        grad_partial,
        w_near,
    )
    finals = [lax.ppermute(m, everyone, back[k]) for k, m in enumerate((final_0, final_1))]
    mine = add_four(mine, after(parts, grads_y, grad_partial))
    mine = add_four(mine, spread(mine, "blk", 8, (2, 4, 6)))
    halves_in = [mine]
    halves_in += [lax.ppermute(mine, "blk", swap_y), lax.ppermute(mine, "seq", swap_core)]
    halves_in += [lax.ppermute(mine, everyone, swap_both)]
    summed = adapter_backward(halves_in, near_embed, inner, near_mlp1, near_mlp2, final_0)

    home = sorted_rows(*after(home, final_0))
    block_out = jnp.stack([m[:, :width] for m in home], 1)
    logs = [m[:, width : width + 3 * HEADS].astype(F32).reshape(half, 3, HEADS).sum(1) for m in home]
    log_total = jnp.stack([jnp.transpose(m) for m in logs], 0)
    input_grad = jnp.stack(sorted_rows(*finals), 1).astype(F32)
    return (block_out, input_grad, summed[0], summed[1], summed[2], summed[3], summed[4], log_total)


def solution(mesh):
    four_by_eight = mesh.shape["seq"] == 4 and mesh.shape["blk"] == 8
    placed = (
        P("blk", "seq", None),
        P("blk", "seq"),
        P(),
        P(),
        P(),
        P(),
        P(),
        P(),
        P(),
        P(),
        P(),
        P(),
        P(),
        P(),
        P(),
        P("blk", "seq", None),
    )
    return jax.shard_map(
        body_rows if four_by_eight else body_plain,
        mesh=mesh,
        in_specs=placed,
        out_specs=(
            P("blk", "seq", None),
            P("blk", "seq", None),
            P(),
            P(),
            P(),
            P(),
            P(),
            P("seq", None, "blk"),
        ),
        check_vma=False,
    )
```

```python
from functools import partial
import math

import jax
import jax.numpy as jnp
from jax import lax
from jax.experimental import pallas as pl
from jax.experimental.pallas import tpu as pltpu
from jax.sharding import PartitionSpec as P

HEADS = 16
HEAD = 64


EPS = 1e-05
NEG = -1e30
HIGH = lax.Precision.HIGHEST


def layer_norm(value_in, gain, bias):
    average = jnp.mean(value_in, axis=-1, keepdims=True)
    centered = value_in - average
    variance = jnp.mean(centered * centered, axis=-1, keepdims=True)
    return centered * lax.rsqrt(variance + EPS) * gain + bias


def adapter(prefix_embed, w_mlp1, b_mlp1, w_mlp2, b_mlp2):
    inner_act = jnp.tanh(jnp.dot(prefix_embed, w_mlp1, precision=HIGH) + b_mlp1)
    return jnp.dot(inner_act, w_mlp2, precision=HIGH) + b_mlp2


def gelu_tanh(pre_act):
    return jax.nn.gelu(pre_act, approximate=True)


def split_heads(block_in):
    return block_in.reshape(block_in.shape[0], block_in.shape[1], HEADS, HEAD)


def allowed(query_pos, query_seg, key_pos, key_seg):
    same_seg = query_seg.T[:, :, None] == key_seg.T[:, None, :]
    causal = key_pos[None, None, :] <= query_pos[None, :, None]
    return jnp.logical_and(same_seg, causal)[:, None]


def scores_of(query_heads, key_block, score_scale):
    return score_scale * jnp.einsum(
        "prhd,krhd->rhpk", query_heads, split_heads(key_block), preferred_element_type=jnp.float32
    )


def block_grads(
    query_heads,
    grad_heads,
    log_total,
    slope_base,
    query_pos,
    query_seg,
    key_block,
    value_block,
    key_pos,
    key_seg,
    score_scale,
):
    scores = scores_of(query_heads, key_block, score_scale)
    scores = jnp.where(allowed(query_pos, query_seg, key_pos, key_seg), scores, NEG)
    weights = jnp.exp(scores - log_total[..., None])
    grad_weights = jnp.einsum(
        "prhd,krhd->rhpk", grad_heads, split_heads(value_block), preferred_element_type=jnp.float32
    )
    slopes = (weights * (grad_weights - slope_base[..., None])).astype(jnp.bfloat16)
    return (weights.astype(jnp.bfloat16), slopes)


def body_plain(
    tokens,
    segment_ids,
    ln1_gain,
    ln1_bias,
    w_qkv,
    w_out,
    ln2_gain,
    ln2_bias,
    w_fc,
    w_proj,
    prefix_embed,
    w_mlp1,
    b_mlp1,
    w_mlp2,
    b_mlp2,
    cotangent,
):
    pos_dev, row_count, width = tokens.shape
    score_scale = HEAD ** (-0.5)
    flat_rows = pos_dev * row_count
    own_pos = lax.axis_index("blk") * pos_dev + jnp.arange(pos_dev)
    inputs = tokens.astype(jnp.float32).reshape(flat_rows, width)
    normed_one = layer_norm(inputs, ln1_gain, ln1_bias).astype(jnp.bfloat16)
    projected = jnp.dot(normed_one, w_qkv, preferred_element_type=jnp.float32).astype(jnp.bfloat16)
    queries = projected[:, :width].reshape(pos_dev, row_count, width)
    keys = projected[:, width : 2 * width].reshape(pos_dev, row_count, width)
    values = projected[:, 2 * width :].reshape(pos_dev, row_count, width)
    query_heads = split_heads(queries)
    prefix_low = adapter(prefix_embed, w_mlp1, b_mlp1, w_mlp2, b_mlp2).astype(jnp.bfloat16)
    prefix_keys = prefix_low[:, :width].reshape(-1, HEADS, HEAD)
    prefix_values = prefix_low[:, width:].reshape(-1, HEADS, HEAD)
    prefix_scores = score_scale * jnp.einsum(
        "prhd,jhd->rhpj", query_heads, prefix_keys, preferred_element_type=jnp.float32
    )
    start_top = jnp.max(prefix_scores, -1)
    start_weights = jnp.exp(prefix_scores - start_top[..., None])
    start_denom = jnp.sum(start_weights, -1)
    start_numer = jnp.einsum(
        "rhpj,jhd->rhpd",
        start_weights.astype(jnp.bfloat16),
        prefix_values,
        preferred_element_type=jnp.float32,
    )
    start_state = (start_top, start_denom, start_numer)
    running = start_state
    key_shards = lax.all_gather(keys, "blk", axis=0, tiled=True)
    value_shards = lax.all_gather(values, "blk", axis=0, tiled=True)
    seg_shards = lax.all_gather(segment_ids, "blk", axis=0, tiled=True)
    num_rows = key_shards.shape[0]
    forward_stride = math.gcd(num_rows, 512)

    def inner(state, block_index):
        running_top, denominator, numerator = state
        offset = block_index * forward_stride
        key_block = lax.dynamic_slice_in_dim(key_shards, offset, forward_stride, 0)
        value_block = lax.dynamic_slice_in_dim(value_shards, offset, forward_stride, 0)
        seg_block = lax.dynamic_slice_in_dim(seg_shards, offset, forward_stride, 0)
        key_pos = offset + jnp.arange(forward_stride)
        scores = jnp.where(
            allowed(own_pos, segment_ids, key_pos, seg_block),
            scores_of(query_heads, key_block, score_scale),
            NEG,
        )
        new_top = jnp.maximum(running_top, jnp.max(scores, -1))
        fading = jnp.exp(running_top - new_top)
        weights = jnp.exp(scores - new_top[..., None])
        denominator = denominator * fading + jnp.sum(weights, -1)
        numerator = numerator * fading[..., None] + jnp.einsum(
            "rhpk,krhd->rhpd",
            weights.astype(jnp.bfloat16),
            split_heads(value_block),
            preferred_element_type=jnp.float32,
        )
        return ((new_top, denominator, numerator), None)

    running, _ = lax.scan(inner, running, jnp.arange(num_rows // forward_stride))
    final_top, final_denom, final_numer = running
    log_total = final_top + jnp.log(final_denom)
    attended = final_numer / final_denom[..., None]
    attended_rows = jnp.transpose(attended, (2, 0, 1, 3)).reshape(flat_rows, width)
    middle = inputs + jnp.dot(
        attended_rows.astype(jnp.bfloat16), w_out, preferred_element_type=jnp.float32
    )
    normed_two = layer_norm(middle, ln2_gain, ln2_bias).astype(jnp.bfloat16)
    hidden_pre = jnp.dot(normed_two, w_fc, preferred_element_type=jnp.float32)
    hidden_act = gelu_tanh(hidden_pre).astype(jnp.bfloat16)
    outputs = middle + jnp.dot(hidden_act, w_proj, preferred_element_type=jnp.float32)
    block_out = outputs.astype(jnp.bfloat16).reshape(pos_dev, row_count, width)
    grad_out = cotangent.reshape(flat_rows, width)
    grad_act = jnp.dot(grad_out, w_proj.T, preferred_element_type=jnp.float32)
    _, gelu_back = jax.vjp(gelu_tanh, hidden_pre)
    grad_pre = gelu_back(grad_act)[0].astype(jnp.bfloat16)
    grad_norm_two = jnp.dot(grad_pre, w_fc.T, preferred_element_type=jnp.float32)
    _, norm_two_back = jax.vjp(partial(layer_norm, gain=ln2_gain, bias=ln2_bias), middle)
    grad_middle = grad_out.astype(jnp.float32) + norm_two_back(grad_norm_two)[0]
    grad_attended = jnp.dot(
        grad_middle.astype(jnp.bfloat16), w_out.T, preferred_element_type=jnp.float32
    ).astype(jnp.bfloat16)
    grad_flat = grad_attended.reshape(pos_dev, row_count, width)
    grad_heads = split_heads(grad_flat)
    slope_base = jnp.sum(jnp.transpose(grad_heads.astype(jnp.float32), (1, 2, 0, 3)) * attended, -1)
    prefix_weights = jnp.exp(prefix_scores - log_total[..., None])
    prefix_dw = jnp.einsum(
        "prhd,jhd->rhpj", grad_heads, prefix_values, preferred_element_type=jnp.float32
    )
    prefix_slopes = (prefix_weights * (prefix_dw - slope_base[..., None])).astype(jnp.bfloat16)
    grad_query = score_scale * jnp.einsum(
        "rhpj,jhd->prhd", prefix_slopes, prefix_keys, preferred_element_type=jnp.float32
    )
    grad_pkeys = score_scale * jnp.einsum(
        "rhpj,prhd->jhd", prefix_slopes, query_heads, preferred_element_type=jnp.float32
    )
    grad_pvalues = jnp.einsum(
        "rhpj,prhd->jhd",
        prefix_weights.astype(jnp.bfloat16),
        grad_heads,
        preferred_element_type=jnp.float32,
    )
    grad_prefix_kv = jnp.concatenate(
        [grad_pkeys.reshape(-1, width), grad_pvalues.reshape(-1, width)], -1
    )
    keys_all, values_all, segs_all = (
        lax.all_gather(keys, "blk", axis=0, tiled=True),
        lax.all_gather(values, "blk", axis=0, tiled=True),
        lax.all_gather(segment_ids, "blk", axis=0, tiled=True),
    )
    length = keys_all.shape[0]
    stride = math.gcd(length, 512)

    def backward_step(grad_q, block_index):
        offset = block_index * stride
        key_block = lax.dynamic_slice_in_dim(keys_all, offset, stride, 0)
        value_block = lax.dynamic_slice_in_dim(values_all, offset, stride, 0)
        seg_block = lax.dynamic_slice_in_dim(segs_all, offset, stride, 0)
        key_pos = offset + jnp.arange(stride)
        weights_low, slopes = block_grads(
            query_heads,
            grad_heads,
            log_total,
            slope_base,
            own_pos,
            segment_ids,
            key_block,
            value_block,
            key_pos,
            seg_block,
            score_scale,
        )
        grad_q = grad_q + score_scale * jnp.einsum(
            "rhpk,krhd->prhd", slopes, split_heads(key_block), preferred_element_type=jnp.float32
        )
        key_term = score_scale * jnp.einsum(
            "rhpk,prhd->krhd", slopes, query_heads, preferred_element_type=jnp.float32
        )
        value_term = jnp.einsum(
            "rhpk,prhd->krhd", weights_low, grad_heads, preferred_element_type=jnp.float32
        )
        return (
            grad_q,
            (
                key_term.reshape(stride, row_count, width),
                value_term.reshape(stride, row_count, width),
            ),
        )

    grad_query, (key_terms, value_terms) = lax.scan(
        backward_step, grad_query, jnp.arange(length // stride)
    )
    key_terms = key_terms.reshape(length, row_count, width)
    value_terms = value_terms.reshape(length, row_count, width)
    grad_keys, grad_values = (
        lax.psum_scatter(key_terms, "blk", scatter_dimension=0, tiled=True),
        lax.psum_scatter(value_terms, "blk", scatter_dimension=0, tiled=True),
    )
    grad_proj = jnp.concatenate(
        [
            grad_query.reshape(flat_rows, width).astype(jnp.bfloat16),
            grad_keys.reshape(flat_rows, width).astype(jnp.bfloat16),
            grad_values.reshape(flat_rows, width).astype(jnp.bfloat16),
        ],
        -1,
    )
    grad_norm_one = jnp.dot(grad_proj, w_qkv.T, preferred_element_type=jnp.float32)
    _, norm_one_back = jax.vjp(partial(layer_norm, gain=ln1_gain, bias=ln1_bias), inputs)
    input_grad = (grad_middle + norm_one_back(grad_norm_one)[0]).reshape(pos_dev, row_count, width)
    _, adapter_back = jax.vjp(adapter, prefix_embed, w_mlp1, b_mlp1, w_mlp2, b_mlp2)
    local_grads = adapter_back(grad_prefix_kv)
    summed = lax.psum(
        (local_grads[0], local_grads[1], local_grads[2], local_grads[3], local_grads[4]),
        ("seq", "blk"),
    )
    return (block_out, input_grad, summed[0], summed[1], summed[2], summed[3], summed[4], log_total)


F32 = jnp.float32
BF16 = jnp.bfloat16
LANES = 128
PRE_ROWS = 16
MIB = 1 << 20


def nn(left, right):
    return jnp.dot(left, right, preferred_element_type=F32)


def nt(left, right):
    return lax.dot_general(left, right, (((1,), (1,)), ((), ())), preferred_element_type=F32)


def norm_parts(value_in):
    average = jnp.mean(value_in, axis=-1, keepdims=True)
    centered = value_in - average
    variance = jnp.mean(centered * centered, axis=-1, keepdims=True)
    inverse = lax.rsqrt(variance + EPS)
    return centered * inverse, inverse


def norm_back(unit, inverse, gain, grad):
    scaled = grad * gain
    first = jnp.mean(scaled, axis=-1, keepdims=True)
    second = jnp.mean(scaled * unit, axis=-1, keepdims=True)
    return inverse * (scaled - first - unit * second)


def iota(shape, dim):
    return lax.broadcasted_iota(jnp.int32, shape, dim)


def place():
    blk = lax.axis_index("blk")
    return (blk // 2) % 2, lax.axis_index("seq") % 2, blk % 2


def positions(index, half, row, core, y_at):
    upper = (index >= half).astype(jnp.int32)
    slot = upper + row - 2 * upper * row
    block = (2 * core + slot) * 2 + y_at
    return block * half + index - upper * half


def members(core, y_at):
    return ((core, y_at), (1 - core, y_at), (core, 1 - y_at), (1 - core, 1 - y_at))


def all_positions(shape, dim, half, row, core, y_at):
    part = tuple(2 * half if d == dim else n for d, n in enumerate(shape))
    return jnp.concatenate(
        [positions(iota(part, dim), half, row, c, y) for c, y in members(core, y_at)], dim
    )


def vmem():
    return pl.BlockSpec(memory_space=pltpu.VMEM)


def hbm():
    return pl.BlockSpec(memory_space=pltpu.HBM)


def kept_in_hbm(*arrays):
    return [pltpu.with_memory_space_constraint(a, pltpu.HBM) for a in arrays]


def by_tiles(block):
    half, pair, width = block.shape
    tiles = jnp.transpose(block.reshape(half, pair, width // LANES, LANES), (0, 2, 1, 3))
    return tiles.reshape(half, pair * width // LANES, LANES)


def from_tiles(tiles, width):
    half, count, _ = tiles.shape
    pair = count * LANES // width
    block = jnp.transpose(tiles.reshape(half, width // LANES, pair, LANES), (0, 2, 1, 3))
    return block.reshape(half, pair, width)


def odd_place():
    return (lax.axis_index("blk") // 2) % 2 == 1


def split_kernel(marked, *refs):
    tokens, ids, (out_0, out_1, work) = refs[0], refs[1], refs[-3:]
    half, count, _ = tokens.shape
    odd = odd_place()
    work[...] = tokens[...].astype(F32).reshape(half * count, LANES)
    for i in range(count // 2):
        at = pl.ds(i * LANES, LANES)
        first, second = (work[pl.ds(2 * i + r, half, stride=count)] for r in range(2))
        out_0[:, at] = jnp.where(odd, second, first).astype(BF16)
        out_1[:, at] = jnp.where(odd, first, second).astype(BF16)
    if marked:
        width = count // 2 * LANES
        first, second = (
            jnp.where(iota((LANES, half), 0) == ids[r : r + 1], 1.0, 0.0).T for r in range(2)
        )
        out_0[:, width:] = jnp.where(odd, second, first).astype(BF16)
        out_1[:, width:] = jnp.where(odd, first, second).astype(BF16)


def split_rows(block, segment_ids=None):
    tiles = by_tiles(block)
    half, count, _ = tiles.shape
    extra = () if segment_ids is None else kept_in_hbm(segment_ids.T)
    width = count // 2 * LANES + LANES * len(extra)
    return pl.pallas_call(
        partial(split_kernel, bool(extra)),
        in_specs=[vmem()] * (1 + len(extra)),
        out_specs=[vmem()] * 2,
        out_shape=[jax.ShapeDtypeStruct((half, width), BF16)] * 2,
        scratch_shapes=[pltpu.VMEM((half * count, LANES), F32)],
        compiler_params=pltpu.CompilerParams(vmem_limit_bytes=4 * MIB),
        cost_estimate=pl.CostEstimate(flops=1 << 20, bytes_accessed=1 << 19, transcendentals=0),
        name="split",
    )(*kept_in_hbm(tiles), *extra)


def land_kernel(logs, *refs):
    msg_0, msg_1, out = refs[0], refs[1], refs[2]
    work = refs[-1]
    half, count, _ = out.shape
    width = count // 2 * LANES
    odd = odd_place()
    for i in range(count // 2):
        at = pl.ds(i * LANES, LANES)
        one, two = msg_0[:half, at].astype(F32), msg_1[:half, at].astype(F32)
        work[pl.ds(2 * i, half, stride=count)] = jnp.where(odd, two, one)
        work[pl.ds(2 * i + 1, half, stride=count)] = jnp.where(odd, one, two)
    out[...] = work[...].reshape(out.shape).astype(out.dtype)
    if logs:
        heads = refs[3].shape[1]
        one, two = (m[:half, width:].astype(F32) for m in (msg_0, msg_1))
        for r, chosen in enumerate((jnp.where(odd, two, one), jnp.where(odd, one, two))):
            summed = chosen + jnp.roll(chosen, -heads, 1) + jnp.roll(chosen, -2 * heads, 1)
            refs[3][r] = summed.T[:heads]


def land(messages, half, width, dtype, logs):
    count = 2 * width // LANES
    out = pl.pallas_call(
        partial(land_kernel, logs),
        in_specs=[vmem()] * 2,
        out_specs=[vmem()] * (1 + logs),
        out_shape=[jax.ShapeDtypeStruct((half, count, LANES), dtype)]
        + [jax.ShapeDtypeStruct((2, HEADS, half), F32)] * logs,
        scratch_shapes=[pltpu.VMEM((half * count, LANES), F32)],
        compiler_params=pltpu.CompilerParams(vmem_limit_bytes=4 * MIB),
        cost_estimate=pl.CostEstimate(flops=1000, bytes_accessed=1000, transcendentals=0),
        name="land",
    )(*messages)
    return (from_tiles(out[0], width), *out[1:])


def project_kernel(count, *refs):
    messages, (gain, bias, weight, out, marks, normed) = refs[:count], refs[count:]
    half, width = messages[0].shape[0], normed.shape[1]
    for i, message in enumerate(messages):
        rows = pl.ds(i * half, half)
        unit, _ = norm_parts(message[:, :width].astype(F32))
        normed[rows] = (unit * gain[...] + bias[...]).astype(BF16)
        marks[rows] = message[:, width:]
    for i in range(3):
        at = pl.ds(i * width, width)
        out[:, at] = nn(normed[...], weight[:, at]).astype(BF16)


def project(messages, gain, bias, weight):
    count, half = len(messages), messages[0].shape[0]
    width, columns = weight.shape
    rows = count * half
    return pl.pallas_call(
        partial(project_kernel, count),
        in_specs=[vmem()] * (count + 3),
        out_specs=[vmem()] * 2,
        out_shape=[
            jax.ShapeDtypeStruct((rows, columns), BF16),
            jax.ShapeDtypeStruct((rows, LANES), BF16),
        ],
        scratch_shapes=[pltpu.VMEM((rows, width), BF16)],
        compiler_params=pltpu.CompilerParams(vmem_limit_bytes=16 * MIB),
        cost_estimate=pl.CostEstimate(
            flops=2 * rows * width * columns, bytes_accessed=2 * width * columns, transcendentals=0
        ),
        name="project",
    )(*messages, gain[None], bias[None], weight)


def halves(value_in):
    high = value_in.astype(BF16)
    return high, (value_in - high.astype(F32)).astype(BF16)


def pad_rows(value_in, rows):
    return jnp.concatenate(
        [value_in, jnp.zeros((rows - value_in.shape[0], value_in.shape[1]), value_in.dtype)], 0
    )


def three_products(product, left, weight):
    rows = left.shape[0]
    high, low = halves(left)
    w_high, w_low = halves(weight)
    both = product(jnp.concatenate([high, low], 0), w_high)
    return both[:rows] + both[rows:] + product(high, w_low)


def adapter_kernel(
    h_embed,
    w_mlp1,
    h_mlp1,
    w_mlp2,
    h_mlp2,
    w_qkv,
    out,
    inner,
    v_qkv,
    embed,
    turned,
    v_mlp1,
    v_mlp2,
    b_mlp1,
    b_mlp2,
    sems,
):
    steps, step = v_mlp2.shape[0], v_mlp2.shape[2]
    small = []
    for i, (source, target) in enumerate(
        ((h_embed, embed), (h_mlp1, b_mlp1), (h_mlp2, b_mlp2), (w_mlp1, v_mlp1))
    ):
        small.append(pltpu.make_async_copy(source, target, sems.at[steps + i]))
        small[-1].start()
    rest = []
    for i in range(steps):
        copy = pltpu.make_async_copy(w_mlp2.at[:, pl.ds(i * step, step)], v_mlp2.at[i], sems.at[i])
        copy.start()
        rest.append(copy)
    weights = pltpu.make_async_copy(w_qkv, v_qkv, sems.at[steps + len(small)])
    weights.start()
    for copy in small:
        copy.wait()
    source = pad_rows(embed[...], PRE_ROWS)
    act = jnp.tanh(three_products(nn, source, v_mlp1[...]) + b_mlp1[...])
    inner[...] = act
    columns, hidden = steps * step, v_mlp1.shape[1]
    for i in range(v_mlp1.shape[0] // hidden):
        part = v_mlp1[pl.ds(i * hidden, hidden)].astype(BF16)
        turned[pl.ds(columns + i * hidden, hidden)] = part.T
    for i, copy in enumerate(rest):
        copy.wait()
        turned[pl.ds(i * step, step)] = v_mlp2[i].astype(BF16).T
        span = pl.ds(i * step, step)
        part = three_products(nn, act, v_mlp2[i]) + b_mlp2[:, span]
        out[:, span] = jnp.where(iota(part.shape, 0) < embed.shape[0], part, 0.0).astype(BF16)
    weights.wait()


def adapter_forward(embed, w_mlp1, b_mlp1, w_mlp2, b_mlp2, w_qkv):
    width, hidden = w_mlp1.shape
    columns = w_mlp2.shape[1]
    steps = 4
    return pl.pallas_call(
        adapter_kernel,
        in_specs=[hbm()] * 6,
        out_specs=[vmem()] * 5,
        out_shape=[
            jax.ShapeDtypeStruct((PRE_ROWS, columns), BF16),
            jax.ShapeDtypeStruct((PRE_ROWS, hidden), F32),
            pltpu.VMEM(w_qkv.shape, w_qkv.dtype),
            pltpu.VMEM(embed.shape, F32),
            pltpu.VMEM((columns + width, hidden), BF16),
        ],
        scratch_shapes=[
            pltpu.VMEM((width, hidden), F32),
            pltpu.VMEM((steps, hidden, columns // steps), F32),
            pltpu.VMEM((1, hidden), F32),
            pltpu.VMEM((1, columns), F32),
            pltpu.SemaphoreType.DMA((5 + steps,)),
        ],
        compiler_params=pltpu.CompilerParams(vmem_limit_bytes=20 * MIB),
        cost_estimate=pl.CostEstimate(flops=1 << 32, bytes_accessed=6 * MIB, transcendentals=1 << 13),
        name="adapter",
    )(*kept_in_hbm(embed, w_mlp1, b_mlp1[None], w_mlp2, b_mlp2[None], w_qkv))


def outer(left, right):
    l_high, l_low = halves(left)
    r_high, r_low = halves(right)
    return lax.dot_general(
        jnp.concatenate([l_high, l_high, l_low], 0),
        jnp.concatenate([r_high, r_low, r_high], 0),
        (((0,), (0,)), ((), ())),
        preferred_element_type=F32,
    )


def two_products(left, weight):
    high, low = halves(left)
    both = nn(jnp.concatenate([high, low], 0), weight)
    return both[: left.shape[0]] + both[left.shape[0] :]


def adapter_back_kernel(
    part_0,
    part_1,
    part_2,
    part_3,
    embed,
    inner,
    turned,
    order,
    grad_prefix,
    grad_mlp1,
    grad_bias1,
    grad_mlp2,
    grad_bias2,
    o_mlp1,
    o_mlp2,
    sems,
):
    del order
    steps, step = o_mlp2.shape[0], o_mlp2.shape[2]
    first, second, third, fourth = (p[...].astype(F32) for p in (part_0, part_1, part_2, part_3))
    grads = (first + second) + (third + fourth)
    act = inner[...]
    stores = []
    grad_bias2[...] = jnp.sum(grads, 0, keepdims=True)
    for i in range(steps):
        o_mlp2[i] = outer(act, grads[:, i * step : (i + 1) * step])
        stores.append(
            pltpu.make_async_copy(o_mlp2.at[i], grad_mlp2.at[:, pl.ds(i * step, step)], sems.at[i])
        )
        stores[-1].start()
    columns, (width, hidden) = steps * step, o_mlp1.shape
    back = two_products(grads, turned[:columns]) * (1.0 - act * act)
    grad_bias1[...] = jnp.sum(back, 0, keepdims=True)
    o_mlp1[...] = outer(pad_rows(embed[...], PRE_ROWS), back)
    stores.append(pltpu.make_async_copy(o_mlp1, grad_mlp1, sems.at[steps]))
    stores[-1].start()
    for i in range(width // hidden):
        part = two_products(back, turned[pl.ds(columns + i * hidden, hidden)])
        grad_prefix[:, pl.ds(i * hidden, hidden)] = part[: embed.shape[0]]
    for copy in stores:
        copy.wait()


def adapter_backward(parts, embed, inner, turned, order):
    hidden, width = turned.shape[1], embed.shape[1]
    columns = turned.shape[0] - width
    steps = 4
    out = pl.pallas_call(
        adapter_back_kernel,
        in_specs=[vmem()] * 7 + [pl.BlockSpec(memory_space=pl.ANY)],
        out_specs=[vmem(), hbm(), vmem(), hbm(), vmem()],
        out_shape=[
            jax.ShapeDtypeStruct(embed.shape, F32),
            jax.ShapeDtypeStruct((width, hidden), F32),
            jax.ShapeDtypeStruct((1, hidden), F32),
            jax.ShapeDtypeStruct((hidden, columns), F32),
            jax.ShapeDtypeStruct((1, columns), F32),
        ],
        scratch_shapes=[
            pltpu.VMEM((width, hidden), F32),
            pltpu.VMEM((steps, hidden, columns // steps), F32),
            pltpu.SemaphoreType.DMA((steps + 1,)),
        ],
        compiler_params=pltpu.CompilerParams(vmem_limit_bytes=16 * MIB),
        cost_estimate=pl.CostEstimate(flops=1000, bytes_accessed=1000, transcendentals=0),
        name="adapter_back",
    )(*parts, embed, inner, turned, order)
    return out[0], out[1], out[2][0], out[3], out[4][0]


def head_mask(rows):
    return iota((rows, LANES), 1) < HEAD


def two_heads(pair, low):
    zero = jnp.zeros_like(pair)
    return jnp.concatenate([jnp.where(low, pair, zero), jnp.where(low, zero, pair)], 0)


def join_heads(stacked, low):
    rows = stacked.shape[0] // 2
    return jnp.where(low, stacked[:rows], stacked[rows:])


def picks(rows, pair, first, value):
    lane = iota((rows, LANES), 1)
    inside = jnp.logical_and(lane >= first, lane < first + 3 * HEADS)
    parts = [
        jnp.where(jnp.logical_and(inside, lane % HEADS == 2 * pair + i), value, 0.0) for i in range(2)
    ]
    return jnp.concatenate(parts, 0)


def three_parts(value_in, first):
    lane = iota(value_in.shape, 1)
    high = value_in.astype(BF16).astype(F32)
    rest = value_in - high
    middle = rest.astype(BF16).astype(F32)
    low = rest - middle
    part = (lane - first) // HEADS
    chosen = jnp.where(part == 0, high, jnp.where(part == 1, middle, low))
    inside = jnp.logical_and(lane >= first, lane < first + 3 * HEADS)
    return jnp.where(inside, chosen, 0.0)


def key_bias(marks_own, marks_a, marks_b, half, count):
    row, core, y_at = place()
    rows = 2 * half
    own = positions(iota((rows, 1), 0), half, row, core, y_at)
    other = all_positions((1, 8 * half), 1, half, row, core, y_at)
    same = nt(marks_own, jnp.concatenate([marks_a, marks_b], 0))
    visible = jnp.logical_and(same > 0.5, other <= own)
    token_bias = jnp.where(visible, 0.0, NEG)
    prefix_bias = jnp.where(iota((rows, LANES), 1) < count, 0.0, NEG)
    return jnp.concatenate([token_bias, prefix_bias], 1)


def with_prefix(part_a, part_b, prefix):
    pad = jnp.zeros((LANES - prefix.shape[0], prefix.shape[1]), prefix.dtype)
    return jnp.concatenate([part_a, part_b, prefix, pad], 0)


def middle_kernel(
    count,
    qkv_a,
    qkv_b,
    marks_a,
    marks_b,
    prefix_kv,
    own_0,
    own_1,
    cot_0,
    cot_1,
    gain,
    bias,
    w_out,
    w_fc,
    w_proj,
    back_0,
    back_1,
    grad_out_heads,
    grad_middle,
    grad_prefix_kv,
    v_out,
    v_fc,
    v_proj,
    sems,
    scores_bias,
    attended,
    stats,
    middle,
    normed,
    total,
    grad_norm,
    cot,
):
    half, rows = own_0.shape[0], 2 * own_0.shape[0]
    width = middle.shape[1]
    steps, step = v_fc.shape[0], v_fc.shape[2]
    copies = [pltpu.make_async_copy(w_out, v_out, sems.at[0])]
    for i in range(steps):
        span = pl.ds(i * step, step)
        copies.append(pltpu.make_async_copy(w_fc.at[:, span], v_fc.at[i], sems.at[1 + 2 * i]))
        copies.append(pltpu.make_async_copy(w_proj.at[span], v_proj.at[i], sems.at[2 + 2 * i]))
    for copy in copies:
        copy.start()

    scores_bias[...] = key_bias(marks_a[:rows], marks_a[...], marks_b[...], half, count)
    low = head_mask(rows)
    lane = iota((rows, LANES), 1)
    stats[...] = jnp.zeros_like(stats)

    def attend(pair, carry):
        at = pl.ds(pl.multiple_of(pair * LANES, LANES), LANES)
        at_k = pl.ds(pl.multiple_of(width + pair * LANES, LANES), LANES)
        at_v = pl.ds(pl.multiple_of(2 * width + pair * LANES, LANES), LANES)
        query = two_heads(qkv_a[:rows, at] * jnp.asarray(HEAD**-0.5, BF16), low)
        keys = with_prefix(qkv_a[:, at_k], qkv_b[:, at_k], prefix_kv[:, at])
        values = with_prefix(qkv_a[:, at_v], qkv_b[:, at_v], prefix_kv[:, at_k])
        scores = nt(query, keys)
        mask = scores_bias[...]
        scores = scores + jnp.concatenate([mask, mask], 0)
        top = jnp.max(scores, -1, keepdims=True)
        weights = jnp.exp(scores - top)
        denominator = jnp.sum(weights, -1, keepdims=True)
        mixed = nn(weights.astype(BF16), values) / denominator
        attended[:, at] = join_heads(mixed, low)
        log_total = top + jnp.log(denominator)
        inside = lane < 3 * HEADS
        for i in range(2):
            here = jnp.logical_and(inside, lane % HEADS == 2 * pair + i)
            stats[...] = jnp.where(here, log_total[i * rows : (i + 1) * rows], stats[...])
        return carry

    lax.fori_loop(0, HEADS // 2, attend, 0, unroll=4)

    copies[0].wait()
    inputs = jnp.concatenate([own_0[:, :width], own_1[:, :width]], 0).astype(F32)
    middle[...] = inputs + nn(attended[...].astype(BF16), v_out[...])
    unit, _ = norm_parts(middle[...])
    normed[...] = (unit * gain[...] + bias[...]).astype(BF16)
    cot[...] = jnp.concatenate([cot_0[...], cot_1[...]], 0)
    total[...] = middle[...]
    grad_norm[...] = jnp.zeros_like(grad_norm)

    def feed(i, carry):
        for which in (0, 1):
            pltpu.make_async_copy(
                (v_fc, v_proj)[which].at[i], (v_fc, v_proj)[which].at[i], sems.at[1 + 2 * i + which]
            ).wait()
        fc, proj = v_fc[i], v_proj[i]
        pre = nn(normed[...], fc)
        grad_act = nt(cot[...], proj)
        cubic = 0.044715 * pre * pre
        curve = jnp.tanh(math.sqrt(2 / math.pi) * pre * (1.0 + cubic))
        act = 0.5 * pre * (1.0 + curve)
        slope = 0.5 * (1.0 + curve) + 0.5 * math.sqrt(2 / math.pi) * pre * (1.0 - curve * curve) * (
            1.0 + 3.0 * cubic
        )
        grad_pre = (grad_act * slope).astype(BF16)
        total[...] += nn(act.astype(BF16), proj)
        grad_norm[...] += nt(grad_pre, fc)
        return carry

    lax.fori_loop(0, steps, feed, 0, unroll=True)

    out = total[...].astype(BF16)
    back_0[:half, :width] = out[:half]
    back_1[:half, :width] = out[half:]
    unit, inverse = norm_parts(middle[...])
    grads = cot[...].astype(F32) + norm_back(unit, inverse, gain[...], grad_norm[...])
    grad_middle[...] = grads
    grad_heads = nt(grads.astype(BF16), v_out[...]).astype(BF16)
    grad_out_heads[:, :width] = grad_heads
    product = grad_heads.astype(F32) * attended[...]
    ones = jnp.where(
        jnp.logical_and(
            iota((width, LANES), 0) // HEAD == iota((width, LANES), 1) % HEADS,
            jnp.logical_and(
                iota((width, LANES), 1) >= 3 * HEADS, iota((width, LANES), 1) < 6 * HEADS
            ),
        ),
        1.0,
        0.0,
    ).astype(BF16)
    bases = jnp.zeros((rows, LANES), F32)
    for _ in range(3):
        part = product.astype(BF16)
        bases = bases + nn(part, ones)
        product = product - part.astype(F32)
    marks = three_parts(stats[...], 0) + three_parts(bases, 3 * HEADS)
    marks = marks.astype(BF16)
    grad_out_heads[:, width:] = marks
    back_0[:half, width:] = marks[:half]
    back_1[:half, width:] = marks[half:]
    back_0[half:] = jnp.zeros_like(back_0[half:])
    back_1[half:] = jnp.zeros_like(back_1[half:])
    prefix_grads(qkv_a, grad_out_heads, marks, prefix_kv, count, grad_prefix_kv)


def middle_part(count, qkv_a, qkv_b, marks_a, marks_b, prefix_kv, own, cots, gain, bias, w_out, w_fc, w_proj):
    half, width = cots[0].shape
    rows = 2 * half
    hidden = w_fc.shape[1]
    steps = 2
    step = hidden // steps
    wide = width + LANES
    return pl.pallas_call(
        partial(middle_kernel, count),
        in_specs=[vmem()] * 11 + [hbm()] * 3,
        out_specs=[vmem()] * 5,
        out_shape=[
            jax.ShapeDtypeStruct((half + tail_rows(count), wide), BF16),
            jax.ShapeDtypeStruct((half + tail_rows(count), wide), BF16),
            jax.ShapeDtypeStruct((rows, wide), BF16),
            jax.ShapeDtypeStruct((rows, width), F32),
            jax.ShapeDtypeStruct(prefix_kv.shape, BF16),
        ],
        scratch_shapes=[
            pltpu.VMEM((width, width), BF16),
            pltpu.VMEM((steps, width, step), BF16),
            pltpu.VMEM((steps, step, width), BF16),
            pltpu.SemaphoreType.DMA((1 + 2 * steps,)),
            pltpu.VMEM((rows, 4 * rows + LANES), F32),
            pltpu.VMEM((rows, width), F32),
            pltpu.VMEM((rows, LANES), F32),
            pltpu.VMEM((rows, width), F32),
            pltpu.VMEM((rows, width), BF16),
            pltpu.VMEM((rows, width), F32),
            pltpu.VMEM((rows, width), F32),
            pltpu.VMEM((rows, width), BF16),
        ],
        compiler_params=pltpu.CompilerParams(vmem_limit_bytes=36 * MIB),
        cost_estimate=pl.CostEstimate(flops=1 << 31, bytes_accessed=1000, transcendentals=0),
        name="middle",
    )(
        qkv_a, qkv_b, marks_a, marks_b, prefix_kv, *own, *cots, gain[None], bias[None], *kept_in_hbm(w_out, w_fc, w_proj)
    )


def key_grads(keys, values, queries, grads, marks, pair, low, mask):
    rows = keys.shape[0]
    scale = jnp.asarray(HEAD**-0.5, BF16)
    left = jnp.concatenate(
        [two_heads(keys * scale, low), picks(rows, pair, 0, -1.0).astype(BF16)], 1
    )
    scores = nt(left, jnp.concatenate([queries, marks], 1))
    weights = jnp.exp(scores + jnp.concatenate([mask, mask], 0))
    left = jnp.concatenate(
        [two_heads(values, low), picks(rows, pair, 3 * HEADS, -1.0).astype(BF16)], 1
    )
    slopes = weights * nt(left, jnp.concatenate([grads, marks], 1))
    key_grad = nn(slopes.astype(BF16), queries)
    value_grad = nn(weights.astype(BF16), grads)
    return join_heads(key_grad, low) * HEAD**-0.5, join_heads(value_grad, low)


def tail_rows(count):
    return -(-2 * count // PRE_ROWS) * PRE_ROWS


def prefix_grads(queries, grads, marks, prefix_kv, used, out):
    count, rows, width = prefix_kv.shape[0], grads.shape[0], grads.shape[1] - LANES
    low = head_mask(count)
    mask = jnp.where(iota((count, rows), 0) < used, 0.0, NEG)

    def step(pair, carry):
        at = pl.ds(pl.multiple_of(pair * LANES, LANES), LANES)
        at_v = pl.ds(pl.multiple_of(width + pair * LANES, LANES), LANES)
        key_grad, value_grad = key_grads(
            prefix_kv[:, at], prefix_kv[:, at_v], queries[:rows, at], grads[:, at], marks, pair, low, mask
        )
        out[:, at] = key_grad.astype(BF16)
        out[:, at_v] = value_grad.astype(BF16)
        return carry

    lax.fori_loop(0, HEADS // 2, step, 0, unroll=True)


def pack_kernel(count, own, part_0, part_1, part_2, _0, _1, back_0, back_1):
    total = own[...].astype(F32) + part_0[...].astype(F32)
    total = total + (part_1[...].astype(F32) + part_2[...].astype(F32))
    width = total.shape[1] // 2
    rows = tail_rows(count)
    tail = pad_rows(jnp.concatenate([total[:count, :width], total[:count, width:]], 0), rows).astype(BF16)
    at = pl.ds(back_0.shape[0] - rows, rows)
    back_0[at, :width] = tail
    back_1[at, :width] = tail


def pack(count, terms, back_0, back_1):
    return pl.pallas_call(
        partial(pack_kernel, count),
        in_specs=[vmem()] * 6,
        out_specs=[vmem()] * 2,
        out_shape=[jax.ShapeDtypeStruct(back_0.shape, BF16)] * 2,
        input_output_aliases={4: 0, 5: 1},
        compiler_params=pltpu.CompilerParams(vmem_limit_bytes=4 * MIB),
        cost_estimate=pl.CostEstimate(flops=1 << 20, bytes_accessed=1 << 19, transcendentals=0),
        name="pack",
    )(*terms, back_0, back_1)


def unpack_kernel(count, home_0, home_1, out):
    width = out.shape[1] // 2
    rows = tail_rows(count)
    at = pl.ds(home_0.shape[0] - rows, rows)
    first, second = home_0[at, :width].astype(F32), home_1[at, :width].astype(F32)
    total = first + second
    out[:, :width] = pad_rows(total[:count], PRE_ROWS).astype(BF16)
    out[:, width:] = pad_rows(total[count : 2 * count], PRE_ROWS).astype(BF16)


def unpack(count, width, home_0, home_1):
    return pl.pallas_call(
        partial(unpack_kernel, count),
        in_specs=[vmem()] * 2,
        out_specs=vmem(),
        out_shape=jax.ShapeDtypeStruct((PRE_ROWS, 2 * width), BF16),
        compiler_params=pltpu.CompilerParams(vmem_limit_bytes=4 * MIB),
        cost_estimate=pl.CostEstimate(flops=1000, bytes_accessed=1000, transcendentals=0),
        name="unpack",
    )(home_0, home_1)


def query_kernel(
    count,
    qkv_a,
    qkv_b,
    marks_a,
    marks_b,
    prefix_kv,
    grads,
    weight,
    order,
    out,
    scores_bias,
    grad_query,
):
    del order
    rows, width = grad_query.shape
    scores_bias[...] = key_bias(marks_a[:rows], marks_a[...], marks_b[...], rows // 2, count)
    low = head_mask(rows)
    marks = grads[:, width:]
    marks_twice = jnp.concatenate([marks, marks], 0)
    ones = jnp.ones((4 * rows + LANES, LANES), BF16)

    def step(pair, carry):
        at = pl.ds(pl.multiple_of(pair * LANES, LANES), LANES)
        at_k = pl.ds(pl.multiple_of(width + pair * LANES, LANES), LANES)
        at_v = pl.ds(pl.multiple_of(2 * width + pair * LANES, LANES), LANES)
        keys = with_prefix(qkv_a[:, at_k], qkv_b[:, at_k], prefix_kv[:, at])
        values = with_prefix(qkv_a[:, at_v], qkv_b[:, at_v], prefix_kv[:, at_k])
        query = two_heads(qkv_a[:rows, at] * jnp.asarray(HEAD**-0.5, BF16), low)
        tops = marks_twice * picks(rows, pair, 0, -1.0).astype(BF16)
        scores = nt(jnp.concatenate([query, tops], 1), jnp.concatenate([keys, ones], 1))
        mask = scores_bias[...]
        weights = jnp.exp(scores + jnp.concatenate([mask, mask], 0))
        bases = marks_twice * picks(rows, pair, 3 * HEADS, -1.0).astype(BF16)
        left = jnp.concatenate([two_heads(grads[:, at], low), bases], 1)
        slopes = weights * nt(left, jnp.concatenate([values, ones], 1))
        grad = join_heads(nn(slopes.astype(BF16), keys), low)
        grad_query[:, at] = (grad * HEAD**-0.5).astype(BF16)
        return carry

    lax.fori_loop(0, HEADS // 2, step, 0, unroll=True)
    out[...] = nt(grad_query[...], weight[:, :width])


def query_part(count, qkv_a, qkv_b, marks_a, marks_b, prefix_kv, grads, weight, order):
    rows, width = grads.shape[0], grads.shape[1] - LANES
    return pl.pallas_call(
        partial(query_kernel, count),
        in_specs=[vmem()] * 7 + [pl.BlockSpec(memory_space=pl.ANY)],
        out_specs=vmem(),
        out_shape=jax.ShapeDtypeStruct((rows, width), F32),
        scratch_shapes=[pltpu.VMEM((rows, 4 * rows + LANES), F32), pltpu.VMEM((rows, width), BF16)],
        compiler_params=pltpu.CompilerParams(vmem_limit_bytes=16 * MIB),
        cost_estimate=pl.CostEstimate(flops=1000, bytes_accessed=1000, transcendentals=0),
        name="query",
    )(qkv_a, qkv_b, marks_a, marks_b, prefix_kv, grads, weight, order)


def final_kernel(
    qkv_a,
    qkv_b,
    marks_a,
    marks_b,
    grads_0,
    grads_1,
    grads_2,
    grads_3,
    own_0,
    own_1,
    gain,
    grad_middle,
    grad_partial,
    weight,
    back_0,
    back_1,
    scores_bias,
    grad_keys,
):
    half, rows = own_0.shape[0], 2 * own_0.shape[0]
    width = grad_middle.shape[1]
    row, core, y_at = place()
    own = positions(iota((rows, 1), 0), half, row, core, y_at)
    other = all_positions((1, 8 * half), 1, half, row, core, y_at)
    same = nt(marks_a[:rows], jnp.concatenate([marks_a[...], marks_b[...]], 0))
    visible = jnp.logical_and(same > 0.5, own <= other)
    scores_bias[...] = jnp.where(visible, 0.0, NEG)
    low = head_mask(rows)
    blocks = (grads_0, grads_1, grads_2, grads_3)
    marks = jnp.concatenate([g[:, width:] for g in blocks], 0)

    def step(pair, carry):
        at = pl.ds(pl.multiple_of(pair * LANES, LANES), LANES)
        at_k = pl.ds(pl.multiple_of(width + pair * LANES, LANES), LANES)
        at_v = pl.ds(pl.multiple_of(2 * width + pair * LANES, LANES), LANES)
        queries = jnp.concatenate([qkv_a[:, at], qkv_b[:, at]], 0)
        grads = jnp.concatenate([g[:, at] for g in blocks], 0)
        key_grad, value_grad = key_grads(
            qkv_a[:rows, at_k], qkv_a[:rows, at_v], queries, grads, marks, pair, low, scores_bias[...]
        )
        grad_keys[:, at] = key_grad.astype(BF16)
        grad_keys[:, at_k] = value_grad.astype(BF16)
        return carry

    lax.fori_loop(0, HEADS // 2, step, 0, unroll=True)
    grad_norm = grad_partial[...] + nt(grad_keys[...], weight[:, width:])
    inputs = jnp.concatenate([own_0[:, :width], own_1[:, :width]], 0).astype(F32)
    unit, inverse = norm_parts(inputs)
    out = (grad_middle[...] + norm_back(unit, inverse, gain[...], grad_norm)).astype(BF16)
    back_0[...] = out[:half]
    back_1[...] = out[half:]


def final_part(qkv_a, qkv_b, marks_a, marks_b, grads, own, gain, grad_middle, grad_partial, weight):
    rows, width = grad_middle.shape
    half = rows // 2
    return pl.pallas_call(
        final_kernel,
        in_specs=[vmem()] * 14,
        out_specs=[vmem()] * 2,
        out_shape=[jax.ShapeDtypeStruct((half, width), BF16)] * 2,
        scratch_shapes=[
            pltpu.VMEM((rows, 4 * rows), F32),
            pltpu.VMEM((rows, 2 * width), BF16),
        ],
        compiler_params=pltpu.CompilerParams(vmem_limit_bytes=30 * MIB),
        cost_estimate=pl.CostEstimate(flops=1000, bytes_accessed=1000, transcendentals=0),
        name="final",
    )(qkv_a, qkv_b, marks_a, marks_b, *grads, *own, gain[None], grad_middle, grad_partial, weight)


def routes(k):
    pairs = []
    for seq in range(4):
        for blk in range(8):
            group, z_at, y_at = seq % 2, blk // 2, blk % 2
            row = (z_at + k) % 2
            pairs.append((seq * 8 + blk, (seq - group + z_at // 2) * 8 + (2 * group + row) * 2 + y_at))
    return pairs


def body_rows(
    tokens,
    segment_ids,
    ln1_gain,
    ln1_bias,
    w_qkv,
    w_out,
    ln2_gain,
    ln2_bias,
    w_fc,
    w_proj,
    prefix_embed,
    w_mlp1,
    b_mlp1,
    w_mlp2,
    b_mlp2,
    cotangent,
):
    half, _, width = tokens.shape
    everyone = ("seq", "blk")
    there = [routes(k) for k in range(2)]
    back = [[(b, a) for a, b in pairs] for pairs in there]
    swap_core = [(i, i ^ 1) for i in range(4)]
    swap_y = [(i, i ^ 1) for i in range(8)]
    swap_both = [(i, i ^ 9) for i in range(32)]
    def after(value, *done):
        return lax.optimization_barrier((value, done))[0]

    out_msgs = split_rows(tokens, segment_ids)
    cot_msgs = split_rows(cotangent)
    own = [lax.ppermute(m, everyone, there[k]) for k, m in enumerate(out_msgs)]
    prefix_kv, inner, w_near, near_embed, turned = adapter_forward(
        prefix_embed, w_mlp1, b_mlp1, w_mlp2, b_mlp2, w_qkv
    )
    count = prefix_embed.shape[0]
    own = after(own, inner)
    across = [lax.ppermute(m, "blk", swap_y) for m in own]
    beside = [lax.ppermute(m, "seq", swap_core) for m in own]
    cots = [lax.ppermute(m, everyone, there[k]) for k, m in enumerate(after(cot_msgs, beside))]
    beyond = [lax.ppermute(m, "seq", swap_core) for m in across]

    qkv_a, marks_a = project(own + beside, ln1_gain, ln1_bias, w_near)
    qkv_b, marks_b = project(across + beyond, ln1_gain, ln1_bias, w_near)
    back_0, back_1, grads, grad_middle, grad_prefix_kv = middle_part(
        count, qkv_a, qkv_b, marks_a, marks_b, prefix_kv, own, cots, ln2_gain, ln2_bias, w_out, w_fc, w_proj
    )
    grads_y = lax.ppermute(grads, "blk", swap_y)
    grads_c = lax.ppermute(grads, "seq", swap_core)
    parts = [lax.ppermute(grad_prefix_kv, "seq", [(i, i ^ far) for i in range(4)]) for far in (2, 1, 3)]
    packed = pack(count, (grad_prefix_kv, *parts), back_0, back_1)
    home = [lax.ppermute(m, everyone, back[k]) for k, m in enumerate(packed)]
    grad_partial = query_part(
        count, qkv_a, qkv_b, marks_a, marks_b, prefix_kv, grads, w_near, packed[0]
    )
    grads_yc = lax.ppermute(after(grads_y, grad_partial), "seq", swap_core)
    final_0, final_1 = final_part(
        qkv_a,
        qkv_b,
        marks_a,
        marks_b,
        (grads, grads_c, grads_y, grads_yc),
        own,
        ln1_gain,
        grad_middle,
        grad_partial,
        w_near,
    )
    finals = [lax.ppermute(m, everyone, back[k]) for k, m in enumerate((final_0, final_1))]
    gathered = [unpack(count, width, *home)]
    gathered += [lax.ppermute(gathered[0], "seq", swap_core), lax.ppermute(gathered[0], "blk", swap_y)]
    gathered += [lax.ppermute(gathered[0], everyone, swap_both)]
    summed = adapter_backward(gathered, near_embed, inner, turned, finals[0])

    block_out, log_total = land(after(home, final_0), half, width, BF16, True)
    (input_grad,) = land(finals, half, width, F32, False)
    return (block_out, input_grad, summed[0], summed[1], summed[2], summed[3], summed[4], log_total)


def solution(mesh):
    four_by_eight = mesh.shape["seq"] == 4 and mesh.shape["blk"] == 8
    placed = (
        P("blk", "seq", None),
        P("blk", "seq"),
        P(),
        P(),
        P(),
        P(),
        P(),
        P(),
        P(),
        P(),
        P(),
        P(),
        P(),
        P(),
        P(),
        P("blk", "seq", None),
    )
    return jax.shard_map(
        body_rows if four_by_eight else body_plain,
        mesh=mesh,
        in_specs=placed,
        out_specs=(
            P("blk", "seq", None),
            P("blk", "seq", None),
            P(),
            P(),
            P(),
            P(),
            P(),
            P("seq", None, "blk"),
        ),
        check_vma=False,
    )
```

```python
from functools import partial
import math

import jax
import jax.numpy as jnp
from jax import lax
from jax.experimental import pallas as pl
from jax.experimental.pallas import tpu as pltpu
from jax.sharding import PartitionSpec as P

HEADS = 16
HEAD = 64


EPS = 1e-05
NEG = -1e30
HIGH = lax.Precision.HIGHEST


def layer_norm(value_in, gain, bias):
    average = jnp.mean(value_in, axis=-1, keepdims=True)
    centered = value_in - average
    variance = jnp.mean(centered * centered, axis=-1, keepdims=True)
    return centered * lax.rsqrt(variance + EPS) * gain + bias


def adapter(prefix_embed, w_mlp1, b_mlp1, w_mlp2, b_mlp2):
    inner_act = jnp.tanh(jnp.dot(prefix_embed, w_mlp1, precision=HIGH) + b_mlp1)
    return jnp.dot(inner_act, w_mlp2, precision=HIGH) + b_mlp2


def gelu_tanh(pre_act):
    return jax.nn.gelu(pre_act, approximate=True)


def split_heads(block_in):
    return block_in.reshape(block_in.shape[0], block_in.shape[1], HEADS, HEAD)


def allowed(query_pos, query_seg, key_pos, key_seg):
    same_seg = query_seg.T[:, :, None] == key_seg.T[:, None, :]
    causal = key_pos[None, None, :] <= query_pos[None, :, None]
    return jnp.logical_and(same_seg, causal)[:, None]


def scores_of(query_heads, key_block, score_scale):
    return score_scale * jnp.einsum(
        "prhd,krhd->rhpk", query_heads, split_heads(key_block), preferred_element_type=jnp.float32
    )


def block_grads(
    query_heads,
    grad_heads,
    log_total,
    slope_base,
    query_pos,
    query_seg,
    key_block,
    value_block,
    key_pos,
    key_seg,
    score_scale,
):
    scores = scores_of(query_heads, key_block, score_scale)
    scores = jnp.where(allowed(query_pos, query_seg, key_pos, key_seg), scores, NEG)
    weights = jnp.exp(scores - log_total[..., None])
    grad_weights = jnp.einsum(
        "prhd,krhd->rhpk", grad_heads, split_heads(value_block), preferred_element_type=jnp.float32
    )
    slopes = (weights * (grad_weights - slope_base[..., None])).astype(jnp.bfloat16)
    return (weights.astype(jnp.bfloat16), slopes)


def body_plain(
    tokens,
    segment_ids,
    ln1_gain,
    ln1_bias,
    w_qkv,
    w_out,
    ln2_gain,
    ln2_bias,
    w_fc,
    w_proj,
    prefix_embed,
    w_mlp1,
    b_mlp1,
    w_mlp2,
    b_mlp2,
    cotangent,
):
    pos_dev, row_count, width = tokens.shape
    score_scale = HEAD ** (-0.5)
    flat_rows = pos_dev * row_count
    own_pos = lax.axis_index("blk") * pos_dev + jnp.arange(pos_dev)
    inputs = tokens.astype(jnp.float32).reshape(flat_rows, width)
    normed_one = layer_norm(inputs, ln1_gain, ln1_bias).astype(jnp.bfloat16)
    projected = jnp.dot(normed_one, w_qkv, preferred_element_type=jnp.float32).astype(jnp.bfloat16)
    queries = projected[:, :width].reshape(pos_dev, row_count, width)
    keys = projected[:, width : 2 * width].reshape(pos_dev, row_count, width)
    values = projected[:, 2 * width :].reshape(pos_dev, row_count, width)
    query_heads = split_heads(queries)
    prefix_low = adapter(prefix_embed, w_mlp1, b_mlp1, w_mlp2, b_mlp2).astype(jnp.bfloat16)
    prefix_keys = prefix_low[:, :width].reshape(-1, HEADS, HEAD)
    prefix_values = prefix_low[:, width:].reshape(-1, HEADS, HEAD)
    prefix_scores = score_scale * jnp.einsum(
        "prhd,jhd->rhpj", query_heads, prefix_keys, preferred_element_type=jnp.float32
    )
    start_top = jnp.max(prefix_scores, -1)
    start_weights = jnp.exp(prefix_scores - start_top[..., None])
    start_denom = jnp.sum(start_weights, -1)
    start_numer = jnp.einsum(
        "rhpj,jhd->rhpd",
        start_weights.astype(jnp.bfloat16),
        prefix_values,
        preferred_element_type=jnp.float32,
    )
    start_state = (start_top, start_denom, start_numer)
    running = start_state
    key_shards = lax.all_gather(keys, "blk", axis=0, tiled=True)
    value_shards = lax.all_gather(values, "blk", axis=0, tiled=True)
    seg_shards = lax.all_gather(segment_ids, "blk", axis=0, tiled=True)
    num_rows = key_shards.shape[0]
    forward_stride = math.gcd(num_rows, 512)

    def inner(state, block_index):
        running_top, denominator, numerator = state
        offset = block_index * forward_stride
        key_block = lax.dynamic_slice_in_dim(key_shards, offset, forward_stride, 0)
        value_block = lax.dynamic_slice_in_dim(value_shards, offset, forward_stride, 0)
        seg_block = lax.dynamic_slice_in_dim(seg_shards, offset, forward_stride, 0)
        key_pos = offset + jnp.arange(forward_stride)
        scores = jnp.where(
            allowed(own_pos, segment_ids, key_pos, seg_block),
            scores_of(query_heads, key_block, score_scale),
            NEG,
        )
        new_top = jnp.maximum(running_top, jnp.max(scores, -1))
        fading = jnp.exp(running_top - new_top)
        weights = jnp.exp(scores - new_top[..., None])
        denominator = denominator * fading + jnp.sum(weights, -1)
        numerator = numerator * fading[..., None] + jnp.einsum(
            "rhpk,krhd->rhpd",
            weights.astype(jnp.bfloat16),
            split_heads(value_block),
            preferred_element_type=jnp.float32,
        )
        return ((new_top, denominator, numerator), None)

    running, _ = lax.scan(inner, running, jnp.arange(num_rows // forward_stride))
    final_top, final_denom, final_numer = running
    log_total = final_top + jnp.log(final_denom)
    attended = final_numer / final_denom[..., None]
    attended_rows = jnp.transpose(attended, (2, 0, 1, 3)).reshape(flat_rows, width)
    middle = inputs + jnp.dot(
        attended_rows.astype(jnp.bfloat16), w_out, preferred_element_type=jnp.float32
    )
    normed_two = layer_norm(middle, ln2_gain, ln2_bias).astype(jnp.bfloat16)
    hidden_pre = jnp.dot(normed_two, w_fc, preferred_element_type=jnp.float32)
    hidden_act = gelu_tanh(hidden_pre).astype(jnp.bfloat16)
    outputs = middle + jnp.dot(hidden_act, w_proj, preferred_element_type=jnp.float32)
    block_out = outputs.astype(jnp.bfloat16).reshape(pos_dev, row_count, width)
    grad_out = cotangent.reshape(flat_rows, width)
    grad_act = jnp.dot(grad_out, w_proj.T, preferred_element_type=jnp.float32)
    _, gelu_back = jax.vjp(gelu_tanh, hidden_pre)
    grad_pre = gelu_back(grad_act)[0].astype(jnp.bfloat16)
    grad_norm_two = jnp.dot(grad_pre, w_fc.T, preferred_element_type=jnp.float32)
    _, norm_two_back = jax.vjp(partial(layer_norm, gain=ln2_gain, bias=ln2_bias), middle)
    grad_middle = grad_out.astype(jnp.float32) + norm_two_back(grad_norm_two)[0]
    grad_attended = jnp.dot(
        grad_middle.astype(jnp.bfloat16), w_out.T, preferred_element_type=jnp.float32
    ).astype(jnp.bfloat16)
    grad_flat = grad_attended.reshape(pos_dev, row_count, width)
    grad_heads = split_heads(grad_flat)
    slope_base = jnp.sum(jnp.transpose(grad_heads.astype(jnp.float32), (1, 2, 0, 3)) * attended, -1)
    prefix_weights = jnp.exp(prefix_scores - log_total[..., None])
    prefix_dw = jnp.einsum(
        "prhd,jhd->rhpj", grad_heads, prefix_values, preferred_element_type=jnp.float32
    )
    prefix_slopes = (prefix_weights * (prefix_dw - slope_base[..., None])).astype(jnp.bfloat16)
    grad_query = score_scale * jnp.einsum(
        "rhpj,jhd->prhd", prefix_slopes, prefix_keys, preferred_element_type=jnp.float32
    )
    grad_pkeys = score_scale * jnp.einsum(
        "rhpj,prhd->jhd", prefix_slopes, query_heads, preferred_element_type=jnp.float32
    )
    grad_pvalues = jnp.einsum(
        "rhpj,prhd->jhd",
        prefix_weights.astype(jnp.bfloat16),
        grad_heads,
        preferred_element_type=jnp.float32,
    )
    grad_prefix_kv = jnp.concatenate(
        [grad_pkeys.reshape(-1, width), grad_pvalues.reshape(-1, width)], -1
    )
    keys_all, values_all, segs_all = (
        lax.all_gather(keys, "blk", axis=0, tiled=True),
        lax.all_gather(values, "blk", axis=0, tiled=True),
        lax.all_gather(segment_ids, "blk", axis=0, tiled=True),
    )
    length = keys_all.shape[0]
    stride = math.gcd(length, 512)

    def backward_step(grad_q, block_index):
        offset = block_index * stride
        key_block = lax.dynamic_slice_in_dim(keys_all, offset, stride, 0)
        value_block = lax.dynamic_slice_in_dim(values_all, offset, stride, 0)
        seg_block = lax.dynamic_slice_in_dim(segs_all, offset, stride, 0)
        key_pos = offset + jnp.arange(stride)
        weights_low, slopes = block_grads(
            query_heads,
            grad_heads,
            log_total,
            slope_base,
            own_pos,
            segment_ids,
            key_block,
            value_block,
            key_pos,
            seg_block,
            score_scale,
        )
        grad_q = grad_q + score_scale * jnp.einsum(
            "rhpk,krhd->prhd", slopes, split_heads(key_block), preferred_element_type=jnp.float32
        )
        key_term = score_scale * jnp.einsum(
            "rhpk,prhd->krhd", slopes, query_heads, preferred_element_type=jnp.float32
        )
        value_term = jnp.einsum(
            "rhpk,prhd->krhd", weights_low, grad_heads, preferred_element_type=jnp.float32
        )
        return (
            grad_q,
            (
                key_term.reshape(stride, row_count, width),
                value_term.reshape(stride, row_count, width),
            ),
        )

    grad_query, (key_terms, value_terms) = lax.scan(
        backward_step, grad_query, jnp.arange(length // stride)
    )
    key_terms = key_terms.reshape(length, row_count, width)
    value_terms = value_terms.reshape(length, row_count, width)
    grad_keys, grad_values = (
        lax.psum_scatter(key_terms, "blk", scatter_dimension=0, tiled=True),
        lax.psum_scatter(value_terms, "blk", scatter_dimension=0, tiled=True),
    )
    grad_proj = jnp.concatenate(
        [
            grad_query.reshape(flat_rows, width).astype(jnp.bfloat16),
            grad_keys.reshape(flat_rows, width).astype(jnp.bfloat16),
            grad_values.reshape(flat_rows, width).astype(jnp.bfloat16),
        ],
        -1,
    )
    grad_norm_one = jnp.dot(grad_proj, w_qkv.T, preferred_element_type=jnp.float32)
    _, norm_one_back = jax.vjp(partial(layer_norm, gain=ln1_gain, bias=ln1_bias), inputs)
    input_grad = (grad_middle + norm_one_back(grad_norm_one)[0]).reshape(pos_dev, row_count, width)
    _, adapter_back = jax.vjp(adapter, prefix_embed, w_mlp1, b_mlp1, w_mlp2, b_mlp2)
    local_grads = adapter_back(grad_prefix_kv)
    summed = lax.psum(
        (local_grads[0], local_grads[1], local_grads[2], local_grads[3], local_grads[4]),
        ("seq", "blk"),
    )
    return (block_out, input_grad, summed[0], summed[1], summed[2], summed[3], summed[4], log_total)


F32 = jnp.float32
BF16 = jnp.bfloat16
LANES = 128
PRE_ROWS = 16
MIB = 1 << 20


def nn(left, right):
    return jnp.dot(left, right, preferred_element_type=F32)


def nt(left, right):
    return lax.dot_general(left, right, (((1,), (1,)), ((), ())), preferred_element_type=F32)


def norm_parts(value_in):
    average = jnp.mean(value_in, axis=-1, keepdims=True)
    centered = value_in - average
    variance = jnp.mean(centered * centered, axis=-1, keepdims=True)
    inverse = lax.rsqrt(variance + EPS)
    return centered * inverse, inverse


def norm_back(unit, inverse, gain, grad):
    scaled = grad * gain
    first = jnp.mean(scaled, axis=-1, keepdims=True)
    second = jnp.mean(scaled * unit, axis=-1, keepdims=True)
    return inverse * (scaled - first - unit * second)


def iota(shape, dim):
    return lax.broadcasted_iota(jnp.int32, shape, dim)


def place():
    blk = lax.axis_index("blk")
    return (blk // 2) % 2, lax.axis_index("seq") % 2, blk % 2


def positions(index, half, row, core, y_at):
    upper = (index >= half).astype(jnp.int32)
    slot = upper + row - 2 * upper * row
    block = (2 * core + slot) * 2 + y_at
    return block * half + index - upper * half


def members(core, y_at):
    return ((core, y_at), (1 - core, y_at), (core, 1 - y_at), (1 - core, 1 - y_at))


def all_positions(shape, dim, half, row, core, y_at):
    part = tuple(2 * half if d == dim else n for d, n in enumerate(shape))
    return jnp.concatenate(
        [positions(iota(part, dim), half, row, c, y) for c, y in members(core, y_at)], dim
    )


def vmem():
    return pl.BlockSpec(memory_space=pltpu.VMEM)


def hbm():
    return pl.BlockSpec(memory_space=pltpu.HBM)


def kept_in_hbm(*arrays):
    return [pltpu.with_memory_space_constraint(a, pltpu.HBM) for a in arrays]


def by_tiles(block):
    half, pair, width = block.shape
    tiles = jnp.transpose(block.reshape(half, pair, width // LANES, LANES), (0, 2, 1, 3))
    return tiles.reshape(half, pair * width // LANES, LANES)


def from_tiles(tiles, width):
    half, count, _ = tiles.shape
    pair = count * LANES // width
    block = jnp.transpose(tiles.reshape(half, width // LANES, pair, LANES), (0, 2, 1, 3))
    return block.reshape(half, pair, width)


def odd_place():
    return (lax.axis_index("blk") // 2) % 2 == 1


def split_kernel(marked, *refs):
    tokens, ids, (out_0, out_1, work) = refs[0], refs[1], refs[-3:]
    half, count, _ = tokens.shape
    odd = odd_place()
    work[...] = tokens[...].astype(F32).reshape(half * count, LANES)
    for i in range(count // 2):
        at = pl.ds(i * LANES, LANES)
        first, second = (work[pl.ds(2 * i + r, half, stride=count)] for r in range(2))
        out_0[:, at] = jnp.where(odd, second, first).astype(BF16)
        out_1[:, at] = jnp.where(odd, first, second).astype(BF16)
    if marked:
        width = count // 2 * LANES
        first, second = (
            jnp.where(iota((LANES, half), 0) == ids[r : r + 1], 1.0, 0.0).T for r in range(2)
        )
        out_0[:, width:] = jnp.where(odd, second, first).astype(BF16)
        out_1[:, width:] = jnp.where(odd, first, second).astype(BF16)


def split_rows(block, segment_ids=None):
    tiles = by_tiles(block)
    half, count, _ = tiles.shape
    extra = () if segment_ids is None else kept_in_hbm(segment_ids.T)
    width = count // 2 * LANES + LANES * len(extra)
    return pl.pallas_call(
        partial(split_kernel, bool(extra)),
        in_specs=[vmem()] * (1 + len(extra)),
        out_specs=[vmem()] * 2,
        out_shape=[jax.ShapeDtypeStruct((half, width), BF16)] * 2,
        scratch_shapes=[pltpu.VMEM((half * count, LANES), F32)],
        compiler_params=pltpu.CompilerParams(vmem_limit_bytes=4 * MIB),
        cost_estimate=pl.CostEstimate(flops=1 << 20, bytes_accessed=1 << 19, transcendentals=0),
        name="split",
    )(*kept_in_hbm(tiles), *extra)


def place_rows(msg_0, msg_1, work):
    width = msg_0.shape[1] // LANES * LANES
    count = 2 * (width // LANES)
    half = work.shape[0] // count
    odd = odd_place()
    for i in range(count // 2):
        at = pl.ds(i * LANES, LANES)
        one, two = msg_0[:half, at].astype(F32), msg_1[:half, at].astype(F32)
        work[pl.ds(2 * i, half, stride=count)] = jnp.where(odd, two, one)
        work[pl.ds(2 * i + 1, half, stride=count)] = jnp.where(odd, one, two)


def land_kernel(msg_0, msg_1, out, logs, work):
    half, count, _ = out.shape
    heads, width = logs.shape[1], count // 2 * LANES
    place_rows(msg_0.at[:, pl.ds(0, width)], msg_1.at[:, pl.ds(0, width)], work)
    out[...] = work[...].reshape(out.shape).astype(out.dtype)
    odd = odd_place()
    one, two = (m[:half, width:].astype(F32) for m in (msg_0, msg_1))
    for r, chosen in enumerate((jnp.where(odd, two, one), jnp.where(odd, one, two))):
        summed = chosen + jnp.roll(chosen, -heads, 1) + jnp.roll(chosen, -2 * heads, 1)
        logs[r] = summed.T[:heads]


def land(messages, half, width):
    count = 2 * width // LANES
    out = pl.pallas_call(
        land_kernel,
        in_specs=[vmem()] * 2,
        out_specs=[vmem()] * 2,
        out_shape=[
            jax.ShapeDtypeStruct((half, count, LANES), BF16),
            jax.ShapeDtypeStruct((2, HEADS, half), F32),
        ],
        scratch_shapes=[pltpu.VMEM((half * count, LANES), F32)],
        compiler_params=pltpu.CompilerParams(vmem_limit_bytes=4 * MIB),
        cost_estimate=pl.CostEstimate(flops=1000, bytes_accessed=1000, transcendentals=0),
        name="land",
    )(*messages)
    return from_tiles(out[0], width), out[1]


def project_kernel(count, *refs):
    messages, (gain, bias, weight, out, marks, normed) = refs[:count], refs[count:]
    half, width = messages[0].shape[0], normed.shape[1]
    for i, message in enumerate(messages):
        rows = pl.ds(i * half, half)
        unit, _ = norm_parts(message[:, :width].astype(F32))
        normed[rows] = (unit * gain[...] + bias[...]).astype(BF16)
        marks[rows] = message[:, width:]
    for i in range(3):
        at = pl.ds(i * width, width)
        out[:, at] = nn(normed[...], weight[:, at]).astype(BF16)


def project(messages, gain, bias, weight):
    count, half = len(messages), messages[0].shape[0]
    width, columns = weight.shape
    rows = count * half
    return pl.pallas_call(
        partial(project_kernel, count),
        in_specs=[vmem()] * (count + 3),
        out_specs=[vmem()] * 2,
        out_shape=[
            jax.ShapeDtypeStruct((rows, columns), BF16),
            jax.ShapeDtypeStruct((rows, LANES), BF16),
        ],
        scratch_shapes=[pltpu.VMEM((rows, width), BF16)],
        compiler_params=pltpu.CompilerParams(vmem_limit_bytes=16 * MIB),
        cost_estimate=pl.CostEstimate(
            flops=2 * rows * width * columns, bytes_accessed=2 * width * columns, transcendentals=0
        ),
        name="project",
    )(*messages, gain[None], bias[None], weight)


def halves(value_in):
    high = value_in.astype(BF16)
    return high, (value_in - high.astype(F32)).astype(BF16)


def pad_rows(value_in, rows):
    return jnp.concatenate(
        [value_in, jnp.zeros((rows - value_in.shape[0], value_in.shape[1]), value_in.dtype)], 0
    )


def three_products(product, left, weight):
    rows = left.shape[0]
    high, low = halves(left)
    w_high, w_low = halves(weight)
    both = product(jnp.concatenate([high, low], 0), w_high)
    return both[:rows] + both[rows:] + product(high, w_low)


def adapter_kernel(
    h_embed,
    w_mlp1,
    h_mlp1,
    w_mlp2,
    h_mlp2,
    w_qkv,
    out,
    inner,
    v_qkv,
    embed,
    turned,
    v_mlp1,
    v_mlp2,
    b_mlp1,
    b_mlp2,
    sems,
):
    steps, step = v_mlp2.shape[0], v_mlp2.shape[2]
    small = []
    for i, (source, target) in enumerate(
        ((h_embed, embed), (h_mlp1, b_mlp1), (h_mlp2, b_mlp2), (w_mlp1, v_mlp1))
    ):
        small.append(pltpu.make_async_copy(source, target, sems.at[steps + i]))
        small[-1].start()
    rest = []
    for i in range(steps):
        copy = pltpu.make_async_copy(w_mlp2.at[:, pl.ds(i * step, step)], v_mlp2.at[i], sems.at[i])
        copy.start()
        rest.append(copy)
    weights = pltpu.make_async_copy(w_qkv, v_qkv, sems.at[steps + len(small)])
    weights.start()
    for copy in small:
        copy.wait()
    source = pad_rows(embed[...], PRE_ROWS)
    act = jnp.tanh(three_products(nn, source, v_mlp1[...]) + b_mlp1[...])
    inner[...] = act
    columns, hidden = steps * step, v_mlp1.shape[1]
    for i in range(v_mlp1.shape[0] // hidden):
        part = v_mlp1[pl.ds(i * hidden, hidden)].astype(BF16)
        turned[pl.ds(columns + i * hidden, hidden)] = part.T
    for i, copy in enumerate(rest):
        copy.wait()
        turned[pl.ds(i * step, step)] = v_mlp2[i].astype(BF16).T
        span = pl.ds(i * step, step)
        part = three_products(nn, act, v_mlp2[i]) + b_mlp2[:, span]
        out[:, span] = jnp.where(iota(part.shape, 0) < embed.shape[0], part, 0.0).astype(BF16)
    weights.wait()


def adapter_forward(embed, w_mlp1, b_mlp1, w_mlp2, b_mlp2, w_qkv):
    width, hidden = w_mlp1.shape
    columns = w_mlp2.shape[1]
    steps = 4
    return pl.pallas_call(
        adapter_kernel,
        in_specs=[hbm()] * 6,
        out_specs=[vmem()] * 5,
        out_shape=[
            jax.ShapeDtypeStruct((PRE_ROWS, columns), BF16),
            jax.ShapeDtypeStruct((PRE_ROWS, hidden), F32),
            pltpu.VMEM(w_qkv.shape, w_qkv.dtype),
            pltpu.VMEM(embed.shape, F32),
            pltpu.VMEM((columns + width, hidden), BF16),
        ],
        scratch_shapes=[
            pltpu.VMEM((width, hidden), F32),
            pltpu.VMEM((steps, hidden, columns // steps), F32),
            pltpu.VMEM((1, hidden), F32),
            pltpu.VMEM((1, columns), F32),
            pltpu.SemaphoreType.DMA((5 + steps,)),
        ],
        compiler_params=pltpu.CompilerParams(vmem_limit_bytes=20 * MIB),
        cost_estimate=pl.CostEstimate(flops=1 << 32, bytes_accessed=6 * MIB, transcendentals=1 << 13),
        name="adapter",
    )(*kept_in_hbm(embed, w_mlp1, b_mlp1[None], w_mlp2, b_mlp2[None], w_qkv))


def outer(left, right):
    l_high, l_low = halves(left)
    r_high, r_low = halves(right)
    return lax.dot_general(
        jnp.concatenate([l_high, l_high, l_low], 0),
        jnp.concatenate([r_high, r_low, r_high], 0),
        (((0,), (0,)), ((), ())),
        preferred_element_type=F32,
    )


def two_products(left, weight):
    high, low = halves(left)
    both = nn(jnp.concatenate([high, low], 0), weight)
    return both[: left.shape[0]] + both[left.shape[0] :]


def adapter_back_kernel(
    home_0,
    home_1,
    part_0,
    part_1,
    part_2,
    part_3,
    embed,
    inner,
    turned,
    block,
    grad_prefix,
    grad_mlp1,
    grad_bias1,
    grad_mlp2,
    grad_bias2,
    o_block,
    o_mlp1,
    o_mlp2,
    sems,
):
    steps, step = o_mlp2.shape[0], o_mlp2.shape[2]
    first, second, third, fourth = (p[...].astype(F32) for p in (part_0, part_1, part_2, part_3))
    grads = (first + second) + (third + fourth)
    act = inner[...]
    stores = []
    grad_bias2[...] = jnp.sum(grads, 0, keepdims=True)
    for i in range(steps):
        o_mlp2[i] = outer(act, grads[:, i * step : (i + 1) * step])
        stores.append(
            pltpu.make_async_copy(o_mlp2.at[i], grad_mlp2.at[:, pl.ds(i * step, step)], sems.at[i])
        )
        stores[-1].start()
    columns, (width, hidden) = steps * step, o_mlp1.shape
    place_rows(home_0, home_1, o_block)
    stores.append(pltpu.make_async_copy(o_block, block, sems.at[steps + 1]))
    stores[-1].start()
    back = two_products(grads, turned[:columns]) * (1.0 - act * act)
    grad_bias1[...] = jnp.sum(back, 0, keepdims=True)
    o_mlp1[...] = outer(pad_rows(embed[...], PRE_ROWS), back)
    stores.append(pltpu.make_async_copy(o_mlp1, grad_mlp1, sems.at[steps]))
    stores[-1].start()
    for i in range(width // hidden):
        part = two_products(back, turned[pl.ds(columns + i * hidden, hidden)])
        grad_prefix[:, pl.ds(i * hidden, hidden)] = part[: embed.shape[0]]
    for copy in stores:
        copy.wait()


def finish(finals, parts, embed, inner, turned):
    hidden, width = turned.shape[1], embed.shape[1]
    columns = turned.shape[0] - width
    half = finals[0].shape[0]
    steps = 4
    tiles = 2 * width // LANES
    out = pl.pallas_call(
        adapter_back_kernel,
        in_specs=[vmem()] * 9,
        out_specs=[hbm(), vmem(), hbm(), vmem(), hbm(), vmem()],
        out_shape=[
            jax.ShapeDtypeStruct((half * tiles, LANES), F32),
            jax.ShapeDtypeStruct(embed.shape, F32),
            jax.ShapeDtypeStruct((width, hidden), F32),
            jax.ShapeDtypeStruct((1, hidden), F32),
            jax.ShapeDtypeStruct((hidden, columns), F32),
            jax.ShapeDtypeStruct((1, columns), F32),
        ],
        scratch_shapes=[
            pltpu.VMEM((half * tiles, LANES), F32),
            pltpu.VMEM((width, hidden), F32),
            pltpu.VMEM((steps, hidden, columns // steps), F32),
            pltpu.SemaphoreType.DMA((steps + 2,)),
        ],
        compiler_params=pltpu.CompilerParams(vmem_limit_bytes=16 * MIB),
        cost_estimate=pl.CostEstimate(flops=1000, bytes_accessed=1000, transcendentals=0),
        name="finish",
    )(*finals, *parts, embed, inner, turned)
    block = from_tiles(out[0].reshape(half, tiles, LANES), width)
    return block, (out[1], out[2], out[3][0], out[4], out[5][0])


def head_mask(rows):
    return iota((rows, LANES), 1) < HEAD


def two_heads(pair, low):
    zero = jnp.zeros_like(pair)
    return jnp.concatenate([jnp.where(low, pair, zero), jnp.where(low, zero, pair)], 0)


def join_heads(stacked, low):
    rows = stacked.shape[0] // 2
    return jnp.where(low, stacked[:rows], stacked[rows:])


def picks(rows, pair, first, value):
    lane = iota((rows, LANES), 1)
    inside = jnp.logical_and(lane >= first, lane < first + 3 * HEADS)
    parts = [
        jnp.where(jnp.logical_and(inside, lane % HEADS == 2 * pair + i), value, 0.0) for i in range(2)
    ]
    return jnp.concatenate(parts, 0)


def three_parts(value_in, first):
    lane = iota(value_in.shape, 1)
    high = value_in.astype(BF16).astype(F32)
    rest = value_in - high
    middle = rest.astype(BF16).astype(F32)
    low = rest - middle
    part = (lane - first) // HEADS
    chosen = jnp.where(part == 0, high, jnp.where(part == 1, middle, low))
    inside = jnp.logical_and(lane >= first, lane < first + 3 * HEADS)
    return jnp.where(inside, chosen, 0.0)


def key_bias(marks_own, marks_a, marks_b, half, count):
    row, core, y_at = place()
    rows = 2 * half
    own = positions(iota((rows, 1), 0), half, row, core, y_at)
    other = all_positions((1, 8 * half), 1, half, row, core, y_at)
    same = nt(marks_own, jnp.concatenate([marks_a, marks_b], 0))
    visible = jnp.logical_and(same > 0.5, other <= own)
    token_bias = jnp.where(visible, 0.0, NEG)
    prefix_bias = jnp.where(iota((rows, LANES), 1) < count, 0.0, NEG)
    return jnp.concatenate([token_bias, prefix_bias], 1)


def with_prefix(part_a, part_b, prefix):
    pad = jnp.zeros((LANES - prefix.shape[0], prefix.shape[1]), prefix.dtype)
    return jnp.concatenate([part_a, part_b, prefix, pad], 0)


def middle_kernel(
    count,
    qkv_a,
    qkv_b,
    marks_a,
    marks_b,
    prefix_kv,
    own_0,
    own_1,
    cot_0,
    cot_1,
    gain,
    bias,
    w_out,
    w_fc,
    w_proj,
    back_0,
    back_1,
    grad_out_heads,
    grad_middle,
    v_out,
    v_fc,
    v_proj,
    sems,
    scores_bias,
    attended,
    stats,
    middle,
    normed,
    total,
    grad_norm,
    cot,
):
    half, rows = own_0.shape[0], 2 * own_0.shape[0]
    width = middle.shape[1]
    steps, step = v_fc.shape[0], v_fc.shape[2]
    copies = [pltpu.make_async_copy(w_out, v_out, sems.at[0])]
    for i in range(steps):
        span = pl.ds(i * step, step)
        copies.append(pltpu.make_async_copy(w_fc.at[:, span], v_fc.at[i], sems.at[1 + 2 * i]))
        copies.append(pltpu.make_async_copy(w_proj.at[span], v_proj.at[i], sems.at[2 + 2 * i]))
    for copy in copies:
        copy.start()

    scores_bias[...] = key_bias(marks_a[:rows], marks_a[...], marks_b[...], half, count)
    low = head_mask(rows)
    lane = iota((rows, LANES), 1)
    stats[...] = jnp.zeros_like(stats)

    def attend(pair, carry):
        at = pl.ds(pl.multiple_of(pair * LANES, LANES), LANES)
        at_k = pl.ds(pl.multiple_of(width + pair * LANES, LANES), LANES)
        at_v = pl.ds(pl.multiple_of(2 * width + pair * LANES, LANES), LANES)
        query = two_heads(qkv_a[:rows, at] * jnp.asarray(HEAD**-0.5, BF16), low)
        keys = with_prefix(qkv_a[:, at_k], qkv_b[:, at_k], prefix_kv[:, at])
        values = with_prefix(qkv_a[:, at_v], qkv_b[:, at_v], prefix_kv[:, at_k])
        scores = nt(query, keys)
        mask = scores_bias[...]
        scores = scores + jnp.concatenate([mask, mask], 0)
        top = jnp.max(scores, -1, keepdims=True)
        weights = jnp.exp(scores - top)
        denominator = jnp.sum(weights, -1, keepdims=True)
        mixed = nn(weights.astype(BF16), values) / denominator
        attended[:, at] = join_heads(mixed, low)
        log_total = top + jnp.log(denominator)
        inside = lane < 3 * HEADS
        for i in range(2):
            here = jnp.logical_and(inside, lane % HEADS == 2 * pair + i)
            stats[...] = jnp.where(here, log_total[i * rows : (i + 1) * rows], stats[...])
        return carry

    lax.fori_loop(0, HEADS // 2, attend, 0, unroll=4)

    copies[0].wait()
    inputs = jnp.concatenate([own_0[:, :width], own_1[:, :width]], 0).astype(F32)
    middle[...] = inputs + nn(attended[...].astype(BF16), v_out[...])
    unit, _ = norm_parts(middle[...])
    normed[...] = (unit * gain[...] + bias[...]).astype(BF16)
    cot[...] = jnp.concatenate([cot_0[...], cot_1[...]], 0)
    total[...] = middle[...]
    grad_norm[...] = jnp.zeros_like(grad_norm)

    def feed(i, carry):
        for which in (0, 1):
            pltpu.make_async_copy(
                (v_fc, v_proj)[which].at[i], (v_fc, v_proj)[which].at[i], sems.at[1 + 2 * i + which]
            ).wait()
        fc, proj = v_fc[i], v_proj[i]
        pre = nn(normed[...], fc)
        grad_act = nt(cot[...], proj)
        cubic = 0.044715 * pre * pre
        curve = jnp.tanh(math.sqrt(2 / math.pi) * pre * (1.0 + cubic))
        act = 0.5 * pre * (1.0 + curve)
        slope = 0.5 * (1.0 + curve) + 0.5 * math.sqrt(2 / math.pi) * pre * (1.0 - curve * curve) * (
            1.0 + 3.0 * cubic
        )
        grad_pre = (grad_act * slope).astype(BF16)
        total[...] += nn(act.astype(BF16), proj)
        grad_norm[...] += nt(grad_pre, fc)
        return carry

    lax.fori_loop(0, steps, feed, 0, unroll=True)

    out = total[...].astype(BF16)
    back_0[:half, :width] = out[:half]
    back_1[:half, :width] = out[half:]
    unit, inverse = norm_parts(middle[...])
    grads = cot[...].astype(F32) + norm_back(unit, inverse, gain[...], grad_norm[...])
    grad_middle[...] = grads
    grad_heads = nt(grads.astype(BF16), v_out[...]).astype(BF16)
    grad_out_heads[:, :width] = grad_heads
    product = grad_heads.astype(F32) * attended[...]
    ones = jnp.where(
        jnp.logical_and(
            iota((width, LANES), 0) // HEAD == iota((width, LANES), 1) % HEADS,
            jnp.logical_and(
                iota((width, LANES), 1) >= 3 * HEADS, iota((width, LANES), 1) < 6 * HEADS
            ),
        ),
        1.0,
        0.0,
    ).astype(BF16)
    bases = jnp.zeros((rows, LANES), F32)
    for _ in range(3):
        part = product.astype(BF16)
        bases = bases + nn(part, ones)
        product = product - part.astype(F32)
    marks = three_parts(stats[...], 0) + three_parts(bases, 3 * HEADS)
    marks = marks.astype(BF16)
    grad_out_heads[:, width:] = marks
    back_0[:half, width:] = marks[:half]
    back_1[:half, width:] = marks[half:]
    back_0[half:] = jnp.zeros_like(back_0[half:])
    back_1[half:] = jnp.zeros_like(back_1[half:])


def middle_part(count, qkv_a, qkv_b, marks_a, marks_b, prefix_kv, own, cots, gain, bias, w_out, w_fc, w_proj):
    half, width = cots[0].shape
    rows = 2 * half
    hidden = w_fc.shape[1]
    steps = 2
    step = hidden // steps
    wide = width + LANES
    return pl.pallas_call(
        partial(middle_kernel, count),
        in_specs=[vmem()] * 11 + [hbm()] * 3,
        out_specs=[vmem()] * 4,
        out_shape=[
            jax.ShapeDtypeStruct((half + tail_rows(count), wide), BF16),
            jax.ShapeDtypeStruct((half + tail_rows(count), wide), BF16),
            jax.ShapeDtypeStruct((rows, wide), BF16),
            jax.ShapeDtypeStruct((rows, width), F32),
        ],
        scratch_shapes=[
            pltpu.VMEM((width, width), BF16),
            pltpu.VMEM((steps, width, step), BF16),
            pltpu.VMEM((steps, step, width), BF16),
            pltpu.SemaphoreType.DMA((1 + 2 * steps,)),
            pltpu.VMEM((rows, 4 * rows + LANES), F32),
            pltpu.VMEM((rows, width), F32),
            pltpu.VMEM((rows, LANES), F32),
            pltpu.VMEM((rows, width), F32),
            pltpu.VMEM((rows, width), BF16),
            pltpu.VMEM((rows, width), F32),
            pltpu.VMEM((rows, width), F32),
            pltpu.VMEM((rows, width), BF16),
        ],
        compiler_params=pltpu.CompilerParams(vmem_limit_bytes=36 * MIB),
        cost_estimate=pl.CostEstimate(flops=1 << 31, bytes_accessed=1000, transcendentals=0),
        name="middle",
    )(
        qkv_a, qkv_b, marks_a, marks_b, prefix_kv, *own, *cots, gain[None], bias[None], *kept_in_hbm(w_out, w_fc, w_proj)
    )


def key_grads(keys, values, queries, grads, marks, pair, low, mask):
    rows = keys.shape[0]
    scale = jnp.asarray(HEAD**-0.5, BF16)
    left = jnp.concatenate(
        [two_heads(keys * scale, low), picks(rows, pair, 0, -1.0).astype(BF16)], 1
    )
    scores = nt(left, jnp.concatenate([queries, marks], 1))
    weights = jnp.exp(scores + jnp.concatenate([mask, mask], 0))
    left = jnp.concatenate(
        [two_heads(values, low), picks(rows, pair, 3 * HEADS, -1.0).astype(BF16)], 1
    )
    slopes = weights * nt(left, jnp.concatenate([grads, marks], 1))
    key_grad = nn(slopes.astype(BF16), queries)
    value_grad = nn(weights.astype(BF16), grads)
    return join_heads(key_grad, low) * HEAD**-0.5, join_heads(value_grad, low)


def tail_rows(count):
    return -(-2 * count // PRE_ROWS) * PRE_ROWS


def prefix_kernel(used, queries, grads, prefix_kv, out):
    count, rows, width = prefix_kv.shape[0], grads.shape[0], grads.shape[1] - LANES
    marks = grads[:, width:]
    low = head_mask(count)
    mask = jnp.where(iota((count, rows), 0) < used, 0.0, NEG)

    def step(pair, carry):
        at = pl.ds(pl.multiple_of(pair * LANES, LANES), LANES)
        at_v = pl.ds(pl.multiple_of(width + pair * LANES, LANES), LANES)
        key_grad, value_grad = key_grads(
            prefix_kv[:, at], prefix_kv[:, at_v], queries[:rows, at], grads[:, at], marks, pair, low, mask
        )
        out[:, at] = key_grad.astype(BF16)
        out[:, at_v] = value_grad.astype(BF16)
        return carry

    lax.fori_loop(0, HEADS // 2, step, 0, unroll=True)


def prefix_part(count, qkv_a, grads, prefix_kv):
    return pl.pallas_call(
        partial(prefix_kernel, count),
        in_specs=[vmem()] * 3,
        out_specs=vmem(),
        out_shape=jax.ShapeDtypeStruct(prefix_kv.shape, BF16),
        compiler_params=pltpu.CompilerParams(vmem_limit_bytes=8 * MIB),
        cost_estimate=pl.CostEstimate(flops=1000, bytes_accessed=1000, transcendentals=0),
        name="prefix",
    )(qkv_a, grads, prefix_kv)


def pack_kernel(count, own, part_0, part_1, part_2, _0, _1, back_0, back_1):
    total = own[...].astype(F32) + part_0[...].astype(F32)
    total = total + (part_1[...].astype(F32) + part_2[...].astype(F32))
    width = total.shape[1] // 2
    rows = tail_rows(count)
    tail = pad_rows(jnp.concatenate([total[:count, :width], total[:count, width:]], 0), rows).astype(BF16)
    at = pl.ds(back_0.shape[0] - rows, rows)
    back_0[at, :width] = tail
    back_1[at, :width] = tail


def pack(count, terms, back_0, back_1):
    return pl.pallas_call(
        partial(pack_kernel, count),
        in_specs=[vmem()] * 6,
        out_specs=[vmem()] * 2,
        out_shape=[jax.ShapeDtypeStruct(back_0.shape, BF16)] * 2,
        input_output_aliases={4: 0, 5: 1},
        compiler_params=pltpu.CompilerParams(vmem_limit_bytes=4 * MIB),
        cost_estimate=pl.CostEstimate(flops=1 << 20, bytes_accessed=1 << 19, transcendentals=0),
        name="pack",
    )(*terms, back_0, back_1)


def unpack_kernel(count, home_0, home_1, out):
    width = out.shape[1] // 2
    rows = tail_rows(count)
    at = pl.ds(home_0.shape[0] - rows, rows)
    first, second = home_0[at, :width].astype(F32), home_1[at, :width].astype(F32)
    total = first + second
    out[:, :width] = pad_rows(total[:count], PRE_ROWS).astype(BF16)
    out[:, width:] = pad_rows(total[count : 2 * count], PRE_ROWS).astype(BF16)


def unpack(count, width, home_0, home_1):
    return pl.pallas_call(
        partial(unpack_kernel, count),
        in_specs=[vmem()] * 2,
        out_specs=vmem(),
        out_shape=jax.ShapeDtypeStruct((PRE_ROWS, 2 * width), BF16),
        compiler_params=pltpu.CompilerParams(vmem_limit_bytes=4 * MIB),
        cost_estimate=pl.CostEstimate(flops=1000, bytes_accessed=1000, transcendentals=0),
        name="unpack",
    )(home_0, home_1)


def query_kernel(
    count,
    qkv_a,
    qkv_b,
    marks_a,
    marks_b,
    prefix_kv,
    grads,
    weight,
    order,
    out,
    scores_bias,
    grad_query,
):
    del order
    rows, width = grad_query.shape
    scores_bias[...] = key_bias(marks_a[:rows], marks_a[...], marks_b[...], rows // 2, count)
    low = head_mask(rows)
    marks = grads[:, width:]
    marks_twice = jnp.concatenate([marks, marks], 0)
    ones = jnp.ones((4 * rows + LANES, LANES), BF16)

    def step(pair, carry):
        at = pl.ds(pl.multiple_of(pair * LANES, LANES), LANES)
        at_k = pl.ds(pl.multiple_of(width + pair * LANES, LANES), LANES)
        at_v = pl.ds(pl.multiple_of(2 * width + pair * LANES, LANES), LANES)
        keys = with_prefix(qkv_a[:, at_k], qkv_b[:, at_k], prefix_kv[:, at])
        values = with_prefix(qkv_a[:, at_v], qkv_b[:, at_v], prefix_kv[:, at_k])
        query = two_heads(qkv_a[:rows, at] * jnp.asarray(HEAD**-0.5, BF16), low)
        tops = marks_twice * picks(rows, pair, 0, -1.0).astype(BF16)
        scores = nt(jnp.concatenate([query, tops], 1), jnp.concatenate([keys, ones], 1))
        mask = scores_bias[...]
        weights = jnp.exp(scores + jnp.concatenate([mask, mask], 0))
        bases = marks_twice * picks(rows, pair, 3 * HEADS, -1.0).astype(BF16)
        left = jnp.concatenate([two_heads(grads[:, at], low), bases], 1)
        slopes = weights * nt(left, jnp.concatenate([values, ones], 1))
        grad = join_heads(nn(slopes.astype(BF16), keys), low)
        grad_query[:, at] = (grad * HEAD**-0.5).astype(BF16)
        return carry

    lax.fori_loop(0, HEADS // 2, step, 0, unroll=True)
    out[...] = nt(grad_query[...], weight[:, :width])


def query_part(count, qkv_a, qkv_b, marks_a, marks_b, prefix_kv, grads, weight, order):
    rows, width = grads.shape[0], grads.shape[1] - LANES
    return pl.pallas_call(
        partial(query_kernel, count),
        in_specs=[vmem()] * 7 + [pl.BlockSpec(memory_space=pl.ANY)],
        out_specs=vmem(),
        out_shape=jax.ShapeDtypeStruct((rows, width), F32),
        scratch_shapes=[pltpu.VMEM((rows, 4 * rows + LANES), F32), pltpu.VMEM((rows, width), BF16)],
        compiler_params=pltpu.CompilerParams(vmem_limit_bytes=16 * MIB),
        cost_estimate=pl.CostEstimate(flops=1 << 31, bytes_accessed=1000, transcendentals=0),
        name="query",
    )(qkv_a, qkv_b, marks_a, marks_b, prefix_kv, grads, weight, order)


def final_kernel(
    qkv_a,
    qkv_b,
    marks_a,
    marks_b,
    grads_0,
    grads_1,
    grads_2,
    grads_3,
    own_0,
    own_1,
    gain,
    grad_middle,
    grad_partial,
    weight,
    back_0,
    back_1,
    scores_bias,
    grad_keys,
):
    half, rows = own_0.shape[0], 2 * own_0.shape[0]
    width = grad_middle.shape[1]
    row, core, y_at = place()
    own = positions(iota((rows, 1), 0), half, row, core, y_at)
    other = all_positions((1, 8 * half), 1, half, row, core, y_at)
    same = nt(marks_a[:rows], jnp.concatenate([marks_a[...], marks_b[...]], 0))
    visible = jnp.logical_and(same > 0.5, own <= other)
    scores_bias[...] = jnp.where(visible, 0.0, NEG)
    low = head_mask(rows)
    blocks = (grads_0, grads_1, grads_2, grads_3)
    marks = jnp.concatenate([g[:, width:] for g in blocks], 0)

    def step(pair, carry):
        at = pl.ds(pl.multiple_of(pair * LANES, LANES), LANES)
        at_k = pl.ds(pl.multiple_of(width + pair * LANES, LANES), LANES)
        at_v = pl.ds(pl.multiple_of(2 * width + pair * LANES, LANES), LANES)
        queries = jnp.concatenate([qkv_a[:, at], qkv_b[:, at]], 0)
        grads = jnp.concatenate([g[:, at] for g in blocks], 0)
        key_grad, value_grad = key_grads(
            qkv_a[:rows, at_k], qkv_a[:rows, at_v], queries, grads, marks, pair, low, scores_bias[...]
        )
        grad_keys[:, at] = key_grad.astype(BF16)
        grad_keys[:, at_k] = value_grad.astype(BF16)
        return carry

    lax.fori_loop(0, HEADS // 2, step, 0, unroll=True)
    grad_norm = grad_partial[...] + nt(grad_keys[...], weight[:, width:])
    inputs = jnp.concatenate([own_0[:, :width], own_1[:, :width]], 0).astype(F32)
    unit, inverse = norm_parts(inputs)
    out = (grad_middle[...] + norm_back(unit, inverse, gain[...], grad_norm)).astype(BF16)
    back_0[...] = out[:half]
    back_1[...] = out[half:]


def final_part(qkv_a, qkv_b, marks_a, marks_b, grads, own, gain, grad_middle, grad_partial, weight):
    rows, width = grad_middle.shape
    half = rows // 2
    return pl.pallas_call(
        final_kernel,
        in_specs=[vmem()] * 14,
        out_specs=[vmem()] * 2,
        out_shape=[jax.ShapeDtypeStruct((half, width), BF16)] * 2,
        scratch_shapes=[
            pltpu.VMEM((rows, 4 * rows), F32),
            pltpu.VMEM((rows, 2 * width), BF16),
        ],
        compiler_params=pltpu.CompilerParams(vmem_limit_bytes=30 * MIB),
        cost_estimate=pl.CostEstimate(flops=1000, bytes_accessed=1000, transcendentals=0),
        name="final",
    )(qkv_a, qkv_b, marks_a, marks_b, *grads, *own, gain[None], grad_middle, grad_partial, weight)


def routes(k):
    pairs = []
    for seq in range(4):
        for blk in range(8):
            group, z_at, y_at = seq % 2, blk // 2, blk % 2
            row = (z_at + k) % 2
            pairs.append((seq * 8 + blk, (seq - group + z_at // 2) * 8 + (2 * group + row) * 2 + y_at))
    return pairs


def body_rows(
    tokens,
    segment_ids,
    ln1_gain,
    ln1_bias,
    w_qkv,
    w_out,
    ln2_gain,
    ln2_bias,
    w_fc,
    w_proj,
    prefix_embed,
    w_mlp1,
    b_mlp1,
    w_mlp2,
    b_mlp2,
    cotangent,
):
    half, _, width = tokens.shape
    everyone = ("seq", "blk")
    there = [routes(k) for k in range(2)]
    back = [[(b, a) for a, b in pairs] for pairs in there]
    swap_core = [(i, i ^ 1) for i in range(4)]
    swap_y = [(i, i ^ 1) for i in range(8)]
    swap_both = [(i, i ^ 9) for i in range(32)]
    def after(value, *done):
        return lax.optimization_barrier((value, done))[0]

    out_msgs = split_rows(tokens, segment_ids)
    cot_msgs = split_rows(cotangent)
    own = [lax.ppermute(m, everyone, there[k]) for k, m in enumerate(out_msgs)]
    prefix_kv, inner, w_near, near_embed, turned = adapter_forward(
        prefix_embed, w_mlp1, b_mlp1, w_mlp2, b_mlp2, w_qkv
    )
    count = prefix_embed.shape[0]
    own = after(own, inner)
    across = [lax.ppermute(m, "blk", swap_y) for m in own]
    beside = [lax.ppermute(m, "seq", swap_core) for m in own]
    cots = [lax.ppermute(m, everyone, there[k]) for k, m in enumerate(after(cot_msgs, beside))]
    beyond = [lax.ppermute(m, "seq", swap_core) for m in across]

    qkv_a, marks_a = project(own + beside, ln1_gain, ln1_bias, w_near)
    qkv_b, marks_b = project(across + beyond, ln1_gain, ln1_bias, w_near)
    back_0, back_1, grads, grad_middle = middle_part(
        count, qkv_a, qkv_b, marks_a, marks_b, prefix_kv, own, cots, ln2_gain, ln2_bias, w_out, w_fc, w_proj
    )
    grads_y = lax.ppermute(grads, "blk", swap_y)
    grads_c = lax.ppermute(grads, "seq", swap_core)
    grad_prefix_kv = prefix_part(count, qkv_a, grads, prefix_kv)
    parts = [lax.ppermute(grad_prefix_kv, "seq", [(i, i ^ far) for i in range(4)]) for far in (2, 1, 3)]
    grad_partial = query_part(
        count, qkv_a, qkv_b, marks_a, marks_b, prefix_kv, grads, w_near, grad_prefix_kv
    )
    packed = pack(count, (grad_prefix_kv, *after(parts, grad_partial)), back_0, back_1)
    home = [lax.ppermute(m, everyone, back[k]) for k, m in enumerate(packed)]
    grads_yc = lax.ppermute(after(grads_y, packed), "seq", swap_core)
    final_0, final_1 = final_part(
        qkv_a,
        qkv_b,
        marks_a,
        marks_b,
        (grads, grads_c, grads_y, grads_yc),
        own,
        ln1_gain,
        grad_middle,
        grad_partial,
        w_near,
    )
    finals = [lax.ppermute(m, everyone, back[k]) for k, m in enumerate((final_0, final_1))]
    gathered = [unpack(count, width, *home)]
    gathered += [lax.ppermute(gathered[0], "seq", swap_core), lax.ppermute(gathered[0], "blk", swap_y)]
    gathered += [lax.ppermute(gathered[0], everyone, swap_both)]
    input_grad, summed = finish(finals, gathered, near_embed, inner, turned)
    block_out, log_total = land(after(home, final_0), half, width)
    return (block_out, input_grad, summed[0], summed[1], summed[2], summed[3], summed[4], log_total)


def solution(mesh):
    four_by_eight = mesh.shape["seq"] == 4 and mesh.shape["blk"] == 8
    placed = (
        P("blk", "seq", None),
        P("blk", "seq"),
        P(),
        P(),
        P(),
        P(),
        P(),
        P(),
        P(),
        P(),
        P(),
        P(),
        P(),
        P(),
        P(),
        P("blk", "seq", None),
    )
    return jax.shard_map(
        body_rows if four_by_eight else body_plain,
        mesh=mesh,
        in_specs=placed,
        out_specs=(
            P("blk", "seq", None),
            P("blk", "seq", None),
            P(),
            P(),
            P(),
            P(),
            P(),
            P("seq", None, "blk"),
        ),
        check_vma=False,
    )
```

```python
from functools import partial
import math

import jax
import jax.numpy as jnp
from jax import lax
from jax.experimental import pallas as pl
from jax.experimental.pallas import tpu as pltpu
from jax.sharding import PartitionSpec as P

HEADS = 16
HEAD = 64


EPS = 1e-05
NEG = -1e30
HIGH = lax.Precision.HIGHEST


def layer_norm(value_in, gain, bias):
    average = jnp.mean(value_in, axis=-1, keepdims=True)
    centered = value_in - average
    variance = jnp.mean(centered * centered, axis=-1, keepdims=True)
    return centered * lax.rsqrt(variance + EPS) * gain + bias


def adapter(prefix_embed, w_mlp1, b_mlp1, w_mlp2, b_mlp2):
    inner_act = jnp.tanh(jnp.dot(prefix_embed, w_mlp1, precision=HIGH) + b_mlp1)
    return jnp.dot(inner_act, w_mlp2, precision=HIGH) + b_mlp2


def gelu_tanh(pre_act):
    return jax.nn.gelu(pre_act, approximate=True)


def split_heads(block_in):
    return block_in.reshape(block_in.shape[0], block_in.shape[1], HEADS, HEAD)


def allowed(query_pos, query_seg, key_pos, key_seg):
    same_seg = query_seg.T[:, :, None] == key_seg.T[:, None, :]
    causal = key_pos[None, None, :] <= query_pos[None, :, None]
    return jnp.logical_and(same_seg, causal)[:, None]


def scores_of(query_heads, key_block, score_scale):
    return score_scale * jnp.einsum(
        "prhd,krhd->rhpk", query_heads, split_heads(key_block), preferred_element_type=jnp.float32
    )


def block_grads(
    query_heads,
    grad_heads,
    log_total,
    slope_base,
    query_pos,
    query_seg,
    key_block,
    value_block,
    key_pos,
    key_seg,
    score_scale,
):
    scores = scores_of(query_heads, key_block, score_scale)
    scores = jnp.where(allowed(query_pos, query_seg, key_pos, key_seg), scores, NEG)
    weights = jnp.exp(scores - log_total[..., None])
    grad_weights = jnp.einsum(
        "prhd,krhd->rhpk", grad_heads, split_heads(value_block), preferred_element_type=jnp.float32
    )
    slopes = (weights * (grad_weights - slope_base[..., None])).astype(jnp.bfloat16)
    return (weights.astype(jnp.bfloat16), slopes)


def body_plain(
    tokens,
    segment_ids,
    ln1_gain,
    ln1_bias,
    w_qkv,
    w_out,
    ln2_gain,
    ln2_bias,
    w_fc,
    w_proj,
    prefix_embed,
    w_mlp1,
    b_mlp1,
    w_mlp2,
    b_mlp2,
    cotangent,
):
    pos_dev, row_count, width = tokens.shape
    score_scale = HEAD ** (-0.5)
    flat_rows = pos_dev * row_count
    own_pos = lax.axis_index("blk") * pos_dev + jnp.arange(pos_dev)
    inputs = tokens.astype(jnp.float32).reshape(flat_rows, width)
    normed_one = layer_norm(inputs, ln1_gain, ln1_bias).astype(jnp.bfloat16)
    projected = jnp.dot(normed_one, w_qkv, preferred_element_type=jnp.float32).astype(jnp.bfloat16)
    queries = projected[:, :width].reshape(pos_dev, row_count, width)
    keys = projected[:, width : 2 * width].reshape(pos_dev, row_count, width)
    values = projected[:, 2 * width :].reshape(pos_dev, row_count, width)
    query_heads = split_heads(queries)
    prefix_low = adapter(prefix_embed, w_mlp1, b_mlp1, w_mlp2, b_mlp2).astype(jnp.bfloat16)
    prefix_keys = prefix_low[:, :width].reshape(-1, HEADS, HEAD)
    prefix_values = prefix_low[:, width:].reshape(-1, HEADS, HEAD)
    prefix_scores = score_scale * jnp.einsum(
        "prhd,jhd->rhpj", query_heads, prefix_keys, preferred_element_type=jnp.float32
    )
    start_top = jnp.max(prefix_scores, -1)
    start_weights = jnp.exp(prefix_scores - start_top[..., None])
    start_denom = jnp.sum(start_weights, -1)
    start_numer = jnp.einsum(
        "rhpj,jhd->rhpd",
        start_weights.astype(jnp.bfloat16),
        prefix_values,
        preferred_element_type=jnp.float32,
    )
    start_state = (start_top, start_denom, start_numer)
    running = start_state
    key_shards = lax.all_gather(keys, "blk", axis=0, tiled=True)
    value_shards = lax.all_gather(values, "blk", axis=0, tiled=True)
    seg_shards = lax.all_gather(segment_ids, "blk", axis=0, tiled=True)
    num_rows = key_shards.shape[0]
    forward_stride = math.gcd(num_rows, 512)

    def inner(state, block_index):
        running_top, denominator, numerator = state
        offset = block_index * forward_stride
        key_block = lax.dynamic_slice_in_dim(key_shards, offset, forward_stride, 0)
        value_block = lax.dynamic_slice_in_dim(value_shards, offset, forward_stride, 0)
        seg_block = lax.dynamic_slice_in_dim(seg_shards, offset, forward_stride, 0)
        key_pos = offset + jnp.arange(forward_stride)
        scores = jnp.where(
            allowed(own_pos, segment_ids, key_pos, seg_block),
            scores_of(query_heads, key_block, score_scale),
            NEG,
        )
        new_top = jnp.maximum(running_top, jnp.max(scores, -1))
        fading = jnp.exp(running_top - new_top)
        weights = jnp.exp(scores - new_top[..., None])
        denominator = denominator * fading + jnp.sum(weights, -1)
        numerator = numerator * fading[..., None] + jnp.einsum(
            "rhpk,krhd->rhpd",
            weights.astype(jnp.bfloat16),
            split_heads(value_block),
            preferred_element_type=jnp.float32,
        )
        return ((new_top, denominator, numerator), None)

    running, _ = lax.scan(inner, running, jnp.arange(num_rows // forward_stride))
    final_top, final_denom, final_numer = running
    log_total = final_top + jnp.log(final_denom)
    attended = final_numer / final_denom[..., None]
    attended_rows = jnp.transpose(attended, (2, 0, 1, 3)).reshape(flat_rows, width)
    middle = inputs + jnp.dot(
        attended_rows.astype(jnp.bfloat16), w_out, preferred_element_type=jnp.float32
    )
    normed_two = layer_norm(middle, ln2_gain, ln2_bias).astype(jnp.bfloat16)
    hidden_pre = jnp.dot(normed_two, w_fc, preferred_element_type=jnp.float32)
    hidden_act = gelu_tanh(hidden_pre).astype(jnp.bfloat16)
    outputs = middle + jnp.dot(hidden_act, w_proj, preferred_element_type=jnp.float32)
    block_out = outputs.astype(jnp.bfloat16).reshape(pos_dev, row_count, width)
    grad_out = cotangent.reshape(flat_rows, width)
    grad_act = jnp.dot(grad_out, w_proj.T, preferred_element_type=jnp.float32)
    _, gelu_back = jax.vjp(gelu_tanh, hidden_pre)
    grad_pre = gelu_back(grad_act)[0].astype(jnp.bfloat16)
    grad_norm_two = jnp.dot(grad_pre, w_fc.T, preferred_element_type=jnp.float32)
    _, norm_two_back = jax.vjp(partial(layer_norm, gain=ln2_gain, bias=ln2_bias), middle)
    grad_middle = grad_out.astype(jnp.float32) + norm_two_back(grad_norm_two)[0]
    grad_attended = jnp.dot(
        grad_middle.astype(jnp.bfloat16), w_out.T, preferred_element_type=jnp.float32
    ).astype(jnp.bfloat16)
    grad_flat = grad_attended.reshape(pos_dev, row_count, width)
    grad_heads = split_heads(grad_flat)
    slope_base = jnp.sum(jnp.transpose(grad_heads.astype(jnp.float32), (1, 2, 0, 3)) * attended, -1)
    prefix_weights = jnp.exp(prefix_scores - log_total[..., None])
    prefix_dw = jnp.einsum(
        "prhd,jhd->rhpj", grad_heads, prefix_values, preferred_element_type=jnp.float32
    )
    prefix_slopes = (prefix_weights * (prefix_dw - slope_base[..., None])).astype(jnp.bfloat16)
    grad_query = score_scale * jnp.einsum(
        "rhpj,jhd->prhd", prefix_slopes, prefix_keys, preferred_element_type=jnp.float32
    )
    grad_pkeys = score_scale * jnp.einsum(
        "rhpj,prhd->jhd", prefix_slopes, query_heads, preferred_element_type=jnp.float32
    )
    grad_pvalues = jnp.einsum(
        "rhpj,prhd->jhd",
        prefix_weights.astype(jnp.bfloat16),
        grad_heads,
        preferred_element_type=jnp.float32,
    )
    grad_prefix_kv = jnp.concatenate(
        [grad_pkeys.reshape(-1, width), grad_pvalues.reshape(-1, width)], -1
    )
    keys_all, values_all, segs_all = (
        lax.all_gather(keys, "blk", axis=0, tiled=True),
        lax.all_gather(values, "blk", axis=0, tiled=True),
        lax.all_gather(segment_ids, "blk", axis=0, tiled=True),
    )
    length = keys_all.shape[0]
    stride = math.gcd(length, 512)

    def backward_step(grad_q, block_index):
        offset = block_index * stride
        key_block = lax.dynamic_slice_in_dim(keys_all, offset, stride, 0)
        value_block = lax.dynamic_slice_in_dim(values_all, offset, stride, 0)
        seg_block = lax.dynamic_slice_in_dim(segs_all, offset, stride, 0)
        key_pos = offset + jnp.arange(stride)
        weights_low, slopes = block_grads(
            query_heads,
            grad_heads,
            log_total,
            slope_base,
            own_pos,
            segment_ids,
            key_block,
            value_block,
            key_pos,
            seg_block,
            score_scale,
        )
        grad_q = grad_q + score_scale * jnp.einsum(
            "rhpk,krhd->prhd", slopes, split_heads(key_block), preferred_element_type=jnp.float32
        )
        key_term = score_scale * jnp.einsum(
            "rhpk,prhd->krhd", slopes, query_heads, preferred_element_type=jnp.float32
        )
        value_term = jnp.einsum(
            "rhpk,prhd->krhd", weights_low, grad_heads, preferred_element_type=jnp.float32
        )
        return (
            grad_q,
            (
                key_term.reshape(stride, row_count, width),
                value_term.reshape(stride, row_count, width),
            ),
        )

    grad_query, (key_terms, value_terms) = lax.scan(
        backward_step, grad_query, jnp.arange(length // stride)
    )
    key_terms = key_terms.reshape(length, row_count, width)
    value_terms = value_terms.reshape(length, row_count, width)
    grad_keys, grad_values = (
        lax.psum_scatter(key_terms, "blk", scatter_dimension=0, tiled=True),
        lax.psum_scatter(value_terms, "blk", scatter_dimension=0, tiled=True),
    )
    grad_proj = jnp.concatenate(
        [
            grad_query.reshape(flat_rows, width).astype(jnp.bfloat16),
            grad_keys.reshape(flat_rows, width).astype(jnp.bfloat16),
            grad_values.reshape(flat_rows, width).astype(jnp.bfloat16),
        ],
        -1,
    )
    grad_norm_one = jnp.dot(grad_proj, w_qkv.T, preferred_element_type=jnp.float32)
    _, norm_one_back = jax.vjp(partial(layer_norm, gain=ln1_gain, bias=ln1_bias), inputs)
    input_grad = (grad_middle + norm_one_back(grad_norm_one)[0]).reshape(pos_dev, row_count, width)
    _, adapter_back = jax.vjp(adapter, prefix_embed, w_mlp1, b_mlp1, w_mlp2, b_mlp2)
    local_grads = adapter_back(grad_prefix_kv)
    summed = lax.psum(
        (local_grads[0], local_grads[1], local_grads[2], local_grads[3], local_grads[4]),
        ("seq", "blk"),
    )
    return (block_out, input_grad, summed[0], summed[1], summed[2], summed[3], summed[4], log_total)


F32 = jnp.float32
BF16 = jnp.bfloat16
LANES = 128
PRE_ROWS = 16
MIB = 1 << 20


def nn(left, right):
    return jnp.dot(left, right, preferred_element_type=F32)


def nt(left, right):
    return lax.dot_general(left, right, (((1,), (1,)), ((), ())), preferred_element_type=F32)


def norm_parts(value_in):
    average = jnp.mean(value_in, axis=-1, keepdims=True)
    centered = value_in - average
    variance = jnp.mean(centered * centered, axis=-1, keepdims=True)
    inverse = lax.rsqrt(variance + EPS)
    return centered * inverse, inverse


def norm_back(unit, inverse, gain, grad):
    scaled = grad * gain
    first = jnp.mean(scaled, axis=-1, keepdims=True)
    second = jnp.mean(scaled * unit, axis=-1, keepdims=True)
    return inverse * (scaled - first - unit * second)


def iota(shape, dim):
    return lax.broadcasted_iota(jnp.int32, shape, dim)


def place():
    blk = lax.axis_index("blk")
    return (blk // 2) % 2, lax.axis_index("seq") % 2, blk % 2


def positions(index, half, row, core, y_at):
    upper = (index >= half).astype(jnp.int32)
    slot = upper + row - 2 * upper * row
    block = (2 * core + slot) * 2 + y_at
    return block * half + index - upper * half


def members(core, y_at):
    return ((core, y_at), (1 - core, y_at), (core, 1 - y_at), (1 - core, 1 - y_at))


def all_positions(shape, dim, half, row, core, y_at):
    part = tuple(2 * half if d == dim else n for d, n in enumerate(shape))
    return jnp.concatenate(
        [positions(iota(part, dim), half, row, c, y) for c, y in members(core, y_at)], dim
    )


def vmem():
    return pl.BlockSpec(memory_space=pltpu.VMEM)


def hbm():
    return pl.BlockSpec(memory_space=pltpu.HBM)


def kept_in_hbm(*arrays):
    return [pltpu.with_memory_space_constraint(a, pltpu.HBM) for a in arrays]


def by_tiles(block):
    half, pair, width = block.shape
    tiles = jnp.transpose(block.reshape(half, pair, width // LANES, LANES), (0, 2, 1, 3))
    return tiles.reshape(half, pair * width // LANES, LANES)


def from_tiles(tiles, width):
    half, count, _ = tiles.shape
    pair = count * LANES // width
    block = jnp.transpose(tiles.reshape(half, width // LANES, pair, LANES), (0, 2, 1, 3))
    return block.reshape(half, pair, width)


def odd_place():
    return (lax.axis_index("blk") // 2) % 2 == 1


def split_kernel(marked, *refs):
    tokens, ids, (out_0, out_1, work) = refs[0], refs[1], refs[-3:]
    half, count, _ = tokens.shape
    odd = odd_place()
    work[...] = tokens[...].astype(F32).reshape(half * count, LANES)
    for i in range(count // 2):
        at = pl.ds(i * LANES, LANES)
        first, second = (work[pl.ds(2 * i + r, half, stride=count)] for r in range(2))
        out_0[:, at] = jnp.where(odd, second, first).astype(BF16)
        out_1[:, at] = jnp.where(odd, first, second).astype(BF16)
    if marked:
        width = count // 2 * LANES
        first, second = (
            jnp.where(iota((LANES, half), 0) == ids[r : r + 1], 1.0, 0.0).T for r in range(2)
        )
        out_0[:, width:] = jnp.where(odd, second, first).astype(BF16)
        out_1[:, width:] = jnp.where(odd, first, second).astype(BF16)


def split_rows(block, segment_ids=None):
    tiles = by_tiles(block)
    half, count, _ = tiles.shape
    extra = () if segment_ids is None else kept_in_hbm(segment_ids.T)
    width = count // 2 * LANES + LANES * len(extra)
    return pl.pallas_call(
        partial(split_kernel, bool(extra)),
        in_specs=[vmem()] * (1 + len(extra)),
        out_specs=[vmem()] * 2,
        out_shape=[jax.ShapeDtypeStruct((half, width), BF16)] * 2,
        scratch_shapes=[pltpu.VMEM((half * count, LANES), F32)],
        compiler_params=pltpu.CompilerParams(vmem_limit_bytes=4 * MIB),
        cost_estimate=pl.CostEstimate(flops=1 << 20, bytes_accessed=1 << 19, transcendentals=0),
        name="split",
    )(*kept_in_hbm(tiles), *extra)


def place_rows(msg_0, msg_1, work):
    count = 2 * msg_0.shape[1] // LANES
    half = work.shape[0] // count
    odd = odd_place()
    for i in range(count // 2):
        at = pl.ds(i * LANES, LANES)
        one, two = msg_0[:half, at].astype(F32), msg_1[:half, at].astype(F32)
        work[pl.ds(2 * i, half, stride=count)] = jnp.where(odd, two, one)
        work[pl.ds(2 * i + 1, half, stride=count)] = jnp.where(odd, one, two)


def land_kernel(first_row, msg_0, msg_1, out, logs, work):
    half = out.shape[0]
    heads = logs.shape[1]
    place_rows(msg_0, msg_1, work)
    out[...] = work[...].reshape(out.shape).astype(out.dtype)
    odd = odd_place()
    found = []
    for k, message in enumerate((msg_0, msg_1)):
        rows = message[half:].astype(F32)[first_row : first_row + GROUP]
        slots = [rows[:, i * LANES + k * half : i * LANES + (k + 1) * half] for i in range(3 * heads // GROUP)]
        groups = [slots[i] + slots[i + 1] + slots[i + 2] for i in range(0, len(slots), 3)]
        found.append(jnp.concatenate(groups, 0))
    logs[0] = jnp.where(odd, found[1], found[0])
    logs[1] = jnp.where(odd, found[0], found[1])


def land(count_prefix, messages, half, width):
    count = 2 * width // LANES
    out = pl.pallas_call(
        partial(land_kernel, prefix_rows(count_prefix)),
        in_specs=[vmem()] * 2,
        out_specs=[vmem()] * 2,
        out_shape=[
            jax.ShapeDtypeStruct((half, count, LANES), BF16),
            jax.ShapeDtypeStruct((2, HEADS, half), F32),
        ],
        scratch_shapes=[pltpu.VMEM((half * count, LANES), F32)],
        compiler_params=pltpu.CompilerParams(vmem_limit_bytes=4 * MIB),
        cost_estimate=pl.CostEstimate(flops=1000, bytes_accessed=1000, transcendentals=0),
        name="land",
    )(*messages)
    return from_tiles(out[0], width), out[1]


def project_kernel(count, *refs):
    messages, (gain, bias, weight, out, marks, normed) = refs[:count], refs[count:]
    half, width = messages[0].shape[0], normed.shape[1]
    for i, message in enumerate(messages):
        rows = pl.ds(i * half, half)
        unit, _ = norm_parts(message[:, :width].astype(F32))
        normed[rows] = (unit * gain[...] + bias[...]).astype(BF16)
        marks[rows] = message[:, width:]
    for i in range(3):
        at = pl.ds(i * width, width)
        out[:, at] = nn(normed[...], weight[:, at]).astype(BF16)


def project(messages, gain, bias, weight):
    count, half = len(messages), messages[0].shape[0]
    width, columns = weight.shape
    rows = count * half
    return pl.pallas_call(
        partial(project_kernel, count),
        in_specs=[vmem()] * (count + 3),
        out_specs=[vmem()] * 2,
        out_shape=[
            jax.ShapeDtypeStruct((rows, columns), BF16),
            jax.ShapeDtypeStruct((rows, LANES), BF16),
        ],
        scratch_shapes=[pltpu.VMEM((rows, width), BF16)],
        compiler_params=pltpu.CompilerParams(vmem_limit_bytes=16 * MIB),
        cost_estimate=pl.CostEstimate(
            flops=2 * rows * width * columns, bytes_accessed=2 * width * columns, transcendentals=0
        ),
        name="project",
    )(*messages, gain[None], bias[None], weight)


def halves(value_in):
    high = value_in.astype(BF16)
    return high, (value_in - high.astype(F32)).astype(BF16)


def pad_rows(value_in, rows):
    if rows == value_in.shape[0]:
        return value_in
    return jnp.concatenate(
        [value_in, jnp.zeros((rows - value_in.shape[0], value_in.shape[1]), value_in.dtype)], 0
    )


def three_products(product, left, weight):
    rows = left.shape[0]
    high, low = halves(left)
    w_high, w_low = halves(weight)
    both = product(jnp.concatenate([high, low], 0), w_high)
    return both[:rows] + both[rows:] + product(high, w_low)


def adapter_kernel(
    h_embed,
    w_mlp1,
    h_mlp1,
    w_mlp2,
    h_mlp2,
    w_qkv,
    out,
    inner,
    v_qkv,
    w_back,
    embed,
    turned,
    v_mlp1,
    v_mlp2,
    b_mlp1,
    b_mlp2,
    sems,
):
    steps, step = v_mlp2.shape[0], v_mlp2.shape[2]
    small = []
    for i, (source, target) in enumerate(
        ((h_embed, embed), (h_mlp1, b_mlp1), (h_mlp2, b_mlp2), (w_mlp1, v_mlp1))
    ):
        small.append(pltpu.make_async_copy(source, target, sems.at[steps + i]))
        small[-1].start()
    width = w_qkv.shape[0]
    weights = []
    for i in range(3):
        at = pl.ds(i * width, width)
        weights.append(
            pltpu.make_async_copy(w_qkv.at[:, at], v_qkv.at[:, at], sems.at[steps + len(small) + i])
        )
        weights[-1].start()
    rest = []
    for i in range(steps):
        copy = pltpu.make_async_copy(w_mlp2.at[:, pl.ds(i * step, step)], v_mlp2.at[i], sems.at[i])
        copy.start()
        rest.append(copy)
    for copy in small:
        copy.wait()
    source = pad_rows(embed[...], PRE_ROWS)
    act = jnp.tanh(three_products(nn, source, v_mlp1[...]) + b_mlp1[...])
    inner[...] = act
    columns, hidden = steps * step, v_mlp1.shape[1]
    for i in range(v_mlp1.shape[0] // hidden):
        part = v_mlp1[pl.ds(i * hidden, hidden)].astype(BF16)
        turned[pl.ds(columns + i * hidden, hidden)] = part.T
    for i, copy in enumerate(weights):
        at = pl.ds(i * width, width)
        copy.wait()
        w_back[at] = v_qkv[:, at].T
    for i, copy in enumerate(rest):
        copy.wait()
        turned[pl.ds(i * step, step)] = v_mlp2[i].astype(BF16).T
        span = pl.ds(i * step, step)
        part = three_products(nn, act, v_mlp2[i]) + b_mlp2[:, span]
        out[:, span] = jnp.where(iota(part.shape, 0) < embed.shape[0], part, 0.0).astype(BF16)


def adapter_forward(embed, w_mlp1, b_mlp1, w_mlp2, b_mlp2, w_qkv):
    width, hidden = w_mlp1.shape
    columns = w_mlp2.shape[1]
    steps = 4
    return pl.pallas_call(
        adapter_kernel,
        in_specs=[hbm()] * 6,
        out_specs=[vmem()] * 6,
        out_shape=[
            jax.ShapeDtypeStruct((PRE_ROWS, columns), BF16),
            jax.ShapeDtypeStruct((PRE_ROWS, hidden), F32),
            pltpu.VMEM(w_qkv.shape, w_qkv.dtype),
            pltpu.VMEM(w_qkv.shape[::-1], w_qkv.dtype),
            pltpu.VMEM(embed.shape, F32),
            pltpu.VMEM((columns + width, hidden), BF16),
        ],
        scratch_shapes=[
            pltpu.VMEM((width, hidden), F32),
            pltpu.VMEM((steps, hidden, columns // steps), F32),
            pltpu.VMEM((1, hidden), F32),
            pltpu.VMEM((1, columns), F32),
            pltpu.SemaphoreType.DMA((7 + steps,)),
        ],
        compiler_params=pltpu.CompilerParams(vmem_limit_bytes=20 * MIB),
        cost_estimate=pl.CostEstimate(flops=1 << 32, bytes_accessed=6 * MIB, transcendentals=1 << 13),
        name="adapter",
    )(*kept_in_hbm(embed, w_mlp1, b_mlp1[None], w_mlp2, b_mlp2[None], w_qkv))


def outer(left, right):
    l_high, l_low = halves(left)
    r_high, r_low = halves(right)
    return lax.dot_general(
        jnp.concatenate([l_high, l_high, l_low], 0),
        jnp.concatenate([r_high, r_low, r_high], 0),
        (((0,), (0,)), ((), ())),
        preferred_element_type=F32,
    )


def two_products(left, weight):
    high, low = halves(left)
    both = nn(jnp.concatenate([high, low], 0), weight)
    return both[: left.shape[0]] + both[left.shape[0] :]


def adapter_back_kernel(
    home_0,
    home_1,
    part_0,
    part_1,
    part_2,
    part_3,
    embed,
    inner,
    turned,
    block,
    grad_prefix,
    grad_mlp1,
    grad_bias1,
    grad_mlp2,
    grad_bias2,
    o_block,
    o_mlp1,
    o_mlp2,
    sems,
):
    steps, step = o_mlp2.shape[0], o_mlp2.shape[2]
    first, second, third, fourth = (p[...].astype(F32) for p in (part_0, part_1, part_2, part_3))
    grads = (first + second) + (third + fourth)
    act = inner[...]
    stores = []
    grad_bias2[...] = jnp.sum(grads, 0, keepdims=True)
    for i in range(steps):
        o_mlp2[i] = outer(act, grads[:, i * step : (i + 1) * step])
        stores.append(
            pltpu.make_async_copy(o_mlp2.at[i], grad_mlp2.at[:, pl.ds(i * step, step)], sems.at[i])
        )
        stores[-1].start()
    columns, (width, hidden) = steps * step, o_mlp1.shape
    place_rows(home_0, home_1, o_block)
    stores.append(pltpu.make_async_copy(o_block, block, sems.at[steps + 1]))
    stores[-1].start()
    back = two_products(grads, turned[:columns]) * (1.0 - act * act)
    grad_bias1[...] = jnp.sum(back, 0, keepdims=True)
    o_mlp1[...] = outer(pad_rows(embed[...], PRE_ROWS), back)
    stores.append(pltpu.make_async_copy(o_mlp1, grad_mlp1, sems.at[steps]))
    stores[-1].start()
    for i in range(width // hidden):
        part = two_products(back, turned[pl.ds(columns + i * hidden, hidden)])
        grad_prefix[:, pl.ds(i * hidden, hidden)] = part[: embed.shape[0]]
    for copy in stores:
        copy.wait()


def finish(finals, parts, embed, inner, turned):
    hidden, width = turned.shape[1], embed.shape[1]
    columns = turned.shape[0] - width
    half = finals[0].shape[0]
    steps = 4
    tiles = 2 * width // LANES
    out = pl.pallas_call(
        adapter_back_kernel,
        in_specs=[vmem()] * 9,
        out_specs=[hbm(), vmem(), hbm(), vmem(), hbm(), vmem()],
        out_shape=[
            jax.ShapeDtypeStruct((half * tiles, LANES), F32),
            jax.ShapeDtypeStruct(embed.shape, F32),
            jax.ShapeDtypeStruct((width, hidden), F32),
            jax.ShapeDtypeStruct((1, hidden), F32),
            jax.ShapeDtypeStruct((hidden, columns), F32),
            jax.ShapeDtypeStruct((1, columns), F32),
        ],
        scratch_shapes=[
            pltpu.VMEM((half * tiles, LANES), F32),
            pltpu.VMEM((width, hidden), F32),
            pltpu.VMEM((steps, hidden, columns // steps), F32),
            pltpu.SemaphoreType.DMA((steps + 2,)),
        ],
        compiler_params=pltpu.CompilerParams(vmem_limit_bytes=16 * MIB),
        cost_estimate=pl.CostEstimate(flops=1000, bytes_accessed=1000, transcendentals=0),
        name="finish",
    )(*finals, *parts, embed, inner, turned)
    block = from_tiles(out[0].reshape(half, tiles, LANES), width)
    return block, (out[1], out[2], out[3][0], out[4], out[5][0])


def head_mask(rows):
    return iota((rows, LANES), 1) < HEAD


def two_heads(pair, low):
    zero = jnp.zeros_like(pair)
    return jnp.concatenate([jnp.where(low, pair, zero), jnp.where(low, zero, pair)], 0)


def join_heads(stacked, low):
    rows = stacked.shape[0] // 2
    return jnp.where(low, stacked[:rows], stacked[rows:])


def picks(rows, pair, first, value):
    lane = iota((rows, LANES), 1)
    inside = jnp.logical_and(lane >= first, lane < first + 3 * HEADS)
    parts = [
        jnp.where(jnp.logical_and(inside, lane % HEADS == 2 * pair + i), value, 0.0) for i in range(2)
    ]
    return jnp.concatenate(parts, 0)


def three_parts(value_in, first):
    lane = iota(value_in.shape, 1)
    high = value_in.astype(BF16).astype(F32)
    rest = value_in - high
    middle = rest.astype(BF16).astype(F32)
    low = rest - middle
    part = (lane - first) // HEADS
    chosen = jnp.where(part == 0, high, jnp.where(part == 1, middle, low))
    inside = jnp.logical_and(lane >= first, lane < first + 3 * HEADS)
    return jnp.where(inside, chosen, 0.0)


def key_bias(marks_own, marks_a, marks_b, half, count):
    row, core, y_at = place()
    rows = 2 * half
    own = positions(iota((rows, 1), 0), half, row, core, y_at)
    other = all_positions((1, 8 * half), 1, half, row, core, y_at)
    same = nt(marks_own, jnp.concatenate([marks_a, marks_b], 0))
    visible = jnp.logical_and(same > 0.5, other <= own)
    token_bias = jnp.where(visible, 0.0, NEG)
    prefix_bias = jnp.where(iota((rows, LANES), 1) < count, 0.0, NEG)
    return jnp.concatenate([token_bias, prefix_bias], 1)


def with_prefix(part_a, part_b, prefix):
    pad = jnp.zeros((LANES - prefix.shape[0], prefix.shape[1]), prefix.dtype)
    return jnp.concatenate([part_a, part_b, prefix, pad], 0)


def middle_kernel(
    count,
    qkv_a,
    qkv_b,
    marks_a,
    marks_b,
    prefix_kv,
    own_0,
    own_1,
    cot_0,
    cot_1,
    gain,
    bias,
    w_out,
    w_fc,
    w_proj,
    back_0,
    back_1,
    grad_out_heads,
    grad_middle,
    v_out,
    v_fc,
    v_proj,
    sems,
    scores_bias,
    attended,
    stats,
    middle,
    normed,
    total,
    grad_norm,
    cot,
):
    half, rows = own_0.shape[0], 2 * own_0.shape[0]
    width = middle.shape[1]
    steps, step = v_fc.shape[0], v_fc.shape[2]
    copies = [pltpu.make_async_copy(w_out, v_out, sems.at[0])]
    for i in range(steps):
        span = pl.ds(i * step, step)
        copies.append(pltpu.make_async_copy(w_fc.at[:, span], v_fc.at[i], sems.at[1 + 2 * i]))
        copies.append(pltpu.make_async_copy(w_proj.at[span], v_proj.at[i], sems.at[2 + 2 * i]))
    for copy in copies:
        copy.start()

    scores_bias[...] = key_bias(marks_a[:rows], marks_a[...], marks_b[...], half, count)
    low = head_mask(rows)
    lane = iota((rows, LANES), 1)
    stats[...] = jnp.zeros_like(stats)

    def attend(pair, carry):
        at = pl.ds(pl.multiple_of(pair * LANES, LANES), LANES)
        at_k = pl.ds(pl.multiple_of(width + pair * LANES, LANES), LANES)
        at_v = pl.ds(pl.multiple_of(2 * width + pair * LANES, LANES), LANES)
        query = two_heads(qkv_a[:rows, at] * jnp.asarray(HEAD**-0.5, BF16), low)
        keys = with_prefix(qkv_a[:, at_k], qkv_b[:, at_k], prefix_kv[:, at])
        values = with_prefix(qkv_a[:, at_v], qkv_b[:, at_v], prefix_kv[:, at_k])
        scores = nt(query, keys)
        mask = scores_bias[...]
        scores = scores + jnp.concatenate([mask, mask], 0)
        top = jnp.max(scores, -1, keepdims=True)
        weights = jnp.exp(scores - top)
        denominator = jnp.sum(weights, -1, keepdims=True)
        mixed = nn(weights.astype(BF16), values) / denominator
        attended[:, at] = join_heads(mixed, low)
        log_total = top + jnp.log(denominator)
        inside = lane < 3 * HEADS
        for i in range(2):
            here = jnp.logical_and(inside, lane % HEADS == 2 * pair + i)
            stats[...] = jnp.where(here, log_total[i * rows : (i + 1) * rows], stats[...])
        return carry

    lax.fori_loop(0, HEADS // 2, attend, 0, unroll=4)

    copies[0].wait()
    inputs = jnp.concatenate([own_0[:, :width], own_1[:, :width]], 0).astype(F32)
    middle[...] = inputs + nn(attended[...].astype(BF16), v_out[...])
    unit, _ = norm_parts(middle[...])
    normed[...] = (unit * gain[...] + bias[...]).astype(BF16)
    cot[...] = jnp.concatenate([cot_0[...], cot_1[...]], 0)
    total[...] = middle[...]
    grad_norm[...] = jnp.zeros_like(grad_norm)

    def feed(i, carry):
        for which in (0, 1):
            pltpu.make_async_copy(
                (v_fc, v_proj)[which].at[i], (v_fc, v_proj)[which].at[i], sems.at[1 + 2 * i + which]
            ).wait()
        fc, proj = v_fc[i], v_proj[i]
        pre = nn(normed[...], fc)
        grad_act = nt(cot[...], proj)
        cubic = 0.044715 * pre * pre
        curve = jnp.tanh(math.sqrt(2 / math.pi) * pre * (1.0 + cubic))
        act = 0.5 * pre * (1.0 + curve)
        slope = 0.5 * (1.0 + curve) + 0.5 * math.sqrt(2 / math.pi) * pre * (1.0 - curve * curve) * (
            1.0 + 3.0 * cubic
        )
        grad_pre = (grad_act * slope).astype(BF16)
        total[...] += nn(act.astype(BF16), proj)
        grad_norm[...] += nt(grad_pre, fc)
        return carry

    lax.fori_loop(0, steps, feed, 0, unroll=True)

    out = total[...].astype(BF16)
    back_0[:half] = out[:half]
    back_1[:half] = out[half:]
    unit, inverse = norm_parts(middle[...])
    grads = cot[...].astype(F32) + norm_back(unit, inverse, gain[...], grad_norm[...])
    grad_middle[...] = grads
    grad_heads = nt(grads.astype(BF16), v_out[...]).astype(BF16)
    grad_out_heads[:, :width] = grad_heads
    product = grad_heads.astype(F32) * attended[...]
    ones = jnp.where(
        jnp.logical_and(
            iota((width, LANES), 0) // HEAD == iota((width, LANES), 1) % HEADS,
            jnp.logical_and(
                iota((width, LANES), 1) >= 3 * HEADS, iota((width, LANES), 1) < 6 * HEADS
            ),
        ),
        1.0,
        0.0,
    ).astype(BF16)
    bases = jnp.zeros((rows, LANES), F32)
    for _ in range(2):
        part = product.astype(BF16)
        bases = bases + nn(part, ones)
        product = product - part.astype(F32)
    marks = three_parts(stats[...], 0) + three_parts(bases, 3 * HEADS)
    marks = marks.astype(BF16)
    grad_out_heads[:, width:] = marks


def middle_part(count, qkv_a, qkv_b, marks_a, marks_b, prefix_kv, own, cots, gain, bias, w_out, w_fc, w_proj):
    half, width = cots[0].shape
    rows = 2 * half
    hidden = w_fc.shape[1]
    steps = 2
    step = hidden // steps
    wide = width + LANES
    return pl.pallas_call(
        partial(middle_kernel, count),
        in_specs=[vmem()] * 11 + [hbm()] * 3,
        out_specs=[vmem()] * 4,
        out_shape=[
            jax.ShapeDtypeStruct((half + tail_rows(count), width), BF16),
            jax.ShapeDtypeStruct((half + tail_rows(count), width), BF16),
            jax.ShapeDtypeStruct((rows, wide), BF16),
            jax.ShapeDtypeStruct((rows, width), F32),
        ],
        scratch_shapes=[
            pltpu.VMEM((width, width), BF16),
            pltpu.VMEM((steps, width, step), BF16),
            pltpu.VMEM((steps, step, width), BF16),
            pltpu.SemaphoreType.DMA((1 + 2 * steps,)),
            pltpu.VMEM((rows, 4 * rows + LANES), F32),
            pltpu.VMEM((rows, width), F32),
            pltpu.VMEM((rows, LANES), F32),
            pltpu.VMEM((rows, width), F32),
            pltpu.VMEM((rows, width), BF16),
            pltpu.VMEM((rows, width), F32),
            pltpu.VMEM((rows, width), F32),
            pltpu.VMEM((rows, width), BF16),
        ],
        compiler_params=pltpu.CompilerParams(vmem_limit_bytes=36 * MIB),
        cost_estimate=pl.CostEstimate(flops=1 << 31, bytes_accessed=1000, transcendentals=0),
        name="middle",
    )(
        qkv_a, qkv_b, marks_a, marks_b, prefix_kv, *own, *cots, gain[None], bias[None], *kept_in_hbm(w_out, w_fc, w_proj)
    )


def key_grads(keys, values, queries, grads, turned_marks, pair, low, mask):
    rows = keys.shape[0]
    scale = jnp.asarray(HEAD**-0.5, BF16)
    left = jnp.concatenate(
        [two_heads(keys * scale, low), picks(rows, pair, 0, -1.0).astype(BF16)], 1
    )
    scores = nn(left, jnp.concatenate([queries.T, turned_marks], 0))
    weights = jnp.exp(scores + jnp.concatenate([mask, mask], 0))
    left = jnp.concatenate(
        [two_heads(values, low), picks(rows, pair, 3 * HEADS, -1.0).astype(BF16)], 1
    )
    slopes = weights * nn(left, jnp.concatenate([grads.T, turned_marks], 0))
    key_grad = nn(slopes.astype(BF16), queries)
    value_grad = nn(weights.astype(BF16), grads)
    return join_heads(key_grad, low) * HEAD**-0.5, join_heads(value_grad, low)


GROUP = 8


def prefix_rows(count):
    return -(-2 * count // GROUP) * GROUP


def tail_rows(count):
    return -(-(prefix_rows(count) + GROUP) // PRE_ROWS) * PRE_ROWS


def prefix_kernel(used, queries, grads, prefix_kv, out):
    count, rows, width = prefix_kv.shape[0], grads.shape[0], grads.shape[1] - LANES
    marks = grads[:, width:].T
    low = head_mask(count)
    mask = jnp.where(iota((count, rows), 0) < used, 0.0, NEG)

    def step(pair, carry):
        at = pl.ds(pl.multiple_of(pair * LANES, LANES), LANES)
        at_v = pl.ds(pl.multiple_of(width + pair * LANES, LANES), LANES)
        key_grad, value_grad = key_grads(
            prefix_kv[:, at], prefix_kv[:, at_v], queries[:rows, at], grads[:, at], marks, pair, low, mask
        )
        out[:, at] = key_grad.astype(BF16)
        out[:, at_v] = value_grad.astype(BF16)
        return carry

    lax.fori_loop(0, HEADS // 2, step, 0, unroll=True)


def prefix_part(count, qkv_a, grads, prefix_kv):
    return pl.pallas_call(
        partial(prefix_kernel, count),
        in_specs=[vmem()] * 3,
        out_specs=vmem(),
        out_shape=jax.ShapeDtypeStruct(prefix_kv.shape, BF16),
        compiler_params=pltpu.CompilerParams(vmem_limit_bytes=8 * MIB),
        cost_estimate=pl.CostEstimate(flops=1000, bytes_accessed=1000, transcendentals=0),
        name="prefix",
    )(qkv_a, grads, prefix_kv)


def pack_kernel(count, grads, own, part_0, part_1, part_2, _0, _1, back_0, back_1):
    total = own[...].astype(F32) + part_0[...].astype(F32)
    total = total + (part_1[...].astype(F32) + part_2[...].astype(F32))
    width = total.shape[1] // 2
    rows = tail_rows(count)
    both = jnp.concatenate([total[:count, :width], total[:count, width:]], 0)
    marks = grads[:, width:].astype(F32).T
    starts = [part * HEADS + first for first in range(0, HEADS, GROUP) for part in range(3)]
    logs = jnp.concatenate([marks[i : i + GROUP] for i in starts], 1)
    logs = jnp.concatenate([logs, jnp.zeros((GROUP, width - logs.shape[1]), F32)], 1)
    tail = pad_rows(jnp.concatenate([pad_rows(both, prefix_rows(count)), logs], 0), rows).astype(BF16)
    at = pl.ds(back_0.shape[0] - rows, rows)
    back_0[at] = tail
    back_1[at] = tail


def pack(count, grads, terms, back_0, back_1):
    return pl.pallas_call(
        partial(pack_kernel, count),
        in_specs=[vmem()] * 7,
        out_specs=[vmem()] * 2,
        out_shape=[jax.ShapeDtypeStruct(back_0.shape, BF16)] * 2,
        input_output_aliases={5: 0, 6: 1},
        compiler_params=pltpu.CompilerParams(vmem_limit_bytes=4 * MIB),
        cost_estimate=pl.CostEstimate(flops=1 << 20, bytes_accessed=1 << 19, transcendentals=0),
        name="pack",
    )(grads, *terms, back_0, back_1)


def unpack_kernel(count, home_0, home_1, out):
    width = out.shape[1] // 2
    rows = tail_rows(count)
    at = pl.ds(home_0.shape[0] - rows, rows)
    first, second = home_0[at].astype(F32), home_1[at].astype(F32)
    total = first + second
    out[:, :width] = pad_rows(total[:count], PRE_ROWS).astype(BF16)
    out[:, width:] = pad_rows(total[count : 2 * count], PRE_ROWS).astype(BF16)


def unpack(count, width, home_0, home_1):
    return pl.pallas_call(
        partial(unpack_kernel, count),
        in_specs=[vmem()] * 2,
        out_specs=vmem(),
        out_shape=jax.ShapeDtypeStruct((PRE_ROWS, 2 * width), BF16),
        compiler_params=pltpu.CompilerParams(vmem_limit_bytes=4 * MIB),
        cost_estimate=pl.CostEstimate(flops=1000, bytes_accessed=1000, transcendentals=0),
        name="unpack",
    )(home_0, home_1)


def query_kernel(
    count,
    qkv_a,
    qkv_b,
    marks_a,
    marks_b,
    prefix_kv,
    grads,
    weight,
    order,
    out,
    scores_bias,
    grad_query,
):
    del order
    rows, width = grad_query.shape
    scores_bias[...] = key_bias(marks_a[:rows], marks_a[...], marks_b[...], rows // 2, count)
    low = head_mask(rows)
    marks = grads[:, width:]
    marks_twice = jnp.concatenate([marks, marks], 0)
    ones = jnp.ones((LANES, 4 * rows + LANES), BF16)

    def step(pair, carry):
        at = pl.ds(pl.multiple_of(pair * LANES, LANES), LANES)
        at_k = pl.ds(pl.multiple_of(width + pair * LANES, LANES), LANES)
        at_v = pl.ds(pl.multiple_of(2 * width + pair * LANES, LANES), LANES)
        keys = with_prefix(qkv_a[:, at_k], qkv_b[:, at_k], prefix_kv[:, at])
        values = with_prefix(qkv_a[:, at_v], qkv_b[:, at_v], prefix_kv[:, at_k])
        query = two_heads(qkv_a[:rows, at] * jnp.asarray(HEAD**-0.5, BF16), low)
        tops = marks_twice * picks(rows, pair, 0, -1.0).astype(BF16)
        scores = nn(jnp.concatenate([query, tops], 1), jnp.concatenate([keys.T, ones], 0))
        mask = scores_bias[...]
        weights = jnp.exp(scores + jnp.concatenate([mask, mask], 0))
        bases = marks_twice * picks(rows, pair, 3 * HEADS, -1.0).astype(BF16)
        left = jnp.concatenate([two_heads(grads[:, at], low), bases], 1)
        slopes = weights * nn(left, jnp.concatenate([values.T, ones], 0))
        grad = join_heads(nn(slopes.astype(BF16), keys), low)
        grad_query[:, at] = (grad * HEAD**-0.5).astype(BF16)
        return carry

    lax.fori_loop(0, HEADS // 2, step, 0, unroll=True)
    out[...] = nn(grad_query[...], weight[:width])


def query_part(count, qkv_a, qkv_b, marks_a, marks_b, prefix_kv, grads, weight, order):
    rows, width = grads.shape[0], grads.shape[1] - LANES
    return pl.pallas_call(
        partial(query_kernel, count),
        in_specs=[vmem()] * 7 + [pl.BlockSpec(memory_space=pl.ANY)],
        out_specs=vmem(),
        out_shape=jax.ShapeDtypeStruct((rows, width), F32),
        scratch_shapes=[pltpu.VMEM((rows, 4 * rows + LANES), F32), pltpu.VMEM((rows, width), BF16)],
        compiler_params=pltpu.CompilerParams(vmem_limit_bytes=16 * MIB),
        cost_estimate=pl.CostEstimate(flops=1 << 31, bytes_accessed=1000, transcendentals=0),
        name="query",
    )(qkv_a, qkv_b, marks_a, marks_b, prefix_kv, grads, weight, order)


def final_kernel(
    qkv_a,
    qkv_b,
    marks_a,
    marks_b,
    grads_0,
    grads_1,
    grads_2,
    grads_3,
    own_0,
    own_1,
    gain,
    grad_middle,
    grad_partial,
    weight,
    back_0,
    back_1,
    scores_bias,
    grad_keys,
):
    half, rows = own_0.shape[0], 2 * own_0.shape[0]
    width = grad_middle.shape[1]
    row, core, y_at = place()
    own = positions(iota((rows, 1), 0), half, row, core, y_at)
    other = all_positions((1, 8 * half), 1, half, row, core, y_at)
    same = nt(marks_a[:rows], jnp.concatenate([marks_a[...], marks_b[...]], 0))
    visible = jnp.logical_and(same > 0.5, own <= other)
    scores_bias[...] = jnp.where(visible, 0.0, NEG)
    low = head_mask(rows)
    blocks = (grads_0, grads_1, grads_2, grads_3)
    marks = jnp.concatenate([g[:, width:] for g in blocks], 0).T

    def step(pair, carry):
        at = pl.ds(pl.multiple_of(pair * LANES, LANES), LANES)
        at_k = pl.ds(pl.multiple_of(width + pair * LANES, LANES), LANES)
        at_v = pl.ds(pl.multiple_of(2 * width + pair * LANES, LANES), LANES)
        queries = jnp.concatenate([qkv_a[:, at], qkv_b[:, at]], 0)
        grads = jnp.concatenate([g[:, at] for g in blocks], 0)
        key_grad, value_grad = key_grads(
            qkv_a[:rows, at_k], qkv_a[:rows, at_v], queries, grads, marks, pair, low, scores_bias[...]
        )
        grad_keys[:, at] = key_grad.astype(BF16)
        grad_keys[:, at_k] = value_grad.astype(BF16)
        return carry

    lax.fori_loop(0, HEADS // 2, step, 0, unroll=True)
    grad_norm = grad_partial[...] + nn(grad_keys[...], weight[width:])
    inputs = jnp.concatenate([own_0[:, :width], own_1[:, :width]], 0).astype(F32)
    unit, inverse = norm_parts(inputs)
    out = (grad_middle[...] + norm_back(unit, inverse, gain[...], grad_norm)).astype(BF16)
    back_0[...] = out[:half]
    back_1[...] = out[half:]


def final_part(qkv_a, qkv_b, marks_a, marks_b, grads, own, gain, grad_middle, grad_partial, weight):
    rows, width = grad_middle.shape
    half = rows // 2
    return pl.pallas_call(
        final_kernel,
        in_specs=[vmem()] * 14,
        out_specs=[vmem()] * 2,
        out_shape=[jax.ShapeDtypeStruct((half, width), BF16)] * 2,
        scratch_shapes=[
            pltpu.VMEM((rows, 4 * rows), F32),
            pltpu.VMEM((rows, 2 * width), BF16),
        ],
        compiler_params=pltpu.CompilerParams(vmem_limit_bytes=16 * MIB),
        cost_estimate=pl.CostEstimate(flops=1000, bytes_accessed=1000, transcendentals=0),
        name="final",
    )(qkv_a, qkv_b, marks_a, marks_b, *grads, *own, gain[None], grad_middle, grad_partial, weight)


def routes(k):
    pairs = []
    for seq in range(4):
        for blk in range(8):
            group, z_at, y_at = seq % 2, blk // 2, blk % 2
            row = (z_at + k) % 2
            pairs.append((seq * 8 + blk, (seq - group + z_at // 2) * 8 + (2 * group + row) * 2 + y_at))
    return pairs


def body_rows(
    tokens,
    segment_ids,
    ln1_gain,
    ln1_bias,
    w_qkv,
    w_out,
    ln2_gain,
    ln2_bias,
    w_fc,
    w_proj,
    prefix_embed,
    w_mlp1,
    b_mlp1,
    w_mlp2,
    b_mlp2,
    cotangent,
):
    half, _, width = tokens.shape
    everyone = ("seq", "blk")
    there = [routes(k) for k in range(2)]
    back = [[(b, a) for a, b in pairs] for pairs in there]
    swap_core = [(i, i ^ 1) for i in range(4)]
    swap_y = [(i, i ^ 1) for i in range(8)]
    swap_both = [(i, i ^ 9) for i in range(32)]
    def after(value, *done):
        return lax.optimization_barrier((value, done))[0]

    out_msgs = split_rows(tokens, segment_ids)
    cot_msgs = split_rows(cotangent)
    own = [lax.ppermute(m, everyone, there[k]) for k, m in enumerate(out_msgs)]
    prefix_kv, inner, w_near, w_back, near_embed, turned = adapter_forward(
        prefix_embed, w_mlp1, b_mlp1, w_mlp2, b_mlp2, w_qkv
    )
    count = prefix_embed.shape[0]
    own = after(own, inner)
    across = [lax.ppermute(m, "blk", swap_y) for m in own]
    beside = [lax.ppermute(m, "seq", swap_core) for m in own]
    cots = [lax.ppermute(m, everyone, there[k]) for k, m in enumerate(after(cot_msgs, beside))]
    beyond = [lax.ppermute(m, "seq", swap_core) for m in across]

    qkv_a, marks_a = project(own + beside, ln1_gain, ln1_bias, w_near)
    qkv_b, marks_b = project(across + beyond, ln1_gain, ln1_bias, w_near)
    back_0, back_1, grads, grad_middle = middle_part(
        count, qkv_a, qkv_b, marks_a, marks_b, prefix_kv, own, cots, ln2_gain, ln2_bias, w_out, w_fc, w_proj
    )
    grads_y = lax.ppermute(grads, "blk", swap_y)
    grads_c = lax.ppermute(grads, "seq", swap_core)
    grad_prefix_kv = prefix_part(count, qkv_a, grads, prefix_kv)
    parts = [lax.ppermute(grad_prefix_kv, "seq", [(i, i ^ far) for i in range(4)]) for far in (2, 1, 3)]
    grad_partial = query_part(
        count, qkv_a, qkv_b, marks_a, marks_b, prefix_kv, grads, w_back, grad_prefix_kv
    )
    packed = pack(count, grads, (grad_prefix_kv, *after(parts, grad_partial)), back_0, back_1)
    home = [lax.ppermute(m, everyone, back[k]) for k, m in enumerate(packed)]
    grads_yc = lax.ppermute(after(grads_y, packed), "seq", swap_core)
    final_0, final_1 = final_part(
        qkv_a,
        qkv_b,
        marks_a,
        marks_b,
        (grads, grads_c, grads_y, grads_yc),
        own,
        ln1_gain,
        grad_middle,
        grad_partial,
        w_back,
    )
    finals = [lax.ppermute(m, everyone, back[k]) for k, m in enumerate((final_0, final_1))]
    gathered = [unpack(count, width, *home)]
    gathered += [lax.ppermute(gathered[0], "seq", swap_core), lax.ppermute(gathered[0], "blk", swap_y)]
    gathered += [lax.ppermute(gathered[0], everyone, swap_both)]
    input_grad, summed = finish(finals, gathered, near_embed, inner, turned)
    block_out, log_total = land(count, after(home, final_0), half, width)
    return (block_out, input_grad, summed[0], summed[1], summed[2], summed[3], summed[4], log_total)


def solution(mesh):
    four_by_eight = mesh.shape["seq"] == 4 and mesh.shape["blk"] == 8
    placed = (
        P("blk", "seq", None),
        P("blk", "seq"),
        P(),
        P(),
        P(),
        P(),
        P(),
        P(),
        P(),
        P(),
        P(),
        P(),
        P(),
        P(),
        P(),
        P("blk", "seq", None),
    )
    return jax.shard_map(
        body_rows if four_by_eight else body_plain,
        mesh=mesh,
        in_specs=placed,
        out_specs=(
            P("blk", "seq", None),
            P("blk", "seq", None),
            P(),
            P(),
            P(),
            P(),
            P(),
            P("seq", None, "blk"),
        ),
        check_vma=False,
    )
```

```python
from functools import partial
import math

import jax
import jax.numpy as jnp
from jax import lax
from jax.experimental import pallas as pl
from jax.experimental.pallas import tpu as pltpu
from jax.sharding import PartitionSpec as P

HEADS = 16
HEAD = 64


EPS = 1e-05
NEG = -1e30
HIGH = lax.Precision.HIGHEST


def layer_norm(value_in, gain, bias):
    average = jnp.mean(value_in, axis=-1, keepdims=True)
    centered = value_in - average
    variance = jnp.mean(centered * centered, axis=-1, keepdims=True)
    return centered * lax.rsqrt(variance + EPS) * gain + bias


def adapter(prefix_embed, w_mlp1, b_mlp1, w_mlp2, b_mlp2):
    inner_act = jnp.tanh(jnp.dot(prefix_embed, w_mlp1, precision=HIGH) + b_mlp1)
    return jnp.dot(inner_act, w_mlp2, precision=HIGH) + b_mlp2


def gelu_tanh(pre_act):
    return jax.nn.gelu(pre_act, approximate=True)


def split_heads(block_in):
    return block_in.reshape(block_in.shape[0], block_in.shape[1], HEADS, HEAD)


def allowed(query_pos, query_seg, key_pos, key_seg):
    same_seg = query_seg.T[:, :, None] == key_seg.T[:, None, :]
    causal = key_pos[None, None, :] <= query_pos[None, :, None]
    return jnp.logical_and(same_seg, causal)[:, None]


def scores_of(query_heads, key_block, score_scale):
    return score_scale * jnp.einsum(
        "prhd,krhd->rhpk", query_heads, split_heads(key_block), preferred_element_type=jnp.float32
    )


def block_grads(
    query_heads,
    grad_heads,
    log_total,
    slope_base,
    query_pos,
    query_seg,
    key_block,
    value_block,
    key_pos,
    key_seg,
    score_scale,
):
    scores = scores_of(query_heads, key_block, score_scale)
    scores = jnp.where(allowed(query_pos, query_seg, key_pos, key_seg), scores, NEG)
    weights = jnp.exp(scores - log_total[..., None])
    grad_weights = jnp.einsum(
        "prhd,krhd->rhpk", grad_heads, split_heads(value_block), preferred_element_type=jnp.float32
    )
    slopes = (weights * (grad_weights - slope_base[..., None])).astype(jnp.bfloat16)
    return (weights.astype(jnp.bfloat16), slopes)


def body_plain(
    tokens,
    segment_ids,
    ln1_gain,
    ln1_bias,
    w_qkv,
    w_out,
    ln2_gain,
    ln2_bias,
    w_fc,
    w_proj,
    prefix_embed,
    w_mlp1,
    b_mlp1,
    w_mlp2,
    b_mlp2,
    cotangent,
):
    pos_dev, row_count, width = tokens.shape
    score_scale = HEAD ** (-0.5)
    flat_rows = pos_dev * row_count
    own_pos = lax.axis_index("blk") * pos_dev + jnp.arange(pos_dev)
    inputs = tokens.astype(jnp.float32).reshape(flat_rows, width)
    normed_one = layer_norm(inputs, ln1_gain, ln1_bias).astype(jnp.bfloat16)
    projected = jnp.dot(normed_one, w_qkv, preferred_element_type=jnp.float32).astype(jnp.bfloat16)
    queries = projected[:, :width].reshape(pos_dev, row_count, width)
    keys = projected[:, width : 2 * width].reshape(pos_dev, row_count, width)
    values = projected[:, 2 * width :].reshape(pos_dev, row_count, width)
    query_heads = split_heads(queries)
    prefix_low = adapter(prefix_embed, w_mlp1, b_mlp1, w_mlp2, b_mlp2).astype(jnp.bfloat16)
    prefix_keys = prefix_low[:, :width].reshape(-1, HEADS, HEAD)
    prefix_values = prefix_low[:, width:].reshape(-1, HEADS, HEAD)
    prefix_scores = score_scale * jnp.einsum(
        "prhd,jhd->rhpj", query_heads, prefix_keys, preferred_element_type=jnp.float32
    )
    start_top = jnp.max(prefix_scores, -1)
    start_weights = jnp.exp(prefix_scores - start_top[..., None])
    start_denom = jnp.sum(start_weights, -1)
    start_numer = jnp.einsum(
        "rhpj,jhd->rhpd",
        start_weights.astype(jnp.bfloat16),
        prefix_values,
        preferred_element_type=jnp.float32,
    )
    start_state = (start_top, start_denom, start_numer)
    running = start_state
    key_shards = lax.all_gather(keys, "blk", axis=0, tiled=True)
    value_shards = lax.all_gather(values, "blk", axis=0, tiled=True)
    seg_shards = lax.all_gather(segment_ids, "blk", axis=0, tiled=True)
    num_rows = key_shards.shape[0]
    forward_stride = math.gcd(num_rows, 512)

    def inner(state, block_index):
        running_top, denominator, numerator = state
        offset = block_index * forward_stride
        key_block = lax.dynamic_slice_in_dim(key_shards, offset, forward_stride, 0)
        value_block = lax.dynamic_slice_in_dim(value_shards, offset, forward_stride, 0)
        seg_block = lax.dynamic_slice_in_dim(seg_shards, offset, forward_stride, 0)
        key_pos = offset + jnp.arange(forward_stride)
        scores = jnp.where(
            allowed(own_pos, segment_ids, key_pos, seg_block),
            scores_of(query_heads, key_block, score_scale),
            NEG,
        )
        new_top = jnp.maximum(running_top, jnp.max(scores, -1))
        fading = jnp.exp(running_top - new_top)
        weights = jnp.exp(scores - new_top[..., None])
        denominator = denominator * fading + jnp.sum(weights, -1)
        numerator = numerator * fading[..., None] + jnp.einsum(
            "rhpk,krhd->rhpd",
            weights.astype(jnp.bfloat16),
            split_heads(value_block),
            preferred_element_type=jnp.float32,
        )
        return ((new_top, denominator, numerator), None)

    running, _ = lax.scan(inner, running, jnp.arange(num_rows // forward_stride))
    final_top, final_denom, final_numer = running
    log_total = final_top + jnp.log(final_denom)
    attended = final_numer / final_denom[..., None]
    attended_rows = jnp.transpose(attended, (2, 0, 1, 3)).reshape(flat_rows, width)
    middle = inputs + jnp.dot(
        attended_rows.astype(jnp.bfloat16), w_out, preferred_element_type=jnp.float32
    )
    normed_two = layer_norm(middle, ln2_gain, ln2_bias).astype(jnp.bfloat16)
    hidden_pre = jnp.dot(normed_two, w_fc, preferred_element_type=jnp.float32)
    hidden_act = gelu_tanh(hidden_pre).astype(jnp.bfloat16)
    outputs = middle + jnp.dot(hidden_act, w_proj, preferred_element_type=jnp.float32)
    block_out = outputs.astype(jnp.bfloat16).reshape(pos_dev, row_count, width)
    grad_out = cotangent.reshape(flat_rows, width)
    grad_act = jnp.dot(grad_out, w_proj.T, preferred_element_type=jnp.float32)
    _, gelu_back = jax.vjp(gelu_tanh, hidden_pre)
    grad_pre = gelu_back(grad_act)[0].astype(jnp.bfloat16)
    grad_norm_two = jnp.dot(grad_pre, w_fc.T, preferred_element_type=jnp.float32)
    _, norm_two_back = jax.vjp(partial(layer_norm, gain=ln2_gain, bias=ln2_bias), middle)
    grad_middle = grad_out.astype(jnp.float32) + norm_two_back(grad_norm_two)[0]
    grad_attended = jnp.dot(
        grad_middle.astype(jnp.bfloat16), w_out.T, preferred_element_type=jnp.float32
    ).astype(jnp.bfloat16)
    grad_flat = grad_attended.reshape(pos_dev, row_count, width)
    grad_heads = split_heads(grad_flat)
    slope_base = jnp.sum(jnp.transpose(grad_heads.astype(jnp.float32), (1, 2, 0, 3)) * attended, -1)
    prefix_weights = jnp.exp(prefix_scores - log_total[..., None])
    prefix_dw = jnp.einsum(
        "prhd,jhd->rhpj", grad_heads, prefix_values, preferred_element_type=jnp.float32
    )
    prefix_slopes = (prefix_weights * (prefix_dw - slope_base[..., None])).astype(jnp.bfloat16)
    grad_query = score_scale * jnp.einsum(
        "rhpj,jhd->prhd", prefix_slopes, prefix_keys, preferred_element_type=jnp.float32
    )
    grad_pkeys = score_scale * jnp.einsum(
        "rhpj,prhd->jhd", prefix_slopes, query_heads, preferred_element_type=jnp.float32
    )
    grad_pvalues = jnp.einsum(
        "rhpj,prhd->jhd",
        prefix_weights.astype(jnp.bfloat16),
        grad_heads,
        preferred_element_type=jnp.float32,
    )
    grad_prefix_kv = jnp.concatenate(
        [grad_pkeys.reshape(-1, width), grad_pvalues.reshape(-1, width)], -1
    )
    keys_all, values_all, segs_all = (
        lax.all_gather(keys, "blk", axis=0, tiled=True),
        lax.all_gather(values, "blk", axis=0, tiled=True),
        lax.all_gather(segment_ids, "blk", axis=0, tiled=True),
    )
    length = keys_all.shape[0]
    stride = math.gcd(length, 512)

    def backward_step(grad_q, block_index):
        offset = block_index * stride
        key_block = lax.dynamic_slice_in_dim(keys_all, offset, stride, 0)
        value_block = lax.dynamic_slice_in_dim(values_all, offset, stride, 0)
        seg_block = lax.dynamic_slice_in_dim(segs_all, offset, stride, 0)
        key_pos = offset + jnp.arange(stride)
        weights_low, slopes = block_grads(
            query_heads,
            grad_heads,
            log_total,
            slope_base,
            own_pos,
            segment_ids,
            key_block,
            value_block,
            key_pos,
            seg_block,
            score_scale,
        )
        grad_q = grad_q + score_scale * jnp.einsum(
            "rhpk,krhd->prhd", slopes, split_heads(key_block), preferred_element_type=jnp.float32
        )
        key_term = score_scale * jnp.einsum(
            "rhpk,prhd->krhd", slopes, query_heads, preferred_element_type=jnp.float32
        )
        value_term = jnp.einsum(
            "rhpk,prhd->krhd", weights_low, grad_heads, preferred_element_type=jnp.float32
        )
        return (
            grad_q,
            (
                key_term.reshape(stride, row_count, width),
                value_term.reshape(stride, row_count, width),
            ),
        )

    grad_query, (key_terms, value_terms) = lax.scan(
        backward_step, grad_query, jnp.arange(length // stride)
    )
    key_terms = key_terms.reshape(length, row_count, width)
    value_terms = value_terms.reshape(length, row_count, width)
    grad_keys, grad_values = (
        lax.psum_scatter(key_terms, "blk", scatter_dimension=0, tiled=True),
        lax.psum_scatter(value_terms, "blk", scatter_dimension=0, tiled=True),
    )
    grad_proj = jnp.concatenate(
        [
            grad_query.reshape(flat_rows, width).astype(jnp.bfloat16),
            grad_keys.reshape(flat_rows, width).astype(jnp.bfloat16),
            grad_values.reshape(flat_rows, width).astype(jnp.bfloat16),
        ],
        -1,
    )
    grad_norm_one = jnp.dot(grad_proj, w_qkv.T, preferred_element_type=jnp.float32)
    _, norm_one_back = jax.vjp(partial(layer_norm, gain=ln1_gain, bias=ln1_bias), inputs)
    input_grad = (grad_middle + norm_one_back(grad_norm_one)[0]).reshape(pos_dev, row_count, width)
    _, adapter_back = jax.vjp(adapter, prefix_embed, w_mlp1, b_mlp1, w_mlp2, b_mlp2)
    local_grads = adapter_back(grad_prefix_kv)
    summed = lax.psum(
        (local_grads[0], local_grads[1], local_grads[2], local_grads[3], local_grads[4]),
        ("seq", "blk"),
    )
    return (block_out, input_grad, summed[0], summed[1], summed[2], summed[3], summed[4], log_total)


F32 = jnp.float32
BF16 = jnp.bfloat16
LANES = 128
PRE_ROWS = 16
MIB = 1 << 20


def nn(left, right):
    return jnp.dot(left, right, preferred_element_type=F32)


def nt(left, right):
    return lax.dot_general(left, right, (((1,), (1,)), ((), ())), preferred_element_type=F32)


def norm_parts(value_in):
    average = jnp.mean(value_in, axis=-1, keepdims=True)
    centered = value_in - average
    variance = jnp.mean(centered * centered, axis=-1, keepdims=True)
    inverse = lax.rsqrt(variance + EPS)
    return centered * inverse, inverse


def norm_back(unit, inverse, gain, grad):
    scaled = grad * gain
    first = jnp.mean(scaled, axis=-1, keepdims=True)
    second = jnp.mean(scaled * unit, axis=-1, keepdims=True)
    return inverse * (scaled - first - unit * second)


def iota(shape, dim):
    return lax.broadcasted_iota(jnp.int32, shape, dim)


def place():
    blk = lax.axis_index("blk")
    return (blk // 2) % 2, lax.axis_index("seq") % 2, blk % 2


def positions(index, half, row, core, y_at):
    upper = (index >= half).astype(jnp.int32)
    slot = 1 - (upper + row - 2 * upper * row)
    block = (2 * core + slot) * 2 + y_at
    return block * half + index - upper * half


def members(core, y_at):
    return ((core, y_at), (1 - core, y_at), (core, 1 - y_at), (1 - core, 1 - y_at))


def all_positions(shape, dim, half, row, core, y_at):
    part = tuple(2 * half if d == dim else n for d, n in enumerate(shape))
    return jnp.concatenate(
        [positions(iota(part, dim), half, row, c, y) for c, y in members(core, y_at)], dim
    )


def vmem():
    return pl.BlockSpec(memory_space=pltpu.VMEM)


def hbm():
    return pl.BlockSpec(memory_space=pltpu.HBM)


def kept_in_hbm(*arrays):
    return [pltpu.with_memory_space_constraint(a, pltpu.HBM) for a in arrays]


def by_tiles(block):
    half, pair, width = block.shape
    tiles = jnp.transpose(block.reshape(half, pair, width // LANES, LANES), (0, 2, 1, 3))
    return tiles.reshape(half, pair * width // LANES, LANES)


def from_tiles(tiles, width):
    half, count, _ = tiles.shape
    pair = count * LANES // width
    block = jnp.transpose(tiles.reshape(half, width // LANES, pair, LANES), (0, 2, 1, 3))
    return block.reshape(half, pair, width)


def odd_place():
    return (lax.axis_index("blk") // 2) % 2 == 0


def split_kernel(marked, *refs):
    tokens, ids, (out_0, out_1, work) = refs[0], refs[1], refs[-3:]
    half, count, _ = tokens.shape
    odd = odd_place()
    work[...] = tokens[...].astype(F32).reshape(half * count, LANES)
    for i in range(count // 2):
        at = pl.ds(i * LANES, LANES)
        first, second = (work[pl.ds(2 * i + r, half, stride=count)] for r in range(2))
        out_0[:, at] = jnp.where(odd, second, first).astype(BF16)
        out_1[:, at] = jnp.where(odd, first, second).astype(BF16)
    if marked:
        width = count // 2 * LANES
        first, second = (
            jnp.where(iota((LANES, half), 0) == ids[r : r + 1], 1.0, 0.0).T for r in range(2)
        )
        out_0[:, width:] = jnp.where(odd, second, first).astype(BF16)
        out_1[:, width:] = jnp.where(odd, first, second).astype(BF16)


def split_rows(block, segment_ids=None):
    tiles = by_tiles(block)
    half, count, _ = tiles.shape
    extra = () if segment_ids is None else kept_in_hbm(segment_ids.T)
    width = count // 2 * LANES + LANES * len(extra)
    return pl.pallas_call(
        partial(split_kernel, bool(extra)),
        in_specs=[vmem()] * (1 + len(extra)),
        out_specs=[vmem()] * 2,
        out_shape=[jax.ShapeDtypeStruct((half, width), BF16)] * 2,
        scratch_shapes=[pltpu.VMEM((half * count, LANES), F32)],
        compiler_params=pltpu.CompilerParams(vmem_limit_bytes=4 * MIB),
        cost_estimate=pl.CostEstimate(flops=1 << 31, bytes_accessed=1000, transcendentals=0),
        name="split",
    )(*kept_in_hbm(tiles), *extra)


def place_rows(msg_0, msg_1, work):
    count = 2 * msg_0.shape[1] // LANES
    half = work.shape[0] // count
    odd = odd_place()
    for i in range(count // 2):
        at = pl.ds(i * LANES, LANES)
        one, two = msg_0[:half, at].astype(F32), msg_1[:half, at].astype(F32)
        work[pl.ds(2 * i, half, stride=count)] = jnp.where(odd, two, one)
        work[pl.ds(2 * i + 1, half, stride=count)] = jnp.where(odd, one, two)


def land_kernel(first_row, msg_0, msg_1, out, logs, work):
    half = out.shape[0]
    heads = logs.shape[1]
    place_rows(msg_0, msg_1, work)
    out[...] = work[...].reshape(out.shape).astype(out.dtype)
    odd = odd_place()
    found = []
    for k, message in enumerate((msg_0, msg_1)):
        rows = message[half:].astype(F32)[first_row : first_row + GROUP]
        slots = [rows[:, i * LANES + k * half : i * LANES + (k + 1) * half] for i in range(3 * heads // GROUP)]
        groups = [slots[i] + slots[i + 1] + slots[i + 2] for i in range(0, len(slots), 3)]
        found.append(jnp.concatenate(groups, 0))
    logs[0] = jnp.where(odd, found[1], found[0])
    logs[1] = jnp.where(odd, found[0], found[1])


def land(count_prefix, messages, half, width):
    count = 2 * width // LANES
    out = pl.pallas_call(
        partial(land_kernel, prefix_rows(count_prefix)),
        in_specs=[vmem()] * 2,
        out_specs=[vmem()] * 2,
        out_shape=[
            jax.ShapeDtypeStruct((half, count, LANES), BF16),
            jax.ShapeDtypeStruct((2, HEADS, half), F32),
        ],
        scratch_shapes=[pltpu.VMEM((half * count, LANES), F32)],
        compiler_params=pltpu.CompilerParams(vmem_limit_bytes=4 * MIB),
        cost_estimate=pl.CostEstimate(flops=1000, bytes_accessed=1000, transcendentals=0),
        name="land",
    )(*messages)
    return from_tiles(out[0], width), out[1]


def project_kernel(count, first, *refs):
    messages, (gain, bias, weight, out, marks, normed) = refs[:count], refs[count:]
    half, width = messages[0].shape[0], normed.shape[1]
    for i, message in enumerate(messages):
        rows = pl.ds(i * half, half)
        unit, _ = norm_parts(message[:, :width].astype(F32))
        normed[rows] = (unit * gain[...] + bias[...]).astype(BF16)
        marks[rows] = message[:, width:]
    for i in range(first, 3):
        at = pl.ds(i * width, width)
        out[:, at] = nn(normed[...], weight[:, at]).astype(BF16)


def project(messages, gain, bias, weight, first=0):
    count, half = len(messages), messages[0].shape[0]
    width, columns = weight.shape
    rows = count * half
    return pl.pallas_call(
        partial(project_kernel, count, first),
        in_specs=[vmem()] * (count + 3),
        out_specs=[vmem()] * (2 + first),
        out_shape=[
            jax.ShapeDtypeStruct((rows, columns), BF16),
            jax.ShapeDtypeStruct((rows, LANES), BF16),
        ]
        + [jax.ShapeDtypeStruct((rows, width), BF16)] * first,
        scratch_shapes=[pltpu.VMEM((rows, width), BF16)] * (1 - first),
        compiler_params=pltpu.CompilerParams(vmem_limit_bytes=16 * MIB),
        cost_estimate=pl.CostEstimate(
            flops=2 * rows * width * columns, bytes_accessed=2 * width * columns, transcendentals=0
        ),
        name="project",
    )(*messages, gain[None], bias[None], weight)


def halves(value_in):
    high = value_in.astype(BF16)
    return high, (value_in - high.astype(F32)).astype(BF16)


def pad_rows(value_in, rows):
    if rows == value_in.shape[0]:
        return value_in
    return jnp.concatenate(
        [value_in, jnp.zeros((rows - value_in.shape[0], value_in.shape[1]), value_in.dtype)], 0
    )


def three_products(product, left, weight):
    rows = left.shape[0]
    high, low = halves(left)
    w_high, w_low = halves(weight)
    both = product(jnp.concatenate([high, low], 0), w_high)
    return both[:rows] + both[rows:] + product(high, w_low)


def adapter_kernel(
    h_embed,
    w_mlp1,
    h_mlp1,
    w_mlp2,
    h_mlp2,
    w_qkv,
    out,
    inner,
    v_qkv,
    w_back,
    embed,
    turned,
    v_mlp1,
    v_mlp2,
    b_mlp1,
    b_mlp2,
    sems,
):
    steps, step = v_mlp2.shape[0], v_mlp2.shape[2]
    small = []
    for i, (source, target) in enumerate(
        ((h_embed, embed), (h_mlp1, b_mlp1), (h_mlp2, b_mlp2), (w_mlp1, v_mlp1))
    ):
        small.append(pltpu.make_async_copy(source, target, sems.at[steps + i]))
        small[-1].start()
    width = w_qkv.shape[0]
    weights = []
    for i in range(3):
        at = pl.ds(i * width, width)
        weights.append(
            pltpu.make_async_copy(w_qkv.at[:, at], v_qkv.at[:, at], sems.at[steps + len(small) + i])
        )
        weights[-1].start()
    rest = []
    for i in range(steps):
        copy = pltpu.make_async_copy(w_mlp2.at[:, pl.ds(i * step, step)], v_mlp2.at[i], sems.at[i])
        copy.start()
        rest.append(copy)
    for copy in small:
        copy.wait()
    source = pad_rows(embed[...], PRE_ROWS)
    act = jnp.tanh(three_products(nn, source, v_mlp1[...]) + b_mlp1[...])
    inner[...] = act
    columns, hidden = steps * step, v_mlp1.shape[1]
    for i in range(v_mlp1.shape[0] // hidden):
        part = v_mlp1[pl.ds(i * hidden, hidden)].astype(BF16)
        turned[pl.ds(columns + i * hidden, hidden)] = part.T
    for i, copy in enumerate(weights):
        at = pl.ds(i * width, width)
        copy.wait()
        w_back[at] = v_qkv[:, at].T
    for i, copy in enumerate(rest):
        copy.wait()
        turned[pl.ds(i * step, step)] = v_mlp2[i].astype(BF16).T
        span = pl.ds(i * step, step)
        part = three_products(nn, act, v_mlp2[i]) + b_mlp2[:, span]
        out[:, span] = jnp.where(iota(part.shape, 0) < embed.shape[0], part, 0.0).astype(BF16)


def adapter_forward(embed, w_mlp1, b_mlp1, w_mlp2, b_mlp2, w_qkv):
    width, hidden = w_mlp1.shape
    columns = w_mlp2.shape[1]
    steps = 4
    return pl.pallas_call(
        adapter_kernel,
        in_specs=[hbm()] * 6,
        out_specs=[vmem()] * 6,
        out_shape=[
            jax.ShapeDtypeStruct((PRE_ROWS, columns), BF16),
            jax.ShapeDtypeStruct((PRE_ROWS, hidden), F32),
            pltpu.VMEM(w_qkv.shape, w_qkv.dtype),
            pltpu.VMEM(w_qkv.shape[::-1], w_qkv.dtype),
            pltpu.VMEM(embed.shape, F32),
            pltpu.VMEM((columns + width, hidden), BF16),
        ],
        scratch_shapes=[
            pltpu.VMEM((width, hidden), F32),
            pltpu.VMEM((steps, hidden, columns // steps), F32),
            pltpu.VMEM((1, hidden), F32),
            pltpu.VMEM((1, columns), F32),
            pltpu.SemaphoreType.DMA((7 + steps,)),
        ],
        compiler_params=pltpu.CompilerParams(vmem_limit_bytes=20 * MIB),
        cost_estimate=pl.CostEstimate(flops=1 << 32, bytes_accessed=6 * MIB, transcendentals=1 << 13),
        name="adapter",
    )(*kept_in_hbm(embed, w_mlp1, b_mlp1[None], w_mlp2, b_mlp2[None], w_qkv))


def outer(left, right):
    l_high, l_low = halves(left)
    r_high, r_low = halves(right)
    return lax.dot_general(
        jnp.concatenate([l_high, l_high, l_low], 0),
        jnp.concatenate([r_high, r_low, r_high], 0),
        (((0,), (0,)), ((), ())),
        preferred_element_type=F32,
    )


def two_products(left, weight):
    high, low = halves(left)
    both = nn(jnp.concatenate([high, low], 0), weight)
    return both[: left.shape[0]] + both[left.shape[0] :]


def adapter_back_kernel(
    home_0,
    home_1,
    part_0,
    part_1,
    part_2,
    part_3,
    embed,
    inner,
    turned,
    block,
    grad_prefix,
    grad_mlp1,
    grad_bias1,
    grad_mlp2,
    grad_bias2,
    o_block,
    o_mlp1,
    o_mlp2,
    sems,
):
    steps, step = o_mlp2.shape[0], o_mlp2.shape[2]
    first, second, third, fourth = (p[...].astype(F32) for p in (part_0, part_1, part_2, part_3))
    grads = (first + second) + (third + fourth)
    act = inner[...]
    stores = []
    grad_bias2[...] = jnp.sum(grads, 0, keepdims=True)
    for i in range(steps):
        o_mlp2[i] = outer(act, grads[:, i * step : (i + 1) * step])
        stores.append(
            pltpu.make_async_copy(o_mlp2.at[i], grad_mlp2.at[:, pl.ds(i * step, step)], sems.at[i])
        )
        stores[-1].start()
    columns, (width, hidden) = steps * step, o_mlp1.shape
    place_rows(home_0, home_1, o_block)
    stores.append(pltpu.make_async_copy(o_block, block, sems.at[steps + 1]))
    stores[-1].start()
    back = two_products(grads, turned[:columns]) * (1.0 - act * act)
    grad_bias1[...] = jnp.sum(back, 0, keepdims=True)
    o_mlp1[...] = outer(pad_rows(embed[...], PRE_ROWS), back)
    stores.append(pltpu.make_async_copy(o_mlp1, grad_mlp1, sems.at[steps]))
    stores[-1].start()
    for i in range(width // hidden):
        part = two_products(back, turned[pl.ds(columns + i * hidden, hidden)])
        grad_prefix[:, pl.ds(i * hidden, hidden)] = part[: embed.shape[0]]
    for copy in stores:
        copy.wait()


def finish(finals, parts, embed, inner, turned):
    hidden, width = turned.shape[1], embed.shape[1]
    columns = turned.shape[0] - width
    half = finals[0].shape[0]
    steps = 4
    tiles = 2 * width // LANES
    out = pl.pallas_call(
        adapter_back_kernel,
        in_specs=[vmem()] * 9,
        out_specs=[hbm(), vmem(), hbm(), vmem(), hbm(), vmem()],
        out_shape=[
            jax.ShapeDtypeStruct((half * tiles, LANES), F32),
            jax.ShapeDtypeStruct(embed.shape, F32),
            jax.ShapeDtypeStruct((width, hidden), F32),
            jax.ShapeDtypeStruct((1, hidden), F32),
            jax.ShapeDtypeStruct((hidden, columns), F32),
            jax.ShapeDtypeStruct((1, columns), F32),
        ],
        scratch_shapes=[
            pltpu.VMEM((half * tiles, LANES), F32),
            pltpu.VMEM((width, hidden), F32),
            pltpu.VMEM((steps, hidden, columns // steps), F32),
            pltpu.SemaphoreType.DMA((steps + 2,)),
        ],
        compiler_params=pltpu.CompilerParams(vmem_limit_bytes=16 * MIB),
        cost_estimate=pl.CostEstimate(flops=1000, bytes_accessed=1000, transcendentals=0),
        name="finish",
    )(*finals, *parts, embed, inner, turned)
    block = from_tiles(out[0].reshape(half, tiles, LANES), width)
    return block, (out[1], out[2], out[3][0], out[4], out[5][0])


def head_mask(rows):
    return iota((rows, LANES), 1) < HEAD


def two_heads(pair, low):
    zero = jnp.zeros_like(pair)
    return jnp.concatenate([jnp.where(low, pair, zero), jnp.where(low, zero, pair)], 0)


def join_heads(stacked, low):
    rows = stacked.shape[0] // 2
    return jnp.where(low, stacked[:rows], stacked[rows:])


def picks(rows, pair, first, value):
    lane = iota((rows, LANES), 1)
    inside = jnp.logical_and(lane >= first, lane < first + 3 * HEADS)
    parts = [
        jnp.where(jnp.logical_and(inside, lane % HEADS == 2 * pair + i), value, 0.0) for i in range(2)
    ]
    return jnp.concatenate(parts, 0)


def three_parts(value_in, first):
    lane = iota(value_in.shape, 1)
    high = value_in.astype(BF16).astype(F32)
    rest = value_in - high
    middle = rest.astype(BF16).astype(F32)
    low = rest - middle
    part = (lane - first) // HEADS
    chosen = jnp.where(part == 0, high, jnp.where(part == 1, middle, low))
    inside = jnp.logical_and(lane >= first, lane < first + 3 * HEADS)
    return jnp.where(inside, chosen, 0.0)


def key_bias(marks_own, marks_a, marks_b, half, count):
    row, core, y_at = place()
    rows = 2 * half
    own = positions(iota((rows, 1), 0), half, row, core, y_at)
    other = all_positions((1, 8 * half), 1, half, row, core, y_at)
    same = nt(marks_own, jnp.concatenate([marks_a, marks_b], 0))
    visible = jnp.logical_and(same > 0.5, other <= own)
    token_bias = jnp.where(visible, 0.0, NEG)
    prefix_bias = jnp.where(iota((rows, LANES), 1) < count, 0.0, NEG)
    return jnp.concatenate([token_bias, prefix_bias], 1)


def with_prefix(part_a, part_b, prefix):
    pad = jnp.zeros((LANES - prefix.shape[0], prefix.shape[1]), prefix.dtype)
    return jnp.concatenate([part_a, part_b, prefix, pad], 0)


def middle_kernel(
    count,
    qkv_a,
    qkv_b,
    marks_a,
    marks_b,
    prefix_kv,
    own_0,
    own_1,
    cot_0,
    cot_1,
    gain,
    bias,
    w_out,
    w_fc,
    w_proj,
    back_0,
    back_1,
    grad_out_heads,
    grad_middle,
    v_out,
    v_fc,
    v_proj,
    sems,
    scores_bias,
    attended,
    stats,
    middle,
    normed,
    total,
    grad_norm,
    cot,
):
    half, rows = own_0.shape[0], 2 * own_0.shape[0]
    width = middle.shape[1]
    steps, step = v_fc.shape[0], v_fc.shape[2]
    copies = [pltpu.make_async_copy(w_out, v_out, sems.at[0])]
    for i in range(steps):
        span = pl.ds(i * step, step)
        copies.append(pltpu.make_async_copy(w_fc.at[:, span], v_fc.at[i], sems.at[1 + 2 * i]))
        copies.append(pltpu.make_async_copy(w_proj.at[span], v_proj.at[i], sems.at[2 + 2 * i]))
    for copy in copies:
        copy.start()

    scores_bias[...] = key_bias(marks_a[:rows], marks_a[...], marks_b[...], half, count)
    low = head_mask(rows)
    lane = iota((rows, LANES), 1)
    stats[...] = jnp.zeros_like(stats)

    def attend(pair, carry):
        at = pl.ds(pl.multiple_of(pair * LANES, LANES), LANES)
        at_k = pl.ds(pl.multiple_of(width + pair * LANES, LANES), LANES)
        at_v = pl.ds(pl.multiple_of(2 * width + pair * LANES, LANES), LANES)
        query = two_heads(qkv_a[:rows, at] * jnp.asarray(HEAD**-0.5, BF16), low)
        keys = with_prefix(qkv_a[:, at_k], qkv_b[:, at_k], prefix_kv[:, at])
        values = with_prefix(qkv_a[:, at_v], qkv_b[:, at_v], prefix_kv[:, at_k])
        scores = nt(query, keys)
        mask = scores_bias[...]
        scores = scores + jnp.concatenate([mask, mask], 0)
        top = jnp.max(scores, -1, keepdims=True)
        weights = jnp.exp(scores - top)
        denominator = jnp.sum(weights, -1, keepdims=True)
        mixed = nn(weights.astype(BF16), values) / denominator
        attended[:, at] = join_heads(mixed, low)
        log_total = top + jnp.log(denominator)
        inside = lane < 3 * HEADS
        for i in range(2):
            here = jnp.logical_and(inside, lane % HEADS == 2 * pair + i)
            stats[...] = jnp.where(here, log_total[i * rows : (i + 1) * rows], stats[...])
        return carry

    lax.fori_loop(0, HEADS // 2, attend, 0, unroll=4)

    copies[0].wait()
    inputs = jnp.concatenate([own_0[:, :width], own_1[:, :width]], 0).astype(F32)
    middle[...] = inputs + nn(attended[...].astype(BF16), v_out[...])
    unit, _ = norm_parts(middle[...])
    normed[...] = (unit * gain[...] + bias[...]).astype(BF16)
    cot[...] = jnp.concatenate([cot_0[...], cot_1[...]], 0)
    total[...] = middle[...]
    grad_norm[...] = jnp.zeros_like(grad_norm)

    def feed(i, carry):
        for which in (0, 1):
            pltpu.make_async_copy(
                (v_fc, v_proj)[which].at[i], (v_fc, v_proj)[which].at[i], sems.at[1 + 2 * i + which]
            ).wait()
        fc, proj = v_fc[i], v_proj[i]
        pre = nn(normed[...], fc)
        grad_act = nt(cot[...], proj)
        cubic = 0.044715 * pre * pre
        curve = jnp.tanh(math.sqrt(2 / math.pi) * pre * (1.0 + cubic))
        act = 0.5 * pre * (1.0 + curve)
        slope = 0.5 * (1.0 + curve) + 0.5 * math.sqrt(2 / math.pi) * pre * (1.0 - curve * curve) * (
            1.0 + 3.0 * cubic
        )
        grad_pre = (grad_act * slope).astype(BF16)
        total[...] += nn(act.astype(BF16), proj)
        grad_norm[...] += nt(grad_pre, fc)
        return carry

    lax.fori_loop(0, steps, feed, 0, unroll=True)

    out = total[...].astype(BF16)
    back_0[:half] = out[:half]
    back_1[:half] = out[half:]
    unit, inverse = norm_parts(middle[...])
    grads = cot[...].astype(F32) + norm_back(unit, inverse, gain[...], grad_norm[...])
    grad_middle[...] = grads
    grad_heads = nt(grads.astype(BF16), v_out[...]).astype(BF16)
    grad_out_heads[:, :width] = grad_heads
    product = grad_heads.astype(F32) * attended[...]
    ones = jnp.where(
        jnp.logical_and(
            iota((width, LANES), 0) // HEAD == iota((width, LANES), 1) % HEADS,
            jnp.logical_and(
                iota((width, LANES), 1) >= 3 * HEADS, iota((width, LANES), 1) < 6 * HEADS
            ),
        ),
        1.0,
        0.0,
    ).astype(BF16)
    bases = jnp.zeros((rows, LANES), F32)
    for _ in range(2):
        part = product.astype(BF16)
        bases = bases + nn(part, ones)
        product = product - part.astype(F32)
    marks = three_parts(stats[...], 0) + three_parts(bases, 3 * HEADS)
    marks = marks.astype(BF16)
    grad_out_heads[:, width:] = marks


def middle_part(count, qkv_a, qkv_b, marks_a, marks_b, prefix_kv, own, cots, gain, bias, w_out, w_fc, w_proj):
    half, width = cots[0].shape
    rows = 2 * half
    hidden = w_fc.shape[1]
    steps = 2
    step = hidden // steps
    wide = width + LANES
    return pl.pallas_call(
        partial(middle_kernel, count),
        in_specs=[vmem()] * 11 + [hbm()] * 3,
        out_specs=[vmem()] * 4,
        out_shape=[
            jax.ShapeDtypeStruct((half + tail_rows(count), width), BF16),
            jax.ShapeDtypeStruct((half + tail_rows(count), width), BF16),
            jax.ShapeDtypeStruct((rows, wide), BF16),
            jax.ShapeDtypeStruct((rows, width), F32),
        ],
        scratch_shapes=[
            pltpu.VMEM((width, width), BF16),
            pltpu.VMEM((steps, width, step), BF16),
            pltpu.VMEM((steps, step, width), BF16),
            pltpu.SemaphoreType.DMA((1 + 2 * steps,)),
            pltpu.VMEM((rows, 4 * rows + LANES), F32),
            pltpu.VMEM((rows, width), F32),
            pltpu.VMEM((rows, LANES), F32),
            pltpu.VMEM((rows, width), F32),
            pltpu.VMEM((rows, width), BF16),
            pltpu.VMEM((rows, width), F32),
            pltpu.VMEM((rows, width), F32),
            pltpu.VMEM((rows, width), BF16),
        ],
        compiler_params=pltpu.CompilerParams(vmem_limit_bytes=36 * MIB),
        cost_estimate=pl.CostEstimate(flops=1 << 31, bytes_accessed=1000, transcendentals=0),
        name="middle",
    )(
        qkv_a, qkv_b, marks_a, marks_b, prefix_kv, *own, *cots, gain[None], bias[None], *kept_in_hbm(w_out, w_fc, w_proj)
    )


def key_grads(keys, values, queries, grads, turned_marks, pair, low, mask):
    rows = keys.shape[0]
    scale = jnp.asarray(HEAD**-0.5, BF16)
    left = jnp.concatenate(
        [two_heads(keys * scale, low), picks(rows, pair, 0, -1.0).astype(BF16)], 1
    )
    scores = nn(left, jnp.concatenate([queries.T, turned_marks], 0))
    weights = jnp.exp(scores + jnp.concatenate([mask, mask], 0))
    left = jnp.concatenate(
        [two_heads(values, low), picks(rows, pair, 3 * HEADS, -1.0).astype(BF16)], 1
    )
    slopes = weights * nn(left, jnp.concatenate([grads.T, turned_marks], 0))
    key_grad = nn(slopes.astype(BF16), queries)
    value_grad = nn(weights.astype(BF16), grads)
    return join_heads(key_grad, low) * HEAD**-0.5, join_heads(value_grad, low)


GROUP = 8


def prefix_rows(count):
    return -(-2 * count // GROUP) * GROUP


def tail_rows(count):
    return -(-(prefix_rows(count) + GROUP) // PRE_ROWS) * PRE_ROWS


def prefix_kernel(used, queries, grads, prefix_kv, out):
    count, rows, width = prefix_kv.shape[0], grads.shape[0], grads.shape[1] - LANES
    marks = grads[:, width:].T
    low = head_mask(count)
    mask = jnp.where(iota((count, rows), 0) < used, 0.0, NEG)

    def step(pair, carry):
        at = pl.ds(pl.multiple_of(pair * LANES, LANES), LANES)
        at_v = pl.ds(pl.multiple_of(width + pair * LANES, LANES), LANES)
        key_grad, value_grad = key_grads(
            prefix_kv[:, at], prefix_kv[:, at_v], queries[:rows, at], grads[:, at], marks, pair, low, mask
        )
        out[:, at] = key_grad.astype(BF16)
        out[:, at_v] = value_grad.astype(BF16)
        return carry

    lax.fori_loop(0, HEADS // 2, step, 0, unroll=True)


def prefix_part(count, qkv_a, grads, prefix_kv):
    return pl.pallas_call(
        partial(prefix_kernel, count),
        in_specs=[vmem()] * 3,
        out_specs=vmem(),
        out_shape=jax.ShapeDtypeStruct(prefix_kv.shape, BF16),
        compiler_params=pltpu.CompilerParams(vmem_limit_bytes=8 * MIB),
        cost_estimate=pl.CostEstimate(flops=1000, bytes_accessed=1000, transcendentals=0),
        name="prefix",
    )(qkv_a, grads, prefix_kv)


def pack_kernel(count, grads, own, part_0, part_1, part_2, _0, _1, back_0, back_1):
    total = own[...].astype(F32) + part_0[...].astype(F32)
    total = total + (part_1[...].astype(F32) + part_2[...].astype(F32))
    width = total.shape[1] // 2
    rows = tail_rows(count)
    both = jnp.concatenate([total[:count, :width], total[:count, width:]], 0)
    marks = grads[:, width:].astype(F32).T
    starts = [part * HEADS + first for first in range(0, HEADS, GROUP) for part in range(3)]
    logs = jnp.concatenate([marks[i : i + GROUP] for i in starts], 1)
    logs = jnp.concatenate([logs, jnp.zeros((GROUP, width - logs.shape[1]), F32)], 1)
    tail = pad_rows(jnp.concatenate([pad_rows(both, prefix_rows(count)), logs], 0), rows).astype(BF16)
    at = pl.ds(back_0.shape[0] - rows, rows)
    back_0[at] = tail
    back_1[at] = tail


def pack(count, grads, terms, back_0, back_1):
    return pl.pallas_call(
        partial(pack_kernel, count),
        in_specs=[vmem()] * 7,
        out_specs=[vmem()] * 2,
        out_shape=[jax.ShapeDtypeStruct(back_0.shape, BF16)] * 2,
        input_output_aliases={5: 0, 6: 1},
        compiler_params=pltpu.CompilerParams(vmem_limit_bytes=4 * MIB),
        cost_estimate=pl.CostEstimate(flops=1 << 20, bytes_accessed=1 << 19, transcendentals=0),
        name="pack",
    )(grads, *terms, back_0, back_1)


def unpack_kernel(count, home_0, home_1, out):
    width = out.shape[1] // 2
    rows = tail_rows(count)
    at = pl.ds(home_0.shape[0] - rows, rows)
    first, second = home_0[at].astype(F32), home_1[at].astype(F32)
    total = first + second
    out[:, :width] = pad_rows(total[:count], PRE_ROWS).astype(BF16)
    out[:, width:] = pad_rows(total[count : 2 * count], PRE_ROWS).astype(BF16)


def unpack(count, width, home_0, home_1):
    return pl.pallas_call(
        partial(unpack_kernel, count),
        in_specs=[vmem()] * 2,
        out_specs=vmem(),
        out_shape=jax.ShapeDtypeStruct((PRE_ROWS, 2 * width), BF16),
        compiler_params=pltpu.CompilerParams(vmem_limit_bytes=4 * MIB),
        cost_estimate=pl.CostEstimate(flops=1000, bytes_accessed=1000, transcendentals=0),
        name="unpack",
    )(home_0, home_1)


def query_kernel(
    count,
    qkv_a,
    qkv_b,
    marks_a,
    marks_b,
    prefix_kv,
    grads,
    weight,
    normed_b,
    w_queries,
    order,
    out,
    qkv_out,
    scores_bias,
    grad_query,
):
    del order
    rows, width = grad_query.shape
    scores_bias[...] = key_bias(marks_a[:rows], marks_a[...], marks_b[...], rows // 2, count)
    low = head_mask(rows)
    marks = grads[:, width:]
    marks_twice = jnp.concatenate([marks, marks], 0)
    ones = jnp.ones((LANES, 4 * rows + LANES), BF16)

    def step(pair, carry):
        at = pl.ds(pl.multiple_of(pair * LANES, LANES), LANES)
        at_k = pl.ds(pl.multiple_of(width + pair * LANES, LANES), LANES)
        at_v = pl.ds(pl.multiple_of(2 * width + pair * LANES, LANES), LANES)
        keys = with_prefix(qkv_a[:, at_k], qkv_b[:, at_k], prefix_kv[:, at])
        values = with_prefix(qkv_a[:, at_v], qkv_b[:, at_v], prefix_kv[:, at_k])
        query = two_heads(qkv_a[:rows, at] * jnp.asarray(HEAD**-0.5, BF16), low)
        tops = marks_twice * picks(rows, pair, 0, -1.0).astype(BF16)
        scores = nn(jnp.concatenate([query, tops], 1), jnp.concatenate([keys.T, ones], 0))
        mask = scores_bias[...]
        weights = jnp.exp(scores + jnp.concatenate([mask, mask], 0))
        bases = marks_twice * picks(rows, pair, 3 * HEADS, -1.0).astype(BF16)
        left = jnp.concatenate([two_heads(grads[:, at], low), bases], 1)
        slopes = weights * nn(left, jnp.concatenate([values.T, ones], 0))
        grad = join_heads(nn(slopes.astype(BF16), keys), low)
        grad_query[:, at] = (grad * HEAD**-0.5).astype(BF16)
        return carry

    lax.fori_loop(0, HEADS // 2, step, 0, unroll=True)
    out[...] = nn(grad_query[...], weight[:width])
    qkv_out[:, :width] = nn(normed_b[...], w_queries[:, :width]).astype(BF16)


def query_part(
    count, qkv_a, qkv_b, marks_a, marks_b, prefix_kv, grads, weight, normed_b, w_queries, order
):
    rows, width = grads.shape[0], grads.shape[1] - LANES
    return pl.pallas_call(
        partial(query_kernel, count),
        in_specs=[vmem()] * 9 + [pl.BlockSpec(memory_space=pl.ANY)],
        out_specs=[vmem()] * 2,
        out_shape=[jax.ShapeDtypeStruct((rows, width), F32), jax.ShapeDtypeStruct(qkv_b.shape, BF16)],
        input_output_aliases={1: 1},
        scratch_shapes=[pltpu.VMEM((rows, 4 * rows + LANES), F32), pltpu.VMEM((rows, width), BF16)],
        compiler_params=pltpu.CompilerParams(vmem_limit_bytes=16 * MIB),
        cost_estimate=pl.CostEstimate(flops=1 << 31, bytes_accessed=1000, transcendentals=0),
        name="query",
    )(qkv_a, qkv_b, marks_a, marks_b, prefix_kv, grads, weight, normed_b, w_queries, order)


def final_kernel(
    qkv_a,
    qkv_b,
    marks_a,
    marks_b,
    grads_0,
    grads_1,
    grads_2,
    grads_3,
    own_0,
    own_1,
    gain,
    grad_middle,
    grad_partial,
    weight,
    back_0,
    back_1,
    scores_bias,
    grad_keys,
):
    half, rows = own_0.shape[0], 2 * own_0.shape[0]
    width = grad_middle.shape[1]
    row, core, y_at = place()
    own = positions(iota((rows, 1), 0), half, row, core, y_at)
    other = all_positions((1, 8 * half), 1, half, row, core, y_at)
    same = nt(marks_a[:rows], jnp.concatenate([marks_a[...], marks_b[...]], 0))
    visible = jnp.logical_and(same > 0.5, own <= other)
    scores_bias[...] = jnp.where(visible, 0.0, NEG)
    low = head_mask(rows)
    blocks = (grads_0, grads_1, grads_2, grads_3)
    marks = jnp.concatenate([g[:, width:] for g in blocks], 0).T

    def step(pair, carry):
        at = pl.ds(pl.multiple_of(pair * LANES, LANES), LANES)
        at_k = pl.ds(pl.multiple_of(width + pair * LANES, LANES), LANES)
        at_v = pl.ds(pl.multiple_of(2 * width + pair * LANES, LANES), LANES)
        queries = jnp.concatenate([qkv_a[:, at], qkv_b[:, at]], 0)
        grads = jnp.concatenate([g[:, at] for g in blocks], 0)
        key_grad, value_grad = key_grads(
            qkv_a[:rows, at_k], qkv_a[:rows, at_v], queries, grads, marks, pair, low, scores_bias[...]
        )
        grad_keys[:, at] = key_grad.astype(BF16)
        grad_keys[:, at_k] = value_grad.astype(BF16)
        return carry

    lax.fori_loop(0, HEADS // 2, step, 0, unroll=True)
    grad_norm = grad_partial[...] + nn(grad_keys[...], weight[width:])
    inputs = jnp.concatenate([own_0[:, :width], own_1[:, :width]], 0).astype(F32)
    unit, inverse = norm_parts(inputs)
    out = (grad_middle[...] + norm_back(unit, inverse, gain[...], grad_norm)).astype(BF16)
    back_0[...] = out[:half]
    back_1[...] = out[half:]


def final_part(qkv_a, qkv_b, marks_a, marks_b, grads, own, gain, grad_middle, grad_partial, weight):
    rows, width = grad_middle.shape
    half = rows // 2
    return pl.pallas_call(
        final_kernel,
        in_specs=[vmem()] * 14,
        out_specs=[vmem()] * 2,
        out_shape=[jax.ShapeDtypeStruct((half, width), BF16)] * 2,
        scratch_shapes=[
            pltpu.VMEM((rows, 4 * rows), F32),
            pltpu.VMEM((rows, 2 * width), BF16),
        ],
        compiler_params=pltpu.CompilerParams(vmem_limit_bytes=16 * MIB),
        cost_estimate=pl.CostEstimate(flops=1000, bytes_accessed=1000, transcendentals=0),
        name="final",
    )(qkv_a, qkv_b, marks_a, marks_b, *grads, *own, gain[None], grad_middle, grad_partial, weight)


def routes(k):
    pairs = []
    for seq in range(4):
        for blk in range(8):
            group, z_at, y_at = seq % 2, blk // 2, blk % 2
            row = (z_at + k + 1) % 2
            pairs.append((seq * 8 + blk, (seq - group + z_at // 2) * 8 + (2 * group + row) * 2 + y_at))
    return pairs


def body_rows(
    tokens,
    segment_ids,
    ln1_gain,
    ln1_bias,
    w_qkv,
    w_out,
    ln2_gain,
    ln2_bias,
    w_fc,
    w_proj,
    prefix_embed,
    w_mlp1,
    b_mlp1,
    w_mlp2,
    b_mlp2,
    cotangent,
):
    half, _, width = tokens.shape
    everyone = ("seq", "blk")
    there = [routes(k) for k in range(2)]
    back = [[(b, a) for a, b in pairs] for pairs in there]
    swap_core = [(i, i ^ 1) for i in range(4)]
    swap_y = [(i, i ^ 1) for i in range(8)]
    swap_both = [(i, i ^ 9) for i in range(32)]
    def after(value, *done):
        return lax.optimization_barrier((value, done))[0]

    out_msgs = split_rows(tokens, segment_ids)
    cot_msgs = split_rows(cotangent)
    own = [lax.ppermute(m, everyone, there[k]) for k, m in enumerate(out_msgs)]
    prefix_kv, inner, w_near, w_back, near_embed, turned = adapter_forward(
        prefix_embed, w_mlp1, b_mlp1, w_mlp2, b_mlp2, w_qkv
    )
    count = prefix_embed.shape[0]
    own = after(own, inner)
    across = [lax.ppermute(m, "blk", swap_y) for m in own]
    beside = [lax.ppermute(m, "seq", swap_core) for m in own]
    cots = [lax.ppermute(m, everyone, there[k]) for k, m in enumerate(after(cot_msgs, beside))]
    beyond = [lax.ppermute(m, "seq", swap_core) for m in across]

    qkv_a, marks_a = project(own + beside, ln1_gain, ln1_bias, w_near)
    kv_b, marks_b, normed_b = project(across + beyond, ln1_gain, ln1_bias, w_near, 1)
    back_0, back_1, grads, grad_middle = middle_part(
        count, qkv_a, kv_b, marks_a, marks_b, prefix_kv, own, cots, ln2_gain, ln2_bias, w_out, w_fc, w_proj
    )
    grads_y = lax.ppermute(grads, "blk", swap_y)
    grads_c = lax.ppermute(grads, "seq", swap_core)
    grad_prefix_kv = prefix_part(count, qkv_a, grads, prefix_kv)
    parts = [lax.ppermute(grad_prefix_kv, "seq", [(i, i ^ far) for i in range(4)]) for far in (2, 1, 3)]
    grad_partial, qkv_b = query_part(
        count, qkv_a, kv_b, marks_a, marks_b, prefix_kv, grads, w_back, normed_b, w_near, grad_prefix_kv
    )
    packed = pack(count, grads, (grad_prefix_kv, *after(parts, grad_partial)), back_0, back_1)
    home = [lax.ppermute(m, everyone, back[k]) for k, m in enumerate(packed)]
    grads_yc = lax.ppermute(after(grads_y, packed), "seq", swap_core)
    final_0, final_1 = final_part(
        qkv_a,
        qkv_b,
        marks_a,
        marks_b,
        (grads, grads_c, grads_y, grads_yc),
        own,
        ln1_gain,
        grad_middle,
        grad_partial,
        w_back,
    )
    finals = [lax.ppermute(m, everyone, back[k]) for k, m in enumerate((final_0, final_1))]
    gathered = [unpack(count, width, *home)]
    gathered += [lax.ppermute(gathered[0], "seq", swap_core), lax.ppermute(gathered[0], "blk", swap_y)]
    gathered += [lax.ppermute(gathered[0], everyone, swap_both)]
    input_grad, summed = finish(finals, gathered, near_embed, inner, turned)
    block_out, log_total = land(count, after(home, final_0), half, width)
    return (block_out, input_grad, summed[0], summed[1], summed[2], summed[3], summed[4], log_total)


def solution(mesh):
    four_by_eight = mesh.shape["seq"] == 4 and mesh.shape["blk"] == 8
    placed = (
        P("blk", "seq", None),
        P("blk", "seq"),
        P(),
        P(),
        P(),
        P(),
        P(),
        P(),
        P(),
        P(),
        P(),
        P(),
        P(),
        P(),
        P(),
        P("blk", "seq", None),
    )
    return jax.shard_map(
        body_rows if four_by_eight else body_plain,
        mesh=mesh,
        in_specs=placed,
        out_specs=(
            P("blk", "seq", None),
            P("blk", "seq", None),
            P(),
            P(),
            P(),
            P(),
            P(),
            P("seq", None, "blk"),
        ),
        check_vma=False,
    )
```

```python
from functools import partial
import math

import jax
import jax.numpy as jnp
from jax import lax
from jax.experimental import pallas as pl
from jax.experimental.pallas import tpu as pltpu
from jax.sharding import PartitionSpec as P

HEADS = 16
HEAD = 64


EPS = 1e-05
NEG = -1e30
HIGH = lax.Precision.HIGHEST


def layer_norm(value_in, gain, bias):
    average = jnp.mean(value_in, axis=-1, keepdims=True)
    centered = value_in - average
    variance = jnp.mean(centered * centered, axis=-1, keepdims=True)
    return centered * lax.rsqrt(variance + EPS) * gain + bias


def adapter(prefix_embed, w_mlp1, b_mlp1, w_mlp2, b_mlp2):
    inner_act = jnp.tanh(jnp.dot(prefix_embed, w_mlp1, precision=HIGH) + b_mlp1)
    return jnp.dot(inner_act, w_mlp2, precision=HIGH) + b_mlp2


def gelu_tanh(pre_act):
    return jax.nn.gelu(pre_act, approximate=True)


def split_heads(block_in):
    return block_in.reshape(block_in.shape[0], block_in.shape[1], HEADS, HEAD)


def allowed(query_pos, query_seg, key_pos, key_seg):
    same_seg = query_seg.T[:, :, None] == key_seg.T[:, None, :]
    causal = key_pos[None, None, :] <= query_pos[None, :, None]
    return jnp.logical_and(same_seg, causal)[:, None]


def scores_of(query_heads, key_block, score_scale):
    return score_scale * jnp.einsum(
        "prhd,krhd->rhpk", query_heads, split_heads(key_block), preferred_element_type=jnp.float32
    )


def block_grads(
    query_heads,
    grad_heads,
    log_total,
    slope_base,
    query_pos,
    query_seg,
    key_block,
    value_block,
    key_pos,
    key_seg,
    score_scale,
):
    scores = scores_of(query_heads, key_block, score_scale)
    scores = jnp.where(allowed(query_pos, query_seg, key_pos, key_seg), scores, NEG)
    weights = jnp.exp(scores - log_total[..., None])
    grad_weights = jnp.einsum(
        "prhd,krhd->rhpk", grad_heads, split_heads(value_block), preferred_element_type=jnp.float32
    )
    slopes = (weights * (grad_weights - slope_base[..., None])).astype(jnp.bfloat16)
    return (weights.astype(jnp.bfloat16), slopes)


def body_plain(
    tokens,
    segment_ids,
    ln1_gain,
    ln1_bias,
    w_qkv,
    w_out,
    ln2_gain,
    ln2_bias,
    w_fc,
    w_proj,
    prefix_embed,
    w_mlp1,
    b_mlp1,
    w_mlp2,
    b_mlp2,
    cotangent,
):
    pos_dev, row_count, width = tokens.shape
    score_scale = HEAD ** (-0.5)
    flat_rows = pos_dev * row_count
    own_pos = lax.axis_index("blk") * pos_dev + jnp.arange(pos_dev)
    inputs = tokens.astype(jnp.float32).reshape(flat_rows, width)
    normed_one = layer_norm(inputs, ln1_gain, ln1_bias).astype(jnp.bfloat16)
    projected = jnp.dot(normed_one, w_qkv, preferred_element_type=jnp.float32).astype(jnp.bfloat16)
    queries = projected[:, :width].reshape(pos_dev, row_count, width)
    keys = projected[:, width : 2 * width].reshape(pos_dev, row_count, width)
    values = projected[:, 2 * width :].reshape(pos_dev, row_count, width)
    query_heads = split_heads(queries)
    prefix_low = adapter(prefix_embed, w_mlp1, b_mlp1, w_mlp2, b_mlp2).astype(jnp.bfloat16)
    prefix_keys = prefix_low[:, :width].reshape(-1, HEADS, HEAD)
    prefix_values = prefix_low[:, width:].reshape(-1, HEADS, HEAD)
    prefix_scores = score_scale * jnp.einsum(
        "prhd,jhd->rhpj", query_heads, prefix_keys, preferred_element_type=jnp.float32
    )
    start_top = jnp.max(prefix_scores, -1)
    start_weights = jnp.exp(prefix_scores - start_top[..., None])
    start_denom = jnp.sum(start_weights, -1)
    start_numer = jnp.einsum(
        "rhpj,jhd->rhpd",
        start_weights.astype(jnp.bfloat16),
        prefix_values,
        preferred_element_type=jnp.float32,
    )
    start_state = (start_top, start_denom, start_numer)
    running = start_state
    key_shards = lax.all_gather(keys, "blk", axis=0, tiled=True)
    value_shards = lax.all_gather(values, "blk", axis=0, tiled=True)
    seg_shards = lax.all_gather(segment_ids, "blk", axis=0, tiled=True)
    num_rows = key_shards.shape[0]
    forward_stride = math.gcd(num_rows, 512)

    def inner(state, block_index):
        running_top, denominator, numerator = state
        offset = block_index * forward_stride
        key_block = lax.dynamic_slice_in_dim(key_shards, offset, forward_stride, 0)
        value_block = lax.dynamic_slice_in_dim(value_shards, offset, forward_stride, 0)
        seg_block = lax.dynamic_slice_in_dim(seg_shards, offset, forward_stride, 0)
        key_pos = offset + jnp.arange(forward_stride)
        scores = jnp.where(
            allowed(own_pos, segment_ids, key_pos, seg_block),
            scores_of(query_heads, key_block, score_scale),
            NEG,
        )
        new_top = jnp.maximum(running_top, jnp.max(scores, -1))
        fading = jnp.exp(running_top - new_top)
        weights = jnp.exp(scores - new_top[..., None])
        denominator = denominator * fading + jnp.sum(weights, -1)
        numerator = numerator * fading[..., None] + jnp.einsum(
            "rhpk,krhd->rhpd",
            weights.astype(jnp.bfloat16),
            split_heads(value_block),
            preferred_element_type=jnp.float32,
        )
        return ((new_top, denominator, numerator), None)

    running, _ = lax.scan(inner, running, jnp.arange(num_rows // forward_stride))
    final_top, final_denom, final_numer = running
    log_total = final_top + jnp.log(final_denom)
    attended = final_numer / final_denom[..., None]
    attended_rows = jnp.transpose(attended, (2, 0, 1, 3)).reshape(flat_rows, width)
    middle = inputs + jnp.dot(
        attended_rows.astype(jnp.bfloat16), w_out, preferred_element_type=jnp.float32
    )
    normed_two = layer_norm(middle, ln2_gain, ln2_bias).astype(jnp.bfloat16)
    hidden_pre = jnp.dot(normed_two, w_fc, preferred_element_type=jnp.float32)
    hidden_act = gelu_tanh(hidden_pre).astype(jnp.bfloat16)
    outputs = middle + jnp.dot(hidden_act, w_proj, preferred_element_type=jnp.float32)
    block_out = outputs.astype(jnp.bfloat16).reshape(pos_dev, row_count, width)
    grad_out = cotangent.reshape(flat_rows, width)
    grad_act = jnp.dot(grad_out, w_proj.T, preferred_element_type=jnp.float32)
    _, gelu_back = jax.vjp(gelu_tanh, hidden_pre)
    grad_pre = gelu_back(grad_act)[0].astype(jnp.bfloat16)
    grad_norm_two = jnp.dot(grad_pre, w_fc.T, preferred_element_type=jnp.float32)
    _, norm_two_back = jax.vjp(partial(layer_norm, gain=ln2_gain, bias=ln2_bias), middle)
    grad_middle = grad_out.astype(jnp.float32) + norm_two_back(grad_norm_two)[0]
    grad_attended = jnp.dot(
        grad_middle.astype(jnp.bfloat16), w_out.T, preferred_element_type=jnp.float32
    ).astype(jnp.bfloat16)
    grad_flat = grad_attended.reshape(pos_dev, row_count, width)
    grad_heads = split_heads(grad_flat)
    slope_base = jnp.sum(jnp.transpose(grad_heads.astype(jnp.float32), (1, 2, 0, 3)) * attended, -1)
    prefix_weights = jnp.exp(prefix_scores - log_total[..., None])
    prefix_dw = jnp.einsum(
        "prhd,jhd->rhpj", grad_heads, prefix_values, preferred_element_type=jnp.float32
    )
    prefix_slopes = (prefix_weights * (prefix_dw - slope_base[..., None])).astype(jnp.bfloat16)
    grad_query = score_scale * jnp.einsum(
        "rhpj,jhd->prhd", prefix_slopes, prefix_keys, preferred_element_type=jnp.float32
    )
    grad_pkeys = score_scale * jnp.einsum(
        "rhpj,prhd->jhd", prefix_slopes, query_heads, preferred_element_type=jnp.float32
    )
    grad_pvalues = jnp.einsum(
        "rhpj,prhd->jhd",
        prefix_weights.astype(jnp.bfloat16),
        grad_heads,
        preferred_element_type=jnp.float32,
    )
    grad_prefix_kv = jnp.concatenate(
        [grad_pkeys.reshape(-1, width), grad_pvalues.reshape(-1, width)], -1
    )
    keys_all, values_all, segs_all = (
        lax.all_gather(keys, "blk", axis=0, tiled=True),
        lax.all_gather(values, "blk", axis=0, tiled=True),
        lax.all_gather(segment_ids, "blk", axis=0, tiled=True),
    )
    length = keys_all.shape[0]
    stride = math.gcd(length, 512)

    def backward_step(grad_q, block_index):
        offset = block_index * stride
        key_block = lax.dynamic_slice_in_dim(keys_all, offset, stride, 0)
        value_block = lax.dynamic_slice_in_dim(values_all, offset, stride, 0)
        seg_block = lax.dynamic_slice_in_dim(segs_all, offset, stride, 0)
        key_pos = offset + jnp.arange(stride)
        weights_low, slopes = block_grads(
            query_heads,
            grad_heads,
            log_total,
            slope_base,
            own_pos,
            segment_ids,
            key_block,
            value_block,
            key_pos,
            seg_block,
            score_scale,
        )
        grad_q = grad_q + score_scale * jnp.einsum(
            "rhpk,krhd->prhd", slopes, split_heads(key_block), preferred_element_type=jnp.float32
        )
        key_term = score_scale * jnp.einsum(
            "rhpk,prhd->krhd", slopes, query_heads, preferred_element_type=jnp.float32
        )
        value_term = jnp.einsum(
            "rhpk,prhd->krhd", weights_low, grad_heads, preferred_element_type=jnp.float32
        )
        return (
            grad_q,
            (
                key_term.reshape(stride, row_count, width),
                value_term.reshape(stride, row_count, width),
            ),
        )

    grad_query, (key_terms, value_terms) = lax.scan(
        backward_step, grad_query, jnp.arange(length // stride)
    )
    key_terms = key_terms.reshape(length, row_count, width)
    value_terms = value_terms.reshape(length, row_count, width)
    grad_keys, grad_values = (
        lax.psum_scatter(key_terms, "blk", scatter_dimension=0, tiled=True),
        lax.psum_scatter(value_terms, "blk", scatter_dimension=0, tiled=True),
    )
    grad_proj = jnp.concatenate(
        [
            grad_query.reshape(flat_rows, width).astype(jnp.bfloat16),
            grad_keys.reshape(flat_rows, width).astype(jnp.bfloat16),
            grad_values.reshape(flat_rows, width).astype(jnp.bfloat16),
        ],
        -1,
    )
    grad_norm_one = jnp.dot(grad_proj, w_qkv.T, preferred_element_type=jnp.float32)
    _, norm_one_back = jax.vjp(partial(layer_norm, gain=ln1_gain, bias=ln1_bias), inputs)
    input_grad = (grad_middle + norm_one_back(grad_norm_one)[0]).reshape(pos_dev, row_count, width)
    _, adapter_back = jax.vjp(adapter, prefix_embed, w_mlp1, b_mlp1, w_mlp2, b_mlp2)
    local_grads = adapter_back(grad_prefix_kv)
    summed = lax.psum(
        (local_grads[0], local_grads[1], local_grads[2], local_grads[3], local_grads[4]),
        ("seq", "blk"),
    )
    return (block_out, input_grad, summed[0], summed[1], summed[2], summed[3], summed[4], log_total)


F32 = jnp.float32
BF16 = jnp.bfloat16
LANES = 128
PRE_ROWS = 16
MIB = 1 << 20


def nn(left, right):
    return jnp.dot(left, right, preferred_element_type=F32)


def nt(left, right):
    return lax.dot_general(left, right, (((1,), (1,)), ((), ())), preferred_element_type=F32)


def norm_parts(value_in):
    average = jnp.mean(value_in, axis=-1, keepdims=True)
    centered = value_in - average
    variance = jnp.mean(centered * centered, axis=-1, keepdims=True)
    inverse = lax.rsqrt(variance + EPS)
    return centered * inverse, inverse


def norm_back(unit, inverse, gain, grad):
    scaled = grad * gain
    first = jnp.mean(scaled, axis=-1, keepdims=True)
    second = jnp.mean(scaled * unit, axis=-1, keepdims=True)
    return inverse * (scaled - first - unit * second)


def iota(shape, dim):
    return lax.broadcasted_iota(jnp.int32, shape, dim)


def place():
    blk = lax.axis_index("blk")
    return (blk // 2) % 2, lax.axis_index("seq") % 2, blk % 2


def positions(index, half, row, core, y_at):
    upper = (index >= half).astype(jnp.int32)
    slot = 1 - (upper + row - 2 * upper * row)
    block = (2 * core + slot) * 2 + y_at
    return block * half + index - upper * half


def members(core, y_at):
    return ((core, y_at), (1 - core, y_at), (core, 1 - y_at), (1 - core, 1 - y_at))


def all_positions(shape, dim, half, row, core, y_at):
    part = tuple(2 * half if d == dim else n for d, n in enumerate(shape))
    return jnp.concatenate(
        [positions(iota(part, dim), half, row, c, y) for c, y in members(core, y_at)], dim
    )


def vmem():
    return pl.BlockSpec(memory_space=pltpu.VMEM)


def hbm():
    return pl.BlockSpec(memory_space=pltpu.HBM)


def kept_in_hbm(*arrays):
    return [pltpu.with_memory_space_constraint(a, pltpu.HBM) for a in arrays]


def by_tiles(block):
    half, pair, width = block.shape
    tiles = jnp.transpose(block.reshape(half, pair, width // LANES, LANES), (0, 2, 1, 3))
    return tiles.reshape(half, pair * width // LANES, LANES)


def from_tiles(tiles, width):
    half, count, _ = tiles.shape
    pair = count * LANES // width
    block = jnp.transpose(tiles.reshape(half, width // LANES, pair, LANES), (0, 2, 1, 3))
    return block.reshape(half, pair, width)


def odd_place():
    return (lax.axis_index("blk") // 2) % 2 == 0


def split_kernel(marked, *refs):
    tokens, ids, (out_0, out_1, work) = refs[0], refs[1], refs[-3:]
    half, count, _ = tokens.shape
    odd = odd_place()
    work[...] = tokens[...].astype(F32).reshape(half * count, LANES)
    for i in range(count // 2):
        at = pl.ds(i * LANES, LANES)
        first, second = (work[pl.ds(2 * i + r, half, stride=count)] for r in range(2))
        out_0[:, at] = jnp.where(odd, second, first).astype(BF16)
        out_1[:, at] = jnp.where(odd, first, second).astype(BF16)
    if marked:
        width = count // 2 * LANES
        first, second = (
            jnp.where(iota((LANES, half), 0) == ids[r : r + 1], 1.0, 0.0).T for r in range(2)
        )
        out_0[:, width:] = jnp.where(odd, second, first).astype(BF16)
        out_1[:, width:] = jnp.where(odd, first, second).astype(BF16)


def split_rows(block, segment_ids=None):
    tiles = by_tiles(block)
    half, count, _ = tiles.shape
    extra = () if segment_ids is None else kept_in_hbm(segment_ids.T)
    width = count // 2 * LANES + LANES * len(extra)
    return pl.pallas_call(
        partial(split_kernel, bool(extra)),
        in_specs=[vmem()] * (1 + len(extra)),
        out_specs=[vmem()] * 2,
        out_shape=[jax.ShapeDtypeStruct((half, width), BF16)] * 2,
        scratch_shapes=[pltpu.VMEM((half * count, LANES), F32)],
        compiler_params=pltpu.CompilerParams(vmem_limit_bytes=4 * MIB),
        cost_estimate=pl.CostEstimate(flops=1 << 31, bytes_accessed=1000, transcendentals=0),
        name="split",
    )(*kept_in_hbm(tiles), *extra)


def place_rows(msg_0, msg_1, work):
    count = 2 * msg_0.shape[1] // LANES
    half = work.shape[0] // count
    odd = odd_place()
    for i in range(count // 2):
        at = pl.ds(i * LANES, LANES)
        one, two = msg_0[:half, at].astype(F32), msg_1[:half, at].astype(F32)
        work[pl.ds(2 * i, half, stride=count)] = jnp.where(odd, two, one)
        work[pl.ds(2 * i + 1, half, stride=count)] = jnp.where(odd, one, two)


def land_kernel(first_row, msg_0, msg_1, out, logs, work):
    half = out.shape[0]
    heads = logs.shape[1]
    place_rows(msg_0, msg_1, work)
    out[...] = work[...].reshape(out.shape).astype(out.dtype)
    odd = odd_place()
    found = []
    for k, message in enumerate((msg_0, msg_1)):
        rows = message[half:].astype(F32)[first_row : first_row + GROUP]
        slots = [rows[:, i * LANES + k * half : i * LANES + (k + 1) * half] for i in range(3 * heads // GROUP)]
        groups = [slots[i] + slots[i + 1] + slots[i + 2] for i in range(0, len(slots), 3)]
        found.append(jnp.concatenate(groups, 0))
    logs[0] = jnp.where(odd, found[1], found[0])
    logs[1] = jnp.where(odd, found[0], found[1])


def land(count_prefix, messages, half, width):
    count = 2 * width // LANES
    out = pl.pallas_call(
        partial(land_kernel, prefix_rows(count_prefix)),
        in_specs=[vmem()] * 2,
        out_specs=[vmem()] * 2,
        out_shape=[
            jax.ShapeDtypeStruct((half, count, LANES), BF16),
            jax.ShapeDtypeStruct((2, HEADS, half), F32),
        ],
        scratch_shapes=[pltpu.VMEM((half * count, LANES), F32)],
        compiler_params=pltpu.CompilerParams(vmem_limit_bytes=4 * MIB),
        cost_estimate=pl.CostEstimate(flops=1000, bytes_accessed=1000, transcendentals=0),
        name="land",
    )(*messages)
    return from_tiles(out[0], width), out[1]


def project_kernel(count, first, *refs):
    messages, (gain, bias, weight, out, marks, normed) = refs[:count], refs[count:]
    half, width = messages[0].shape[0], normed.shape[1]
    for i, message in enumerate(messages):
        rows = pl.ds(i * half, half)
        unit, _ = norm_parts(message[:, :width].astype(F32))
        normed[rows] = (unit * gain[...] + bias[...]).astype(BF16)
        marks[rows] = message[:, width:]
    for i in range(first, 3):
        at = pl.ds(i * width, width)
        out[:, at] = nn(normed[...], weight[:, at]).astype(BF16)


def project(messages, gain, bias, weight, first=0):
    count, half = len(messages), messages[0].shape[0]
    width, columns = weight.shape
    rows = count * half
    return pl.pallas_call(
        partial(project_kernel, count, first),
        in_specs=[vmem()] * (count + 3),
        out_specs=[vmem()] * (2 + first),
        out_shape=[
            jax.ShapeDtypeStruct((rows, columns), BF16),
            jax.ShapeDtypeStruct((rows, LANES), BF16),
        ]
        + [jax.ShapeDtypeStruct((rows, width), BF16)] * first,
        scratch_shapes=[pltpu.VMEM((rows, width), BF16)] * (1 - first),
        compiler_params=pltpu.CompilerParams(vmem_limit_bytes=16 * MIB),
        cost_estimate=pl.CostEstimate(
            flops=2 * rows * width * columns, bytes_accessed=2 * width * columns, transcendentals=0
        ),
        name="project",
    )(*messages, gain[None], bias[None], weight)


def halves(value_in):
    high = value_in.astype(BF16)
    return high, (value_in - high.astype(F32)).astype(BF16)


def pad_rows(value_in, rows):
    if rows == value_in.shape[0]:
        return value_in
    return jnp.concatenate(
        [value_in, jnp.zeros((rows - value_in.shape[0], value_in.shape[1]), value_in.dtype)], 0
    )


def three_products(product, left, weight):
    rows = left.shape[0]
    high, low = halves(left)
    w_high, w_low = halves(weight)
    both = product(jnp.concatenate([high, low], 0), w_high)
    return both[:rows] + both[rows:] + product(high, w_low)


def adapter_kernel(
    h_embed,
    w_mlp1,
    h_mlp1,
    w_mlp2,
    h_mlp2,
    w_qkv,
    out,
    inner,
    v_qkv,
    w_back,
    embed,
    turned,
    v_mlp1,
    v_mlp2,
    b_mlp1,
    b_mlp2,
    sems,
):
    steps, step = v_mlp2.shape[0], v_mlp2.shape[2]
    small = []
    for i, (source, target) in enumerate(
        ((h_embed, embed), (h_mlp1, b_mlp1), (h_mlp2, b_mlp2), (w_mlp1, v_mlp1))
    ):
        small.append(pltpu.make_async_copy(source, target, sems.at[steps + i]))
        small[-1].start()
    width = w_qkv.shape[0]
    weights = []
    for i in range(3):
        at = pl.ds(i * width, width)
        weights.append(
            pltpu.make_async_copy(w_qkv.at[:, at], v_qkv.at[:, at], sems.at[steps + len(small) + i])
        )
        weights[-1].start()
    rest = []
    for i in range(steps):
        copy = pltpu.make_async_copy(w_mlp2.at[:, pl.ds(i * step, step)], v_mlp2.at[i], sems.at[i])
        copy.start()
        rest.append(copy)
    for copy in small:
        copy.wait()
    source = pad_rows(embed[...], PRE_ROWS)
    act = jnp.tanh(three_products(nn, source, v_mlp1[...]) + b_mlp1[...])
    inner[...] = act
    columns, hidden = steps * step, v_mlp1.shape[1]
    for i in range(v_mlp1.shape[0] // hidden):
        part = v_mlp1[pl.ds(i * hidden, hidden)].astype(BF16)
        turned[pl.ds(columns + i * hidden, hidden)] = part.T
    for i, copy in enumerate(weights):
        at = pl.ds(i * width, width)
        copy.wait()
        w_back[at] = v_qkv[:, at].T
    for i, copy in enumerate(rest):
        copy.wait()
        turned[pl.ds(i * step, step)] = v_mlp2[i].astype(BF16).T
        span = pl.ds(i * step, step)
        part = three_products(nn, act, v_mlp2[i]) + b_mlp2[:, span]
        out[:, span] = jnp.where(iota(part.shape, 0) < embed.shape[0], part, 0.0).astype(BF16)


def adapter_forward(embed, w_mlp1, b_mlp1, w_mlp2, b_mlp2, w_qkv):
    width, hidden = w_mlp1.shape
    columns = w_mlp2.shape[1]
    steps = 4
    return pl.pallas_call(
        adapter_kernel,
        in_specs=[hbm()] * 6,
        out_specs=[vmem()] * 6,
        out_shape=[
            jax.ShapeDtypeStruct((PRE_ROWS, columns), BF16),
            jax.ShapeDtypeStruct((PRE_ROWS, hidden), F32),
            pltpu.VMEM(w_qkv.shape, w_qkv.dtype),
            pltpu.VMEM(w_qkv.shape[::-1], w_qkv.dtype),
            pltpu.VMEM(embed.shape, F32),
            pltpu.VMEM((columns + width, hidden), BF16),
        ],
        scratch_shapes=[
            pltpu.VMEM((width, hidden), F32),
            pltpu.VMEM((steps, hidden, columns // steps), F32),
            pltpu.VMEM((1, hidden), F32),
            pltpu.VMEM((1, columns), F32),
            pltpu.SemaphoreType.DMA((7 + steps,)),
        ],
        compiler_params=pltpu.CompilerParams(vmem_limit_bytes=20 * MIB),
        cost_estimate=pl.CostEstimate(flops=1 << 32, bytes_accessed=6 * MIB, transcendentals=1 << 13),
        name="adapter",
    )(*kept_in_hbm(embed, w_mlp1, b_mlp1[None], w_mlp2, b_mlp2[None], w_qkv))


def outer(left, right):
    l_high, l_low = halves(left)
    r_high, r_low = halves(right)
    return lax.dot_general(
        jnp.concatenate([l_high, l_high, l_low], 0),
        jnp.concatenate([r_high, r_low, r_high], 0),
        (((0,), (0,)), ((), ())),
        preferred_element_type=F32,
    )


def two_products(left, weight):
    high, low = halves(left)
    both = nn(jnp.concatenate([high, low], 0), weight)
    return both[: left.shape[0]] + both[left.shape[0] :]


def adapter_back_kernel(
    home_0,
    home_1,
    part_0,
    part_1,
    part_2,
    part_3,
    embed,
    inner,
    turned,
    block,
    grad_prefix,
    grad_mlp1,
    grad_bias1,
    grad_mlp2,
    grad_bias2,
    o_block,
    o_mlp1,
    o_mlp2,
    sems,
):
    steps, step = o_mlp2.shape[0], o_mlp2.shape[2]
    first, second, third, fourth = (p[...].astype(F32) for p in (part_0, part_1, part_2, part_3))
    grads = (first + second) + (third + fourth)
    act = inner[...]
    stores = []
    grad_bias2[...] = jnp.sum(grads, 0, keepdims=True)
    for i in range(steps):
        o_mlp2[i] = outer(act, grads[:, i * step : (i + 1) * step])
        stores.append(
            pltpu.make_async_copy(o_mlp2.at[i], grad_mlp2.at[:, pl.ds(i * step, step)], sems.at[i])
        )
        stores[-1].start()
    columns, (width, hidden) = steps * step, o_mlp1.shape
    place_rows(home_0, home_1, o_block)
    stores.append(pltpu.make_async_copy(o_block, block, sems.at[steps + 1]))
    stores[-1].start()
    back = two_products(grads, turned[:columns]) * (1.0 - act * act)
    grad_bias1[...] = jnp.sum(back, 0, keepdims=True)
    o_mlp1[...] = outer(pad_rows(embed[...], PRE_ROWS), back)
    stores.append(pltpu.make_async_copy(o_mlp1, grad_mlp1, sems.at[steps]))
    stores[-1].start()
    for i in range(width // hidden):
        part = two_products(back, turned[pl.ds(columns + i * hidden, hidden)])
        grad_prefix[:, pl.ds(i * hidden, hidden)] = part[: embed.shape[0]]
    for copy in stores:
        copy.wait()


def finish(finals, parts, embed, inner, turned):
    hidden, width = turned.shape[1], embed.shape[1]
    columns = turned.shape[0] - width
    half = finals[0].shape[0]
    steps = 4
    tiles = 2 * width // LANES
    out = pl.pallas_call(
        adapter_back_kernel,
        in_specs=[vmem()] * 9,
        out_specs=[hbm(), vmem(), hbm(), vmem(), hbm(), vmem()],
        out_shape=[
            jax.ShapeDtypeStruct((half * tiles, LANES), F32),
            jax.ShapeDtypeStruct(embed.shape, F32),
            jax.ShapeDtypeStruct((width, hidden), F32),
            jax.ShapeDtypeStruct((1, hidden), F32),
            jax.ShapeDtypeStruct((hidden, columns), F32),
            jax.ShapeDtypeStruct((1, columns), F32),
        ],
        scratch_shapes=[
            pltpu.VMEM((half * tiles, LANES), F32),
            pltpu.VMEM((width, hidden), F32),
            pltpu.VMEM((steps, hidden, columns // steps), F32),
            pltpu.SemaphoreType.DMA((steps + 2,)),
        ],
        compiler_params=pltpu.CompilerParams(vmem_limit_bytes=16 * MIB),
        cost_estimate=pl.CostEstimate(flops=1000, bytes_accessed=1000, transcendentals=0),
        name="finish",
    )(*finals, *parts, embed, inner, turned)
    block = from_tiles(out[0].reshape(half, tiles, LANES), width)
    return block, (out[1], out[2], out[3][0], out[4], out[5][0])


def head_mask(rows):
    return iota((rows, LANES), 1) < HEAD


def two_heads(pair, low):
    zero = jnp.zeros_like(pair)
    return jnp.concatenate([jnp.where(low, pair, zero), jnp.where(low, zero, pair)], 0)


def join_heads(stacked, low):
    rows = stacked.shape[0] // 2
    return jnp.where(low, stacked[:rows], stacked[rows:])


def picks(rows, pair, first, value):
    lane = iota((rows, LANES), 1)
    inside = jnp.logical_and(lane >= first, lane < first + 3 * HEADS)
    parts = [
        jnp.where(jnp.logical_and(inside, lane % HEADS == 2 * pair + i), value, 0.0) for i in range(2)
    ]
    return jnp.concatenate(parts, 0)


def three_parts(value_in, first):
    lane = iota(value_in.shape, 1)
    high = value_in.astype(BF16).astype(F32)
    rest = value_in - high
    middle = rest.astype(BF16).astype(F32)
    low = rest - middle
    part = (lane - first) // HEADS
    chosen = jnp.where(part == 0, high, jnp.where(part == 1, middle, low))
    inside = jnp.logical_and(lane >= first, lane < first + 3 * HEADS)
    return jnp.where(inside, chosen, 0.0)


def key_bias(marks_own, marks_a, marks_b, half, count):
    row, core, y_at = place()
    rows = 2 * half
    own = positions(iota((rows, 1), 0), half, row, core, y_at)
    other = all_positions((1, 8 * half), 1, half, row, core, y_at)
    same = nt(marks_own, jnp.concatenate([marks_a, marks_b], 0))
    visible = jnp.logical_and(same > 0.5, other <= own)
    token_bias = jnp.where(visible, 0.0, NEG)
    prefix_bias = jnp.where(iota((rows, LANES), 1) < count, 0.0, NEG)
    return jnp.concatenate([token_bias, prefix_bias], 1)


def with_prefix(part_a, part_b, prefix):
    pad = jnp.zeros((LANES - prefix.shape[0], prefix.shape[1]), prefix.dtype)
    return jnp.concatenate([part_a, part_b, prefix, pad], 0)


def middle_kernel(
    count,
    qkv_a,
    qkv_b,
    marks_a,
    marks_b,
    prefix_kv,
    own_0,
    own_1,
    cot_0,
    cot_1,
    gain,
    bias,
    w_out,
    w_fc,
    w_proj,
    back_0,
    back_1,
    grad_out_heads,
    grad_middle,
    v_out,
    v_fc,
    v_proj,
    sems,
    scores_bias,
    attended,
    stats,
    middle,
    normed,
    total,
    grad_norm,
    cot,
):
    half, rows = own_0.shape[0], 2 * own_0.shape[0]
    width = middle.shape[1]
    steps, step = v_fc.shape[0], v_fc.shape[2]
    copies = [pltpu.make_async_copy(w_out, v_out, sems.at[0])]
    for i in range(steps):
        span = pl.ds(i * step, step)
        copies.append(pltpu.make_async_copy(w_fc.at[:, span], v_fc.at[i], sems.at[1 + 2 * i]))
        copies.append(pltpu.make_async_copy(w_proj.at[span], v_proj.at[i], sems.at[2 + 2 * i]))
    for copy in copies:
        copy.start()

    scores_bias[...] = key_bias(marks_a[:rows], marks_a[...], marks_b[...], half, count)
    low = head_mask(rows)
    lane = iota((rows, LANES), 1)
    stats[...] = jnp.zeros_like(stats)

    def attend(pair, carry):
        at = pl.ds(pl.multiple_of(pair * LANES, LANES), LANES)
        at_k = pl.ds(pl.multiple_of(width + pair * LANES, LANES), LANES)
        at_v = pl.ds(pl.multiple_of(2 * width + pair * LANES, LANES), LANES)
        query = two_heads(qkv_a[:rows, at] * jnp.asarray(HEAD**-0.5, BF16), low)
        keys = with_prefix(qkv_a[:, at_k], qkv_b[:, at_k], prefix_kv[:, at])
        values = with_prefix(qkv_a[:, at_v], qkv_b[:, at_v], prefix_kv[:, at_k])
        scores = nt(query, keys)
        mask = scores_bias[...]
        scores = scores + jnp.concatenate([mask, mask], 0)
        top = jnp.max(scores, -1, keepdims=True)
        weights = jnp.exp(scores - top)
        denominator = jnp.sum(weights, -1, keepdims=True)
        mixed = nn(weights.astype(BF16), values) / denominator
        attended[:, at] = join_heads(mixed, low)
        log_total = top + jnp.log(denominator)
        inside = lane < 3 * HEADS
        for i in range(2):
            here = jnp.logical_and(inside, lane % HEADS == 2 * pair + i)
            stats[...] = jnp.where(here, log_total[i * rows : (i + 1) * rows], stats[...])
        return carry

    lax.fori_loop(0, HEADS // 2, attend, 0, unroll=4)

    copies[0].wait()
    inputs = jnp.concatenate([own_0[:, :width], own_1[:, :width]], 0).astype(F32)
    middle[...] = inputs + nn(attended[...].astype(BF16), v_out[...])
    unit, _ = norm_parts(middle[...])
    normed[...] = (unit * gain[...] + bias[...]).astype(BF16)
    cot[...] = jnp.concatenate([cot_0[...], cot_1[...]], 0)
    total[...] = middle[...]
    grad_norm[...] = jnp.zeros_like(grad_norm)

    def feed(i, carry):
        for which in (0, 1):
            pltpu.make_async_copy(
                (v_fc, v_proj)[which].at[i], (v_fc, v_proj)[which].at[i], sems.at[1 + 2 * i + which]
            ).wait()
        fc, proj = v_fc[i], v_proj[i]
        pre = nn(normed[...], fc)
        grad_act = nt(cot[...], proj)
        cubic = 0.044715 * pre * pre
        curve = jnp.tanh(math.sqrt(2 / math.pi) * pre * (1.0 + cubic))
        act = 0.5 * pre * (1.0 + curve)
        slope = 0.5 * (1.0 + curve) + 0.5 * math.sqrt(2 / math.pi) * pre * (1.0 - curve * curve) * (
            1.0 + 3.0 * cubic
        )
        grad_pre = (grad_act * slope).astype(BF16)
        total[...] += nn(act.astype(BF16), proj)
        grad_norm[...] += nt(grad_pre, fc)
        return carry

    lax.fori_loop(0, steps, feed, 0, unroll=True)

    out = total[...].astype(BF16)
    back_0[:half] = out[:half]
    back_1[:half] = out[half:]
    unit, inverse = norm_parts(middle[...])
    grads = cot[...].astype(F32) + norm_back(unit, inverse, gain[...], grad_norm[...])
    grad_middle[...] = grads
    grad_heads = nt(grads.astype(BF16), v_out[...]).astype(BF16)
    grad_out_heads[:, :width] = grad_heads
    product = grad_heads.astype(F32) * attended[...]
    ones = jnp.where(
        jnp.logical_and(
            iota((width, LANES), 0) // HEAD == iota((width, LANES), 1) % HEADS,
            jnp.logical_and(
                iota((width, LANES), 1) >= 3 * HEADS, iota((width, LANES), 1) < 6 * HEADS
            ),
        ),
        1.0,
        0.0,
    ).astype(BF16)
    bases = jnp.zeros((rows, LANES), F32)
    for _ in range(2):
        part = product.astype(BF16)
        bases = bases + nn(part, ones)
        product = product - part.astype(F32)
    marks = three_parts(stats[...], 0) + three_parts(bases, 3 * HEADS)
    marks = marks.astype(BF16)
    grad_out_heads[:, width:] = marks


def middle_part(count, qkv_a, qkv_b, marks_a, marks_b, prefix_kv, own, cots, gain, bias, w_out, w_fc, w_proj):
    half, width = cots[0].shape
    rows = 2 * half
    hidden = w_fc.shape[1]
    steps = 2
    step = hidden // steps
    wide = width + LANES
    return pl.pallas_call(
        partial(middle_kernel, count),
        in_specs=[vmem()] * 11 + [hbm()] * 3,
        out_specs=[vmem()] * 4,
        out_shape=[
            jax.ShapeDtypeStruct((half + tail_rows(count), width), BF16),
            jax.ShapeDtypeStruct((half + tail_rows(count), width), BF16),
            jax.ShapeDtypeStruct((rows, wide), BF16),
            jax.ShapeDtypeStruct((rows, width), F32),
        ],
        scratch_shapes=[
            pltpu.VMEM((width, width), BF16),
            pltpu.VMEM((steps, width, step), BF16),
            pltpu.VMEM((steps, step, width), BF16),
            pltpu.SemaphoreType.DMA((1 + 2 * steps,)),
            pltpu.VMEM((rows, 4 * rows + LANES), F32),
            pltpu.VMEM((rows, width), F32),
            pltpu.VMEM((rows, LANES), F32),
            pltpu.VMEM((rows, width), F32),
            pltpu.VMEM((rows, width), BF16),
            pltpu.VMEM((rows, width), F32),
            pltpu.VMEM((rows, width), F32),
            pltpu.VMEM((rows, width), BF16),
        ],
        compiler_params=pltpu.CompilerParams(vmem_limit_bytes=36 * MIB),
        cost_estimate=pl.CostEstimate(flops=1 << 31, bytes_accessed=1000, transcendentals=0),
        name="middle",
    )(
        qkv_a, qkv_b, marks_a, marks_b, prefix_kv, *own, *cots, gain[None], bias[None], *kept_in_hbm(w_out, w_fc, w_proj)
    )


def key_grads(keys, values, queries, grads, turned_marks, pair, low, mask):
    rows = keys.shape[0]
    scale = jnp.asarray(HEAD**-0.5, BF16)
    left = jnp.concatenate(
        [two_heads(keys * scale, low), picks(rows, pair, 0, -1.0).astype(BF16)], 1
    )
    scores = nn(left, jnp.concatenate([queries.T, turned_marks], 0))
    weights = jnp.exp(scores + jnp.concatenate([mask, mask], 0))
    left = jnp.concatenate(
        [two_heads(values, low), picks(rows, pair, 3 * HEADS, -1.0).astype(BF16)], 1
    )
    slopes = weights * nn(left, jnp.concatenate([grads.T, turned_marks], 0))
    key_grad = nn(slopes.astype(BF16), queries)
    value_grad = nn(weights.astype(BF16), grads)
    return join_heads(key_grad, low) * HEAD**-0.5, join_heads(value_grad, low)


GROUP = 8


def prefix_rows(count):
    return -(-2 * count // GROUP) * GROUP


def tail_rows(count):
    return -(-(prefix_rows(count) + GROUP) // PRE_ROWS) * PRE_ROWS


def prefix_kernel(used, queries, grads, prefix_kv, out):
    count, rows, width = prefix_kv.shape[0], grads.shape[0], grads.shape[1] - LANES
    marks = grads[:, width:].T
    low = head_mask(count)
    mask = jnp.where(iota((count, rows), 0) < used, 0.0, NEG)

    def step(pair, carry):
        at = pl.ds(pl.multiple_of(pair * LANES, LANES), LANES)
        at_v = pl.ds(pl.multiple_of(width + pair * LANES, LANES), LANES)
        key_grad, value_grad = key_grads(
            prefix_kv[:, at], prefix_kv[:, at_v], queries[:rows, at], grads[:, at], marks, pair, low, mask
        )
        out[:, at] = key_grad.astype(BF16)
        out[:, at_v] = value_grad.astype(BF16)
        return carry

    lax.fori_loop(0, HEADS // 2, step, 0, unroll=True)


def prefix_part(count, qkv_a, grads, prefix_kv):
    return pl.pallas_call(
        partial(prefix_kernel, count),
        in_specs=[vmem()] * 3,
        out_specs=vmem(),
        out_shape=jax.ShapeDtypeStruct(prefix_kv.shape, BF16),
        compiler_params=pltpu.CompilerParams(vmem_limit_bytes=8 * MIB),
        cost_estimate=pl.CostEstimate(flops=1000, bytes_accessed=1000, transcendentals=0),
        name="prefix",
    )(qkv_a, grads, prefix_kv)


def pack_kernel(count, grads, own, part_0, part_1, part_2, _0, _1, back_0, back_1):
    total = own[...].astype(F32) + part_0[...].astype(F32)
    total = total + (part_1[...].astype(F32) + part_2[...].astype(F32))
    width = total.shape[1] // 2
    rows = tail_rows(count)
    both = jnp.concatenate([total[:count, :width], total[:count, width:]], 0)
    marks = grads[:, width:].astype(F32).T
    starts = [part * HEADS + first for first in range(0, HEADS, GROUP) for part in range(3)]
    logs = jnp.concatenate([marks[i : i + GROUP] for i in starts], 1)
    logs = jnp.concatenate([logs, jnp.zeros((GROUP, width - logs.shape[1]), F32)], 1)
    tail = pad_rows(jnp.concatenate([pad_rows(both, prefix_rows(count)), logs], 0), rows).astype(BF16)
    at = pl.ds(back_0.shape[0] - rows, rows)
    back_0[at] = tail
    back_1[at] = tail


def pack(count, grads, terms, back_0, back_1):
    return pl.pallas_call(
        partial(pack_kernel, count),
        in_specs=[vmem()] * 7,
        out_specs=[vmem()] * 2,
        out_shape=[jax.ShapeDtypeStruct(back_0.shape, BF16)] * 2,
        input_output_aliases={5: 0, 6: 1},
        compiler_params=pltpu.CompilerParams(vmem_limit_bytes=4 * MIB),
        cost_estimate=pl.CostEstimate(flops=1 << 20, bytes_accessed=1 << 19, transcendentals=0),
        name="pack",
    )(grads, *terms, back_0, back_1)


def unpack_kernel(count, home_0, home_1, out):
    width = out.shape[1] // 2
    rows = tail_rows(count)
    at = pl.ds(home_0.shape[0] - rows, rows)
    first, second = home_0[at].astype(F32), home_1[at].astype(F32)
    total = first + second
    out[:, :width] = pad_rows(total[:count], PRE_ROWS).astype(BF16)
    out[:, width:] = pad_rows(total[count : 2 * count], PRE_ROWS).astype(BF16)


def unpack(count, width, home_0, home_1):
    return pl.pallas_call(
        partial(unpack_kernel, count),
        in_specs=[vmem()] * 2,
        out_specs=vmem(),
        out_shape=jax.ShapeDtypeStruct((PRE_ROWS, 2 * width), BF16),
        compiler_params=pltpu.CompilerParams(vmem_limit_bytes=4 * MIB),
        cost_estimate=pl.CostEstimate(flops=1000, bytes_accessed=1000, transcendentals=0),
        name="unpack",
    )(home_0, home_1)


def query_kernel(
    count,
    qkv_a,
    qkv_b,
    marks_a,
    marks_b,
    prefix_kv,
    grads,
    weight,
    normed_b,
    w_queries,
    order,
    out,
    qkv_out,
    scores_bias,
    grad_query,
):
    del order
    rows, width = grad_query.shape
    scores_bias[...] = key_bias(marks_a[:rows], marks_a[...], marks_b[...], rows // 2, count)
    low = head_mask(rows)
    marks = grads[:, width:]
    marks_twice = jnp.concatenate([marks, marks], 0)
    ones = jnp.ones((LANES, 4 * rows + LANES), BF16)

    def step(pair, carry):
        at = pl.ds(pl.multiple_of(pair * LANES, LANES), LANES)
        at_k = pl.ds(pl.multiple_of(width + pair * LANES, LANES), LANES)
        at_v = pl.ds(pl.multiple_of(2 * width + pair * LANES, LANES), LANES)
        keys = with_prefix(qkv_a[:, at_k], qkv_b[:, at_k], prefix_kv[:, at])
        values = with_prefix(qkv_a[:, at_v], qkv_b[:, at_v], prefix_kv[:, at_k])
        query = two_heads(qkv_a[:rows, at] * jnp.asarray(HEAD**-0.5, BF16), low)
        tops = marks_twice * picks(rows, pair, 0, -1.0).astype(BF16)
        scores = nn(jnp.concatenate([query, tops], 1), jnp.concatenate([keys.T, ones], 0))
        mask = scores_bias[...]
        weights = jnp.exp(scores + jnp.concatenate([mask, mask], 0))
        bases = marks_twice * picks(rows, pair, 3 * HEADS, -1.0).astype(BF16)
        left = jnp.concatenate([two_heads(grads[:, at], low), bases], 1)
        slopes = weights * nn(left, jnp.concatenate([values.T, ones], 0))
        grad = join_heads(nn(slopes.astype(BF16), keys), low)
        grad_query[:, at] = (grad * HEAD**-0.5).astype(BF16)
        return carry

    lax.fori_loop(0, HEADS // 2, step, 0, unroll=True)
    out[...] = nn(grad_query[...], weight[:width])
    qkv_out[:, :width] = nn(normed_b[...], w_queries[:, :width]).astype(BF16)


def query_part(
    count, qkv_a, qkv_b, marks_a, marks_b, prefix_kv, grads, weight, normed_b, w_queries, order
):
    rows, width = grads.shape[0], grads.shape[1] - LANES
    return pl.pallas_call(
        partial(query_kernel, count),
        in_specs=[vmem()] * 9 + [pl.BlockSpec(memory_space=pl.ANY)],
        out_specs=[vmem()] * 2,
        out_shape=[jax.ShapeDtypeStruct((rows, width), F32), jax.ShapeDtypeStruct(qkv_b.shape, BF16)],
        input_output_aliases={1: 1},
        scratch_shapes=[pltpu.VMEM((rows, 4 * rows + LANES), F32), pltpu.VMEM((rows, width), BF16)],
        compiler_params=pltpu.CompilerParams(vmem_limit_bytes=16 * MIB),
        cost_estimate=pl.CostEstimate(flops=1 << 31, bytes_accessed=1000, transcendentals=0),
        name="query",
    )(qkv_a, qkv_b, marks_a, marks_b, prefix_kv, grads, weight, normed_b, w_queries, order)


def final_kernel(
    qkv_a,
    qkv_b,
    marks_a,
    marks_b,
    grads_0,
    grads_1,
    grads_2,
    grads_3,
    own_0,
    own_1,
    gain,
    grad_middle,
    grad_partial,
    weight,
    back_0,
    back_1,
    scores_bias,
    grad_keys,
):
    half, rows = own_0.shape[0], 2 * own_0.shape[0]
    width = grad_middle.shape[1]
    row, core, y_at = place()
    own = positions(iota((rows, 1), 0), half, row, core, y_at)
    other = all_positions((1, 8 * half), 1, half, row, core, y_at)
    same = nt(marks_a[:rows], jnp.concatenate([marks_a[...], marks_b[...]], 0))
    visible = jnp.logical_and(same > 0.5, own <= other)
    scores_bias[...] = jnp.where(visible, 0.0, NEG)
    low = head_mask(rows)
    blocks = (grads_0, grads_1, grads_2, grads_3)
    marks = jnp.concatenate([g[:, width:] for g in blocks], 0).T

    def step(pair, carry):
        at = pl.ds(pl.multiple_of(pair * LANES, LANES), LANES)
        at_k = pl.ds(pl.multiple_of(width + pair * LANES, LANES), LANES)
        at_v = pl.ds(pl.multiple_of(2 * width + pair * LANES, LANES), LANES)
        queries = jnp.concatenate([qkv_a[:, at], qkv_b[:, at]], 0)
        grads = jnp.concatenate([g[:, at] for g in blocks], 0)
        key_grad, value_grad = key_grads(
            qkv_a[:rows, at_k], qkv_a[:rows, at_v], queries, grads, marks, pair, low, scores_bias[...]
        )
        grad_keys[:, at] = key_grad.astype(BF16)
        grad_keys[:, at_k] = value_grad.astype(BF16)
        return carry

    lax.fori_loop(0, HEADS // 2, step, 0, unroll=True)
    grad_norm = grad_partial[...] + nn(grad_keys[...], weight[width:])
    inputs = jnp.concatenate([own_0[:, :width], own_1[:, :width]], 0).astype(F32)
    unit, inverse = norm_parts(inputs)
    out = (grad_middle[...] + norm_back(unit, inverse, gain[...], grad_norm)).astype(BF16)
    back_0[...] = out[:half]
    back_1[...] = out[half:]


def final_part(qkv_a, qkv_b, marks_a, marks_b, grads, own, gain, grad_middle, grad_partial, weight):
    rows, width = grad_middle.shape
    half = rows // 2
    return pl.pallas_call(
        final_kernel,
        in_specs=[vmem()] * 14,
        out_specs=[vmem()] * 2,
        out_shape=[jax.ShapeDtypeStruct((half, width), BF16)] * 2,
        scratch_shapes=[
            pltpu.VMEM((rows, 4 * rows), F32),
            pltpu.VMEM((rows, 2 * width), BF16),
        ],
        compiler_params=pltpu.CompilerParams(vmem_limit_bytes=16 * MIB),
        cost_estimate=pl.CostEstimate(flops=1000, bytes_accessed=1000, transcendentals=0),
        name="final",
    )(qkv_a, qkv_b, marks_a, marks_b, *grads, *own, gain[None], grad_middle, grad_partial, weight)


def routes(k):
    pairs = []
    for seq in range(4):
        for blk in range(8):
            group, z_at, y_at = seq % 2, blk // 2, blk % 2
            row = (z_at + k + 1) % 2
            pairs.append((seq * 8 + blk, (seq - group + z_at // 2) * 8 + (2 * group + row) * 2 + y_at))
    return pairs


def body_rows(
    tokens,
    segment_ids,
    ln1_gain,
    ln1_bias,
    w_qkv,
    w_out,
    ln2_gain,
    ln2_bias,
    w_fc,
    w_proj,
    prefix_embed,
    w_mlp1,
    b_mlp1,
    w_mlp2,
    b_mlp2,
    cotangent,
):
    half, _, width = tokens.shape
    everyone = ("seq", "blk")
    there = [routes(k) for k in range(2)]
    back = [[(b, a) for a, b in pairs] for pairs in there]
    swap_core = [(i, i ^ 1) for i in range(4)]
    swap_y = [(i, i ^ 1) for i in range(8)]
    swap_both = [(i, i ^ 9) for i in range(32)]
    def after(value, *done):
        return lax.optimization_barrier((value, done))[0]

    out_msgs = split_rows(tokens, segment_ids)
    cot_msgs = split_rows(cotangent)
    own = [lax.ppermute(m, everyone, there[k]) for k, m in enumerate(out_msgs)]
    prefix_kv, inner, w_near, w_back, near_embed, turned = adapter_forward(
        prefix_embed, w_mlp1, b_mlp1, w_mlp2, b_mlp2, w_qkv
    )
    count = prefix_embed.shape[0]
    own = after(own, inner)
    across = [lax.ppermute(m, "blk", swap_y) for m in own]
    beside = [lax.ppermute(m, "seq", swap_core) for m in own]
    cots = [lax.ppermute(m, everyone, there[k]) for k, m in enumerate(after(cot_msgs, beside))]
    beyond = [lax.ppermute(m, "seq", swap_core) for m in across]

    qkv_a, marks_a = project(own + beside, ln1_gain, ln1_bias, w_near)
    kv_b, marks_b, normed_b = project(across + beyond, ln1_gain, ln1_bias, w_near, 1)
    back_0, back_1, grads, grad_middle = middle_part(
        count, qkv_a, kv_b, marks_a, marks_b, prefix_kv, own, cots, ln2_gain, ln2_bias, w_out, w_fc, w_proj
    )
    grads_y = lax.ppermute(grads, "blk", swap_y)
    grads_c = lax.ppermute(grads, "seq", swap_core)
    grad_prefix_kv = prefix_part(count, qkv_a, grads, prefix_kv)
    parts = [lax.ppermute(grad_prefix_kv, "seq", [(i, i ^ far) for i in range(4)]) for far in (2, 1, 3)]
    grad_partial, qkv_b = query_part(
        count, qkv_a, kv_b, marks_a, marks_b, prefix_kv, grads, w_back, normed_b, w_near, grad_prefix_kv
    )
    packed = pack(count, grads, (grad_prefix_kv, *after(parts, grad_partial)), back_0, back_1)
    home = [lax.ppermute(m, everyone, back[k]) for k, m in enumerate(packed)]
    grads_yc = lax.ppermute(after(grads_y, packed), "seq", swap_core)
    final_0, final_1 = final_part(
        qkv_a,
        qkv_b,
        marks_a,
        marks_b,
        (grads, grads_c, grads_y, grads_yc),
        own,
        ln1_gain,
        grad_middle,
        grad_partial,
        w_back,
    )
    finals = [lax.ppermute(m, everyone, back[k]) for k, m in enumerate((final_0, final_1))]
    gathered = [unpack(count, width, *home)]
    gathered += [lax.ppermute(gathered[0], "seq", swap_core), lax.ppermute(gathered[0], "blk", swap_y)]
    gathered += [lax.ppermute(gathered[0], everyone, swap_both)]
    input_grad, summed = finish(finals, gathered, near_embed, inner, turned)
    block_out, log_total = land(count, after(home, gathered[0]), half, width)
    return (block_out, input_grad, summed[0], summed[1], summed[2], summed[3], summed[4], log_total)


def solution(mesh):
    four_by_eight = mesh.shape["seq"] == 4 and mesh.shape["blk"] == 8
    placed = (
        P("blk", "seq", None),
        P("blk", "seq"),
        P(),
        P(),
        P(),
        P(),
        P(),
        P(),
        P(),
        P(),
        P(),
        P(),
        P(),
        P(),
        P(),
        P("blk", "seq", None),
    )
    return jax.shard_map(
        body_rows if four_by_eight else body_plain,
        mesh=mesh,
        in_specs=placed,
        out_specs=(
            P("blk", "seq", None),
            P("blk", "seq", None),
            P(),
            P(),
            P(),
            P(),
            P(),
            P("seq", None, "blk"),
        ),
        check_vma=False,
    )
```

```python
from functools import partial
import math

import jax
import jax.numpy as jnp
from jax import lax
from jax.experimental import pallas as pl
from jax.experimental.pallas import tpu as pltpu
from jax.sharding import PartitionSpec as P

HEADS = 16
HEAD = 64


EPS = 1e-05
NEG = -1e30
HIGH = lax.Precision.HIGHEST


def layer_norm(value_in, gain, bias):
    average = jnp.mean(value_in, axis=-1, keepdims=True)
    centered = value_in - average
    variance = jnp.mean(centered * centered, axis=-1, keepdims=True)
    return centered * lax.rsqrt(variance + EPS) * gain + bias


def adapter(prefix_embed, w_mlp1, b_mlp1, w_mlp2, b_mlp2):
    inner_act = jnp.tanh(jnp.dot(prefix_embed, w_mlp1, precision=HIGH) + b_mlp1)
    return jnp.dot(inner_act, w_mlp2, precision=HIGH) + b_mlp2


def gelu_tanh(pre_act):
    return jax.nn.gelu(pre_act, approximate=True)


def split_heads(block_in):
    return block_in.reshape(block_in.shape[0], block_in.shape[1], HEADS, HEAD)


def allowed(query_pos, query_seg, key_pos, key_seg):
    same_seg = query_seg.T[:, :, None] == key_seg.T[:, None, :]
    causal = key_pos[None, None, :] <= query_pos[None, :, None]
    return jnp.logical_and(same_seg, causal)[:, None]


def scores_of(query_heads, key_block, score_scale):
    return score_scale * jnp.einsum(
        "prhd,krhd->rhpk", query_heads, split_heads(key_block), preferred_element_type=jnp.float32
    )


def block_grads(
    query_heads,
    grad_heads,
    log_total,
    slope_base,
    query_pos,
    query_seg,
    key_block,
    value_block,
    key_pos,
    key_seg,
    score_scale,
):
    scores = scores_of(query_heads, key_block, score_scale)
    scores = jnp.where(allowed(query_pos, query_seg, key_pos, key_seg), scores, NEG)
    weights = jnp.exp(scores - log_total[..., None])
    grad_weights = jnp.einsum(
        "prhd,krhd->rhpk", grad_heads, split_heads(value_block), preferred_element_type=jnp.float32
    )
    slopes = (weights * (grad_weights - slope_base[..., None])).astype(jnp.bfloat16)
    return (weights.astype(jnp.bfloat16), slopes)


def body_plain(
    tokens,
    segment_ids,
    ln1_gain,
    ln1_bias,
    w_qkv,
    w_out,
    ln2_gain,
    ln2_bias,
    w_fc,
    w_proj,
    prefix_embed,
    w_mlp1,
    b_mlp1,
    w_mlp2,
    b_mlp2,
    cotangent,
):
    pos_dev, row_count, width = tokens.shape
    score_scale = HEAD ** (-0.5)
    flat_rows = pos_dev * row_count
    own_pos = lax.axis_index("blk") * pos_dev + jnp.arange(pos_dev)
    inputs = tokens.astype(jnp.float32).reshape(flat_rows, width)
    normed_one = layer_norm(inputs, ln1_gain, ln1_bias).astype(jnp.bfloat16)
    projected = jnp.dot(normed_one, w_qkv, preferred_element_type=jnp.float32).astype(jnp.bfloat16)
    queries = projected[:, :width].reshape(pos_dev, row_count, width)
    keys = projected[:, width : 2 * width].reshape(pos_dev, row_count, width)
    values = projected[:, 2 * width :].reshape(pos_dev, row_count, width)
    query_heads = split_heads(queries)
    prefix_low = adapter(prefix_embed, w_mlp1, b_mlp1, w_mlp2, b_mlp2).astype(jnp.bfloat16)
    prefix_keys = prefix_low[:, :width].reshape(-1, HEADS, HEAD)
    prefix_values = prefix_low[:, width:].reshape(-1, HEADS, HEAD)
    prefix_scores = score_scale * jnp.einsum(
        "prhd,jhd->rhpj", query_heads, prefix_keys, preferred_element_type=jnp.float32
    )
    start_top = jnp.max(prefix_scores, -1)
    start_weights = jnp.exp(prefix_scores - start_top[..., None])
    start_denom = jnp.sum(start_weights, -1)
    start_numer = jnp.einsum(
        "rhpj,jhd->rhpd",
        start_weights.astype(jnp.bfloat16),
        prefix_values,
        preferred_element_type=jnp.float32,
    )
    start_state = (start_top, start_denom, start_numer)
    running = start_state
    key_shards = lax.all_gather(keys, "blk", axis=0, tiled=True)
    value_shards = lax.all_gather(values, "blk", axis=0, tiled=True)
    seg_shards = lax.all_gather(segment_ids, "blk", axis=0, tiled=True)
    num_rows = key_shards.shape[0]
    forward_stride = math.gcd(num_rows, 512)

    def inner(state, block_index):
        running_top, denominator, numerator = state
        offset = block_index * forward_stride
        key_block = lax.dynamic_slice_in_dim(key_shards, offset, forward_stride, 0)
        value_block = lax.dynamic_slice_in_dim(value_shards, offset, forward_stride, 0)
        seg_block = lax.dynamic_slice_in_dim(seg_shards, offset, forward_stride, 0)
        key_pos = offset + jnp.arange(forward_stride)
        scores = jnp.where(
            allowed(own_pos, segment_ids, key_pos, seg_block),
            scores_of(query_heads, key_block, score_scale),
            NEG,
        )
        new_top = jnp.maximum(running_top, jnp.max(scores, -1))
        fading = jnp.exp(running_top - new_top)
        weights = jnp.exp(scores - new_top[..., None])
        denominator = denominator * fading + jnp.sum(weights, -1)
        numerator = numerator * fading[..., None] + jnp.einsum(
            "rhpk,krhd->rhpd",
            weights.astype(jnp.bfloat16),
            split_heads(value_block),
            preferred_element_type=jnp.float32,
        )
        return ((new_top, denominator, numerator), None)

    running, _ = lax.scan(inner, running, jnp.arange(num_rows // forward_stride))
    final_top, final_denom, final_numer = running
    log_total = final_top + jnp.log(final_denom)
    attended = final_numer / final_denom[..., None]
    attended_rows = jnp.transpose(attended, (2, 0, 1, 3)).reshape(flat_rows, width)
    middle = inputs + jnp.dot(
        attended_rows.astype(jnp.bfloat16), w_out, preferred_element_type=jnp.float32
    )
    normed_two = layer_norm(middle, ln2_gain, ln2_bias).astype(jnp.bfloat16)
    hidden_pre = jnp.dot(normed_two, w_fc, preferred_element_type=jnp.float32)
    hidden_act = gelu_tanh(hidden_pre).astype(jnp.bfloat16)
    outputs = middle + jnp.dot(hidden_act, w_proj, preferred_element_type=jnp.float32)
    block_out = outputs.astype(jnp.bfloat16).reshape(pos_dev, row_count, width)
    grad_out = cotangent.reshape(flat_rows, width)
    grad_act = jnp.dot(grad_out, w_proj.T, preferred_element_type=jnp.float32)
    _, gelu_back = jax.vjp(gelu_tanh, hidden_pre)
    grad_pre = gelu_back(grad_act)[0].astype(jnp.bfloat16)
    grad_norm_two = jnp.dot(grad_pre, w_fc.T, preferred_element_type=jnp.float32)
    _, norm_two_back = jax.vjp(partial(layer_norm, gain=ln2_gain, bias=ln2_bias), middle)
    grad_middle = grad_out.astype(jnp.float32) + norm_two_back(grad_norm_two)[0]
    grad_attended = jnp.dot(
        grad_middle.astype(jnp.bfloat16), w_out.T, preferred_element_type=jnp.float32
    ).astype(jnp.bfloat16)
    grad_flat = grad_attended.reshape(pos_dev, row_count, width)
    grad_heads = split_heads(grad_flat)
    slope_base = jnp.sum(jnp.transpose(grad_heads.astype(jnp.float32), (1, 2, 0, 3)) * attended, -1)
    prefix_weights = jnp.exp(prefix_scores - log_total[..., None])
    prefix_dw = jnp.einsum(
        "prhd,jhd->rhpj", grad_heads, prefix_values, preferred_element_type=jnp.float32
    )
    prefix_slopes = (prefix_weights * (prefix_dw - slope_base[..., None])).astype(jnp.bfloat16)
    grad_query = score_scale * jnp.einsum(
        "rhpj,jhd->prhd", prefix_slopes, prefix_keys, preferred_element_type=jnp.float32
    )
    grad_pkeys = score_scale * jnp.einsum(
        "rhpj,prhd->jhd", prefix_slopes, query_heads, preferred_element_type=jnp.float32
    )
    grad_pvalues = jnp.einsum(
        "rhpj,prhd->jhd",
        prefix_weights.astype(jnp.bfloat16),
        grad_heads,
        preferred_element_type=jnp.float32,
    )
    grad_prefix_kv = jnp.concatenate(
        [grad_pkeys.reshape(-1, width), grad_pvalues.reshape(-1, width)], -1
    )
    keys_all, values_all, segs_all = (
        lax.all_gather(keys, "blk", axis=0, tiled=True),
        lax.all_gather(values, "blk", axis=0, tiled=True),
        lax.all_gather(segment_ids, "blk", axis=0, tiled=True),
    )
    length = keys_all.shape[0]
    stride = math.gcd(length, 512)

    def backward_step(grad_q, block_index):
        offset = block_index * stride
        key_block = lax.dynamic_slice_in_dim(keys_all, offset, stride, 0)
        value_block = lax.dynamic_slice_in_dim(values_all, offset, stride, 0)
        seg_block = lax.dynamic_slice_in_dim(segs_all, offset, stride, 0)
        key_pos = offset + jnp.arange(stride)
        weights_low, slopes = block_grads(
            query_heads,
            grad_heads,
            log_total,
            slope_base,
            own_pos,
            segment_ids,
            key_block,
            value_block,
            key_pos,
            seg_block,
            score_scale,
        )
        grad_q = grad_q + score_scale * jnp.einsum(
            "rhpk,krhd->prhd", slopes, split_heads(key_block), preferred_element_type=jnp.float32
        )
        key_term = score_scale * jnp.einsum(
            "rhpk,prhd->krhd", slopes, query_heads, preferred_element_type=jnp.float32
        )
        value_term = jnp.einsum(
            "rhpk,prhd->krhd", weights_low, grad_heads, preferred_element_type=jnp.float32
        )
        return (
            grad_q,
            (
                key_term.reshape(stride, row_count, width),
                value_term.reshape(stride, row_count, width),
            ),
        )

    grad_query, (key_terms, value_terms) = lax.scan(
        backward_step, grad_query, jnp.arange(length // stride)
    )
    key_terms = key_terms.reshape(length, row_count, width)
    value_terms = value_terms.reshape(length, row_count, width)
    grad_keys, grad_values = (
        lax.psum_scatter(key_terms, "blk", scatter_dimension=0, tiled=True),
        lax.psum_scatter(value_terms, "blk", scatter_dimension=0, tiled=True),
    )
    grad_proj = jnp.concatenate(
        [
            grad_query.reshape(flat_rows, width).astype(jnp.bfloat16),
            grad_keys.reshape(flat_rows, width).astype(jnp.bfloat16),
            grad_values.reshape(flat_rows, width).astype(jnp.bfloat16),
        ],
        -1,
    )
    grad_norm_one = jnp.dot(grad_proj, w_qkv.T, preferred_element_type=jnp.float32)
    _, norm_one_back = jax.vjp(partial(layer_norm, gain=ln1_gain, bias=ln1_bias), inputs)
    input_grad = (grad_middle + norm_one_back(grad_norm_one)[0]).reshape(pos_dev, row_count, width)
    _, adapter_back = jax.vjp(adapter, prefix_embed, w_mlp1, b_mlp1, w_mlp2, b_mlp2)
    local_grads = adapter_back(grad_prefix_kv)
    summed = lax.psum(
        (local_grads[0], local_grads[1], local_grads[2], local_grads[3], local_grads[4]),
        ("seq", "blk"),
    )
    return (block_out, input_grad, summed[0], summed[1], summed[2], summed[3], summed[4], log_total)


F32 = jnp.float32
BF16 = jnp.bfloat16
LANES = 128
PRE_ROWS = 16
MIB = 1 << 20


def nn(left, right):
    return jnp.dot(left, right, preferred_element_type=F32)


def nt(left, right):
    return lax.dot_general(left, right, (((1,), (1,)), ((), ())), preferred_element_type=F32)


def norm_parts(value_in):
    average = jnp.mean(value_in, axis=-1, keepdims=True)
    centered = value_in - average
    variance = jnp.mean(centered * centered, axis=-1, keepdims=True)
    inverse = lax.rsqrt(variance + EPS)
    return centered * inverse, inverse


def norm_back(unit, inverse, gain, grad):
    scaled = grad * gain
    first = jnp.mean(scaled, axis=-1, keepdims=True)
    second = jnp.mean(scaled * unit, axis=-1, keepdims=True)
    return inverse * (scaled - first - unit * second)


def iota(shape, dim):
    return lax.broadcasted_iota(jnp.int32, shape, dim)


def place():
    blk = lax.axis_index("blk")
    return (blk // 2) % 2, lax.axis_index("seq") % 2, blk % 2


def positions(index, half, row, core, y_at):
    upper = (index >= half).astype(jnp.int32)
    slot = 1 - (upper + row - 2 * upper * row)
    block = (2 * core + slot) * 2 + y_at
    return block * half + index - upper * half


def members(core, y_at):
    return ((core, y_at), (1 - core, y_at), (core, 1 - y_at), (1 - core, 1 - y_at))


def all_positions(shape, dim, half, row, core, y_at):
    part = tuple(2 * half if d == dim else n for d, n in enumerate(shape))
    return jnp.concatenate(
        [positions(iota(part, dim), half, row, c, y) for c, y in members(core, y_at)], dim
    )


def vmem():
    return pl.BlockSpec(memory_space=pltpu.VMEM)


def hbm():
    return pl.BlockSpec(memory_space=pltpu.HBM)


def kept_in_hbm(*arrays):
    return [pltpu.with_memory_space_constraint(a, pltpu.HBM) for a in arrays]


def by_tiles(block):
    half, pair, width = block.shape
    tiles = jnp.transpose(block.reshape(half, pair, width // LANES, LANES), (0, 2, 1, 3))
    return tiles.reshape(half, pair * width // LANES, LANES)


def from_tiles(tiles, width):
    half, count, _ = tiles.shape
    pair = count * LANES // width
    block = jnp.transpose(tiles.reshape(half, width // LANES, pair, LANES), (0, 2, 1, 3))
    return block.reshape(half, pair, width)


def odd_place():
    return (lax.axis_index("blk") // 2) % 2 == 0


def split_kernel(marked, *refs):
    tokens, ids, (out_0, out_1, work) = refs[0], refs[1], refs[-3:]
    half, count, _ = tokens.shape
    odd = odd_place()
    work[pl.ds(0, half * count)] = tokens[...].astype(F32).reshape(half * count, LANES)
    for i in range(count // 2):
        at = pl.ds(i * LANES, LANES)
        first, second = (work[pl.ds(2 * i + r, half, stride=count)] for r in range(2))
        out_0[:, at] = jnp.where(odd, second, first).astype(BF16)
        out_1[:, at] = jnp.where(odd, first, second).astype(BF16)
    if marked:
        width = count // 2 * LANES
        first, second = (
            jnp.where(iota((LANES, half), 0) == ids[r : r + 1], 1.0, 0.0).T for r in range(2)
        )
        out_0[:, width:] = jnp.where(odd, second, first).astype(BF16)
        out_1[:, width:] = jnp.where(odd, first, second).astype(BF16)


def split_rows(block, segment_ids=None):
    tiles = by_tiles(block)
    half, count, _ = tiles.shape
    extra = () if segment_ids is None else kept_in_hbm(segment_ids.T)
    width = count // 2 * LANES + LANES * len(extra)
    return pl.pallas_call(
        partial(split_kernel, bool(extra)),
        in_specs=[vmem()] * (1 + len(extra)),
        out_specs=[vmem()] * 2,
        out_shape=[jax.ShapeDtypeStruct((half, width), BF16)] * 2,
        scratch_shapes=[pltpu.VMEM(((half + 1) * count, LANES), F32)],
        compiler_params=pltpu.CompilerParams(vmem_limit_bytes=4 * MIB),
        cost_estimate=pl.CostEstimate(flops=1 << 31, bytes_accessed=1000, transcendentals=0),
        name="split",
    )(*kept_in_hbm(tiles), *extra)


def place_rows(msg_0, msg_1, work):
    count = 2 * msg_0.shape[1] // LANES
    half = work.shape[0] // count - 1
    odd = odd_place()
    for i in range(count // 2):
        at = pl.ds(i * LANES, LANES)
        one, two = msg_0[:half, at].astype(F32), msg_1[:half, at].astype(F32)
        work[pl.ds(2 * i, half, stride=count)] = jnp.where(odd, two, one)
        work[pl.ds(2 * i + 1, half, stride=count)] = jnp.where(odd, one, two)


def land_kernel(first_row, msg_0, msg_1, out, logs, work):
    half = out.shape[0]
    heads = logs.shape[1]
    place_rows(msg_0, msg_1, work)
    out[...] = work[pl.ds(0, half * out.shape[1])].reshape(out.shape).astype(out.dtype)
    odd = odd_place()
    found = []
    for k, message in enumerate((msg_0, msg_1)):
        rows = message[half:].astype(F32)[first_row : first_row + GROUP]
        slots = [rows[:, i * LANES + k * half : i * LANES + (k + 1) * half] for i in range(3 * heads // GROUP)]
        groups = [slots[i] + slots[i + 1] + slots[i + 2] for i in range(0, len(slots), 3)]
        found.append(jnp.concatenate(groups, 0))
    logs[0] = jnp.where(odd, found[1], found[0])
    logs[1] = jnp.where(odd, found[0], found[1])


def land(count_prefix, messages, half, width):
    count = 2 * width // LANES
    out = pl.pallas_call(
        partial(land_kernel, prefix_rows(count_prefix)),
        in_specs=[vmem()] * 2,
        out_specs=[vmem()] * 2,
        out_shape=[
            jax.ShapeDtypeStruct((half, count, LANES), BF16),
            jax.ShapeDtypeStruct((2, HEADS, half), F32),
        ],
        scratch_shapes=[pltpu.VMEM(((half + 1) * count, LANES), F32)],
        compiler_params=pltpu.CompilerParams(vmem_limit_bytes=4 * MIB),
        cost_estimate=pl.CostEstimate(flops=1000, bytes_accessed=1000, transcendentals=0),
        name="land",
    )(*messages)
    return from_tiles(out[0], width), out[1]


def project_kernel(count, first, *refs):
    messages, (gain, bias, weight, out, marks, normed) = refs[:count], refs[count:]
    half, width = messages[0].shape[0], normed.shape[1]
    for i, message in enumerate(messages):
        rows = pl.ds(i * half, half)
        unit, _ = norm_parts(message[:, :width].astype(F32))
        normed[rows] = (unit * gain[...] + bias[...]).astype(BF16)
        marks[rows] = message[:, width:]
    for i in range(first, 3):
        at = pl.ds(i * width, width)
        out[:, at] = nn(normed[...], weight[:, at]).astype(BF16)


def project(messages, gain, bias, weight, first=0):
    count, half = len(messages), messages[0].shape[0]
    width, columns = weight.shape
    rows = count * half
    return pl.pallas_call(
        partial(project_kernel, count, first),
        in_specs=[vmem()] * (count + 3),
        out_specs=[vmem()] * (2 + first),
        out_shape=[
            jax.ShapeDtypeStruct((rows, columns), BF16),
            jax.ShapeDtypeStruct((rows, LANES), BF16),
        ]
        + [jax.ShapeDtypeStruct((rows, width), BF16)] * first,
        scratch_shapes=[pltpu.VMEM((rows, width), BF16)] * (1 - first),
        compiler_params=pltpu.CompilerParams(vmem_limit_bytes=16 * MIB),
        cost_estimate=pl.CostEstimate(
            flops=2 * rows * width * columns, bytes_accessed=2 * width * columns, transcendentals=0
        ),
        name="project",
    )(*messages, gain[None], bias[None], weight)


def halves(value_in):
    high = value_in.astype(BF16)
    return high, (value_in - high.astype(F32)).astype(BF16)


def pad_rows(value_in, rows):
    if rows == value_in.shape[0]:
        return value_in
    return jnp.concatenate(
        [value_in, jnp.zeros((rows - value_in.shape[0], value_in.shape[1]), value_in.dtype)], 0
    )


def three_products(product, left, weight):
    rows = left.shape[0]
    high, low = halves(left)
    w_high, w_low = halves(weight)
    both = product(jnp.concatenate([high, low], 0), w_high)
    return both[:rows] + both[rows:] + product(high, w_low)


def adapter_kernel(
    h_embed,
    w_mlp1,
    h_mlp1,
    w_mlp2,
    h_mlp2,
    w_qkv,
    out,
    inner,
    v_qkv,
    w_back,
    embed,
    turned,
    v_mlp1,
    v_mlp2,
    b_mlp1,
    b_mlp2,
    sems,
):
    steps, step = v_mlp2.shape[0], v_mlp2.shape[2]
    small = []
    for i, (source, target) in enumerate(
        ((h_embed, embed), (h_mlp1, b_mlp1), (h_mlp2, b_mlp2), (w_mlp1, v_mlp1))
    ):
        small.append(pltpu.make_async_copy(source, target, sems.at[steps + i]))
        small[-1].start()
    width = w_qkv.shape[0]
    weights = []
    for i in range(3):
        at = pl.ds(i * width, width)
        weights.append(
            pltpu.make_async_copy(w_qkv.at[:, at], v_qkv.at[:, at], sems.at[steps + len(small) + i])
        )
        weights[-1].start()
    rest = []
    for i in range(steps):
        copy = pltpu.make_async_copy(w_mlp2.at[:, pl.ds(i * step, step)], v_mlp2.at[i], sems.at[i])
        copy.start()
        rest.append(copy)
    for copy in small:
        copy.wait()
    source = pad_rows(embed[...], PRE_ROWS)
    act = jnp.tanh(three_products(nn, source, v_mlp1[...]) + b_mlp1[...])
    inner[...] = act
    columns, hidden = steps * step, v_mlp1.shape[1]
    for i in range(v_mlp1.shape[0] // hidden):
        part = v_mlp1[pl.ds(i * hidden, hidden)].astype(BF16)
        turned[pl.ds(columns + i * hidden, hidden)] = part.T
    for i, copy in enumerate(weights):
        at = pl.ds(i * width, width)
        copy.wait()
        w_back[at] = v_qkv[:, at].T
    for i, copy in enumerate(rest):
        copy.wait()
        turned[pl.ds(i * step, step)] = v_mlp2[i].astype(BF16).T
        span = pl.ds(i * step, step)
        part = three_products(nn, act, v_mlp2[i]) + b_mlp2[:, span]
        out[:, span] = jnp.where(iota(part.shape, 0) < embed.shape[0], part, 0.0).astype(BF16)


def adapter_forward(embed, w_mlp1, b_mlp1, w_mlp2, b_mlp2, w_qkv):
    width, hidden = w_mlp1.shape
    columns = w_mlp2.shape[1]
    steps = 4
    return pl.pallas_call(
        adapter_kernel,
        in_specs=[hbm()] * 6,
        out_specs=[vmem()] * 6,
        out_shape=[
            jax.ShapeDtypeStruct((PRE_ROWS, columns), BF16),
            jax.ShapeDtypeStruct((PRE_ROWS, hidden), F32),
            pltpu.VMEM(w_qkv.shape, w_qkv.dtype),
            pltpu.VMEM(w_qkv.shape[::-1], w_qkv.dtype),
            pltpu.VMEM(embed.shape, F32),
            pltpu.VMEM((columns + width, hidden), BF16),
        ],
        scratch_shapes=[
            pltpu.VMEM((width, hidden), F32),
            pltpu.VMEM((steps, hidden, columns // steps), F32),
            pltpu.VMEM((1, hidden), F32),
            pltpu.VMEM((1, columns), F32),
            pltpu.SemaphoreType.DMA((7 + steps,)),
        ],
        compiler_params=pltpu.CompilerParams(vmem_limit_bytes=20 * MIB),
        cost_estimate=pl.CostEstimate(flops=1 << 32, bytes_accessed=6 * MIB, transcendentals=1 << 13),
        name="adapter",
    )(*kept_in_hbm(embed, w_mlp1, b_mlp1[None], w_mlp2, b_mlp2[None], w_qkv))


def outer(left, right):
    l_high, l_low = halves(left)
    r_high, r_low = halves(right)
    return lax.dot_general(
        jnp.concatenate([l_high, l_high, l_low], 0),
        jnp.concatenate([r_high, r_low, r_high], 0),
        (((0,), (0,)), ((), ())),
        preferred_element_type=F32,
    )


def two_products(left, weight):
    high, low = halves(left)
    both = nn(jnp.concatenate([high, low], 0), weight)
    return both[: left.shape[0]] + both[left.shape[0] :]


def adapter_back_kernel(
    home_0,
    home_1,
    part_0,
    part_1,
    part_2,
    part_3,
    embed,
    inner,
    turned,
    block,
    grad_prefix,
    grad_mlp1,
    grad_bias1,
    grad_mlp2,
    grad_bias2,
    o_block,
    o_mlp1,
    o_mlp2,
    sems,
):
    steps, step = o_mlp2.shape[0], o_mlp2.shape[2]
    first, second, third, fourth = (p[...].astype(F32) for p in (part_0, part_1, part_2, part_3))
    grads = (first + second) + (third + fourth)
    act = inner[...]
    stores = []
    grad_bias2[...] = jnp.sum(grads, 0, keepdims=True)
    for i in range(steps):
        o_mlp2[i] = outer(act, grads[:, i * step : (i + 1) * step])
        stores.append(
            pltpu.make_async_copy(o_mlp2.at[i], grad_mlp2.at[:, pl.ds(i * step, step)], sems.at[i])
        )
        stores[-1].start()
    columns, (width, hidden) = steps * step, o_mlp1.shape
    place_rows(home_0, home_1, o_block)
    stores.append(pltpu.make_async_copy(o_block.at[pl.ds(0, block.shape[0])], block, sems.at[steps + 1]))
    stores[-1].start()
    back = two_products(grads, turned[:columns]) * (1.0 - act * act)
    grad_bias1[...] = jnp.sum(back, 0, keepdims=True)
    o_mlp1[...] = outer(pad_rows(embed[...], PRE_ROWS), back)
    stores.append(pltpu.make_async_copy(o_mlp1, grad_mlp1, sems.at[steps]))
    stores[-1].start()
    for i in range(width // hidden):
        part = two_products(back, turned[pl.ds(columns + i * hidden, hidden)])
        grad_prefix[:, pl.ds(i * hidden, hidden)] = part[: embed.shape[0]]
    for copy in stores:
        copy.wait()


def finish(finals, parts, embed, inner, turned):
    hidden, width = turned.shape[1], embed.shape[1]
    columns = turned.shape[0] - width
    half = finals[0].shape[0]
    steps = 4
    tiles = 2 * width // LANES
    out = pl.pallas_call(
        adapter_back_kernel,
        in_specs=[vmem()] * 9,
        out_specs=[hbm(), vmem(), hbm(), vmem(), hbm(), vmem()],
        out_shape=[
            jax.ShapeDtypeStruct((half * tiles, LANES), F32),
            jax.ShapeDtypeStruct(embed.shape, F32),
            jax.ShapeDtypeStruct((width, hidden), F32),
            jax.ShapeDtypeStruct((1, hidden), F32),
            jax.ShapeDtypeStruct((hidden, columns), F32),
            jax.ShapeDtypeStruct((1, columns), F32),
        ],
        scratch_shapes=[
            pltpu.VMEM(((half + 1) * tiles, LANES), F32),
            pltpu.VMEM((width, hidden), F32),
            pltpu.VMEM((steps, hidden, columns // steps), F32),
            pltpu.SemaphoreType.DMA((steps + 2,)),
        ],
        compiler_params=pltpu.CompilerParams(vmem_limit_bytes=16 * MIB),
        cost_estimate=pl.CostEstimate(flops=1000, bytes_accessed=1000, transcendentals=0),
        name="finish",
    )(*finals, *parts, embed, inner, turned)
    block = from_tiles(out[0].reshape(half, tiles, LANES), width)
    return block, (out[1], out[2], out[3][0], out[4], out[5][0])


def head_mask(rows):
    return iota((rows, LANES), 1) < HEAD


def two_heads(pair, low):
    zero = jnp.zeros_like(pair)
    return jnp.concatenate([jnp.where(low, pair, zero), jnp.where(low, zero, pair)], 0)


def join_heads(stacked, low):
    rows = stacked.shape[0] // 2
    return jnp.where(low, stacked[:rows], stacked[rows:])


def picks(rows, pair, first, value):
    lane = iota((rows, LANES), 1)
    inside = jnp.logical_and(lane >= first, lane < first + 3 * HEADS)
    parts = [
        jnp.where(jnp.logical_and(inside, lane % HEADS == 2 * pair + i), value, 0.0) for i in range(2)
    ]
    return jnp.concatenate(parts, 0)


def three_parts(value_in, first):
    lane = iota(value_in.shape, 1)
    high = value_in.astype(BF16).astype(F32)
    rest = value_in - high
    middle = rest.astype(BF16).astype(F32)
    low = rest - middle
    part = (lane - first) // HEADS
    chosen = jnp.where(part == 0, high, jnp.where(part == 1, middle, low))
    inside = jnp.logical_and(lane >= first, lane < first + 3 * HEADS)
    return jnp.where(inside, chosen, 0.0)


def key_bias(marks_own, marks_a, marks_b, half, count):
    row, core, y_at = place()
    rows = 2 * half
    own = positions(iota((rows, 1), 0), half, row, core, y_at)
    other = all_positions((1, 8 * half), 1, half, row, core, y_at)
    same = nt(marks_own, jnp.concatenate([marks_a, marks_b], 0))
    visible = jnp.logical_and(same > 0.5, other <= own)
    token_bias = jnp.where(visible, 0.0, NEG)
    prefix_bias = jnp.where(iota((rows, LANES), 1) < count, 0.0, NEG)
    return jnp.concatenate([token_bias, prefix_bias], 1)


def with_prefix(part_a, part_b, prefix):
    pad = jnp.zeros((LANES - prefix.shape[0], prefix.shape[1]), prefix.dtype)
    return jnp.concatenate([part_a, part_b, prefix, pad], 0)


def middle_kernel(
    count,
    qkv_a,
    qkv_b,
    marks_a,
    marks_b,
    prefix_kv,
    own_0,
    own_1,
    cot_0,
    cot_1,
    gain,
    bias,
    w_out,
    w_fc,
    w_proj,
    back_0,
    back_1,
    grad_out_heads,
    grad_middle,
    v_out,
    v_fc,
    v_proj,
    sems,
    scores_bias,
    attended,
    stats,
    middle,
    normed,
    total,
    grad_norm,
    cot,
):
    half, rows = own_0.shape[0], 2 * own_0.shape[0]
    width = middle.shape[1]
    steps, step = v_fc.shape[0], v_fc.shape[2]
    copies = [pltpu.make_async_copy(w_out, v_out, sems.at[0])]
    for i in range(steps):
        span = pl.ds(i * step, step)
        copies.append(pltpu.make_async_copy(w_fc.at[:, span], v_fc.at[i], sems.at[1 + 2 * i]))
        copies.append(pltpu.make_async_copy(w_proj.at[span], v_proj.at[i], sems.at[2 + 2 * i]))
    for copy in copies:
        copy.start()

    scores_bias[...] = key_bias(marks_a[:rows], marks_a[...], marks_b[...], half, count)
    low = head_mask(rows)
    lane = iota((rows, LANES), 1)
    stats[...] = jnp.zeros_like(stats)

    def attend(pair, carry):
        at = pl.ds(pl.multiple_of(pair * LANES, LANES), LANES)
        at_k = pl.ds(pl.multiple_of(width + pair * LANES, LANES), LANES)
        at_v = pl.ds(pl.multiple_of(2 * width + pair * LANES, LANES), LANES)
        query = two_heads(qkv_a[:rows, at] * jnp.asarray(HEAD**-0.5, BF16), low)
        keys = with_prefix(qkv_a[:, at_k], qkv_b[:, at_k], prefix_kv[:, at])
        values = with_prefix(qkv_a[:, at_v], qkv_b[:, at_v], prefix_kv[:, at_k])
        scores = nt(query, keys)
        mask = scores_bias[...]
        scores = scores + jnp.concatenate([mask, mask], 0)
        top = jnp.max(scores, -1, keepdims=True)
        weights = jnp.exp(scores - top)
        denominator = jnp.sum(weights, -1, keepdims=True)
        mixed = nn(weights.astype(BF16), values) / denominator
        attended[:, at] = join_heads(mixed, low)
        log_total = top + jnp.log(denominator)
        inside = lane < 3 * HEADS
        for i in range(2):
            here = jnp.logical_and(inside, lane % HEADS == 2 * pair + i)
            stats[...] = jnp.where(here, log_total[i * rows : (i + 1) * rows], stats[...])
        return carry

    lax.fori_loop(0, HEADS // 2, attend, 0, unroll=4)

    copies[0].wait()
    inputs = jnp.concatenate([own_0[:, :width], own_1[:, :width]], 0).astype(F32)
    middle[...] = inputs + nn(attended[...].astype(BF16), v_out[...])
    unit, _ = norm_parts(middle[...])
    normed[...] = (unit * gain[...] + bias[...]).astype(BF16)
    cot[...] = jnp.concatenate([cot_0[...], cot_1[...]], 0)
    total[...] = middle[...]
    grad_norm[...] = jnp.zeros_like(grad_norm)

    def feed(i, carry):
        for which in (0, 1):
            pltpu.make_async_copy(
                (v_fc, v_proj)[which].at[i], (v_fc, v_proj)[which].at[i], sems.at[1 + 2 * i + which]
            ).wait()
        fc, proj = v_fc[i], v_proj[i]
        pre = nn(normed[...], fc)
        grad_act = nt(cot[...], proj)
        cubic = 0.044715 * pre * pre
        curve = jnp.tanh(math.sqrt(2 / math.pi) * pre * (1.0 + cubic))
        act = 0.5 * pre * (1.0 + curve)
        slope = 0.5 * (1.0 + curve) + 0.5 * math.sqrt(2 / math.pi) * pre * (1.0 - curve * curve) * (
            1.0 + 3.0 * cubic
        )
        grad_pre = (grad_act * slope).astype(BF16)
        total[...] += nn(act.astype(BF16), proj)
        grad_norm[...] += nt(grad_pre, fc)
        return carry

    lax.fori_loop(0, steps, feed, 0, unroll=True)

    out = total[...].astype(BF16)
    back_0[:half] = out[:half]
    back_1[:half] = out[half:]
    unit, inverse = norm_parts(middle[...])
    grads = cot[...].astype(F32) + norm_back(unit, inverse, gain[...], grad_norm[...])
    grad_middle[...] = grads
    grad_heads = nt(grads.astype(BF16), v_out[...]).astype(BF16)
    grad_out_heads[:, :width] = grad_heads
    product = grad_heads.astype(F32) * attended[...]
    ones = jnp.where(
        jnp.logical_and(
            iota((width, LANES), 0) // HEAD == iota((width, LANES), 1) % HEADS,
            jnp.logical_and(
                iota((width, LANES), 1) >= 3 * HEADS, iota((width, LANES), 1) < 6 * HEADS
            ),
        ),
        1.0,
        0.0,
    ).astype(BF16)
    bases = jnp.zeros((rows, LANES), F32)
    for _ in range(2):
        part = product.astype(BF16)
        bases = bases + nn(part, ones)
        product = product - part.astype(F32)
    marks = three_parts(stats[...], 0) + three_parts(bases, 3 * HEADS)
    marks = marks.astype(BF16)
    grad_out_heads[:, width:] = marks


def middle_part(count, qkv_a, qkv_b, marks_a, marks_b, prefix_kv, own, cots, gain, bias, w_out, w_fc, w_proj):
    half, width = cots[0].shape
    rows = 2 * half
    hidden = w_fc.shape[1]
    steps = 2
    step = hidden // steps
    wide = width + LANES
    return pl.pallas_call(
        partial(middle_kernel, count),
        in_specs=[vmem()] * 11 + [hbm()] * 3,
        out_specs=[vmem()] * 4,
        out_shape=[
            jax.ShapeDtypeStruct((half + tail_rows(count), width), BF16),
            jax.ShapeDtypeStruct((half + tail_rows(count), width), BF16),
            jax.ShapeDtypeStruct((rows, wide), BF16),
            jax.ShapeDtypeStruct((rows, width), F32),
        ],
        scratch_shapes=[
            pltpu.VMEM((width, width), BF16),
            pltpu.VMEM((steps, width, step), BF16),
            pltpu.VMEM((steps, step, width), BF16),
            pltpu.SemaphoreType.DMA((1 + 2 * steps,)),
            pltpu.VMEM((rows, 4 * rows + LANES), F32),
            pltpu.VMEM((rows, width), F32),
            pltpu.VMEM((rows, LANES), F32),
            pltpu.VMEM((rows, width), F32),
            pltpu.VMEM((rows, width), BF16),
            pltpu.VMEM((rows, width), F32),
            pltpu.VMEM((rows, width), F32),
            pltpu.VMEM((rows, width), BF16),
        ],
        compiler_params=pltpu.CompilerParams(vmem_limit_bytes=36 * MIB),
        cost_estimate=pl.CostEstimate(flops=1 << 31, bytes_accessed=1000, transcendentals=0),
        name="middle",
    )(
        qkv_a, qkv_b, marks_a, marks_b, prefix_kv, *own, *cots, gain[None], bias[None], *kept_in_hbm(w_out, w_fc, w_proj)
    )


def key_grads(keys, values, queries, grads, turned_marks, pair, low, mask):
    rows = keys.shape[0]
    scale = jnp.asarray(HEAD**-0.5, BF16)
    left = jnp.concatenate(
        [two_heads(keys * scale, low), picks(rows, pair, 0, -1.0).astype(BF16)], 1
    )
    scores = nn(left, jnp.concatenate([queries.T, turned_marks], 0))
    weights = jnp.exp(scores + jnp.concatenate([mask, mask], 0))
    left = jnp.concatenate(
        [two_heads(values, low), picks(rows, pair, 3 * HEADS, -1.0).astype(BF16)], 1
    )
    slopes = weights * nn(left, jnp.concatenate([grads.T, turned_marks], 0))
    key_grad = nn(slopes.astype(BF16), queries)
    value_grad = nn(weights.astype(BF16), grads)
    return join_heads(key_grad, low) * HEAD**-0.5, join_heads(value_grad, low)


GROUP = 8


def prefix_rows(count):
    return -(-2 * count // GROUP) * GROUP


def tail_rows(count):
    return -(-(prefix_rows(count) + GROUP) // PRE_ROWS) * PRE_ROWS


def prefix_kernel(used, queries, grads, prefix_kv, out):
    count, rows, width = prefix_kv.shape[0], grads.shape[0], grads.shape[1] - LANES
    marks = grads[:, width:].T
    low = head_mask(count)
    mask = jnp.where(iota((count, rows), 0) < used, 0.0, NEG)

    def step(pair, carry):
        at = pl.ds(pl.multiple_of(pair * LANES, LANES), LANES)
        at_v = pl.ds(pl.multiple_of(width + pair * LANES, LANES), LANES)
        key_grad, value_grad = key_grads(
            prefix_kv[:, at], prefix_kv[:, at_v], queries[:rows, at], grads[:, at], marks, pair, low, mask
        )
        out[:, at] = key_grad.astype(BF16)
        out[:, at_v] = value_grad.astype(BF16)
        return carry

    lax.fori_loop(0, HEADS // 2, step, 0, unroll=True)


def prefix_part(count, qkv_a, grads, prefix_kv):
    return pl.pallas_call(
        partial(prefix_kernel, count),
        in_specs=[vmem()] * 3,
        out_specs=vmem(),
        out_shape=jax.ShapeDtypeStruct(prefix_kv.shape, BF16),
        compiler_params=pltpu.CompilerParams(vmem_limit_bytes=8 * MIB),
        cost_estimate=pl.CostEstimate(flops=1000, bytes_accessed=1000, transcendentals=0),
        name="prefix",
    )(qkv_a, grads, prefix_kv)


def pack_kernel(count, grads, own, part_0, part_1, part_2, _0, _1, back_0, back_1):
    total = own[...].astype(F32) + part_0[...].astype(F32)
    total = total + (part_1[...].astype(F32) + part_2[...].astype(F32))
    width = total.shape[1] // 2
    rows = tail_rows(count)
    both = jnp.concatenate([total[:count, :width], total[:count, width:]], 0)
    marks = grads[:, width:].astype(F32).T
    starts = [part * HEADS + first for first in range(0, HEADS, GROUP) for part in range(3)]
    logs = jnp.concatenate([marks[i : i + GROUP] for i in starts], 1)
    logs = jnp.concatenate([logs, jnp.zeros((GROUP, width - logs.shape[1]), F32)], 1)
    tail = pad_rows(jnp.concatenate([pad_rows(both, prefix_rows(count)), logs], 0), rows).astype(BF16)
    at = pl.ds(back_0.shape[0] - rows, rows)
    back_0[at] = tail
    back_1[at] = tail


def pack(count, grads, terms, back_0, back_1):
    return pl.pallas_call(
        partial(pack_kernel, count),
        in_specs=[vmem()] * 7,
        out_specs=[vmem()] * 2,
        out_shape=[jax.ShapeDtypeStruct(back_0.shape, BF16)] * 2,
        input_output_aliases={5: 0, 6: 1},
        compiler_params=pltpu.CompilerParams(vmem_limit_bytes=4 * MIB),
        cost_estimate=pl.CostEstimate(flops=1 << 20, bytes_accessed=1 << 19, transcendentals=0),
        name="pack",
    )(grads, *terms, back_0, back_1)


def unpack_kernel(count, home_0, home_1, out):
    width = out.shape[1] // 2
    rows = tail_rows(count)
    at = pl.ds(home_0.shape[0] - rows, rows)
    first, second = home_0[at].astype(F32), home_1[at].astype(F32)
    total = first + second
    out[:, :width] = pad_rows(total[:count], PRE_ROWS).astype(BF16)
    out[:, width:] = pad_rows(total[count : 2 * count], PRE_ROWS).astype(BF16)


def unpack(count, width, home_0, home_1):
    return pl.pallas_call(
        partial(unpack_kernel, count),
        in_specs=[vmem()] * 2,
        out_specs=vmem(),
        out_shape=jax.ShapeDtypeStruct((PRE_ROWS, 2 * width), BF16),
        compiler_params=pltpu.CompilerParams(vmem_limit_bytes=4 * MIB),
        cost_estimate=pl.CostEstimate(flops=1000, bytes_accessed=1000, transcendentals=0),
        name="unpack",
    )(home_0, home_1)


def query_kernel(
    count,
    qkv_a,
    qkv_b,
    marks_a,
    marks_b,
    prefix_kv,
    grads,
    weight,
    normed_b,
    w_queries,
    order,
    out,
    qkv_out,
    scores_bias,
    grad_query,
):
    del order
    rows, width = grad_query.shape
    scores_bias[...] = key_bias(marks_a[:rows], marks_a[...], marks_b[...], rows // 2, count)
    low = head_mask(rows)
    marks = grads[:, width:]
    marks_twice = jnp.concatenate([marks, marks], 0)
    ones = jnp.ones((LANES, 4 * rows + LANES), BF16)

    def step(pair, carry):
        at = pl.ds(pl.multiple_of(pair * LANES, LANES), LANES)
        at_k = pl.ds(pl.multiple_of(width + pair * LANES, LANES), LANES)
        at_v = pl.ds(pl.multiple_of(2 * width + pair * LANES, LANES), LANES)
        keys = with_prefix(qkv_a[:, at_k], qkv_b[:, at_k], prefix_kv[:, at])
        values = with_prefix(qkv_a[:, at_v], qkv_b[:, at_v], prefix_kv[:, at_k])
        query = two_heads(qkv_a[:rows, at] * jnp.asarray(HEAD**-0.5, BF16), low)
        tops = marks_twice * picks(rows, pair, 0, -1.0).astype(BF16)
        scores = nn(jnp.concatenate([query, tops], 1), jnp.concatenate([keys.T, ones], 0))
        mask = scores_bias[...]
        weights = jnp.exp(scores + jnp.concatenate([mask, mask], 0))
        bases = marks_twice * picks(rows, pair, 3 * HEADS, -1.0).astype(BF16)
        left = jnp.concatenate([two_heads(grads[:, at], low), bases], 1)
        slopes = weights * nn(left, jnp.concatenate([values.T, ones], 0))
        grad = join_heads(nn(slopes.astype(BF16), keys), low)
        grad_query[:, at] = (grad * HEAD**-0.5).astype(BF16)
        return carry

    lax.fori_loop(0, HEADS // 2, step, 0, unroll=True)
    out[...] = nn(grad_query[...], weight[:width])
    qkv_out[:, :width] = nn(normed_b[...], w_queries[:, :width]).astype(BF16)


def query_part(
    count, qkv_a, qkv_b, marks_a, marks_b, prefix_kv, grads, weight, normed_b, w_queries, order
):
    rows, width = grads.shape[0], grads.shape[1] - LANES
    return pl.pallas_call(
        partial(query_kernel, count),
        in_specs=[vmem()] * 9 + [pl.BlockSpec(memory_space=pl.ANY)],
        out_specs=[vmem()] * 2,
        out_shape=[jax.ShapeDtypeStruct((rows, width), F32), jax.ShapeDtypeStruct(qkv_b.shape, BF16)],
        input_output_aliases={1: 1},
        scratch_shapes=[pltpu.VMEM((rows, 4 * rows + LANES), F32), pltpu.VMEM((rows, width), BF16)],
        compiler_params=pltpu.CompilerParams(vmem_limit_bytes=16 * MIB),
        cost_estimate=pl.CostEstimate(flops=1 << 31, bytes_accessed=1000, transcendentals=0),
        name="query",
    )(qkv_a, qkv_b, marks_a, marks_b, prefix_kv, grads, weight, normed_b, w_queries, order)


def final_kernel(
    qkv_a,
    qkv_b,
    marks_a,
    marks_b,
    grads_0,
    grads_1,
    grads_2,
    grads_3,
    own_0,
    own_1,
    gain,
    grad_middle,
    grad_partial,
    weight,
    back_0,
    back_1,
    scores_bias,
    grad_keys,
):
    half, rows = own_0.shape[0], 2 * own_0.shape[0]
    width = grad_middle.shape[1]
    row, core, y_at = place()
    own = positions(iota((rows, 1), 0), half, row, core, y_at)
    other = all_positions((1, 8 * half), 1, half, row, core, y_at)
    same = nt(marks_a[:rows], jnp.concatenate([marks_a[...], marks_b[...]], 0))
    visible = jnp.logical_and(same > 0.5, own <= other)
    scores_bias[...] = jnp.where(visible, 0.0, NEG)
    low = head_mask(rows)
    blocks = (grads_0, grads_1, grads_2, grads_3)
    marks = jnp.concatenate([g[:, width:] for g in blocks], 0).T

    def step(pair, carry):
        at = pl.ds(pl.multiple_of(pair * LANES, LANES), LANES)
        at_k = pl.ds(pl.multiple_of(width + pair * LANES, LANES), LANES)
        at_v = pl.ds(pl.multiple_of(2 * width + pair * LANES, LANES), LANES)
        queries = jnp.concatenate([qkv_a[:, at], qkv_b[:, at]], 0)
        grads = jnp.concatenate([g[:, at] for g in blocks], 0)
        key_grad, value_grad = key_grads(
            qkv_a[:rows, at_k], qkv_a[:rows, at_v], queries, grads, marks, pair, low, scores_bias[...]
        )
        grad_keys[:, at] = key_grad.astype(BF16)
        grad_keys[:, at_k] = value_grad.astype(BF16)
        return carry

    lax.fori_loop(0, HEADS // 2, step, 0, unroll=True)
    grad_norm = grad_partial[...] + nn(grad_keys[...], weight[width:])
    inputs = jnp.concatenate([own_0[:, :width], own_1[:, :width]], 0).astype(F32)
    unit, inverse = norm_parts(inputs)
    out = (grad_middle[...] + norm_back(unit, inverse, gain[...], grad_norm)).astype(BF16)
    back_0[...] = out[:half]
    back_1[...] = out[half:]


def final_part(qkv_a, qkv_b, marks_a, marks_b, grads, own, gain, grad_middle, grad_partial, weight):
    rows, width = grad_middle.shape
    half = rows // 2
    return pl.pallas_call(
        final_kernel,
        in_specs=[vmem()] * 14,
        out_specs=[vmem()] * 2,
        out_shape=[jax.ShapeDtypeStruct((half, width), BF16)] * 2,
        scratch_shapes=[
            pltpu.VMEM((rows, 4 * rows), F32),
            pltpu.VMEM((rows, 2 * width), BF16),
        ],
        compiler_params=pltpu.CompilerParams(vmem_limit_bytes=16 * MIB),
        cost_estimate=pl.CostEstimate(flops=1000, bytes_accessed=1000, transcendentals=0),
        name="final",
    )(qkv_a, qkv_b, marks_a, marks_b, *grads, *own, gain[None], grad_middle, grad_partial, weight)


def routes(k):
    pairs = []
    for seq in range(4):
        for blk in range(8):
            group, z_at, y_at = seq % 2, blk // 2, blk % 2
            row = (z_at + k + 1) % 2
            pairs.append((seq * 8 + blk, (seq - group + z_at // 2) * 8 + (2 * group + row) * 2 + y_at))
    return pairs


def body_rows(
    tokens,
    segment_ids,
    ln1_gain,
    ln1_bias,
    w_qkv,
    w_out,
    ln2_gain,
    ln2_bias,
    w_fc,
    w_proj,
    prefix_embed,
    w_mlp1,
    b_mlp1,
    w_mlp2,
    b_mlp2,
    cotangent,
):
    half, _, width = tokens.shape
    everyone = ("seq", "blk")
    there = [routes(k) for k in range(2)]
    back = [[(b, a) for a, b in pairs] for pairs in there]
    swap_core = [(i, i ^ 1) for i in range(4)]
    swap_y = [(i, i ^ 1) for i in range(8)]
    swap_both = [(i, i ^ 9) for i in range(32)]
    def after(value, *done):
        return lax.optimization_barrier((value, done))[0]

    out_msgs = split_rows(tokens, segment_ids)
    cot_msgs = split_rows(cotangent)
    own = [lax.ppermute(m, everyone, there[k]) for k, m in enumerate(out_msgs)]
    prefix_kv, inner, w_near, w_back, near_embed, turned = adapter_forward(
        prefix_embed, w_mlp1, b_mlp1, w_mlp2, b_mlp2, w_qkv
    )
    count = prefix_embed.shape[0]
    own = after(own, inner)
    across = [lax.ppermute(m, "blk", swap_y) for m in own]
    beside = [lax.ppermute(m, "seq", swap_core) for m in own]
    cots = [lax.ppermute(m, everyone, there[k]) for k, m in enumerate(after(cot_msgs, beside))]
    beyond = [lax.ppermute(m, "seq", swap_core) for m in across]

    qkv_a, marks_a = project(own + beside, ln1_gain, ln1_bias, w_near)
    kv_b, marks_b, normed_b = project(across + beyond, ln1_gain, ln1_bias, w_near, 1)
    back_0, back_1, grads, grad_middle = middle_part(
        count, qkv_a, kv_b, marks_a, marks_b, prefix_kv, own, cots, ln2_gain, ln2_bias, w_out, w_fc, w_proj
    )
    grads_y = lax.ppermute(grads, "blk", swap_y)
    grads_c = lax.ppermute(grads, "seq", swap_core)
    grad_prefix_kv = prefix_part(count, qkv_a, grads, prefix_kv)
    parts = [lax.ppermute(grad_prefix_kv, "seq", [(i, i ^ far) for i in range(4)]) for far in (2, 1, 3)]
    grad_partial, qkv_b = query_part(
        count, qkv_a, kv_b, marks_a, marks_b, prefix_kv, grads, w_back, normed_b, w_near, grad_prefix_kv
    )
    packed = pack(count, grads, (grad_prefix_kv, *after(parts, grad_partial)), back_0, back_1)
    home = [lax.ppermute(m, everyone, back[k]) for k, m in enumerate(packed)]
    grads_yc = lax.ppermute(after(grads_y, packed), "seq", swap_core)
    final_0, final_1 = final_part(
        qkv_a,
        qkv_b,
        marks_a,
        marks_b,
        (grads, grads_c, grads_y, grads_yc),
        own,
        ln1_gain,
        grad_middle,
        grad_partial,
        w_back,
    )
    finals = [lax.ppermute(m, everyone, back[k]) for k, m in enumerate((final_0, final_1))]
    gathered = [unpack(count, width, *home)]
    gathered += [lax.ppermute(gathered[0], "seq", swap_core), lax.ppermute(gathered[0], "blk", swap_y)]
    gathered += [lax.ppermute(gathered[0], everyone, swap_both)]
    input_grad, summed = finish(finals, gathered, near_embed, inner, turned)
    block_out, log_total = land(count, after(home, gathered[0]), half, width)
    return (block_out, input_grad, summed[0], summed[1], summed[2], summed[3], summed[4], log_total)


def solution(mesh):
    four_by_eight = mesh.shape["seq"] == 4 and mesh.shape["blk"] == 8
    placed = (
        P("blk", "seq", None),
        P("blk", "seq"),
        P(),
        P(),
        P(),
        P(),
        P(),
        P(),
        P(),
        P(),
        P(),
        P(),
        P(),
        P(),
        P(),
        P("blk", "seq", None),
    )
    return jax.shard_map(
        body_rows if four_by_eight else body_plain,
        mesh=mesh,
        in_specs=placed,
        out_specs=(
            P("blk", "seq", None),
            P("blk", "seq", None),
            P(),
            P(),
            P(),
            P(),
            P(),
            P("seq", None, "blk"),
        ),
        check_vma=False,
    )
```

```python
from functools import partial
import math

import jax
import jax.numpy as jnp
from jax import lax
from jax.experimental import pallas as pl
from jax.experimental.pallas import tpu as pltpu
from jax.sharding import PartitionSpec as P

HEADS = 16
HEAD = 64


EPS = 1e-05
NEG = -1e30
HIGH = lax.Precision.HIGHEST


def layer_norm(value_in, gain, bias):
    average = jnp.mean(value_in, axis=-1, keepdims=True)
    centered = value_in - average
    variance = jnp.mean(centered * centered, axis=-1, keepdims=True)
    return centered * lax.rsqrt(variance + EPS) * gain + bias


def adapter(prefix_embed, w_mlp1, b_mlp1, w_mlp2, b_mlp2):
    inner_act = jnp.tanh(jnp.dot(prefix_embed, w_mlp1, precision=HIGH) + b_mlp1)
    return jnp.dot(inner_act, w_mlp2, precision=HIGH) + b_mlp2


def gelu_tanh(pre_act):
    return jax.nn.gelu(pre_act, approximate=True)


def split_heads(block_in):
    return block_in.reshape(block_in.shape[0], block_in.shape[1], HEADS, HEAD)


def allowed(query_pos, query_seg, key_pos, key_seg):
    same_seg = query_seg.T[:, :, None] == key_seg.T[:, None, :]
    causal = key_pos[None, None, :] <= query_pos[None, :, None]
    return jnp.logical_and(same_seg, causal)[:, None]


def scores_of(query_heads, key_block, score_scale):
    return score_scale * jnp.einsum(
        "prhd,krhd->rhpk", query_heads, split_heads(key_block), preferred_element_type=jnp.float32
    )


def block_grads(
    query_heads,
    grad_heads,
    log_total,
    slope_base,
    query_pos,
    query_seg,
    key_block,
    value_block,
    key_pos,
    key_seg,
    score_scale,
):
    scores = scores_of(query_heads, key_block, score_scale)
    scores = jnp.where(allowed(query_pos, query_seg, key_pos, key_seg), scores, NEG)
    weights = jnp.exp(scores - log_total[..., None])
    grad_weights = jnp.einsum(
        "prhd,krhd->rhpk", grad_heads, split_heads(value_block), preferred_element_type=jnp.float32
    )
    slopes = (weights * (grad_weights - slope_base[..., None])).astype(jnp.bfloat16)
    return (weights.astype(jnp.bfloat16), slopes)


def body_plain(
    tokens,
    segment_ids,
    ln1_gain,
    ln1_bias,
    w_qkv,
    w_out,
    ln2_gain,
    ln2_bias,
    w_fc,
    w_proj,
    prefix_embed,
    w_mlp1,
    b_mlp1,
    w_mlp2,
    b_mlp2,
    cotangent,
):
    pos_dev, row_count, width = tokens.shape
    score_scale = HEAD ** (-0.5)
    flat_rows = pos_dev * row_count
    own_pos = lax.axis_index("blk") * pos_dev + jnp.arange(pos_dev)
    inputs = tokens.astype(jnp.float32).reshape(flat_rows, width)
    normed_one = layer_norm(inputs, ln1_gain, ln1_bias).astype(jnp.bfloat16)
    projected = jnp.dot(normed_one, w_qkv, preferred_element_type=jnp.float32).astype(jnp.bfloat16)
    queries = projected[:, :width].reshape(pos_dev, row_count, width)
    keys = projected[:, width : 2 * width].reshape(pos_dev, row_count, width)
    values = projected[:, 2 * width :].reshape(pos_dev, row_count, width)
    query_heads = split_heads(queries)
    prefix_low = adapter(prefix_embed, w_mlp1, b_mlp1, w_mlp2, b_mlp2).astype(jnp.bfloat16)
    prefix_keys = prefix_low[:, :width].reshape(-1, HEADS, HEAD)
    prefix_values = prefix_low[:, width:].reshape(-1, HEADS, HEAD)
    prefix_scores = score_scale * jnp.einsum(
        "prhd,jhd->rhpj", query_heads, prefix_keys, preferred_element_type=jnp.float32
    )
    start_top = jnp.max(prefix_scores, -1)
    start_weights = jnp.exp(prefix_scores - start_top[..., None])
    start_denom = jnp.sum(start_weights, -1)
    start_numer = jnp.einsum(
        "rhpj,jhd->rhpd",
        start_weights.astype(jnp.bfloat16),
        prefix_values,
        preferred_element_type=jnp.float32,
    )
    start_state = (start_top, start_denom, start_numer)
    running = start_state
    key_shards = lax.all_gather(keys, "blk", axis=0, tiled=True)
    value_shards = lax.all_gather(values, "blk", axis=0, tiled=True)
    seg_shards = lax.all_gather(segment_ids, "blk", axis=0, tiled=True)
    num_rows = key_shards.shape[0]
    forward_stride = math.gcd(num_rows, 512)

    def inner(state, block_index):
        running_top, denominator, numerator = state
        offset = block_index * forward_stride
        key_block = lax.dynamic_slice_in_dim(key_shards, offset, forward_stride, 0)
        value_block = lax.dynamic_slice_in_dim(value_shards, offset, forward_stride, 0)
        seg_block = lax.dynamic_slice_in_dim(seg_shards, offset, forward_stride, 0)
        key_pos = offset + jnp.arange(forward_stride)
        scores = jnp.where(
            allowed(own_pos, segment_ids, key_pos, seg_block),
            scores_of(query_heads, key_block, score_scale),
            NEG,
        )
        new_top = jnp.maximum(running_top, jnp.max(scores, -1))
        fading = jnp.exp(running_top - new_top)
        weights = jnp.exp(scores - new_top[..., None])
        denominator = denominator * fading + jnp.sum(weights, -1)
        numerator = numerator * fading[..., None] + jnp.einsum(
            "rhpk,krhd->rhpd",
            weights.astype(jnp.bfloat16),
            split_heads(value_block),
            preferred_element_type=jnp.float32,
        )
        return ((new_top, denominator, numerator), None)

    running, _ = lax.scan(inner, running, jnp.arange(num_rows // forward_stride))
    final_top, final_denom, final_numer = running
    log_total = final_top + jnp.log(final_denom)
    attended = final_numer / final_denom[..., None]
    attended_rows = jnp.transpose(attended, (2, 0, 1, 3)).reshape(flat_rows, width)
    middle = inputs + jnp.dot(
        attended_rows.astype(jnp.bfloat16), w_out, preferred_element_type=jnp.float32
    )
    normed_two = layer_norm(middle, ln2_gain, ln2_bias).astype(jnp.bfloat16)
    hidden_pre = jnp.dot(normed_two, w_fc, preferred_element_type=jnp.float32)
    hidden_act = gelu_tanh(hidden_pre).astype(jnp.bfloat16)
    outputs = middle + jnp.dot(hidden_act, w_proj, preferred_element_type=jnp.float32)
    block_out = outputs.astype(jnp.bfloat16).reshape(pos_dev, row_count, width)
    grad_out = cotangent.reshape(flat_rows, width)
    grad_act = jnp.dot(grad_out, w_proj.T, preferred_element_type=jnp.float32)
    _, gelu_back = jax.vjp(gelu_tanh, hidden_pre)
    grad_pre = gelu_back(grad_act)[0].astype(jnp.bfloat16)
    grad_norm_two = jnp.dot(grad_pre, w_fc.T, preferred_element_type=jnp.float32)
    _, norm_two_back = jax.vjp(partial(layer_norm, gain=ln2_gain, bias=ln2_bias), middle)
    grad_middle = grad_out.astype(jnp.float32) + norm_two_back(grad_norm_two)[0]
    grad_attended = jnp.dot(
        grad_middle.astype(jnp.bfloat16), w_out.T, preferred_element_type=jnp.float32
    ).astype(jnp.bfloat16)
    grad_flat = grad_attended.reshape(pos_dev, row_count, width)
    grad_heads = split_heads(grad_flat)
    slope_base = jnp.sum(jnp.transpose(grad_heads.astype(jnp.float32), (1, 2, 0, 3)) * attended, -1)
    prefix_weights = jnp.exp(prefix_scores - log_total[..., None])
    prefix_dw = jnp.einsum(
        "prhd,jhd->rhpj", grad_heads, prefix_values, preferred_element_type=jnp.float32
    )
    prefix_slopes = (prefix_weights * (prefix_dw - slope_base[..., None])).astype(jnp.bfloat16)
    grad_query = score_scale * jnp.einsum(
        "rhpj,jhd->prhd", prefix_slopes, prefix_keys, preferred_element_type=jnp.float32
    )
    grad_pkeys = score_scale * jnp.einsum(
        "rhpj,prhd->jhd", prefix_slopes, query_heads, preferred_element_type=jnp.float32
    )
    grad_pvalues = jnp.einsum(
        "rhpj,prhd->jhd",
        prefix_weights.astype(jnp.bfloat16),
        grad_heads,
        preferred_element_type=jnp.float32,
    )
    grad_prefix_kv = jnp.concatenate(
        [grad_pkeys.reshape(-1, width), grad_pvalues.reshape(-1, width)], -1
    )
    keys_all, values_all, segs_all = (
        lax.all_gather(keys, "blk", axis=0, tiled=True),
        lax.all_gather(values, "blk", axis=0, tiled=True),
        lax.all_gather(segment_ids, "blk", axis=0, tiled=True),
    )
    length = keys_all.shape[0]
    stride = math.gcd(length, 512)

    def backward_step(grad_q, block_index):
        offset = block_index * stride
        key_block = lax.dynamic_slice_in_dim(keys_all, offset, stride, 0)
        value_block = lax.dynamic_slice_in_dim(values_all, offset, stride, 0)
        seg_block = lax.dynamic_slice_in_dim(segs_all, offset, stride, 0)
        key_pos = offset + jnp.arange(stride)
        weights_low, slopes = block_grads(
            query_heads,
            grad_heads,
            log_total,
            slope_base,
            own_pos,
            segment_ids,
            key_block,
            value_block,
            key_pos,
            seg_block,
            score_scale,
        )
        grad_q = grad_q + score_scale * jnp.einsum(
            "rhpk,krhd->prhd", slopes, split_heads(key_block), preferred_element_type=jnp.float32
        )
        key_term = score_scale * jnp.einsum(
            "rhpk,prhd->krhd", slopes, query_heads, preferred_element_type=jnp.float32
        )
        value_term = jnp.einsum(
            "rhpk,prhd->krhd", weights_low, grad_heads, preferred_element_type=jnp.float32
        )
        return (
            grad_q,
            (
                key_term.reshape(stride, row_count, width),
                value_term.reshape(stride, row_count, width),
            ),
        )

    grad_query, (key_terms, value_terms) = lax.scan(
        backward_step, grad_query, jnp.arange(length // stride)
    )
    key_terms = key_terms.reshape(length, row_count, width)
    value_terms = value_terms.reshape(length, row_count, width)
    grad_keys, grad_values = (
        lax.psum_scatter(key_terms, "blk", scatter_dimension=0, tiled=True),
        lax.psum_scatter(value_terms, "blk", scatter_dimension=0, tiled=True),
    )
    grad_proj = jnp.concatenate(
        [
            grad_query.reshape(flat_rows, width).astype(jnp.bfloat16),
            grad_keys.reshape(flat_rows, width).astype(jnp.bfloat16),
            grad_values.reshape(flat_rows, width).astype(jnp.bfloat16),
        ],
        -1,
    )
    grad_norm_one = jnp.dot(grad_proj, w_qkv.T, preferred_element_type=jnp.float32)
    _, norm_one_back = jax.vjp(partial(layer_norm, gain=ln1_gain, bias=ln1_bias), inputs)
    input_grad = (grad_middle + norm_one_back(grad_norm_one)[0]).reshape(pos_dev, row_count, width)
    _, adapter_back = jax.vjp(adapter, prefix_embed, w_mlp1, b_mlp1, w_mlp2, b_mlp2)
    local_grads = adapter_back(grad_prefix_kv)
    summed = lax.psum(
        (local_grads[0], local_grads[1], local_grads[2], local_grads[3], local_grads[4]),
        ("seq", "blk"),
    )
    return (block_out, input_grad, summed[0], summed[1], summed[2], summed[3], summed[4], log_total)


F32 = jnp.float32
BF16 = jnp.bfloat16
LANES = 128
PRE_ROWS = 16
MIB = 1 << 20


def nn(left, right):
    return jnp.dot(left, right, preferred_element_type=F32)


def nt(left, right):
    return lax.dot_general(left, right, (((1,), (1,)), ((), ())), preferred_element_type=F32)


def norm_parts(value_in):
    average = jnp.mean(value_in, axis=-1, keepdims=True)
    centered = value_in - average
    variance = jnp.mean(centered * centered, axis=-1, keepdims=True)
    inverse = lax.rsqrt(variance + EPS)
    return centered * inverse, inverse


def norm_back(unit, inverse, gain, grad):
    scaled = grad * gain
    first = jnp.mean(scaled, axis=-1, keepdims=True)
    second = jnp.mean(scaled * unit, axis=-1, keepdims=True)
    return inverse * (scaled - first - unit * second)


def iota(shape, dim):
    return lax.broadcasted_iota(jnp.int32, shape, dim)


def place():
    blk = lax.axis_index("blk")
    return (blk // 2) % 2, lax.axis_index("seq") % 2, blk % 2


def positions(index, half, row, core, y_at):
    upper = (index >= half).astype(jnp.int32)
    slot = 1 - (upper + row - 2 * upper * row)
    block = (2 * core + slot) * 2 + y_at
    return block * half + index - upper * half


def members(core, y_at):
    return ((core, y_at), (1 - core, y_at), (core, 1 - y_at), (1 - core, 1 - y_at))


def all_positions(shape, dim, half, row, core, y_at):
    part = tuple(2 * half if d == dim else n for d, n in enumerate(shape))
    return jnp.concatenate(
        [positions(iota(part, dim), half, row, c, y) for c, y in members(core, y_at)], dim
    )


def vmem():
    return pl.BlockSpec(memory_space=pltpu.VMEM)


def hbm():
    return pl.BlockSpec(memory_space=pltpu.HBM)


def kept_in_hbm(*arrays):
    return [pltpu.with_memory_space_constraint(a, pltpu.HBM) for a in arrays]


def by_tiles(block):
    half, pair, width = block.shape
    tiles = jnp.transpose(block.reshape(half, pair, width // LANES, LANES), (0, 2, 1, 3))
    return tiles.reshape(half, pair * width // LANES, LANES)


def from_tiles(tiles, width):
    half, count, _ = tiles.shape
    pair = count * LANES // width
    block = jnp.transpose(tiles.reshape(half, width // LANES, pair, LANES), (0, 2, 1, 3))
    return block.reshape(half, pair, width)


def odd_place():
    return (lax.axis_index("blk") // 2) % 2 == 0


def split_kernel(marked, *refs):
    tokens, ids, (out_0, out_1, work) = refs[0], refs[1], refs[-3:]
    half, count, _ = tokens.shape
    odd = odd_place()
    work[pl.ds(0, half * count)] = tokens[...].astype(F32).reshape(half * count, LANES)
    for i in range(count // 2):
        at = pl.ds(i * LANES, LANES)
        first, second = (work[pl.ds(2 * i + r, half, stride=count)] for r in range(2))
        out_0[:, at] = jnp.where(odd, second, first).astype(BF16)
        out_1[:, at] = jnp.where(odd, first, second).astype(BF16)
    if marked:
        width = count // 2 * LANES
        first, second = (
            jnp.where(iota((LANES, half), 0) == ids[r : r + 1], 1.0, 0.0).T for r in range(2)
        )
        out_0[:, width:] = jnp.where(odd, second, first).astype(BF16)
        out_1[:, width:] = jnp.where(odd, first, second).astype(BF16)


def split_rows(block, segment_ids=None):
    tiles = by_tiles(block)
    half, count, _ = tiles.shape
    extra = () if segment_ids is None else kept_in_hbm(segment_ids.T)
    width = count // 2 * LANES + LANES * len(extra)
    return pl.pallas_call(
        partial(split_kernel, bool(extra)),
        in_specs=[vmem()] * (1 + len(extra)),
        out_specs=[vmem()] * 2,
        out_shape=[jax.ShapeDtypeStruct((half, width), BF16)] * 2,
        scratch_shapes=[pltpu.VMEM(((half + 1) * count, LANES), F32)],
        compiler_params=pltpu.CompilerParams(vmem_limit_bytes=4 * MIB),
        cost_estimate=pl.CostEstimate(flops=1 << 31, bytes_accessed=1000, transcendentals=0),
        name="split",
    )(*kept_in_hbm(tiles), *extra)


def place_rows(msg_0, msg_1, work):
    count = 2 * msg_0.shape[1] // LANES
    half = work.shape[0] // count - 1
    odd = odd_place()
    for i in range(count // 2):
        at = pl.ds(i * LANES, LANES)
        one, two = msg_0[:half, at].astype(F32), msg_1[:half, at].astype(F32)
        work[pl.ds(2 * i, half, stride=count)] = jnp.where(odd, two, one)
        work[pl.ds(2 * i + 1, half, stride=count)] = jnp.where(odd, one, two)


def land_kernel(first_row, msg_0, msg_1, out, logs, work):
    half = out.shape[0]
    heads = logs.shape[1]
    place_rows(msg_0, msg_1, work)
    out[...] = work[pl.ds(0, half * out.shape[1])].reshape(out.shape).astype(out.dtype)
    odd = odd_place()
    found = []
    for k, message in enumerate((msg_0, msg_1)):
        rows = message[half:].astype(F32)[first_row : first_row + GROUP]
        slots = [rows[:, i * LANES + k * half : i * LANES + (k + 1) * half] for i in range(3 * heads // GROUP)]
        groups = [slots[i] + slots[i + 1] + slots[i + 2] for i in range(0, len(slots), 3)]
        found.append(jnp.concatenate(groups, 0))
    logs[0] = jnp.where(odd, found[1], found[0])
    logs[1] = jnp.where(odd, found[0], found[1])


def land(count_prefix, messages, half, width):
    count = 2 * width // LANES
    out = pl.pallas_call(
        partial(land_kernel, prefix_rows(count_prefix)),
        in_specs=[vmem()] * 2,
        out_specs=[vmem()] * 2,
        out_shape=[
            jax.ShapeDtypeStruct((half, count, LANES), BF16),
            jax.ShapeDtypeStruct((2, HEADS, half), F32),
        ],
        scratch_shapes=[pltpu.VMEM(((half + 1) * count, LANES), F32)],
        compiler_params=pltpu.CompilerParams(vmem_limit_bytes=4 * MIB),
        cost_estimate=pl.CostEstimate(flops=1000, bytes_accessed=1000, transcendentals=0),
        name="land",
    )(*messages)
    return from_tiles(out[0], width), out[1]


def project_kernel(count, first, *refs):
    messages, (gain, bias, weight, out, marks, normed) = refs[:count], refs[count:]
    half, width = messages[0].shape[0], normed.shape[1]
    for i, message in enumerate(messages):
        rows = pl.ds(i * half, half)
        unit, _ = norm_parts(message[:, :width].astype(F32))
        normed[rows] = (unit * gain[...] + bias[...]).astype(BF16)
        marks[rows] = message[:, width:]
    for i in range(first, 3):
        at = pl.ds(i * width, width)
        out[:, at] = nn(normed[...], weight[:, at]).astype(BF16)


def project(messages, gain, bias, weight, first=0):
    count, half = len(messages), messages[0].shape[0]
    width, columns = weight.shape
    rows = count * half
    return pl.pallas_call(
        partial(project_kernel, count, first),
        in_specs=[vmem()] * (count + 3),
        out_specs=[vmem()] * (2 + first),
        out_shape=[
            jax.ShapeDtypeStruct((rows, columns), BF16),
            jax.ShapeDtypeStruct((rows, LANES), BF16),
        ]
        + [jax.ShapeDtypeStruct((rows, width), BF16)] * first,
        scratch_shapes=[pltpu.VMEM((rows, width), BF16)] * (1 - first),
        compiler_params=pltpu.CompilerParams(vmem_limit_bytes=16 * MIB),
        cost_estimate=pl.CostEstimate(
            flops=2 * rows * width * columns, bytes_accessed=2 * width * columns, transcendentals=0
        ),
        name="project",
    )(*messages, gain[None], bias[None], weight)


def halves(value_in):
    high = value_in.astype(BF16)
    return high, (value_in - high.astype(F32)).astype(BF16)


def pad_rows(value_in, rows):
    if rows == value_in.shape[0]:
        return value_in
    return jnp.concatenate(
        [value_in, jnp.zeros((rows - value_in.shape[0], value_in.shape[1]), value_in.dtype)], 0
    )


def three_products(product, left, weight):
    rows = left.shape[0]
    high, low = halves(left)
    w_high, w_low = halves(weight)
    both = product(jnp.concatenate([high, low], 0), w_high)
    return both[:rows] + both[rows:] + product(high, w_low)


def adapter_kernel(
    h_embed,
    w_mlp1,
    h_mlp1,
    w_mlp2,
    h_mlp2,
    w_qkv,
    out,
    inner,
    v_qkv,
    w_back,
    embed,
    turned,
    v_mlp1,
    v_mlp2,
    b_mlp1,
    b_mlp2,
    sems,
):
    steps, step = v_mlp2.shape[0], v_mlp2.shape[2]
    small = []
    for i, (source, target) in enumerate(
        ((h_embed, embed), (h_mlp1, b_mlp1), (h_mlp2, b_mlp2), (w_mlp1, v_mlp1))
    ):
        small.append(pltpu.make_async_copy(source, target, sems.at[steps + i]))
        small[-1].start()
    width = w_qkv.shape[0]
    weights = []
    for i in range(3):
        at = pl.ds(i * width, width)
        weights.append(
            pltpu.make_async_copy(w_qkv.at[:, at], v_qkv.at[:, at], sems.at[steps + len(small) + i])
        )
        weights[-1].start()
    rest = []
    for i in range(steps):
        copy = pltpu.make_async_copy(w_mlp2.at[:, pl.ds(i * step, step)], v_mlp2.at[i], sems.at[i])
        copy.start()
        rest.append(copy)
    for copy in small:
        copy.wait()
    source = pad_rows(embed[...], PRE_ROWS)
    act = jnp.tanh(three_products(nn, source, v_mlp1[...]) + b_mlp1[...])
    inner[...] = act
    columns, hidden = steps * step, v_mlp1.shape[1]
    for i in range(v_mlp1.shape[0] // hidden):
        part = v_mlp1[pl.ds(i * hidden, hidden)].astype(BF16)
        turned[pl.ds(columns + i * hidden, hidden)] = part.T
    for i, copy in enumerate(weights):
        at = pl.ds(i * width, width)
        copy.wait()
        w_back[at] = v_qkv[:, at].T
    for i, copy in enumerate(rest):
        copy.wait()
        turned[pl.ds(i * step, step)] = v_mlp2[i].astype(BF16).T
        span = pl.ds(i * step, step)
        part = three_products(nn, act, v_mlp2[i]) + b_mlp2[:, span]
        out[:, span] = jnp.where(iota(part.shape, 0) < embed.shape[0], part, 0.0).astype(BF16)


def adapter_forward(embed, w_mlp1, b_mlp1, w_mlp2, b_mlp2, w_qkv):
    width, hidden = w_mlp1.shape
    columns = w_mlp2.shape[1]
    steps = 4
    return pl.pallas_call(
        adapter_kernel,
        in_specs=[hbm()] * 6,
        out_specs=[vmem()] * 6,
        out_shape=[
            jax.ShapeDtypeStruct((PRE_ROWS, columns), BF16),
            jax.ShapeDtypeStruct((PRE_ROWS, hidden), F32),
            pltpu.VMEM(w_qkv.shape, w_qkv.dtype),
            pltpu.VMEM(w_qkv.shape[::-1], w_qkv.dtype),
            pltpu.VMEM(embed.shape, F32),
            pltpu.VMEM((columns + width, hidden), BF16),
        ],
        scratch_shapes=[
            pltpu.VMEM((width, hidden), F32),
            pltpu.VMEM((steps, hidden, columns // steps), F32),
            pltpu.VMEM((1, hidden), F32),
            pltpu.VMEM((1, columns), F32),
            pltpu.SemaphoreType.DMA((7 + steps,)),
        ],
        compiler_params=pltpu.CompilerParams(vmem_limit_bytes=20 * MIB),
        cost_estimate=pl.CostEstimate(flops=1 << 32, bytes_accessed=6 * MIB, transcendentals=1 << 13),
        name="adapter",
    )(*kept_in_hbm(embed, w_mlp1, b_mlp1[None], w_mlp2, b_mlp2[None], w_qkv))


def outer(left, right):
    l_high, l_low = halves(left)
    r_high, r_low = halves(right)
    return lax.dot_general(
        jnp.concatenate([l_high, l_high, l_low], 0),
        jnp.concatenate([r_high, r_low, r_high], 0),
        (((0,), (0,)), ((), ())),
        preferred_element_type=F32,
    )


def two_products(left, weight):
    high, low = halves(left)
    both = nn(jnp.concatenate([high, low], 0), weight)
    return both[: left.shape[0]] + both[left.shape[0] :]


def adapter_back_kernel(
    home_0,
    home_1,
    part_0,
    part_1,
    part_2,
    part_3,
    embed,
    inner,
    turned,
    block,
    grad_prefix,
    grad_mlp1,
    grad_bias1,
    grad_mlp2,
    grad_bias2,
    o_block,
    o_mlp1,
    o_mlp2,
    sems,
):
    steps, step = o_mlp2.shape[0], o_mlp2.shape[1]
    first, second, third, fourth = (p[...].astype(F32) for p in (part_0, part_1, part_2, part_3))
    grads = (first + second) + (third + fourth)
    act = inner[...]
    stores = []
    grad_bias2[...] = jnp.sum(grads, 0, keepdims=True)
    for i in range(steps):
        o_mlp2[i] = outer(act[:, i * step : (i + 1) * step], grads)
        stores.append(
            pltpu.make_async_copy(o_mlp2.at[i], grad_mlp2.at[pl.ds(i * step, step)], sems.at[i])
        )
        stores[-1].start()
    columns, (width, hidden) = o_mlp2.shape[2], o_mlp1.shape
    place_rows(home_0, home_1, o_block)
    stores.append(pltpu.make_async_copy(o_block.at[pl.ds(0, block.shape[0])], block, sems.at[steps + 1]))
    stores[-1].start()
    back = two_products(grads, turned[:columns]) * (1.0 - act * act)
    grad_bias1[...] = jnp.sum(back, 0, keepdims=True)
    o_mlp1[...] = outer(pad_rows(embed[...], PRE_ROWS), back)
    stores.append(pltpu.make_async_copy(o_mlp1, grad_mlp1, sems.at[steps]))
    stores[-1].start()
    for i in range(width // hidden):
        part = two_products(back, turned[pl.ds(columns + i * hidden, hidden)])
        grad_prefix[:, pl.ds(i * hidden, hidden)] = part[: embed.shape[0]]
    for copy in stores:
        copy.wait()


def finish(finals, parts, embed, inner, turned):
    hidden, width = turned.shape[1], embed.shape[1]
    columns = turned.shape[0] - width
    half = finals[0].shape[0]
    steps = 4
    tiles = 2 * width // LANES
    out = pl.pallas_call(
        adapter_back_kernel,
        in_specs=[vmem()] * 9,
        out_specs=[hbm(), vmem(), hbm(), vmem(), hbm(), vmem()],
        out_shape=[
            jax.ShapeDtypeStruct((half * tiles, LANES), F32),
            jax.ShapeDtypeStruct(embed.shape, F32),
            jax.ShapeDtypeStruct((width, hidden), F32),
            jax.ShapeDtypeStruct((1, hidden), F32),
            jax.ShapeDtypeStruct((hidden, columns), F32),
            jax.ShapeDtypeStruct((1, columns), F32),
        ],
        scratch_shapes=[
            pltpu.VMEM(((half + 1) * tiles, LANES), F32),
            pltpu.VMEM((width, hidden), F32),
            pltpu.VMEM((steps, hidden // steps, columns), F32),
            pltpu.SemaphoreType.DMA((steps + 2,)),
        ],
        compiler_params=pltpu.CompilerParams(vmem_limit_bytes=16 * MIB),
        cost_estimate=pl.CostEstimate(flops=1000, bytes_accessed=1000, transcendentals=0),
        name="finish",
    )(*finals, *parts, embed, inner, turned)
    block = from_tiles(out[0].reshape(half, tiles, LANES), width)
    return block, (out[1], out[2], out[3][0], out[4], out[5][0])


def head_mask(rows):
    return iota((rows, LANES), 1) < HEAD


def two_heads(pair, low):
    zero = jnp.zeros_like(pair)
    return jnp.concatenate([jnp.where(low, pair, zero), jnp.where(low, zero, pair)], 0)


def join_heads(stacked, low):
    rows = stacked.shape[0] // 2
    return jnp.where(low, stacked[:rows], stacked[rows:])


def picks(rows, pair, first, value):
    lane = iota((rows, LANES), 1)
    inside = jnp.logical_and(lane >= first, lane < first + 3 * HEADS)
    parts = [
        jnp.where(jnp.logical_and(inside, lane % HEADS == 2 * pair + i), value, 0.0) for i in range(2)
    ]
    return jnp.concatenate(parts, 0)


def three_parts(value_in, first):
    lane = iota(value_in.shape, 1)
    high = value_in.astype(BF16).astype(F32)
    rest = value_in - high
    middle = rest.astype(BF16).astype(F32)
    low = rest - middle
    part = (lane - first) // HEADS
    chosen = jnp.where(part == 0, high, jnp.where(part == 1, middle, low))
    inside = jnp.logical_and(lane >= first, lane < first + 3 * HEADS)
    return jnp.where(inside, chosen, 0.0)


def key_bias(marks_own, marks_a, marks_b, half, count):
    row, core, y_at = place()
    rows = 2 * half
    own = positions(iota((rows, 1), 0), half, row, core, y_at)
    other = all_positions((1, 8 * half), 1, half, row, core, y_at)
    same = nt(marks_own, jnp.concatenate([marks_a, marks_b], 0))
    visible = jnp.logical_and(same > 0.5, other <= own)
    token_bias = jnp.where(visible, 0.0, NEG)
    prefix_bias = jnp.where(iota((rows, LANES), 1) < count, 0.0, NEG)
    return jnp.concatenate([token_bias, prefix_bias], 1)


def with_prefix(part_a, part_b, prefix):
    pad = jnp.zeros((LANES - prefix.shape[0], prefix.shape[1]), prefix.dtype)
    return jnp.concatenate([part_a, part_b, prefix, pad], 0)


def middle_kernel(
    count,
    qkv_a,
    qkv_b,
    marks_a,
    marks_b,
    prefix_kv,
    own_0,
    own_1,
    cot_0,
    cot_1,
    gain,
    bias,
    w_out,
    w_fc,
    w_proj,
    back_0,
    back_1,
    grad_out_heads,
    grad_middle,
    v_out,
    v_fc,
    v_proj,
    sems,
    scores_bias,
    attended,
    stats,
    middle,
    normed,
    total,
    grad_norm,
    cot,
):
    half, rows = own_0.shape[0], 2 * own_0.shape[0]
    width = middle.shape[1]
    steps, step = v_fc.shape[0], v_fc.shape[2]
    copies = [pltpu.make_async_copy(w_out, v_out, sems.at[0])]
    for i in range(steps):
        span = pl.ds(i * step, step)
        copies.append(pltpu.make_async_copy(w_fc.at[:, span], v_fc.at[i], sems.at[1 + 2 * i]))
        copies.append(pltpu.make_async_copy(w_proj.at[span], v_proj.at[i], sems.at[2 + 2 * i]))
    for copy in copies:
        copy.start()

    scores_bias[...] = key_bias(marks_a[:rows], marks_a[...], marks_b[...], half, count)
    low = head_mask(rows)
    lane = iota((rows, LANES), 1)
    stats[...] = jnp.zeros_like(stats)

    def attend(pair, carry):
        at = pl.ds(pl.multiple_of(pair * LANES, LANES), LANES)
        at_k = pl.ds(pl.multiple_of(width + pair * LANES, LANES), LANES)
        at_v = pl.ds(pl.multiple_of(2 * width + pair * LANES, LANES), LANES)
        query = two_heads(qkv_a[:rows, at] * jnp.asarray(HEAD**-0.5, BF16), low)
        keys = with_prefix(qkv_a[:, at_k], qkv_b[:, at_k], prefix_kv[:, at])
        values = with_prefix(qkv_a[:, at_v], qkv_b[:, at_v], prefix_kv[:, at_k])
        scores = nt(query, keys)
        mask = scores_bias[...]
        scores = scores + jnp.concatenate([mask, mask], 0)
        top = jnp.max(scores, -1, keepdims=True)
        weights = jnp.exp(scores - top)
        denominator = jnp.sum(weights, -1, keepdims=True)
        mixed = nn(weights.astype(BF16), values) / denominator
        attended[:, at] = join_heads(mixed, low)
        log_total = top + jnp.log(denominator)
        inside = lane < 3 * HEADS
        for i in range(2):
            here = jnp.logical_and(inside, lane % HEADS == 2 * pair + i)
            stats[...] = jnp.where(here, log_total[i * rows : (i + 1) * rows], stats[...])
        return carry

    lax.fori_loop(0, HEADS // 2, attend, 0, unroll=4)

    copies[0].wait()
    inputs = jnp.concatenate([own_0[:, :width], own_1[:, :width]], 0).astype(F32)
    middle[...] = inputs + nn(attended[...].astype(BF16), v_out[...])
    unit, _ = norm_parts(middle[...])
    normed[...] = (unit * gain[...] + bias[...]).astype(BF16)
    cot[...] = jnp.concatenate([cot_0[...], cot_1[...]], 0)
    total[...] = middle[...]
    grad_norm[...] = jnp.zeros_like(grad_norm)

    def feed(i, carry):
        for which in (0, 1):
            pltpu.make_async_copy(
                (v_fc, v_proj)[which].at[i], (v_fc, v_proj)[which].at[i], sems.at[1 + 2 * i + which]
            ).wait()
        fc, proj = v_fc[i], v_proj[i]
        pre = nn(normed[...], fc)
        grad_act = nt(cot[...], proj)
        cubic = 0.044715 * pre * pre
        curve = jnp.tanh(math.sqrt(2 / math.pi) * pre * (1.0 + cubic))
        act = 0.5 * pre * (1.0 + curve)
        slope = 0.5 * (1.0 + curve) + 0.5 * math.sqrt(2 / math.pi) * pre * (1.0 - curve * curve) * (
            1.0 + 3.0 * cubic
        )
        grad_pre = (grad_act * slope).astype(BF16)
        total[...] += nn(act.astype(BF16), proj)
        grad_norm[...] += nt(grad_pre, fc)
        return carry

    lax.fori_loop(0, steps, feed, 0, unroll=True)

    out = total[...].astype(BF16)
    back_0[:half] = out[:half]
    back_1[:half] = out[half:]
    unit, inverse = norm_parts(middle[...])
    grads = cot[...].astype(F32) + norm_back(unit, inverse, gain[...], grad_norm[...])
    grad_middle[...] = grads
    grad_heads = nt(grads.astype(BF16), v_out[...]).astype(BF16)
    grad_out_heads[:, :width] = grad_heads
    product = grad_heads.astype(F32) * attended[...]
    ones = jnp.where(
        jnp.logical_and(
            iota((width, LANES), 0) // HEAD == iota((width, LANES), 1) % HEADS,
            jnp.logical_and(
                iota((width, LANES), 1) >= 3 * HEADS, iota((width, LANES), 1) < 6 * HEADS
            ),
        ),
        1.0,
        0.0,
    ).astype(BF16)
    bases = jnp.zeros((rows, LANES), F32)
    for _ in range(2):
        part = product.astype(BF16)
        bases = bases + nn(part, ones)
        product = product - part.astype(F32)
    marks = three_parts(stats[...], 0) + three_parts(bases, 3 * HEADS)
    marks = marks.astype(BF16)
    grad_out_heads[:, width:] = marks


def middle_part(count, qkv_a, qkv_b, marks_a, marks_b, prefix_kv, own, cots, gain, bias, w_out, w_fc, w_proj):
    half, width = cots[0].shape
    rows = 2 * half
    hidden = w_fc.shape[1]
    steps = 2
    step = hidden // steps
    wide = width + LANES
    return pl.pallas_call(
        partial(middle_kernel, count),
        in_specs=[vmem()] * 11 + [hbm()] * 3,
        out_specs=[vmem()] * 4,
        out_shape=[
            jax.ShapeDtypeStruct((half + tail_rows(count), width), BF16),
            jax.ShapeDtypeStruct((half + tail_rows(count), width), BF16),
            jax.ShapeDtypeStruct((rows, wide), BF16),
            jax.ShapeDtypeStruct((rows, width), F32),
        ],
        scratch_shapes=[
            pltpu.VMEM((width, width), BF16),
            pltpu.VMEM((steps, width, step), BF16),
            pltpu.VMEM((steps, step, width), BF16),
            pltpu.SemaphoreType.DMA((1 + 2 * steps,)),
            pltpu.VMEM((rows, 4 * rows + LANES), F32),
            pltpu.VMEM((rows, width), F32),
            pltpu.VMEM((rows, LANES), F32),
            pltpu.VMEM((rows, width), F32),
            pltpu.VMEM((rows, width), BF16),
            pltpu.VMEM((rows, width), F32),
            pltpu.VMEM((rows, width), F32),
            pltpu.VMEM((rows, width), BF16),
        ],
        compiler_params=pltpu.CompilerParams(vmem_limit_bytes=36 * MIB),
        cost_estimate=pl.CostEstimate(flops=1 << 31, bytes_accessed=1000, transcendentals=0),
        name="middle",
    )(
        qkv_a, qkv_b, marks_a, marks_b, prefix_kv, *own, *cots, gain[None], bias[None], *kept_in_hbm(w_out, w_fc, w_proj)
    )


def key_grads(keys, values, queries, grads, turned_marks, pair, low, mask):
    rows = keys.shape[0]
    scale = jnp.asarray(HEAD**-0.5, BF16)
    left = jnp.concatenate(
        [two_heads(keys * scale, low), picks(rows, pair, 0, -1.0).astype(BF16)], 1
    )
    scores = nn(left, jnp.concatenate([queries.T, turned_marks], 0))
    weights = jnp.exp(scores + jnp.concatenate([mask, mask], 0))
    left = jnp.concatenate(
        [two_heads(values, low), picks(rows, pair, 3 * HEADS, -1.0).astype(BF16)], 1
    )
    slopes = weights * nn(left, jnp.concatenate([grads.T, turned_marks], 0))
    key_grad = nn(slopes.astype(BF16), queries)
    value_grad = nn(weights.astype(BF16), grads)
    return join_heads(key_grad, low) * HEAD**-0.5, join_heads(value_grad, low)


GROUP = 8


def prefix_rows(count):
    return -(-2 * count // GROUP) * GROUP


def tail_rows(count):
    return -(-(prefix_rows(count) + GROUP) // PRE_ROWS) * PRE_ROWS


def prefix_kernel(used, queries, grads, prefix_kv, out):
    count, rows, width = prefix_kv.shape[0], grads.shape[0], grads.shape[1] - LANES
    marks = grads[:, width:].T
    low = head_mask(count)
    mask = jnp.where(iota((count, rows), 0) < used, 0.0, NEG)

    def step(pair, carry):
        at = pl.ds(pl.multiple_of(pair * LANES, LANES), LANES)
        at_v = pl.ds(pl.multiple_of(width + pair * LANES, LANES), LANES)
        key_grad, value_grad = key_grads(
            prefix_kv[:, at], prefix_kv[:, at_v], queries[:rows, at], grads[:, at], marks, pair, low, mask
        )
        out[:, at] = key_grad.astype(BF16)
        out[:, at_v] = value_grad.astype(BF16)
        return carry

    lax.fori_loop(0, HEADS // 2, step, 0, unroll=True)


def prefix_part(count, qkv_a, grads, prefix_kv):
    return pl.pallas_call(
        partial(prefix_kernel, count),
        in_specs=[vmem()] * 3,
        out_specs=vmem(),
        out_shape=jax.ShapeDtypeStruct(prefix_kv.shape, BF16),
        compiler_params=pltpu.CompilerParams(vmem_limit_bytes=8 * MIB),
        cost_estimate=pl.CostEstimate(flops=1000, bytes_accessed=1000, transcendentals=0),
        name="prefix",
    )(qkv_a, grads, prefix_kv)


def pack_kernel(count, grads, own, part_0, part_1, part_2, _0, _1, back_0, back_1):
    total = own[...].astype(F32) + part_0[...].astype(F32)
    total = total + (part_1[...].astype(F32) + part_2[...].astype(F32))
    width = total.shape[1] // 2
    rows = tail_rows(count)
    both = jnp.concatenate([total[:count, :width], total[:count, width:]], 0)
    marks = grads[:, width:].astype(F32).T
    starts = [part * HEADS + first for first in range(0, HEADS, GROUP) for part in range(3)]
    logs = jnp.concatenate([marks[i : i + GROUP] for i in starts], 1)
    logs = jnp.concatenate([logs, jnp.zeros((GROUP, width - logs.shape[1]), F32)], 1)
    tail = pad_rows(jnp.concatenate([pad_rows(both, prefix_rows(count)), logs], 0), rows).astype(BF16)
    at = pl.ds(back_0.shape[0] - rows, rows)
    back_0[at] = tail
    back_1[at] = tail


def pack(count, grads, terms, back_0, back_1):
    return pl.pallas_call(
        partial(pack_kernel, count),
        in_specs=[vmem()] * 7,
        out_specs=[vmem()] * 2,
        out_shape=[jax.ShapeDtypeStruct(back_0.shape, BF16)] * 2,
        input_output_aliases={5: 0, 6: 1},
        compiler_params=pltpu.CompilerParams(vmem_limit_bytes=4 * MIB),
        cost_estimate=pl.CostEstimate(flops=1 << 20, bytes_accessed=1 << 19, transcendentals=0),
        name="pack",
    )(grads, *terms, back_0, back_1)


def unpack_kernel(count, home_0, home_1, out):
    width = out.shape[1] // 2
    rows = tail_rows(count)
    at = pl.ds(home_0.shape[0] - rows, rows)
    first, second = home_0[at].astype(F32), home_1[at].astype(F32)
    total = first + second
    out[:, :width] = pad_rows(total[:count], PRE_ROWS).astype(BF16)
    out[:, width:] = pad_rows(total[count : 2 * count], PRE_ROWS).astype(BF16)


def unpack(count, width, home_0, home_1):
    return pl.pallas_call(
        partial(unpack_kernel, count),
        in_specs=[vmem()] * 2,
        out_specs=vmem(),
        out_shape=jax.ShapeDtypeStruct((PRE_ROWS, 2 * width), BF16),
        compiler_params=pltpu.CompilerParams(vmem_limit_bytes=4 * MIB),
        cost_estimate=pl.CostEstimate(flops=1000, bytes_accessed=1000, transcendentals=0),
        name="unpack",
    )(home_0, home_1)


def query_kernel(
    count,
    qkv_a,
    qkv_b,
    marks_a,
    marks_b,
    prefix_kv,
    grads,
    weight,
    normed_b,
    w_queries,
    order,
    out,
    qkv_out,
    scores_bias,
    grad_query,
):
    del order
    rows, width = grad_query.shape
    scores_bias[...] = key_bias(marks_a[:rows], marks_a[...], marks_b[...], rows // 2, count)
    low = head_mask(rows)
    marks = grads[:, width:]
    marks_twice = jnp.concatenate([marks, marks], 0)
    ones = jnp.ones((LANES, 4 * rows + LANES), BF16)

    def step(pair, carry):
        at = pl.ds(pl.multiple_of(pair * LANES, LANES), LANES)
        at_k = pl.ds(pl.multiple_of(width + pair * LANES, LANES), LANES)
        at_v = pl.ds(pl.multiple_of(2 * width + pair * LANES, LANES), LANES)
        keys = with_prefix(qkv_a[:, at_k], qkv_b[:, at_k], prefix_kv[:, at])
        values = with_prefix(qkv_a[:, at_v], qkv_b[:, at_v], prefix_kv[:, at_k])
        query = two_heads(qkv_a[:rows, at] * jnp.asarray(HEAD**-0.5, BF16), low)
        tops = marks_twice * picks(rows, pair, 0, -1.0).astype(BF16)
        scores = nn(jnp.concatenate([query, tops], 1), jnp.concatenate([keys.T, ones], 0))
        mask = scores_bias[...]
        weights = jnp.exp(scores + jnp.concatenate([mask, mask], 0))
        bases = marks_twice * picks(rows, pair, 3 * HEADS, -1.0).astype(BF16)
        left = jnp.concatenate([two_heads(grads[:, at], low), bases], 1)
        slopes = weights * nn(left, jnp.concatenate([values.T, ones], 0))
        grad = join_heads(nn(slopes.astype(BF16), keys), low)
        grad_query[:, at] = (grad * HEAD**-0.5).astype(BF16)
        return carry

    lax.fori_loop(0, HEADS // 2, step, 0, unroll=True)
    out[...] = nn(grad_query[...], weight[:width])
    qkv_out[:, :width] = nn(normed_b[...], w_queries[:, :width]).astype(BF16)


def query_part(
    count, qkv_a, qkv_b, marks_a, marks_b, prefix_kv, grads, weight, normed_b, w_queries, order
):
    rows, width = grads.shape[0], grads.shape[1] - LANES
    return pl.pallas_call(
        partial(query_kernel, count),
        in_specs=[vmem()] * 9 + [pl.BlockSpec(memory_space=pl.ANY)],
        out_specs=[vmem()] * 2,
        out_shape=[jax.ShapeDtypeStruct((rows, width), F32), jax.ShapeDtypeStruct(qkv_b.shape, BF16)],
        input_output_aliases={1: 1},
        scratch_shapes=[pltpu.VMEM((rows, 4 * rows + LANES), F32), pltpu.VMEM((rows, width), BF16)],
        compiler_params=pltpu.CompilerParams(vmem_limit_bytes=16 * MIB),
        cost_estimate=pl.CostEstimate(flops=1 << 31, bytes_accessed=1000, transcendentals=0),
        name="query",
    )(qkv_a, qkv_b, marks_a, marks_b, prefix_kv, grads, weight, normed_b, w_queries, order)


def final_kernel(
    qkv_a,
    qkv_b,
    marks_a,
    marks_b,
    grads_0,
    grads_1,
    grads_2,
    grads_3,
    own_0,
    own_1,
    gain,
    grad_middle,
    grad_partial,
    weight,
    back_0,
    back_1,
    scores_bias,
    grad_keys,
):
    half, rows = own_0.shape[0], 2 * own_0.shape[0]
    width = grad_middle.shape[1]
    row, core, y_at = place()
    own = positions(iota((rows, 1), 0), half, row, core, y_at)
    other = all_positions((1, 8 * half), 1, half, row, core, y_at)
    same = nt(marks_a[:rows], jnp.concatenate([marks_a[...], marks_b[...]], 0))
    visible = jnp.logical_and(same > 0.5, own <= other)
    scores_bias[...] = jnp.where(visible, 0.0, NEG)
    low = head_mask(rows)
    blocks = (grads_0, grads_1, grads_2, grads_3)
    marks = jnp.concatenate([g[:, width:] for g in blocks], 0).T

    def step(pair, carry):
        at = pl.ds(pl.multiple_of(pair * LANES, LANES), LANES)
        at_k = pl.ds(pl.multiple_of(width + pair * LANES, LANES), LANES)
        at_v = pl.ds(pl.multiple_of(2 * width + pair * LANES, LANES), LANES)
        queries = jnp.concatenate([qkv_a[:, at], qkv_b[:, at]], 0)
        grads = jnp.concatenate([g[:, at] for g in blocks], 0)
        key_grad, value_grad = key_grads(
            qkv_a[:rows, at_k], qkv_a[:rows, at_v], queries, grads, marks, pair, low, scores_bias[...]
        )
        grad_keys[:, at] = key_grad.astype(BF16)
        grad_keys[:, at_k] = value_grad.astype(BF16)
        return carry

    lax.fori_loop(0, HEADS // 2, step, 0, unroll=True)
    grad_norm = grad_partial[...] + nn(grad_keys[...], weight[width:])
    inputs = jnp.concatenate([own_0[:, :width], own_1[:, :width]], 0).astype(F32)
    unit, inverse = norm_parts(inputs)
    out = (grad_middle[...] + norm_back(unit, inverse, gain[...], grad_norm)).astype(BF16)
    back_0[...] = out[:half]
    back_1[...] = out[half:]


def final_part(qkv_a, qkv_b, marks_a, marks_b, grads, own, gain, grad_middle, grad_partial, weight):
    rows, width = grad_middle.shape
    half = rows // 2
    return pl.pallas_call(
        final_kernel,
        in_specs=[vmem()] * 14,
        out_specs=[vmem()] * 2,
        out_shape=[jax.ShapeDtypeStruct((half, width), BF16)] * 2,
        scratch_shapes=[
            pltpu.VMEM((rows, 4 * rows), F32),
            pltpu.VMEM((rows, 2 * width), BF16),
        ],
        compiler_params=pltpu.CompilerParams(vmem_limit_bytes=16 * MIB),
        cost_estimate=pl.CostEstimate(flops=1000, bytes_accessed=1000, transcendentals=0),
        name="final",
    )(qkv_a, qkv_b, marks_a, marks_b, *grads, *own, gain[None], grad_middle, grad_partial, weight)


def routes(k):
    pairs = []
    for seq in range(4):
        for blk in range(8):
            group, z_at, y_at = seq % 2, blk // 2, blk % 2
            row = (z_at + k + 1) % 2
            pairs.append((seq * 8 + blk, (seq - group + z_at // 2) * 8 + (2 * group + row) * 2 + y_at))
    return pairs


def body_rows(
    tokens,
    segment_ids,
    ln1_gain,
    ln1_bias,
    w_qkv,
    w_out,
    ln2_gain,
    ln2_bias,
    w_fc,
    w_proj,
    prefix_embed,
    w_mlp1,
    b_mlp1,
    w_mlp2,
    b_mlp2,
    cotangent,
):
    half, _, width = tokens.shape
    everyone = ("seq", "blk")
    there = [routes(k) for k in range(2)]
    back = [[(b, a) for a, b in pairs] for pairs in there]
    swap_core = [(i, i ^ 1) for i in range(4)]
    swap_y = [(i, i ^ 1) for i in range(8)]
    swap_both = [(i, i ^ 9) for i in range(32)]
    def after(value, *done):
        return lax.optimization_barrier((value, done))[0]

    out_msgs = split_rows(tokens, segment_ids)
    cot_msgs = split_rows(cotangent)
    own = [lax.ppermute(m, everyone, there[k]) for k, m in enumerate(out_msgs)]
    prefix_kv, inner, w_near, w_back, near_embed, turned = adapter_forward(
        prefix_embed, w_mlp1, b_mlp1, w_mlp2, b_mlp2, w_qkv
    )
    count = prefix_embed.shape[0]
    own = after(own, inner)
    across = [lax.ppermute(m, "blk", swap_y) for m in own]
    beside = [lax.ppermute(m, "seq", swap_core) for m in own]
    cots = [lax.ppermute(m, everyone, there[k]) for k, m in enumerate(after(cot_msgs, beside))]
    beyond = [lax.ppermute(m, "seq", swap_core) for m in across]

    qkv_a, marks_a = project(own + beside, ln1_gain, ln1_bias, w_near)
    kv_b, marks_b, normed_b = project(across + beyond, ln1_gain, ln1_bias, w_near, 1)
    back_0, back_1, grads, grad_middle = middle_part(
        count, qkv_a, kv_b, marks_a, marks_b, prefix_kv, own, cots, ln2_gain, ln2_bias, w_out, w_fc, w_proj
    )
    grads_y = lax.ppermute(grads, "blk", swap_y)
    grads_c = lax.ppermute(grads, "seq", swap_core)
    grad_prefix_kv = prefix_part(count, qkv_a, grads, prefix_kv)
    parts = [lax.ppermute(grad_prefix_kv, "seq", [(i, i ^ far) for i in range(4)]) for far in (2, 1, 3)]
    grad_partial, qkv_b = query_part(
        count, qkv_a, kv_b, marks_a, marks_b, prefix_kv, grads, w_back, normed_b, w_near, grad_prefix_kv
    )
    packed = pack(count, grads, (grad_prefix_kv, *after(parts, grad_partial)), back_0, back_1)
    home = [lax.ppermute(packed[k], everyone, back[k]) for k in (1, 0)][::-1]
    grads_yc = lax.ppermute(after(grads_y, packed), "seq", swap_core)
    final_0, final_1 = final_part(
        qkv_a,
        qkv_b,
        marks_a,
        marks_b,
        (grads, grads_c, grads_y, grads_yc),
        own,
        ln1_gain,
        grad_middle,
        grad_partial,
        w_back,
    )
    finals = [lax.ppermute(m, everyone, back[k]) for k, m in enumerate((final_0, final_1))]
    gathered = [unpack(count, width, *home)]
    gathered += [lax.ppermute(gathered[0], "seq", swap_core), lax.ppermute(gathered[0], "blk", swap_y)]
    gathered += [lax.ppermute(gathered[0], everyone, swap_both)]
    input_grad, summed = finish(finals, gathered, near_embed, inner, turned)
    block_out, log_total = land(count, after(home, gathered[0]), half, width)
    return (block_out, input_grad, summed[0], summed[1], summed[2], summed[3], summed[4], log_total)


def solution(mesh):
    four_by_eight = mesh.shape["seq"] == 4 and mesh.shape["blk"] == 8
    placed = (
        P("blk", "seq", None),
        P("blk", "seq"),
        P(),
        P(),
        P(),
        P(),
        P(),
        P(),
        P(),
        P(),
        P(),
        P(),
        P(),
        P(),
        P(),
        P("blk", "seq", None),
    )
    return jax.shard_map(
        body_rows if four_by_eight else body_plain,
        mesh=mesh,
        in_specs=placed,
        out_specs=(
            P("blk", "seq", None),
            P("blk", "seq", None),
            P(),
            P(),
            P(),
            P(),
            P(),
            P("seq", None, "blk"),
        ),
        check_vma=False,
    )
```

```python
from functools import partial
import math

import jax
import jax.numpy as jnp
from jax import lax
from jax.experimental import pallas as pl
from jax.experimental.pallas import tpu as pltpu
from jax.sharding import PartitionSpec as P

HEADS = 16
HEAD = 64


EPS = 1e-05
NEG = -1e30
HIGH = lax.Precision.HIGHEST


def layer_norm(value_in, gain, bias):
    average = jnp.mean(value_in, axis=-1, keepdims=True)
    centered = value_in - average
    variance = jnp.mean(centered * centered, axis=-1, keepdims=True)
    return centered * lax.rsqrt(variance + EPS) * gain + bias


def adapter(prefix_embed, w_mlp1, b_mlp1, w_mlp2, b_mlp2):
    inner_act = jnp.tanh(jnp.dot(prefix_embed, w_mlp1, precision=HIGH) + b_mlp1)
    return jnp.dot(inner_act, w_mlp2, precision=HIGH) + b_mlp2


def gelu_tanh(pre_act):
    return jax.nn.gelu(pre_act, approximate=True)


def split_heads(block_in):
    return block_in.reshape(block_in.shape[0], block_in.shape[1], HEADS, HEAD)


def allowed(query_pos, query_seg, key_pos, key_seg):
    same_seg = query_seg.T[:, :, None] == key_seg.T[:, None, :]
    causal = key_pos[None, None, :] <= query_pos[None, :, None]
    return jnp.logical_and(same_seg, causal)[:, None]


def scores_of(query_heads, key_block, score_scale):
    return score_scale * jnp.einsum(
        "prhd,krhd->rhpk", query_heads, split_heads(key_block), preferred_element_type=jnp.float32
    )


def block_grads(
    query_heads,
    grad_heads,
    log_total,
    slope_base,
    query_pos,
    query_seg,
    key_block,
    value_block,
    key_pos,
    key_seg,
    score_scale,
):
    scores = scores_of(query_heads, key_block, score_scale)
    scores = jnp.where(allowed(query_pos, query_seg, key_pos, key_seg), scores, NEG)
    weights = jnp.exp(scores - log_total[..., None])
    grad_weights = jnp.einsum(
        "prhd,krhd->rhpk", grad_heads, split_heads(value_block), preferred_element_type=jnp.float32
    )
    slopes = (weights * (grad_weights - slope_base[..., None])).astype(jnp.bfloat16)
    return (weights.astype(jnp.bfloat16), slopes)


def body_plain(
    tokens,
    segment_ids,
    ln1_gain,
    ln1_bias,
    w_qkv,
    w_out,
    ln2_gain,
    ln2_bias,
    w_fc,
    w_proj,
    prefix_embed,
    w_mlp1,
    b_mlp1,
    w_mlp2,
    b_mlp2,
    cotangent,
):
    pos_dev, row_count, width = tokens.shape
    score_scale = HEAD ** (-0.5)
    flat_rows = pos_dev * row_count
    own_pos = lax.axis_index("blk") * pos_dev + jnp.arange(pos_dev)
    inputs = tokens.astype(jnp.float32).reshape(flat_rows, width)
    normed_one = layer_norm(inputs, ln1_gain, ln1_bias).astype(jnp.bfloat16)
    projected = jnp.dot(normed_one, w_qkv, preferred_element_type=jnp.float32).astype(jnp.bfloat16)
    queries = projected[:, :width].reshape(pos_dev, row_count, width)
    keys = projected[:, width : 2 * width].reshape(pos_dev, row_count, width)
    values = projected[:, 2 * width :].reshape(pos_dev, row_count, width)
    query_heads = split_heads(queries)
    prefix_low = adapter(prefix_embed, w_mlp1, b_mlp1, w_mlp2, b_mlp2).astype(jnp.bfloat16)
    prefix_keys = prefix_low[:, :width].reshape(-1, HEADS, HEAD)
    prefix_values = prefix_low[:, width:].reshape(-1, HEADS, HEAD)
    prefix_scores = score_scale * jnp.einsum(
        "prhd,jhd->rhpj", query_heads, prefix_keys, preferred_element_type=jnp.float32
    )
    start_top = jnp.max(prefix_scores, -1)
    start_weights = jnp.exp(prefix_scores - start_top[..., None])
    start_denom = jnp.sum(start_weights, -1)
    start_numer = jnp.einsum(
        "rhpj,jhd->rhpd",
        start_weights.astype(jnp.bfloat16),
        prefix_values,
        preferred_element_type=jnp.float32,
    )
    start_state = (start_top, start_denom, start_numer)
    running = start_state
    key_shards = lax.all_gather(keys, "blk", axis=0, tiled=True)
    value_shards = lax.all_gather(values, "blk", axis=0, tiled=True)
    seg_shards = lax.all_gather(segment_ids, "blk", axis=0, tiled=True)
    num_rows = key_shards.shape[0]
    forward_stride = math.gcd(num_rows, 512)

    def inner(state, block_index):
        running_top, denominator, numerator = state
        offset = block_index * forward_stride
        key_block = lax.dynamic_slice_in_dim(key_shards, offset, forward_stride, 0)
        value_block = lax.dynamic_slice_in_dim(value_shards, offset, forward_stride, 0)
        seg_block = lax.dynamic_slice_in_dim(seg_shards, offset, forward_stride, 0)
        key_pos = offset + jnp.arange(forward_stride)
        scores = jnp.where(
            allowed(own_pos, segment_ids, key_pos, seg_block),
            scores_of(query_heads, key_block, score_scale),
            NEG,
        )
        new_top = jnp.maximum(running_top, jnp.max(scores, -1))
        fading = jnp.exp(running_top - new_top)
        weights = jnp.exp(scores - new_top[..., None])
        denominator = denominator * fading + jnp.sum(weights, -1)
        numerator = numerator * fading[..., None] + jnp.einsum(
            "rhpk,krhd->rhpd",
            weights.astype(jnp.bfloat16),
            split_heads(value_block),
            preferred_element_type=jnp.float32,
        )
        return ((new_top, denominator, numerator), None)

    running, _ = lax.scan(inner, running, jnp.arange(num_rows // forward_stride))
    final_top, final_denom, final_numer = running
    log_total = final_top + jnp.log(final_denom)
    attended = final_numer / final_denom[..., None]
    attended_rows = jnp.transpose(attended, (2, 0, 1, 3)).reshape(flat_rows, width)
    middle = inputs + jnp.dot(
        attended_rows.astype(jnp.bfloat16), w_out, preferred_element_type=jnp.float32
    )
    normed_two = layer_norm(middle, ln2_gain, ln2_bias).astype(jnp.bfloat16)
    hidden_pre = jnp.dot(normed_two, w_fc, preferred_element_type=jnp.float32)
    hidden_act = gelu_tanh(hidden_pre).astype(jnp.bfloat16)
    outputs = middle + jnp.dot(hidden_act, w_proj, preferred_element_type=jnp.float32)
    block_out = outputs.astype(jnp.bfloat16).reshape(pos_dev, row_count, width)
    grad_out = cotangent.reshape(flat_rows, width)
    grad_act = jnp.dot(grad_out, w_proj.T, preferred_element_type=jnp.float32)
    _, gelu_back = jax.vjp(gelu_tanh, hidden_pre)
    grad_pre = gelu_back(grad_act)[0].astype(jnp.bfloat16)
    grad_norm_two = jnp.dot(grad_pre, w_fc.T, preferred_element_type=jnp.float32)
    _, norm_two_back = jax.vjp(partial(layer_norm, gain=ln2_gain, bias=ln2_bias), middle)
    grad_middle = grad_out.astype(jnp.float32) + norm_two_back(grad_norm_two)[0]
    grad_attended = jnp.dot(
        grad_middle.astype(jnp.bfloat16), w_out.T, preferred_element_type=jnp.float32
    ).astype(jnp.bfloat16)
    grad_flat = grad_attended.reshape(pos_dev, row_count, width)
    grad_heads = split_heads(grad_flat)
    slope_base = jnp.sum(jnp.transpose(grad_heads.astype(jnp.float32), (1, 2, 0, 3)) * attended, -1)
    prefix_weights = jnp.exp(prefix_scores - log_total[..., None])
    prefix_dw = jnp.einsum(
        "prhd,jhd->rhpj", grad_heads, prefix_values, preferred_element_type=jnp.float32
    )
    prefix_slopes = (prefix_weights * (prefix_dw - slope_base[..., None])).astype(jnp.bfloat16)
    grad_query = score_scale * jnp.einsum(
        "rhpj,jhd->prhd", prefix_slopes, prefix_keys, preferred_element_type=jnp.float32
    )
    grad_pkeys = score_scale * jnp.einsum(
        "rhpj,prhd->jhd", prefix_slopes, query_heads, preferred_element_type=jnp.float32
    )
    grad_pvalues = jnp.einsum(
        "rhpj,prhd->jhd",
        prefix_weights.astype(jnp.bfloat16),
        grad_heads,
        preferred_element_type=jnp.float32,
    )
    grad_prefix_kv = jnp.concatenate(
        [grad_pkeys.reshape(-1, width), grad_pvalues.reshape(-1, width)], -1
    )
    keys_all, values_all, segs_all = (
        lax.all_gather(keys, "blk", axis=0, tiled=True),
        lax.all_gather(values, "blk", axis=0, tiled=True),
        lax.all_gather(segment_ids, "blk", axis=0, tiled=True),
    )
    length = keys_all.shape[0]
    stride = math.gcd(length, 512)

    def backward_step(grad_q, block_index):
        offset = block_index * stride
        key_block = lax.dynamic_slice_in_dim(keys_all, offset, stride, 0)
        value_block = lax.dynamic_slice_in_dim(values_all, offset, stride, 0)
        seg_block = lax.dynamic_slice_in_dim(segs_all, offset, stride, 0)
        key_pos = offset + jnp.arange(stride)
        weights_low, slopes = block_grads(
            query_heads,
            grad_heads,
            log_total,
            slope_base,
            own_pos,
            segment_ids,
            key_block,
            value_block,
            key_pos,
            seg_block,
            score_scale,
        )
        grad_q = grad_q + score_scale * jnp.einsum(
            "rhpk,krhd->prhd", slopes, split_heads(key_block), preferred_element_type=jnp.float32
        )
        key_term = score_scale * jnp.einsum(
            "rhpk,prhd->krhd", slopes, query_heads, preferred_element_type=jnp.float32
        )
        value_term = jnp.einsum(
            "rhpk,prhd->krhd", weights_low, grad_heads, preferred_element_type=jnp.float32
        )
        return (
            grad_q,
            (
                key_term.reshape(stride, row_count, width),
                value_term.reshape(stride, row_count, width),
            ),
        )

    grad_query, (key_terms, value_terms) = lax.scan(
        backward_step, grad_query, jnp.arange(length // stride)
    )
    key_terms = key_terms.reshape(length, row_count, width)
    value_terms = value_terms.reshape(length, row_count, width)
    grad_keys, grad_values = (
        lax.psum_scatter(key_terms, "blk", scatter_dimension=0, tiled=True),
        lax.psum_scatter(value_terms, "blk", scatter_dimension=0, tiled=True),
    )
    grad_proj = jnp.concatenate(
        [
            grad_query.reshape(flat_rows, width).astype(jnp.bfloat16),
            grad_keys.reshape(flat_rows, width).astype(jnp.bfloat16),
            grad_values.reshape(flat_rows, width).astype(jnp.bfloat16),
        ],
        -1,
    )
    grad_norm_one = jnp.dot(grad_proj, w_qkv.T, preferred_element_type=jnp.float32)
    _, norm_one_back = jax.vjp(partial(layer_norm, gain=ln1_gain, bias=ln1_bias), inputs)
    input_grad = (grad_middle + norm_one_back(grad_norm_one)[0]).reshape(pos_dev, row_count, width)
    _, adapter_back = jax.vjp(adapter, prefix_embed, w_mlp1, b_mlp1, w_mlp2, b_mlp2)
    local_grads = adapter_back(grad_prefix_kv)
    summed = lax.psum(
        (local_grads[0], local_grads[1], local_grads[2], local_grads[3], local_grads[4]),
        ("seq", "blk"),
    )
    return (block_out, input_grad, summed[0], summed[1], summed[2], summed[3], summed[4], log_total)


F32 = jnp.float32
BF16 = jnp.bfloat16
LANES = 128
PRE_ROWS = 16
MIB = 1 << 20


def nn(left, right):
    return jnp.dot(left, right, preferred_element_type=F32)


def nt(left, right):
    return lax.dot_general(left, right, (((1,), (1,)), ((), ())), preferred_element_type=F32)


def norm_parts(value_in):
    average = jnp.mean(value_in, axis=-1, keepdims=True)
    centered = value_in - average
    variance = jnp.mean(centered * centered, axis=-1, keepdims=True)
    inverse = lax.rsqrt(variance + EPS)
    return centered * inverse, inverse


def norm_back(unit, inverse, gain, grad):
    scaled = grad * gain
    first = jnp.mean(scaled, axis=-1, keepdims=True)
    second = jnp.mean(scaled * unit, axis=-1, keepdims=True)
    return inverse * (scaled - first - unit * second)


def iota(shape, dim):
    return lax.broadcasted_iota(jnp.int32, shape, dim)


def place():
    blk = lax.axis_index("blk")
    return (blk // 2) % 2, lax.axis_index("seq") % 2, blk % 2


def positions(index, half, row, core, y_at):
    upper = (index >= half).astype(jnp.int32)
    slot = 1 - (upper + row - 2 * upper * row)
    block = (2 * core + slot) * 2 + y_at
    return block * half + index - upper * half


def members(core, y_at):
    return ((core, y_at), (1 - core, y_at), (core, 1 - y_at), (1 - core, 1 - y_at))


def all_positions(shape, dim, half, row, core, y_at):
    part = tuple(2 * half if d == dim else n for d, n in enumerate(shape))
    return jnp.concatenate(
        [positions(iota(part, dim), half, row, c, y) for c, y in members(core, y_at)], dim
    )


def vmem():
    return pl.BlockSpec(memory_space=pltpu.VMEM)


def hbm():
    return pl.BlockSpec(memory_space=pltpu.HBM)


def kept_in_hbm(*arrays):
    return [pltpu.with_memory_space_constraint(a, pltpu.HBM) for a in arrays]


def by_tiles(block):
    half, pair, width = block.shape
    tiles = jnp.transpose(block.reshape(half, pair, width // LANES, LANES), (0, 2, 1, 3))
    return tiles.reshape(half, pair * width // LANES, LANES)


def from_tiles(tiles, width):
    half, count, _ = tiles.shape
    pair = count * LANES // width
    block = jnp.transpose(tiles.reshape(half, width // LANES, pair, LANES), (0, 2, 1, 3))
    return block.reshape(half, pair, width)


def odd_place():
    return (lax.axis_index("blk") // 2) % 2 == 0


def split_kernel(marked, *refs):
    tokens, ids, (out_0, out_1, work) = refs[0], refs[1], refs[-3:]
    half, count, _ = tokens.shape
    odd = odd_place()
    work[pl.ds(0, half * count)] = tokens[...].astype(F32).reshape(half * count, LANES)
    for i in range(count // 2):
        at = pl.ds(i * LANES, LANES)
        first, second = (work[pl.ds(2 * i + r, half, stride=count)] for r in range(2))
        out_0[:, at] = jnp.where(odd, second, first).astype(BF16)
        out_1[:, at] = jnp.where(odd, first, second).astype(BF16)
    if marked:
        width = count // 2 * LANES
        first, second = (
            jnp.where(iota((LANES, half), 0) == ids[r : r + 1], 1.0, 0.0).T for r in range(2)
        )
        out_0[:, width:] = jnp.where(odd, second, first).astype(BF16)
        out_1[:, width:] = jnp.where(odd, first, second).astype(BF16)


def split_rows(block, segment_ids=None):
    tiles = by_tiles(block)
    half, count, _ = tiles.shape
    extra = () if segment_ids is None else kept_in_hbm(segment_ids.T)
    width = count // 2 * LANES + LANES * len(extra)
    return pl.pallas_call(
        partial(split_kernel, bool(extra)),
        in_specs=[vmem()] * (1 + len(extra)),
        out_specs=[vmem()] * 2,
        out_shape=[jax.ShapeDtypeStruct((half, width), BF16)] * 2,
        scratch_shapes=[pltpu.VMEM(((half + 1) * count, LANES), F32)],
        compiler_params=pltpu.CompilerParams(vmem_limit_bytes=4 * MIB),
        cost_estimate=pl.CostEstimate(flops=1 << 31, bytes_accessed=1000, transcendentals=0),
        name="split",
    )(*kept_in_hbm(tiles), *extra)


def place_rows(msg_0, msg_1, work):
    count = 2 * msg_0.shape[1] // LANES
    half = work.shape[0] // count - 1
    odd = odd_place()
    for i in range(count // 2):
        at = pl.ds(i * LANES, LANES)
        one, two = msg_0[:half, at].astype(F32), msg_1[:half, at].astype(F32)
        work[pl.ds(2 * i, half, stride=count)] = jnp.where(odd, two, one)
        work[pl.ds(2 * i + 1, half, stride=count)] = jnp.where(odd, one, two)


def land_kernel(first_row, msg_0, msg_1, out, logs, work):
    half = out.shape[0]
    heads = logs.shape[1]
    place_rows(msg_0, msg_1, work)
    out[...] = work[pl.ds(0, half * out.shape[1])].reshape(out.shape).astype(out.dtype)
    odd = odd_place()
    found = []
    for k, message in enumerate((msg_0, msg_1)):
        rows = message[half:].astype(F32)[first_row : first_row + GROUP]
        slots = [rows[:, i * LANES + k * half : i * LANES + (k + 1) * half] for i in range(3 * heads // GROUP)]
        groups = [slots[i] + slots[i + 1] + slots[i + 2] for i in range(0, len(slots), 3)]
        found.append(jnp.concatenate(groups, 0))
    logs[0] = jnp.where(odd, found[1], found[0])
    logs[1] = jnp.where(odd, found[0], found[1])


def land(count_prefix, messages, half, width):
    count = 2 * width // LANES
    out = pl.pallas_call(
        partial(land_kernel, prefix_rows(count_prefix)),
        in_specs=[vmem()] * 2,
        out_specs=[vmem()] * 2,
        out_shape=[
            jax.ShapeDtypeStruct((half, count, LANES), BF16),
            jax.ShapeDtypeStruct((2, HEADS, half), F32),
        ],
        scratch_shapes=[pltpu.VMEM(((half + 1) * count, LANES), F32)],
        compiler_params=pltpu.CompilerParams(vmem_limit_bytes=4 * MIB),
        cost_estimate=pl.CostEstimate(flops=1000, bytes_accessed=1000, transcendentals=0),
        name="land",
    )(*messages)
    return from_tiles(out[0], width), out[1]


def project_kernel(count, first, *refs):
    messages, (gain, bias, weight, out, marks, normed) = refs[:count], refs[count:]
    half, width = messages[0].shape[0], normed.shape[1]
    for i, message in enumerate(messages):
        rows = pl.ds(i * half, half)
        unit, _ = norm_parts(message[:, :width].astype(F32))
        normed[rows] = (unit * gain[...] + bias[...]).astype(BF16)
        marks[rows] = message[:, width:]
    for i in range(first, 3):
        at = pl.ds(i * width, width)
        out[:, at] = nn(normed[...], weight[:, at]).astype(BF16)


def project(messages, gain, bias, weight, first=0):
    count, half = len(messages), messages[0].shape[0]
    width, columns = weight.shape
    rows = count * half
    return pl.pallas_call(
        partial(project_kernel, count, first),
        in_specs=[vmem()] * (count + 3),
        out_specs=[vmem()] * (2 + first),
        out_shape=[
            jax.ShapeDtypeStruct((rows, columns), BF16),
            jax.ShapeDtypeStruct((rows, LANES), BF16),
        ]
        + [jax.ShapeDtypeStruct((rows, width), BF16)] * first,
        scratch_shapes=[pltpu.VMEM((rows, width), BF16)] * (1 - first),
        compiler_params=pltpu.CompilerParams(vmem_limit_bytes=16 * MIB),
        cost_estimate=pl.CostEstimate(
            flops=2 * rows * width * columns, bytes_accessed=2 * width * columns, transcendentals=0
        ),
        name="project",
    )(*messages, gain[None], bias[None], weight)


def halves(value_in):
    high = value_in.astype(BF16)
    return high, (value_in - high.astype(F32)).astype(BF16)


def pad_rows(value_in, rows):
    if rows == value_in.shape[0]:
        return value_in
    return jnp.concatenate(
        [value_in, jnp.zeros((rows - value_in.shape[0], value_in.shape[1]), value_in.dtype)], 0
    )


def three_products(product, left, weight):
    rows = left.shape[0]
    high, low = halves(left)
    w_high, w_low = halves(weight)
    both = product(jnp.concatenate([high, low], 0), w_high)
    return both[:rows] + both[rows:] + product(high, w_low)


def adapter_kernel(
    h_embed,
    w_mlp1,
    h_mlp1,
    w_mlp2,
    h_mlp2,
    w_qkv,
    out,
    inner,
    v_qkv,
    w_back,
    embed,
    turned,
    v_mlp1,
    v_mlp2,
    b_mlp1,
    b_mlp2,
    sems,
):
    steps, step = v_mlp2.shape[0], v_mlp2.shape[2]
    small = []
    for i, (source, target) in enumerate(
        ((h_embed, embed), (h_mlp1, b_mlp1), (h_mlp2, b_mlp2), (w_mlp1, v_mlp1))
    ):
        small.append(pltpu.make_async_copy(source, target, sems.at[steps + i]))
        small[-1].start()
    rest = []
    for i in range(steps):
        copy = pltpu.make_async_copy(w_mlp2.at[:, pl.ds(i * step, step)], v_mlp2.at[i], sems.at[i])
        copy.start()
        rest.append(copy)
    width = w_qkv.shape[0]
    weights = []
    for i in (1, 2, 0):
        at = pl.ds(i * width, width)
        weights.append(
            pltpu.make_async_copy(w_qkv.at[:, at], v_qkv.at[:, at], sems.at[steps + len(small) + i])
        )
        weights[-1].start()
    for copy in small:
        copy.wait()
    source = pad_rows(embed[...], PRE_ROWS)
    act = jnp.tanh(three_products(nn, source, v_mlp1[...]) + b_mlp1[...])
    inner[...] = act
    columns, hidden = steps * step, v_mlp1.shape[1]
    for i in range(v_mlp1.shape[0] // hidden):
        part = v_mlp1[pl.ds(i * hidden, hidden)].astype(BF16)
        turned[pl.ds(columns + i * hidden, hidden)] = part.T
    for i, copy in enumerate(rest):
        copy.wait()
        turned[pl.ds(i * step, step)] = v_mlp2[i].astype(BF16).T
        span = pl.ds(i * step, step)
        part = three_products(nn, act, v_mlp2[i]) + b_mlp2[:, span]
        out[:, span] = jnp.where(iota(part.shape, 0) < embed.shape[0], part, 0.0).astype(BF16)
    for i, copy in zip((1, 2, 0), weights):
        at = pl.ds(i * width, width)
        copy.wait()
        w_back[at] = v_qkv[:, at].T


def adapter_forward(embed, w_mlp1, b_mlp1, w_mlp2, b_mlp2, w_qkv):
    width, hidden = w_mlp1.shape
    columns = w_mlp2.shape[1]
    steps = 4
    return pl.pallas_call(
        adapter_kernel,
        in_specs=[hbm()] * 6,
        out_specs=[vmem()] * 6,
        out_shape=[
            jax.ShapeDtypeStruct((PRE_ROWS, columns), BF16),
            jax.ShapeDtypeStruct((PRE_ROWS, hidden), F32),
            pltpu.VMEM(w_qkv.shape, w_qkv.dtype),
            pltpu.VMEM(w_qkv.shape[::-1], w_qkv.dtype),
            pltpu.VMEM(embed.shape, F32),
            pltpu.VMEM((columns + width, hidden), BF16),
        ],
        scratch_shapes=[
            pltpu.VMEM((width, hidden), F32),
            pltpu.VMEM((steps, hidden, columns // steps), F32),
            pltpu.VMEM((1, hidden), F32),
            pltpu.VMEM((1, columns), F32),
            pltpu.SemaphoreType.DMA((7 + steps,)),
        ],
        compiler_params=pltpu.CompilerParams(vmem_limit_bytes=20 * MIB),
        cost_estimate=pl.CostEstimate(flops=1 << 32, bytes_accessed=6 * MIB, transcendentals=1 << 13),
        name="adapter",
    )(*kept_in_hbm(embed, w_mlp1, b_mlp1[None], w_mlp2, b_mlp2[None], w_qkv))


def outer(left, right):
    l_high, l_low = halves(left)
    r_high, r_low = halves(right)
    return lax.dot_general(
        jnp.concatenate([l_high, l_high, l_low], 0),
        jnp.concatenate([r_high, r_low, r_high], 0),
        (((0,), (0,)), ((), ())),
        preferred_element_type=F32,
    )


def two_products(left, weight):
    high, low = halves(left)
    both = nn(jnp.concatenate([high, low], 0), weight)
    return both[: left.shape[0]] + both[left.shape[0] :]


def adapter_back_kernel(
    home_0,
    home_1,
    part_0,
    part_1,
    part_2,
    part_3,
    embed,
    inner,
    turned,
    block,
    grad_prefix,
    grad_mlp1,
    grad_bias1,
    grad_mlp2,
    grad_bias2,
    o_block,
    o_mlp1,
    o_mlp2,
    sems,
):
    steps, step = o_mlp2.shape[0], o_mlp2.shape[2]
    first, second, third, fourth = (p[...].astype(F32) for p in (part_0, part_1, part_2, part_3))
    grads = (first + second) + (third + fourth)
    act = inner[...]
    stores = []
    grad_bias2[...] = jnp.sum(grads, 0, keepdims=True)
    for i in range(steps):
        o_mlp2[i] = outer(act, grads[:, i * step : (i + 1) * step])
        stores.append(
            pltpu.make_async_copy(o_mlp2.at[i], grad_mlp2.at[:, pl.ds(i * step, step)], sems.at[i])
        )
        stores[-1].start()
    columns, (width, hidden) = steps * step, o_mlp1.shape
    place_rows(home_0, home_1, o_block)
    stores.append(pltpu.make_async_copy(o_block.at[pl.ds(0, block.shape[0])], block, sems.at[steps + 1]))
    stores[-1].start()
    back = two_products(grads, turned[:columns]) * (1.0 - act * act)
    grad_bias1[...] = jnp.sum(back, 0, keepdims=True)
    o_mlp1[...] = outer(pad_rows(embed[...], PRE_ROWS), back)
    stores.append(pltpu.make_async_copy(o_mlp1, grad_mlp1, sems.at[steps]))
    stores[-1].start()
    for i in range(width // hidden):
        part = two_products(back, turned[pl.ds(columns + i * hidden, hidden)])
        grad_prefix[:, pl.ds(i * hidden, hidden)] = part[: embed.shape[0]]
    for copy in stores:
        copy.wait()


def finish(finals, parts, embed, inner, turned):
    hidden, width = turned.shape[1], embed.shape[1]
    columns = turned.shape[0] - width
    half = finals[0].shape[0]
    steps = 4
    tiles = 2 * width // LANES
    out = pl.pallas_call(
        adapter_back_kernel,
        in_specs=[vmem()] * 9,
        out_specs=[hbm(), vmem(), hbm(), vmem(), hbm(), vmem()],
        out_shape=[
            jax.ShapeDtypeStruct((half * tiles, LANES), F32),
            jax.ShapeDtypeStruct(embed.shape, F32),
            jax.ShapeDtypeStruct((width, hidden), F32),
            jax.ShapeDtypeStruct((1, hidden), F32),
            jax.ShapeDtypeStruct((hidden, columns), F32),
            jax.ShapeDtypeStruct((1, columns), F32),
        ],
        scratch_shapes=[
            pltpu.VMEM(((half + 1) * tiles, LANES), F32),
            pltpu.VMEM((width, hidden), F32),
            pltpu.VMEM((steps, hidden, columns // steps), F32),
            pltpu.SemaphoreType.DMA((steps + 2,)),
        ],
        compiler_params=pltpu.CompilerParams(vmem_limit_bytes=16 * MIB),
        cost_estimate=pl.CostEstimate(flops=1000, bytes_accessed=1000, transcendentals=0),
        name="finish",
    )(*finals, *parts, embed, inner, turned)
    block = from_tiles(out[0].reshape(half, tiles, LANES), width)
    return block, (out[1], out[2], out[3][0], out[4], out[5][0])


def head_mask(rows):
    return iota((rows, LANES), 1) < HEAD


def two_heads(pair, low):
    zero = jnp.zeros_like(pair)
    return jnp.concatenate([jnp.where(low, pair, zero), jnp.where(low, zero, pair)], 0)


def join_heads(stacked, low):
    rows = stacked.shape[0] // 2
    return jnp.where(low, stacked[:rows], stacked[rows:])


def picks(rows, pair, first, value):
    lane = iota((rows, LANES), 1)
    inside = jnp.logical_and(lane >= first, lane < first + 3 * HEADS)
    parts = [
        jnp.where(jnp.logical_and(inside, lane % HEADS == 2 * pair + i), value, 0.0) for i in range(2)
    ]
    return jnp.concatenate(parts, 0)


def three_parts(value_in, first):
    lane = iota(value_in.shape, 1)
    high = value_in.astype(BF16).astype(F32)
    rest = value_in - high
    middle = rest.astype(BF16).astype(F32)
    low = rest - middle
    part = (lane - first) // HEADS
    chosen = jnp.where(part == 0, high, jnp.where(part == 1, middle, low))
    inside = jnp.logical_and(lane >= first, lane < first + 3 * HEADS)
    return jnp.where(inside, chosen, 0.0)


def key_bias(marks_own, marks_a, marks_b, half, count):
    row, core, y_at = place()
    rows = 2 * half
    own = positions(iota((rows, 1), 0), half, row, core, y_at)
    other = all_positions((1, 8 * half), 1, half, row, core, y_at)
    same = nt(marks_own, jnp.concatenate([marks_a, marks_b], 0))
    visible = jnp.logical_and(same > 0.5, other <= own)
    token_bias = jnp.where(visible, 0.0, NEG)
    prefix_bias = jnp.where(iota((rows, LANES), 1) < count, 0.0, NEG)
    return jnp.concatenate([token_bias, prefix_bias], 1)


def with_prefix(part_a, part_b, prefix):
    pad = jnp.zeros((LANES - prefix.shape[0], prefix.shape[1]), prefix.dtype)
    return jnp.concatenate([part_a, part_b, prefix, pad], 0)


def middle_kernel(
    count,
    qkv_a,
    qkv_b,
    marks_a,
    marks_b,
    prefix_kv,
    own_0,
    own_1,
    cot_0,
    cot_1,
    gain,
    bias,
    w_out,
    w_fc,
    w_proj,
    back_0,
    back_1,
    grad_out_heads,
    grad_middle,
    v_out,
    v_fc,
    v_proj,
    sems,
    scores_bias,
    attended,
    stats,
    middle,
    normed,
    total,
    grad_norm,
    cot,
):
    half, rows = own_0.shape[0], 2 * own_0.shape[0]
    width = middle.shape[1]
    steps, step = v_fc.shape[0], v_fc.shape[2]
    copies = [pltpu.make_async_copy(w_out, v_out, sems.at[0])]
    for i in range(steps):
        span = pl.ds(i * step, step)
        copies.append(pltpu.make_async_copy(w_fc.at[:, span], v_fc.at[i], sems.at[1 + 2 * i]))
        copies.append(pltpu.make_async_copy(w_proj.at[span], v_proj.at[i], sems.at[2 + 2 * i]))
    for copy in copies:
        copy.start()

    scores_bias[...] = key_bias(marks_a[:rows], marks_a[...], marks_b[...], half, count)
    low = head_mask(rows)
    lane = iota((rows, LANES), 1)
    stats[...] = jnp.zeros_like(stats)

    def attend(pair, carry):
        at = pl.ds(pl.multiple_of(pair * LANES, LANES), LANES)
        at_k = pl.ds(pl.multiple_of(width + pair * LANES, LANES), LANES)
        at_v = pl.ds(pl.multiple_of(2 * width + pair * LANES, LANES), LANES)
        query = two_heads(qkv_a[:rows, at] * jnp.asarray(HEAD**-0.5, BF16), low)
        keys = with_prefix(qkv_a[:, at_k], qkv_b[:, at_k], prefix_kv[:, at])
        values = with_prefix(qkv_a[:, at_v], qkv_b[:, at_v], prefix_kv[:, at_k])
        scores = nt(query, keys)
        mask = scores_bias[...]
        scores = scores + jnp.concatenate([mask, mask], 0)
        top = jnp.max(scores, -1, keepdims=True)
        weights = jnp.exp(scores - top)
        denominator = jnp.sum(weights, -1, keepdims=True)
        mixed = nn(weights.astype(BF16), values) / denominator
        attended[:, at] = join_heads(mixed, low)
        log_total = top + jnp.log(denominator)
        inside = lane < 3 * HEADS
        for i in range(2):
            here = jnp.logical_and(inside, lane % HEADS == 2 * pair + i)
            stats[...] = jnp.where(here, log_total[i * rows : (i + 1) * rows], stats[...])
        return carry

    lax.fori_loop(0, HEADS // 2, attend, 0, unroll=4)

    copies[0].wait()
    inputs = jnp.concatenate([own_0[:, :width], own_1[:, :width]], 0).astype(F32)
    middle[...] = inputs + nn(attended[...].astype(BF16), v_out[...])
    unit, _ = norm_parts(middle[...])
    normed[...] = (unit * gain[...] + bias[...]).astype(BF16)
    cot[...] = jnp.concatenate([cot_0[...], cot_1[...]], 0)
    total[...] = middle[...]
    grad_norm[...] = jnp.zeros_like(grad_norm)

    def feed(i, carry):
        for which in (0, 1):
            pltpu.make_async_copy(
                (v_fc, v_proj)[which].at[i], (v_fc, v_proj)[which].at[i], sems.at[1 + 2 * i + which]
            ).wait()
        fc, proj = v_fc[i], v_proj[i]
        pre = nn(normed[...], fc)
        grad_act = nt(cot[...], proj)
        cubic = 0.044715 * pre * pre
        curve = jnp.tanh(math.sqrt(2 / math.pi) * pre * (1.0 + cubic))
        act = 0.5 * pre * (1.0 + curve)
        slope = 0.5 * (1.0 + curve) + 0.5 * math.sqrt(2 / math.pi) * pre * (1.0 - curve * curve) * (
            1.0 + 3.0 * cubic
        )
        grad_pre = (grad_act * slope).astype(BF16)
        total[...] += nn(act.astype(BF16), proj)
        grad_norm[...] += nt(grad_pre, fc)
        return carry

    lax.fori_loop(0, steps, feed, 0, unroll=True)

    out = total[...].astype(BF16)
    back_0[:half] = out[:half]
    back_1[:half] = out[half:]
    unit, inverse = norm_parts(middle[...])
    grads = cot[...].astype(F32) + norm_back(unit, inverse, gain[...], grad_norm[...])
    grad_middle[...] = grads
    grad_heads = nt(grads.astype(BF16), v_out[...]).astype(BF16)
    grad_out_heads[:, :width] = grad_heads
    product = grad_heads.astype(F32) * attended[...]
    ones = jnp.where(
        jnp.logical_and(
            iota((width, LANES), 0) // HEAD == iota((width, LANES), 1) % HEADS,
            jnp.logical_and(
                iota((width, LANES), 1) >= 3 * HEADS, iota((width, LANES), 1) < 6 * HEADS
            ),
        ),
        1.0,
        0.0,
    ).astype(BF16)
    bases = jnp.zeros((rows, LANES), F32)
    for _ in range(2):
        part = product.astype(BF16)
        bases = bases + nn(part, ones)
        product = product - part.astype(F32)
    marks = three_parts(stats[...], 0) + three_parts(bases, 3 * HEADS)
    marks = marks.astype(BF16)
    grad_out_heads[:, width:] = marks


def middle_part(count, qkv_a, qkv_b, marks_a, marks_b, prefix_kv, own, cots, gain, bias, w_out, w_fc, w_proj):
    half, width = cots[0].shape
    rows = 2 * half
    hidden = w_fc.shape[1]
    steps = 2
    step = hidden // steps
    wide = width + LANES
    return pl.pallas_call(
        partial(middle_kernel, count),
        in_specs=[vmem()] * 11 + [hbm()] * 3,
        out_specs=[vmem()] * 4,
        out_shape=[
            jax.ShapeDtypeStruct((half + tail_rows(count), width), BF16),
            jax.ShapeDtypeStruct((half + tail_rows(count), width), BF16),
            jax.ShapeDtypeStruct((rows, wide), BF16),
            jax.ShapeDtypeStruct((rows, width), F32),
        ],
        scratch_shapes=[
            pltpu.VMEM((width, width), BF16),
            pltpu.VMEM((steps, width, step), BF16),
            pltpu.VMEM((steps, step, width), BF16),
            pltpu.SemaphoreType.DMA((1 + 2 * steps,)),
            pltpu.VMEM((rows, 4 * rows + LANES), F32),
            pltpu.VMEM((rows, width), F32),
            pltpu.VMEM((rows, LANES), F32),
            pltpu.VMEM((rows, width), F32),
            pltpu.VMEM((rows, width), BF16),
            pltpu.VMEM((rows, width), F32),
            pltpu.VMEM((rows, width), F32),
            pltpu.VMEM((rows, width), BF16),
        ],
        compiler_params=pltpu.CompilerParams(vmem_limit_bytes=36 * MIB),
        cost_estimate=pl.CostEstimate(flops=1 << 31, bytes_accessed=1000, transcendentals=0),
        name="middle",
    )(
        qkv_a, qkv_b, marks_a, marks_b, prefix_kv, *own, *cots, gain[None], bias[None], *kept_in_hbm(w_out, w_fc, w_proj)
    )


def key_grads(keys, values, queries, grads, turned_marks, pair, low, mask):
    rows = keys.shape[0]
    scale = jnp.asarray(HEAD**-0.5, BF16)
    left = jnp.concatenate(
        [two_heads(keys * scale, low), picks(rows, pair, 0, -1.0).astype(BF16)], 1
    )
    scores = nn(left, jnp.concatenate([queries.T, turned_marks], 0))
    weights = jnp.exp(scores + jnp.concatenate([mask, mask], 0))
    left = jnp.concatenate(
        [two_heads(values, low), picks(rows, pair, 3 * HEADS, -1.0).astype(BF16)], 1
    )
    slopes = weights * nn(left, jnp.concatenate([grads.T, turned_marks], 0))
    key_grad = nn(slopes.astype(BF16), queries)
    value_grad = nn(weights.astype(BF16), grads)
    return join_heads(key_grad, low) * HEAD**-0.5, join_heads(value_grad, low)


GROUP = 8


def prefix_rows(count):
    return -(-2 * count // GROUP) * GROUP


def tail_rows(count):
    return -(-(prefix_rows(count) + GROUP) // PRE_ROWS) * PRE_ROWS


def prefix_kernel(used, queries, grads, prefix_kv, out):
    count, rows, width = prefix_kv.shape[0], grads.shape[0], grads.shape[1] - LANES
    marks = grads[:, width:].T
    low = head_mask(count)
    mask = jnp.where(iota((count, rows), 0) < used, 0.0, NEG)

    def step(pair, carry):
        at = pl.ds(pl.multiple_of(pair * LANES, LANES), LANES)
        at_v = pl.ds(pl.multiple_of(width + pair * LANES, LANES), LANES)
        key_grad, value_grad = key_grads(
            prefix_kv[:, at], prefix_kv[:, at_v], queries[:rows, at], grads[:, at], marks, pair, low, mask
        )
        out[:, at] = key_grad.astype(BF16)
        out[:, at_v] = value_grad.astype(BF16)
        return carry

    lax.fori_loop(0, HEADS // 2, step, 0, unroll=True)


def prefix_part(count, qkv_a, grads, prefix_kv):
    return pl.pallas_call(
        partial(prefix_kernel, count),
        in_specs=[vmem()] * 3,
        out_specs=vmem(),
        out_shape=jax.ShapeDtypeStruct(prefix_kv.shape, BF16),
        compiler_params=pltpu.CompilerParams(vmem_limit_bytes=8 * MIB),
        cost_estimate=pl.CostEstimate(flops=1000, bytes_accessed=1000, transcendentals=0),
        name="prefix",
    )(qkv_a, grads, prefix_kv)


def pack_kernel(count, grads, own, part_0, part_1, part_2, _0, _1, back_0, back_1):
    total = own[...].astype(F32) + part_0[...].astype(F32)
    total = total + (part_1[...].astype(F32) + part_2[...].astype(F32))
    width = total.shape[1] // 2
    rows = tail_rows(count)
    both = jnp.concatenate([total[:count, :width], total[:count, width:]], 0)
    marks = grads[:, width:].astype(F32).T
    starts = [part * HEADS + first for first in range(0, HEADS, GROUP) for part in range(3)]
    logs = jnp.concatenate([marks[i : i + GROUP] for i in starts], 1)
    logs = jnp.concatenate([logs, jnp.zeros((GROUP, width - logs.shape[1]), F32)], 1)
    tail = pad_rows(jnp.concatenate([pad_rows(both, prefix_rows(count)), logs], 0), rows).astype(BF16)
    at = pl.ds(back_0.shape[0] - rows, rows)
    back_0[at] = tail
    back_1[at] = tail


def pack(count, grads, terms, back_0, back_1):
    return pl.pallas_call(
        partial(pack_kernel, count),
        in_specs=[vmem()] * 7,
        out_specs=[vmem()] * 2,
        out_shape=[jax.ShapeDtypeStruct(back_0.shape, BF16)] * 2,
        input_output_aliases={5: 0, 6: 1},
        compiler_params=pltpu.CompilerParams(vmem_limit_bytes=4 * MIB),
        cost_estimate=pl.CostEstimate(flops=1 << 20, bytes_accessed=1 << 19, transcendentals=0),
        name="pack",
    )(grads, *terms, back_0, back_1)


def unpack_kernel(count, home_0, home_1, out):
    width = out.shape[1] // 2
    rows = tail_rows(count)
    at = pl.ds(home_0.shape[0] - rows, rows)
    first, second = home_0[at].astype(F32), home_1[at].astype(F32)
    total = first + second
    out[:, :width] = pad_rows(total[:count], PRE_ROWS).astype(BF16)
    out[:, width:] = pad_rows(total[count : 2 * count], PRE_ROWS).astype(BF16)


def unpack(count, width, home_0, home_1):
    return pl.pallas_call(
        partial(unpack_kernel, count),
        in_specs=[vmem()] * 2,
        out_specs=vmem(),
        out_shape=jax.ShapeDtypeStruct((PRE_ROWS, 2 * width), BF16),
        compiler_params=pltpu.CompilerParams(vmem_limit_bytes=4 * MIB),
        cost_estimate=pl.CostEstimate(flops=1000, bytes_accessed=1000, transcendentals=0),
        name="unpack",
    )(home_0, home_1)


def query_kernel(
    count,
    qkv_a,
    qkv_b,
    marks_a,
    marks_b,
    prefix_kv,
    grads,
    weight,
    normed_b,
    w_queries,
    order,
    out,
    qkv_out,
    scores_bias,
    grad_query,
):
    del order
    rows, width = grad_query.shape
    scores_bias[...] = key_bias(marks_a[:rows], marks_a[...], marks_b[...], rows // 2, count)
    low = head_mask(rows)
    marks = grads[:, width:]
    marks_twice = jnp.concatenate([marks, marks], 0)
    ones = jnp.ones((LANES, 4 * rows + LANES), BF16)

    def step(pair, carry):
        at = pl.ds(pl.multiple_of(pair * LANES, LANES), LANES)
        at_k = pl.ds(pl.multiple_of(width + pair * LANES, LANES), LANES)
        at_v = pl.ds(pl.multiple_of(2 * width + pair * LANES, LANES), LANES)
        keys = with_prefix(qkv_a[:, at_k], qkv_b[:, at_k], prefix_kv[:, at])
        values = with_prefix(qkv_a[:, at_v], qkv_b[:, at_v], prefix_kv[:, at_k])
        query = two_heads(qkv_a[:rows, at] * jnp.asarray(HEAD**-0.5, BF16), low)
        tops = marks_twice * picks(rows, pair, 0, -1.0).astype(BF16)
        scores = nn(jnp.concatenate([query, tops], 1), jnp.concatenate([keys.T, ones], 0))
        mask = scores_bias[...]
        weights = jnp.exp(scores + jnp.concatenate([mask, mask], 0))
        bases = marks_twice * picks(rows, pair, 3 * HEADS, -1.0).astype(BF16)
        left = jnp.concatenate([two_heads(grads[:, at], low), bases], 1)
        slopes = weights * nn(left, jnp.concatenate([values.T, ones], 0))
        grad = join_heads(nn(slopes.astype(BF16), keys), low)
        grad_query[:, at] = (grad * HEAD**-0.5).astype(BF16)
        return carry

    lax.fori_loop(0, HEADS // 2, step, 0, unroll=True)
    out[...] = nn(grad_query[...], weight[:width])
    qkv_out[:, :width] = nn(normed_b[...], w_queries[:, :width]).astype(BF16)


def query_part(
    count, qkv_a, qkv_b, marks_a, marks_b, prefix_kv, grads, weight, normed_b, w_queries, order
):
    rows, width = grads.shape[0], grads.shape[1] - LANES
    return pl.pallas_call(
        partial(query_kernel, count),
        in_specs=[vmem()] * 9 + [pl.BlockSpec(memory_space=pl.ANY)],
        out_specs=[vmem()] * 2,
        out_shape=[jax.ShapeDtypeStruct((rows, width), F32), jax.ShapeDtypeStruct(qkv_b.shape, BF16)],
        input_output_aliases={1: 1},
        scratch_shapes=[pltpu.VMEM((rows, 4 * rows + LANES), F32), pltpu.VMEM((rows, width), BF16)],
        compiler_params=pltpu.CompilerParams(vmem_limit_bytes=16 * MIB),
        cost_estimate=pl.CostEstimate(flops=1 << 31, bytes_accessed=1000, transcendentals=0),
        name="query",
    )(qkv_a, qkv_b, marks_a, marks_b, prefix_kv, grads, weight, normed_b, w_queries, order)


def final_kernel(
    qkv_a,
    qkv_b,
    marks_a,
    marks_b,
    grads_0,
    grads_1,
    grads_2,
    grads_3,
    own_0,
    own_1,
    gain,
    grad_middle,
    grad_partial,
    weight,
    back_0,
    back_1,
    scores_bias,
    grad_keys,
):
    half, rows = own_0.shape[0], 2 * own_0.shape[0]
    width = grad_middle.shape[1]
    row, core, y_at = place()
    own = positions(iota((rows, 1), 0), half, row, core, y_at)
    other = all_positions((1, 8 * half), 1, half, row, core, y_at)
    same = nt(marks_a[:rows], jnp.concatenate([marks_a[...], marks_b[...]], 0))
    visible = jnp.logical_and(same > 0.5, own <= other)
    scores_bias[...] = jnp.where(visible, 0.0, NEG)
    low = head_mask(rows)
    blocks = (grads_0, grads_1, grads_2, grads_3)
    marks = jnp.concatenate([g[:, width:] for g in blocks], 0).T

    def step(pair, carry):
        at = pl.ds(pl.multiple_of(pair * LANES, LANES), LANES)
        at_k = pl.ds(pl.multiple_of(width + pair * LANES, LANES), LANES)
        at_v = pl.ds(pl.multiple_of(2 * width + pair * LANES, LANES), LANES)
        queries = jnp.concatenate([qkv_a[:, at], qkv_b[:, at]], 0)
        grads = jnp.concatenate([g[:, at] for g in blocks], 0)
        key_grad, value_grad = key_grads(
            qkv_a[:rows, at_k], qkv_a[:rows, at_v], queries, grads, marks, pair, low, scores_bias[...]
        )
        grad_keys[:, at] = key_grad.astype(BF16)
        grad_keys[:, at_k] = value_grad.astype(BF16)
        return carry

    lax.fori_loop(0, HEADS // 2, step, 0, unroll=True)
    grad_norm = grad_partial[...] + nn(grad_keys[...], weight[width:])
    inputs = jnp.concatenate([own_0[:, :width], own_1[:, :width]], 0).astype(F32)
    unit, inverse = norm_parts(inputs)
    out = (grad_middle[...] + norm_back(unit, inverse, gain[...], grad_norm)).astype(BF16)
    back_0[...] = out[:half]
    back_1[...] = out[half:]


def final_part(qkv_a, qkv_b, marks_a, marks_b, grads, own, gain, grad_middle, grad_partial, weight):
    rows, width = grad_middle.shape
    half = rows // 2
    return pl.pallas_call(
        final_kernel,
        in_specs=[vmem()] * 14,
        out_specs=[vmem()] * 2,
        out_shape=[jax.ShapeDtypeStruct((half, width), BF16)] * 2,
        scratch_shapes=[
            pltpu.VMEM((rows, 4 * rows), F32),
            pltpu.VMEM((rows, 2 * width), BF16),
        ],
        compiler_params=pltpu.CompilerParams(vmem_limit_bytes=16 * MIB),
        cost_estimate=pl.CostEstimate(flops=1000, bytes_accessed=1000, transcendentals=0),
        name="final",
    )(qkv_a, qkv_b, marks_a, marks_b, *grads, *own, gain[None], grad_middle, grad_partial, weight)


def routes(k):
    pairs = []
    for seq in range(4):
        for blk in range(8):
            group, z_at, y_at = seq % 2, blk // 2, blk % 2
            row = (z_at + k + 1) % 2
            pairs.append((seq * 8 + blk, (seq - group + z_at // 2) * 8 + (2 * group + row) * 2 + y_at))
    return pairs


def body_rows(
    tokens,
    segment_ids,
    ln1_gain,
    ln1_bias,
    w_qkv,
    w_out,
    ln2_gain,
    ln2_bias,
    w_fc,
    w_proj,
    prefix_embed,
    w_mlp1,
    b_mlp1,
    w_mlp2,
    b_mlp2,
    cotangent,
):
    half, _, width = tokens.shape
    everyone = ("seq", "blk")
    there = [routes(k) for k in range(2)]
    back = [[(b, a) for a, b in pairs] for pairs in there]
    swap_core = [(i, i ^ 1) for i in range(4)]
    swap_y = [(i, i ^ 1) for i in range(8)]
    swap_both = [(i, i ^ 9) for i in range(32)]
    def after(value, *done):
        return lax.optimization_barrier((value, done))[0]

    out_msgs = split_rows(tokens, segment_ids)
    cot_msgs = split_rows(cotangent)
    own = [lax.ppermute(m, everyone, there[k]) for k, m in enumerate(out_msgs)]
    prefix_kv, inner, w_near, w_back, near_embed, turned = adapter_forward(
        prefix_embed, w_mlp1, b_mlp1, w_mlp2, b_mlp2, w_qkv
    )
    count = prefix_embed.shape[0]
    own = after(own, inner)
    across = [lax.ppermute(m, "blk", swap_y) for m in own]
    beside = [lax.ppermute(m, "seq", swap_core) for m in own]
    cots = [lax.ppermute(m, everyone, there[k]) for k, m in enumerate([after(m, b) for m, b in zip(cot_msgs, beside)])]
    beyond = [lax.ppermute(m, "seq", swap_core) for m in across]

    qkv_a, marks_a = project(own + beside, ln1_gain, ln1_bias, w_near)
    kv_b, marks_b, normed_b = project(across + beyond, ln1_gain, ln1_bias, w_near, 1)
    back_0, back_1, grads, grad_middle = middle_part(
        count, qkv_a, kv_b, marks_a, marks_b, prefix_kv, own, cots, ln2_gain, ln2_bias, w_out, w_fc, w_proj
    )
    grads_y = lax.ppermute(grads, "blk", swap_y)
    grads_c = lax.ppermute(grads, "seq", swap_core)
    grad_prefix_kv = prefix_part(count, qkv_a, grads, prefix_kv)
    parts = [lax.ppermute(grad_prefix_kv, "seq", [(i, i ^ far) for i in range(4)]) for far in (2, 1, 3)]
    grad_partial, qkv_b = query_part(
        count, qkv_a, kv_b, marks_a, marks_b, prefix_kv, grads, w_back, normed_b, w_near, grad_prefix_kv
    )
    packed = pack(count, grads, (grad_prefix_kv, *after(parts, grad_partial)), back_0, back_1)
    home = [lax.ppermute(m, everyone, back[k]) for k, m in enumerate(packed)]
    grads_yc = lax.ppermute(after(grads_y, packed), "seq", swap_core)
    final_0, final_1 = final_part(
        qkv_a,
        qkv_b,
        marks_a,
        marks_b,
        (grads, grads_c, grads_y, grads_yc),
        own,
        ln1_gain,
        grad_middle,
        grad_partial,
        w_back,
    )
    finals = [lax.ppermute(m, everyone, back[k]) for k, m in enumerate((final_0, final_1))]
    gathered = [unpack(count, width, *home)]
    gathered += [lax.ppermute(gathered[0], "seq", swap_core), lax.ppermute(gathered[0], "blk", swap_y)]
    gathered += [lax.ppermute(gathered[0], everyone, swap_both)]
    input_grad, summed = finish(finals, gathered, near_embed, inner, turned)
    block_out, log_total = land(count, after(home, gathered[0]), half, width)
    return (block_out, input_grad, summed[0], summed[1], summed[2], summed[3], summed[4], log_total)


def solution(mesh):
    four_by_eight = mesh.shape["seq"] == 4 and mesh.shape["blk"] == 8
    placed = (
        P("blk", "seq", None),
        P("blk", "seq"),
        P(),
        P(),
        P(),
        P(),
        P(),
        P(),
        P(),
        P(),
        P(),
        P(),
        P(),
        P(),
        P(),
        P("blk", "seq", None),
    )
    return jax.shard_map(
        body_rows if four_by_eight else body_plain,
        mesh=mesh,
        in_specs=placed,
        out_specs=(
            P("blk", "seq", None),
            P("blk", "seq", None),
            P(),
            P(),
            P(),
            P(),
            P(),
            P("seq", None, "blk"),
        ),
        check_vma=False,
    )
```
